32 devices in a mesh: wall: 8 (over y, x, core), span: 4 (over z).
Axes of the slice: x: 2, y: 2, z: 4, core: 2. Of those that a mesh axis runs over, the one named last changes fastest.
Arguments:
- field: float32 [4, 3, 2, 256, 6144], P(None, None, None, 'wall', 'span'), may hold values from -6 to 6
- mean_flow: float32 [2, 256], P(None, 'wall'), may hold values from 0.2 to 1.5
- d2_coef: float32 [15, 256], P(None, 'wall'), may hold values from -2 to 2
- wall_coef: float32 [2, 8], replicated, may hold values from -0.4375 to 0.4375
- kx_index: int32 [4], replicated, may hold values from 1 to 7
- patch_of: int32 [6144], P('span'), may hold values from 0 to 63
Outputs:
- new_field: float32 [4, 3, 2, 256, 6144], P(None, None, None, 'wall', 'span')
- wall_grad: float32 [2, 4, 2, 64], replicated
The draws below stay inside these ranges and needn't reach their ends.
All inputs are finite; a program needn't handle non-finite values.
Results may differ from the reference program's by a relative error of at most 0.000073.
Values sent between devices are 32-bit elements; how exact they have to be, the bound alone decides.
No kernel may reach another device: no remote copies, remote signals or barrier semaphores. Data moves between devices by JAX's collectives and lax.ppermute only.
A program may use at most 192 MiB of HBM per device.

```python
import jax
import jax.numpy as jnp
from jax import lax

KX = 4
NZ = 6144
NY = 256
HALO = 7
STEN = 15
PATCH = 64


def set_ends(values, own_key, low, largest):
    longest = values.shape.index(max(values.shape))
    spots = []
    for shift in (0, 1):
        where = [jax.random.randint(jax.random.fold_in(own_key, axis), (), 0, length) for axis, length in enumerate(values.shape)]
        where[longest] = (where[longest] + shift) % values.shape[longest]
        spots.append(tuple(where))
    return values.at[spots[0]].set(low).at[spots[1]].set(largest)


def level_of(own_key, dims, cuts, least, largest):
    factor_of, own = 1.0, jax.random.fold_in(own_key, 6)
    for position, shards_of in cuts:
        draws = jnp.exp(jax.random.uniform(jax.random.fold_in(own, position), (shards_of,), jnp.float32, least / len(cuts), largest / len(cuts)))
        factor_of = factor_of * jnp.repeat(draws, dims[position] // shards_of).reshape([-1 if axis == position else 1 for axis in range(len(dims))])
    return factor_of


def noise(key, shape, spread, most, shards=(), kind=jnp.bfloat16):
    level = level_of(key, shape, shards, -0.22, 0.18) if shards else 1.0
    array = jax.random.normal(key, shape, jnp.float32) * spread * level
    return jnp.minimum(jnp.maximum(array, -most), most).astype(kind)


def setup_inputs(seed: int = 0) -> dict:
    arg_keys = jax.random.split(jax.random.key(seed), 7)
    return {
        "field": noise(arg_keys[0], (KX, 3, 2, NY, NZ), 1.0, 6.0, ((3, 8), (4, 4)), jnp.float32),
        "mean_flow": jnp.clip(0.2 + 1.3 * jax.random.uniform(arg_keys[1], (2, NY), jnp.float32) ** level_of(arg_keys[1], (2, NY), ((1, 8),), -0.2, 0.2), 0.2, 1.5),
        "d2_coef": noise(arg_keys[2], (STEN, NY), 0.15, 2.0, ((1, 8),), jnp.float32),
        "wall_coef": noise(arg_keys[3], (2, HALO + 1), 0.03, 0.4375, (), jnp.float32),
        "kx_index": set_ends(jax.random.randint(arg_keys[4], (KX,), 1, 8), jax.random.fold_in(arg_keys[4], 1), 1, 7).astype(jnp.int32),
        "patch_of": set_ends(jax.random.randint(arg_keys[5], (NZ,), 0, PATCH), jax.random.fold_in(arg_keys[5], 1), 0, PATCH - 1).astype(jnp.int32),
    }


TAU = 0.25
VIS = 0.5


def reference(field, mean_flow, d2_coef, wall_coef, kx_index, patch_of):
    wave_number = kx_index.astype(jnp.float32) * 0.25
    padded = jnp.pad(field, ((0, 0), (0, 0), (0, 0), (HALO, HALO), (0, 0)))
    diffusion = jnp.zeros_like(field)
    for offset in range(STEN):
        diffusion = diffusion + d2_coef[offset][:, None] * padded[:, :, :, offset:offset + NY, :]
    complex_field = field[:, :, 0] + 1j * field[:, :, 1]
    spectrum = jnp.fft.fft(complex_field, axis=-1)
    frequency = jnp.arange(NZ, dtype=jnp.int32)
    signed = jnp.where(frequency > NZ // 2, frequency - NZ, frequency)
    cutoff = NZ // 3
    wave_ratio = signed.astype(jnp.float32) / cutoff
    multiplier = jnp.where(jnp.abs(signed) < cutoff, -VIS * wave_ratio * wave_ratio, 0.0 * wave_ratio)
    returned = jnp.fft.ifft(spectrum * multiplier, axis=-1)
    spanwise = jnp.stack([jnp.real(returned), jnp.imag(returned)], axis=2).astype(field.dtype)
    velocity = mean_flow[0]
    shear_rate = mean_flow[1]
    advect_rate = wave_number[:, None, None, None] * velocity[None, None, :, None]
    advect_real = -advect_rate * field[:, :, 1]
    advect_imag = advect_rate * field[:, :, 0]
    advection = jnp.stack([advect_real, advect_imag], axis=2)
    coupling = shear_rate[None, None, :, None] * field[:, 0]
    advection = advection.at[:, 1].add(-coupling)
    new_field = field + TAU * advection + diffusion + spanwise
    lower_wall = jnp.zeros_like(new_field[:, 0, :, 0, :])
    upper_wall = jnp.zeros_like(new_field[:, 0, :, 0, :])
    for offset in range(HALO + 1):
        lower_wall = lower_wall + wall_coef[0, offset] * new_field[:, 0, :, offset, :]
        upper_wall = upper_wall + wall_coef[1, offset] * new_field[:, 0, :, NY - 1 - offset, :]
    shear_rows = jnp.stack([lower_wall, upper_wall])
    onehot = (patch_of[:, None] == jnp.arange(PATCH, dtype=jnp.int32)[None, :]).astype(field.dtype)
    wall_grad = jnp.einsum("wmcz,zp->wmcp", shear_rows, onehot, precision=lax.Precision.HIGHEST)
    return new_field, wall_grad
```

```python
import functools
import math

import jax
import jax.numpy as jnp
import numpy as np
from jax import lax
from jax.experimental import pallas as pl
from jax.experimental.pallas import tpu as pltpu
from jax.sharding import PartitionSpec as P

HALO = 7
STEN = 15
PATCH = 64
TAU = 0.25
VIS = 0.5

LANES = 128
OUTER = 48
PAD = 8
TILES = OUTER // 2

QUARTER = (0, 4, 2, 1, 5, 9)
KEPT = tuple(4 * q for q in QUARTER) + tuple(2 + 8 * t for t in range(6)) + tuple(4 * q + 1 for q in range(12))


@functools.cache
def spectral_tables(length):
    signed = np.arange(length)
    signed = np.where(signed > length // 2, signed - length, signed)
    cutoff = length // 3
    ratio = signed.astype(np.float64) / cutoff
    multiplier = np.where(np.abs(signed) < cutoff, -VIS * ratio * ratio, 0.0)
    shift = np.arange(LANES)[None, :] - np.arange(LANES)[:, None]
    inner = np.arange(LANES)

    def complex_table(k1):
        wave = k1 + OUTER * inner
        spots = np.arange(-LANES + 1, LANES)
        phase = np.exp(2j * np.pi * ((wave[:, None] * spots[None, :]) % length) / length)
        return ((multiplier[wave][:, None] * phase).sum(axis=0) / LANES)[shift + LANES - 1]

    tables = np.zeros((TILES, 2 * LANES, 2 * LANES))
    tables[0, :LANES, :LANES] = complex_table(0).real / OUTER
    tables[0, LANES:, LANES:] = complex_table(OUTER // 2).real / OUTER
    for tile, k1 in enumerate(KEPT[1:], 1):
        table = complex_table(k1) * 2.0 / OUTER
        tables[tile, :LANES, :LANES] = table.real
        tables[tile, :LANES, LANES:] = table.imag
        tables[tile, LANES:, :LANES] = -table.imag
        tables[tile, LANES:, LANES:] = table.real
    high = tables.astype(jnp.bfloat16)
    low = (tables - high.astype(np.float64)).astype(jnp.bfloat16)
    return np.stack([high, low], axis=1)


def turn(value, numerator, denominator):
    re, im = value
    numerator %= denominator
    if numerator == 0:
        return value
    if 2 * numerator == denominator:
        return (-re, -im)
    if 4 * numerator == denominator:
        return (-im, re)
    if 4 * numerator == 3 * denominator:
        return (im, -re)
    cos = math.cos(2 * math.pi * numerator / denominator)
    sin = math.sin(2 * math.pi * numerator / denominator)
    return (re * cos - im * sin, re * sin + im * cos)


def add(a, b):
    return (a[0] + b[0], a[1] + b[1])


def sub(a, b):
    return (a[0] - b[0], a[1] - b[1])


ROOT = math.sqrt(3.0) / 2.0


def dft3(x, sign):
    total = add(x[1], x[2])
    other = sub(x[1], x[2])
    middle = (x[0][0] - 0.5 * total[0], x[0][1] - 0.5 * total[1])
    side = (-sign * ROOT * other[1], sign * ROOT * other[0])
    return [add(x[0], total), add(middle, side), sub(middle, side)]


def dft6(x, sign):
    even = dft3([add(x[b], x[b + 3]) for b in range(3)], sign)
    odd = dft3([turn(sub(x[b], x[b + 3]), sign * b, 6) for b in range(3)], sign)
    return [even[0], odd[0], even[1], odd[1], even[2], odd[2]]


def dft12(x, sign):
    out = [None] * 12
    parts = [[], [], [], []]
    for b in range(3):
        a0, a1, a2, a3 = x[b], x[b + 3], x[b + 6], x[b + 9]
        s0, s1, d0, d1 = add(a0, a2), add(a1, a3), sub(a0, a2), turn(sub(a1, a3), sign, 4)
        for r, value in enumerate((add(s0, s1), add(d0, d1), sub(s0, s1), sub(d0, d1))):
            parts[r].append(turn(value, sign * b * r, 12))
    for r in range(4):
        for q, value in enumerate(dft3(parts[r], sign)):
            out[4 * q + r] = value
    return out


def real_forward(x):
    whole, halved, turned = [], [], []
    for b in range(12):
        s0, s1 = x[b] + x[b + 24], x[b + 12] + x[b + 36]
        whole.append(s0 + s1)
        halved.append(s0 - s1)
        turned.append(turn((x[b] - x[b + 24], x[b + 36] - x[b + 12]), -b, 48))
    w, h, t = [], [], []
    for b in range(3):
        s0, s1 = whole[b] + whole[b + 6], whole[b + 3] + whole[b + 9]
        w.append(s0 + s1)
        h.append(s0 - s1)
        t.append(turn((whole[b] - whole[b + 6], whole[b + 9] - whole[b + 3]), -b, 12))
    total, other = w[1] + w[2], w[1] - w[2]
    four = (w[0] - 0.5 * total, -ROOT * other)
    two = (h[0] + 0.5 * (h[1] - h[2]), -ROOT * (h[1] + h[2]))
    tiles = [(w[0] + total, h[0] - h[1] + h[2]), four, two] + dft3(t, -1)
    tiles += dft6([turn((halved[b], -halved[b + 6]), -b, 24) for b in range(6)], -1)
    return tiles + dft12(turned, -1)


def real_backward(tiles):
    (zero, half), four, two = tiles[:3]
    w0 = zero + four[0]
    rest, side = zero - 0.5 * four[0], ROOT * four[1]
    w = [w0, rest - side, rest + side]
    h_side = 0.5 * two[0] - ROOT * two[1]
    h = [two[0] + half, h_side - half, -0.5 * two[0] - ROOT * two[1] + half]
    t = [turn(value, b, 12) for b, value in enumerate(dft3(tiles[3:6], 1))]
    whole = [None] * 12
    for b in range(3):
        s, d = w[b] + h[b], w[b] - h[b]
        whole[b], whole[b + 6] = s + t[b][0], s - t[b][0]
        whole[b + 3], whole[b + 9] = d - t[b][1], d + t[b][1]
    halved = [None] * 12
    for b, value in enumerate(dft6(tiles[6:12], 1)):
        halved[b], halved[b + 6] = turn(value, b, 24)
        halved[b + 6] = -halved[b + 6]
    x = [None] * 48
    for b, value in enumerate(dft12(tiles[12:], 1)):
        re, im = turn(value, b, 48)
        s, d = whole[b] + halved[b], whole[b] - halved[b]
        x[b], x[b + 24] = s + re, s - re
        x[b + 12], x[b + 36] = d - im, d + im
    return x


def spectral_kernel(table_ref, line_ref, out_ref, wave_ref):
    source_count, line_count, row_count, width = line_ref.shape
    pieces = width // LANES
    groups = row_count // PAD

    def place(n1):
        return n1 // pieces, pl.ds(n1 % pieces * LANES, LANES)

    def forward(step, _):
        line, rows = step // groups, pl.ds(pl.multiple_of(step % groups * PAD, PAD), PAD)
        values = []
        for n1 in range(OUTER):
            source, lanes = place(n1)
            values.append(line_ref[source, line, rows, lanes])
        spot = pl.ds(pl.multiple_of(step * PAD, PAD), PAD)
        for tile, (re, im) in enumerate(real_forward(values)):
            wave_ref[tile, spot, :LANES] = re
            wave_ref[tile, spot, LANES:] = im
        return 0

    lax.fori_loop(0, line_count * groups, forward, 0)

    def middle(tile, _):
        value = wave_ref[tile]
        high = value.astype(jnp.bfloat16)
        low = (value - high.astype(jnp.float32)).astype(jnp.bfloat16)
        table_high, table_low = table_ref[tile, 0], table_ref[tile, 1]
        wave_ref[tile] = (
            jnp.dot(high, table_low, preferred_element_type=jnp.float32)
            + jnp.dot(low, table_high, preferred_element_type=jnp.float32)
            + jnp.dot(high, table_high, preferred_element_type=jnp.float32)
        )
        return 0

    lax.fori_loop(0, TILES, middle, 0)

    def backward(step, _):
        line, rows = step // groups, pl.ds(pl.multiple_of(step % groups * PAD, PAD), PAD)
        spot = pl.ds(pl.multiple_of(step * PAD, PAD), PAD)
        tiles = [(wave_ref[tile, spot, :LANES], wave_ref[tile, spot, LANES:]) for tile in range(TILES)]
        for n1, value in enumerate(real_backward(tiles)):
            source, lanes = place(n1)
            out_ref[source, line, rows, lanes] = value
        return 0

    lax.fori_loop(0, line_count * groups, backward, 0)


def spanwise_operator(lines, tables):
    source_count, line_count, row_count, width = lines.shape
    rows = line_count * row_count
    flops = 3 * 2 * TILES * rows * (2 * LANES) ** 2
    return pl.pallas_call(
        spectral_kernel,
        out_shape=jax.ShapeDtypeStruct(lines.shape, jnp.float32),
        in_specs=[pl.BlockSpec(memory_space=pltpu.VMEM)] * 2,
        out_specs=pl.BlockSpec(memory_space=pltpu.VMEM),
        scratch_shapes=[pltpu.VMEM((TILES, rows, 2 * LANES), jnp.float32)],
        compiler_params=pltpu.CompilerParams(vmem_limit_bytes=40 << 20),
        cost_estimate=pl.CostEstimate(flops=flops, bytes_accessed=8 * lines.size + 2 * tables.size, transcendentals=0),
        name="spanwise",
    )(tables, lines)


def local_kernel(rate_ref, coef_ref, flow_ref, field_ref, low_ref, high_ref, out_ref, pad_ref):
    _, comp_count, part_count, row_count, width = field_ref.shape
    pad_ref[:, :, :PAD] = low_ref[0]
    pad_ref[:, :, PAD : PAD + row_count] = field_ref[0]
    pad_ref[:, :, PAD + row_count :] = high_ref[0]
    rate = rate_ref[pl.program_id(0)]

    def column(step, _):
        lanes = pl.ds(pl.multiple_of(step * LANES, LANES), LANES)
        for top in range(0, row_count, PAD):
            rows = pl.ds(top, PAD)
            advect = rate * flow_ref[0, rows, :]
            shear = TAU * flow_ref[1, rows, :]
            centre = [[field_ref[0, c, p, rows, lanes] for p in range(2)] for c in range(comp_count)]
            for c in range(comp_count):
                for p in range(2):
                    total = centre[c][p]
                    total = total - advect * centre[c][1] if p == 0 else total + advect * centre[c][0]
                    if c == 1:
                        total = total - shear * centre[0][p]
                    for offset in range(STEN):
                        near = pad_ref[c, p, pl.ds(top + offset + PAD - HALO, PAD), lanes]
                        total = total + coef_ref[offset, rows, :] * near
                    out_ref[0, c, p, rows, lanes] = total
        return 0

    lax.fori_loop(0, width // LANES, column, 0)


def local_terms(field, low, high, rate, coef, flow):
    mode_count, comp_count, part_count, row_count, width = field.shape
    block = (1, comp_count, part_count, row_count, width)
    edge = (1, comp_count, part_count, PAD, width)

    def by_mode(m):
        return (m, 0, 0, 0, 0)

    return pl.pallas_call(
        local_kernel,
        grid=(mode_count,),
        out_shape=jax.ShapeDtypeStruct(field.shape, jnp.float32),
        in_specs=[
            pl.BlockSpec(memory_space=pltpu.SMEM),
            pl.BlockSpec(coef.shape, lambda m: (0, 0, 0)),
            pl.BlockSpec(flow.shape, lambda m: (0, 0, 0)),
            pl.BlockSpec(block, by_mode),
            pl.BlockSpec(edge, by_mode),
            pl.BlockSpec(edge, by_mode),
        ],
        out_specs=pl.BlockSpec(block, by_mode),
        scratch_shapes=[pltpu.VMEM((comp_count, part_count, row_count + 2 * PAD, width), jnp.float32)],
        compiler_params=pltpu.CompilerParams(vmem_limit_bytes=24 << 20),
        cost_estimate=pl.CostEstimate(flops=40 * field.size, bytes_accessed=10 * field.size, transcendentals=0),
        name="local_terms",
    )(rate, coef, flow, field, low, high)


def wall_sum_kernel(weight_ref, base_ref, term_ref, out_ref, shear_ref):
    row_count = base_ref.shape[3]
    for p in range(2):
        new = base_ref[0, 0, p] + term_ref[0, 0, p]
        out_ref[0, 0, p] = new
        low, high = new[:PAD], new[row_count - PAD :]
        shear_ref[0, p] = jnp.sum(low * weight_ref[0][:, :1], axis=0)
        shear_ref[0, 2 + p] = jnp.sum(high * weight_ref[1][:, :1], axis=0)


def sum_kernel(base_ref, term_ref, out_ref):
    out_ref[...] = base_ref[...] + term_ref[...]


def add_first(base, term, weight):
    mode_count, _, part_count, row_count, width = base.shape
    block = pl.BlockSpec((1, 1, part_count, row_count, width), lambda m: (m, 0, 0, 0, 0))
    return pl.pallas_call(
        wall_sum_kernel,
        grid=(mode_count,),
        out_shape=(
            jax.ShapeDtypeStruct(base.shape, jnp.float32),
            jax.ShapeDtypeStruct((mode_count, 4, width), jnp.float32),
        ),
        in_specs=[pl.BlockSpec(weight.shape, lambda m: (0, 0, 0)), block, block],
        out_specs=(block, pl.BlockSpec((1, 4, width), lambda m: (m, 0, 0))),
        input_output_aliases={1: 0},
        cost_estimate=pl.CostEstimate(flops=term.size, bytes_accessed=12 * term.size, transcendentals=0),
        name="add_first",
    )(weight, base, term)


def add_rest(base, term, first):
    mode_count, comp_count, part_count, row_count, width = term.shape
    shape = (1, 1, part_count, row_count, width)
    block = pl.BlockSpec(shape, lambda m, c: (m, c + first, 0, 0, 0))
    return pl.pallas_call(
        sum_kernel,
        grid=(mode_count, comp_count),
        out_shape=jax.ShapeDtypeStruct(base.shape, jnp.float32),
        in_specs=[block, pl.BlockSpec(shape, lambda m, c: (m, c, 0, 0, 0))],
        out_specs=block,
        input_output_aliases={0: 0},
        cost_estimate=pl.CostEstimate(flops=term.size, bytes_accessed=12 * term.size, transcendentals=0),
        name="add_rest",
    )(base, term)


def on_device(field, mean_flow, d2_coef, wall_coef, kx_index, patch_of):
    mode_count, comp_count, part_count, row_count, width = field.shape
    span = lax.axis_size("span")
    wall_count = lax.axis_size("wall")
    wall_index = lax.axis_index("wall")
    mode_split = math.gcd(span, mode_count)
    row_split = span // mode_split
    tables = jnp.asarray(spectral_tables(width * span))

    def to_lines(chunk):
        lines = chunk.reshape(mode_split, -1, row_split, row_count // row_split, width)
        lines = lines.transpose(0, 2, 1, 3, 4).reshape(span, -1, row_count // row_split, width)
        return lax.all_to_all(lines, "span", split_axis=0, concat_axis=0)

    def from_lines(lines, comps):
        blocks = lax.all_to_all(lines, "span", split_axis=0, concat_axis=0)
        blocks = blocks.reshape(mode_split, row_split, -1, row_count // row_split, width)
        return blocks.transpose(0, 2, 1, 3, 4).reshape(mode_count, comps, part_count, row_count, width)

    parts = [(0, 1), (1, comp_count)]
    lines = [to_lines(field[:, first:last]) for first, last in parts]

    forward = [(i, i + 1) for i in range(wall_count - 1)]
    backward = [(i + 1, i) for i in range(wall_count - 1)]
    low = lax.ppermute(field[:, :, :, row_count - PAD :], "wall", forward)
    high = lax.ppermute(field[:, :, :, :PAD], "wall", backward)
    rate = kx_index.astype(jnp.float32) * (0.25 * TAU)
    coef = jnp.broadcast_to(d2_coef[:, :, None], (STEN, row_count, LANES))
    flow = jnp.broadcast_to(mean_flow[:, :, None], (2, row_count, LANES))
    base = local_terms(field, low, high, rate, coef, flow)

    terms = [
        from_lines(spanwise_operator(value, tables), last - first) for value, (first, last) in zip(lines, parts)
    ]
    lower = jnp.where(wall_index == 0, wall_coef[0], 0.0)
    upper = jnp.where(wall_index == wall_count - 1, wall_coef[1, ::-1], 0.0)
    weight = jnp.broadcast_to(jnp.stack([lower, upper])[:, :, None], (2, PAD, LANES))
    base, shear = add_first(base, terms[0], weight)
    onehot = (patch_of[:, None] == jnp.arange(PATCH, dtype=jnp.int32)[None, :]).astype(jnp.float32)
    grad = jnp.einsum("mwz,zq->mwq", shear, onehot, precision=lax.Precision.HIGHEST)
    grad = grad.reshape(mode_count, 2, part_count, PATCH).transpose(1, 0, 2, 3)
    wall_grad = lax.psum(grad, ("wall", "span"))
    new_field = add_rest(base, terms[1], 1)
    return (new_field, wall_grad)


def solution(mesh):
    return jax.shard_map(
        on_device,
        mesh=mesh,
        in_specs=(
            P(None, None, None, "wall", "span"),
            P(None, "wall"),
            P(None, "wall"),
            P(),
            P(),
            P("span"),
        ),
        out_specs=(P(None, None, None, "wall", "span"), P()),
        check_vma=False,
    )
```

```python
import functools
import math

import jax
import jax.numpy as jnp
import numpy as np
from jax import lax
from jax.experimental import pallas as pl
from jax.experimental.pallas import tpu as pltpu
from jax.sharding import PartitionSpec as P

HALO = 7
STEN = 15
PATCH = 64
TAU = 0.25
VIS = 0.5

LANES = 128
OUTER = 48
PAD = 8
TILES = OUTER // 2

QUARTER = (0, 4, 2, 1, 5, 9)
KEPT = tuple(4 * q for q in QUARTER) + tuple(2 + 8 * t for t in range(6)) + tuple(4 * q + 1 for q in range(12))


@functools.cache
def spectral_tables(length):
    signed = np.arange(length)
    signed = np.where(signed > length // 2, signed - length, signed)
    cutoff = length // 3
    ratio = signed.astype(np.float64) / cutoff
    multiplier = np.where(np.abs(signed) < cutoff, -VIS * ratio * ratio, 0.0)
    shift = np.arange(LANES)[None, :] - np.arange(LANES)[:, None]
    inner = np.arange(LANES)

    def complex_table(k1):
        wave = k1 + OUTER * inner
        spots = np.arange(-LANES + 1, LANES)
        phase = np.exp(2j * np.pi * ((wave[:, None] * spots[None, :]) % length) / length)
        return ((multiplier[wave][:, None] * phase).sum(axis=0) / LANES)[shift + LANES - 1]

    tables = np.zeros((TILES, 2 * LANES, 2 * LANES))
    tables[0, :LANES, :LANES] = complex_table(0).real / OUTER
    tables[0, LANES:, LANES:] = complex_table(OUTER // 2).real / OUTER
    for tile, k1 in enumerate(KEPT[1:], 1):
        table = complex_table(k1) * 2.0 / OUTER
        tables[tile, :LANES, :LANES] = table.real
        tables[tile, :LANES, LANES:] = table.imag
        tables[tile, LANES:, :LANES] = -table.imag
        tables[tile, LANES:, LANES:] = table.real
    high = tables.astype(jnp.bfloat16)
    low = (tables - high.astype(np.float64)).astype(jnp.bfloat16)
    return np.stack([high, low], axis=1)


def turn(value, numerator, denominator):
    re, im = value
    numerator %= denominator
    if numerator == 0:
        return value
    if 2 * numerator == denominator:
        return (-re, -im)
    if 4 * numerator == denominator:
        return (-im, re)
    if 4 * numerator == 3 * denominator:
        return (im, -re)
    cos = math.cos(2 * math.pi * numerator / denominator)
    sin = math.sin(2 * math.pi * numerator / denominator)
    return (re * cos - im * sin, re * sin + im * cos)


def add(a, b):
    return (a[0] + b[0], a[1] + b[1])


def sub(a, b):
    return (a[0] - b[0], a[1] - b[1])


ROOT = math.sqrt(3.0) / 2.0


def dft3(x, sign):
    total = add(x[1], x[2])
    other = sub(x[1], x[2])
    middle = (x[0][0] - 0.5 * total[0], x[0][1] - 0.5 * total[1])
    side = (-sign * ROOT * other[1], sign * ROOT * other[0])
    return [add(x[0], total), add(middle, side), sub(middle, side)]


def dft6(x, sign):
    even = dft3([add(x[b], x[b + 3]) for b in range(3)], sign)
    odd = dft3([turn(sub(x[b], x[b + 3]), sign * b, 6) for b in range(3)], sign)
    return [even[0], odd[0], even[1], odd[1], even[2], odd[2]]


def dft12(x, sign):
    out = [None] * 12
    parts = [[], [], [], []]
    for b in range(3):
        a0, a1, a2, a3 = x[b], x[b + 3], x[b + 6], x[b + 9]
        s0, s1, d0, d1 = add(a0, a2), add(a1, a3), sub(a0, a2), turn(sub(a1, a3), sign, 4)
        for r, value in enumerate((add(s0, s1), add(d0, d1), sub(s0, s1), sub(d0, d1))):
            parts[r].append(turn(value, sign * b * r, 12))
    for r in range(4):
        for q, value in enumerate(dft3(parts[r], sign)):
            out[4 * q + r] = value
    return out


def real_forward(x):
    whole, halved, turned = [], [], []
    for b in range(12):
        s0, s1 = x[b] + x[b + 24], x[b + 12] + x[b + 36]
        whole.append(s0 + s1)
        halved.append(s0 - s1)
        turned.append(turn((x[b] - x[b + 24], x[b + 36] - x[b + 12]), -b, 48))
    w, h, t = [], [], []
    for b in range(3):
        s0, s1 = whole[b] + whole[b + 6], whole[b + 3] + whole[b + 9]
        w.append(s0 + s1)
        h.append(s0 - s1)
        t.append(turn((whole[b] - whole[b + 6], whole[b + 9] - whole[b + 3]), -b, 12))
    total, other = w[1] + w[2], w[1] - w[2]
    four = (w[0] - 0.5 * total, -ROOT * other)
    two = (h[0] + 0.5 * (h[1] - h[2]), -ROOT * (h[1] + h[2]))
    tiles = [(w[0] + total, h[0] - h[1] + h[2]), four, two] + dft3(t, -1)
    tiles += dft6([turn((halved[b], -halved[b + 6]), -b, 24) for b in range(6)], -1)
    return tiles + dft12(turned, -1)


def real_backward(tiles):
    (zero, half), four, two = tiles[:3]
    w0 = zero + four[0]
    rest, side = zero - 0.5 * four[0], ROOT * four[1]
    w = [w0, rest - side, rest + side]
    h_side = 0.5 * two[0] - ROOT * two[1]
    h = [two[0] + half, h_side - half, -0.5 * two[0] - ROOT * two[1] + half]
    t = [turn(value, b, 12) for b, value in enumerate(dft3(tiles[3:6], 1))]
    whole = [None] * 12
    for b in range(3):
        s, d = w[b] + h[b], w[b] - h[b]
        whole[b], whole[b + 6] = s + t[b][0], s - t[b][0]
        whole[b + 3], whole[b + 9] = d - t[b][1], d + t[b][1]
    halved = [None] * 12
    for b, value in enumerate(dft6(tiles[6:12], 1)):
        halved[b], halved[b + 6] = turn(value, b, 24)
        halved[b + 6] = -halved[b + 6]
    x = [None] * 48
    for b, value in enumerate(dft12(tiles[12:], 1)):
        re, im = turn(value, b, 48)
        s, d = whole[b] + halved[b], whole[b] - halved[b]
        x[b], x[b + 24] = s + re, s - re
        x[b + 12], x[b + 36] = d - im, d + im
    return x


def spectral_kernel(sheared, me_ref, table_ref, weight_ref, field_ref, *refs):
    line_ref, wave_ref, sems = refs[-3:]
    count, part_count, row_count, width = line_ref.shape
    received, sent = refs[: count - 1], refs[count - 1 : 2 * count - 1]
    pieces = width // LANES
    groups = row_count // PAD
    me, mode, top, comp = me_ref[0], me_ref[1], me_ref[2], me_ref[3]

    copies = []
    for x in range(count):
        if x == 0:
            source = field_ref.at[mode, comp, :, pl.ds(pl.multiple_of(top, PAD), row_count)]
        else:
            source = received[x - 1]
        copies.append(pltpu.make_async_copy(source, line_ref.at[me ^ x], sems.at[x]))
    for copy in copies:
        copy.start()
    for copy in copies:
        copy.wait()

    def place(n1):
        return n1 // pieces, pl.ds(n1 % pieces * LANES, LANES)

    def forward(step, _):
        line, rows = step // groups, pl.ds(pl.multiple_of(step % groups * PAD, PAD), PAD)
        values = []
        for n1 in range(OUTER):
            source, lanes = place(n1)
            values.append(line_ref[source, line, rows, lanes])
        spot = pl.ds(pl.multiple_of(step * PAD, PAD), PAD)
        for tile, (re, im) in enumerate(real_forward(values)):
            wave_ref[tile, spot, :LANES] = re
            wave_ref[tile, spot, LANES:] = im
        return 0

    lax.fori_loop(0, part_count * groups, forward, 0)

    def middle(tile, _):
        value = wave_ref[tile]
        high = value.astype(jnp.bfloat16)
        low = (value - high.astype(jnp.float32)).astype(jnp.bfloat16)
        table_high, table_low = table_ref[tile, 0], table_ref[tile, 1]
        wave_ref[tile] = (
            jnp.dot(high, table_low, preferred_element_type=jnp.float32)
            + jnp.dot(low, table_high, preferred_element_type=jnp.float32)
            + jnp.dot(high, table_high, preferred_element_type=jnp.float32)
        )
        return 0

    lax.fori_loop(0, TILES, middle, 0)

    def backward(step, _):
        line, rows = step // groups, pl.ds(pl.multiple_of(step % groups * PAD, PAD), PAD)
        spot = pl.ds(pl.multiple_of(step * PAD, PAD), PAD)
        tiles = [(wave_ref[tile, spot, :LANES], wave_ref[tile, spot, LANES:]) for tile in range(TILES)]
        for n1, value in enumerate(real_backward(tiles)):
            source, lanes = place(n1)
            line_ref[source, line, rows, lanes] = value
        return 0

    lax.fori_loop(0, part_count * groups, backward, 0)
    copies = [pltpu.make_async_copy(line_ref.at[me ^ x], sent[x], sems.at[x]) for x in range(count)]
    for copy in copies:
        copy.start()
    if sheared:
        shear_ref = refs[2 * count - 1]
        for source in range(count):
            for p in range(part_count):
                lower, upper = line_ref[source, p, :PAD], line_ref[source, p, row_count - PAD :]
                shear_ref[source, p] = jnp.sum(lower * weight_ref[0][:, :1], axis=0)
                shear_ref[source, part_count + p] = jnp.sum(upper * weight_ref[1][:, :1], axis=0)
    for copy in copies:
        copy.wait()


def spanwise_operator(field, received, spots, weight, tables, sheared):
    count = len(received) + 1
    part_count, row_count, width = received[0].shape
    rows = part_count * row_count
    flops = 3 * 2 * TILES * rows * (2 * LANES) ** 2
    anywhere = pl.BlockSpec(memory_space=pl.ANY)
    vector = pl.BlockSpec(memory_space=pltpu.VMEM)
    sent = jax.ShapeDtypeStruct((part_count, row_count, width), jnp.float32)
    shear = jax.ShapeDtypeStruct((count, 2 * part_count, width), jnp.float32)
    return pl.pallas_call(
        functools.partial(spectral_kernel, sheared),
        out_shape=[sent] * count + [shear] * sheared,
        in_specs=[pl.BlockSpec(memory_space=pltpu.SMEM), vector, vector] + [anywhere] * count,
        out_specs=[anywhere] * count + [vector] * sheared,
        scratch_shapes=[
            pltpu.VMEM((count, part_count, row_count, width), jnp.float32),
            pltpu.VMEM((TILES, rows, 2 * LANES), jnp.float32),
            pltpu.SemaphoreType.DMA((count,)),
        ],
        compiler_params=pltpu.CompilerParams(vmem_limit_bytes=32 << 20),
        cost_estimate=pl.CostEstimate(flops=flops, bytes_accessed=8 * count * rows * width, transcendentals=0),
        name="spanwise",
    )(spots, tables, weight, field, *received)


def local_kernel(rate_ref, coef_ref, flow_ref, weight_ref, field_ref, low_ref, high_ref, out_ref, shear_ref, pad_ref):
    _, comp_count, part_count, row_count, width = field_ref.shape
    pad_ref[:, :, :PAD] = low_ref[0]
    pad_ref[:, :, PAD : PAD + row_count] = field_ref[0]
    pad_ref[:, :, PAD + row_count :] = high_ref[0]
    rate = rate_ref[pl.program_id(0)]

    def column(step, _):
        lanes = pl.ds(pl.multiple_of(step * LANES, LANES), LANES)
        for top in range(0, row_count, PAD):
            rows = pl.ds(top, PAD)
            advect = rate * flow_ref[0, rows, :]
            shear = TAU * flow_ref[1, rows, :]
            centre = [[field_ref[0, c, p, rows, lanes] for p in range(2)] for c in range(comp_count)]
            for c in range(comp_count):
                for p in range(2):
                    total = centre[c][p]
                    total = total - advect * centre[c][1] if p == 0 else total + advect * centre[c][0]
                    if c == 1:
                        total = total - shear * centre[0][p]
                    for offset in range(STEN):
                        near = pad_ref[c, p, pl.ds(top + offset + PAD - HALO, PAD), lanes]
                        total = total + coef_ref[offset, rows, :] * near
                    out_ref[0, c, p, rows, lanes] = total
        return 0

    lax.fori_loop(0, width // LANES, column, 0)
    for p in range(part_count):
        lower, upper = out_ref[0, 0, p, :PAD], out_ref[0, 0, p, row_count - PAD :]
        shear_ref[0, p] = jnp.sum(lower * weight_ref[0][:, :1], axis=0)
        shear_ref[0, part_count + p] = jnp.sum(upper * weight_ref[1][:, :1], axis=0)


def local_terms(field, low, high, rate, coef, flow, weight):
    mode_count, comp_count, part_count, row_count, width = field.shape
    block = (1, comp_count, part_count, row_count, width)
    edge = (1, comp_count, part_count, PAD, width)

    def by_mode(m):
        return (m, 0, 0, 0, 0)

    return pl.pallas_call(
        local_kernel,
        grid=(mode_count,),
        out_shape=(
            jax.ShapeDtypeStruct(field.shape, jnp.float32),
            jax.ShapeDtypeStruct((mode_count, 2 * part_count, width), jnp.float32),
        ),
        in_specs=[
            pl.BlockSpec(memory_space=pltpu.SMEM),
            pl.BlockSpec(coef.shape, lambda m: (0, 0, 0)),
            pl.BlockSpec(flow.shape, lambda m: (0, 0, 0)),
            pl.BlockSpec(weight.shape, lambda m: (0, 0, 0)),
            pl.BlockSpec(block, by_mode),
            pl.BlockSpec(edge, by_mode),
            pl.BlockSpec(edge, by_mode),
        ],
        out_specs=(pl.BlockSpec(block, by_mode), pl.BlockSpec((1, 2 * part_count, width), lambda m: (m, 0, 0))),
        scratch_shapes=[pltpu.VMEM((comp_count, part_count, row_count + 2 * PAD, width), jnp.float32)],
        compiler_params=pltpu.CompilerParams(vmem_limit_bytes=24 << 20),
        cost_estimate=pl.CostEstimate(flops=40 * field.size, bytes_accessed=10 * field.size, transcendentals=0),
        name="local_terms",
    )(rate, coef, flow, weight, field, low, high)


def add_kernel(row_split, me_ref, base_ref, *refs):
    buffer_ref, sems = refs[-2:]
    count, part_count, row_count, _ = buffer_ref.shape
    terms, out_ref = refs[:count], refs[count]
    me, comp = me_ref[0], me_ref[3]

    def spot(ref, x):
        other = me ^ x
        top = pl.multiple_of(other % row_split * row_count, PAD)
        return ref.at[other // row_split, comp, :, pl.ds(top, row_count)]

    loads = [pltpu.make_async_copy(spot(base_ref, x), buffer_ref.at[x], sems.at[x]) for x in range(count)]
    stores = [pltpu.make_async_copy(buffer_ref.at[x], spot(out_ref, x), sems.at[x]) for x in range(count)]
    for load in loads:
        load.start()
    for x in range(count):
        loads[x].wait()
        buffer_ref[x] = buffer_ref[x] + terms[x][...]
        stores[x].start()
    for store in stores:
        store.wait()


def add_term(base, terms, spots, row_split):
    count = len(terms)
    size = count * terms[0].size
    return pl.pallas_call(
        functools.partial(add_kernel, row_split),
        out_shape=jax.ShapeDtypeStruct(base.shape, jnp.float32),
        in_specs=[pl.BlockSpec(memory_space=pltpu.SMEM), pl.BlockSpec(memory_space=pl.ANY)]
        + [pl.BlockSpec(memory_space=pltpu.VMEM)] * count,
        out_specs=pl.BlockSpec(memory_space=pl.ANY),
        scratch_shapes=[pltpu.VMEM((count,) + terms[0].shape, jnp.float32), pltpu.SemaphoreType.DMA((count,))],
        input_output_aliases={1: 0},
        compiler_params=pltpu.CompilerParams(vmem_limit_bytes=16 << 20),
        cost_estimate=pl.CostEstimate(flops=size, bytes_accessed=12 * size, transcendentals=0),
        name="add_term",
    )(spots, base, *terms)


def on_device(field, mean_flow, d2_coef, wall_coef, kx_index, patch_of):
    mode_count, comp_count, part_count, row_count, width = field.shape
    span = lax.axis_size("span")
    me = lax.axis_index("span")
    wall_count = lax.axis_size("wall")
    wall_index = lax.axis_index("wall")
    mode_split = math.gcd(span, mode_count)
    row_split = span // mode_split
    line_rows = row_count // row_split
    tables = jnp.asarray(spectral_tables(width * span))
    pairs = [[(i, i ^ x) for i in range(span)] for x in range(span)]

    def block_of(x, comp):
        other = me ^ x
        start = (other // row_split, comp, 0, other % row_split * line_rows, 0)
        return lax.dynamic_slice(field, start, (1, 1, part_count, line_rows, width))[0, 0]

    lines = [
        [lax.ppermute(block_of(x, comp), "span", pairs[x]) for x in range(span - 1, 0, -1)][::-1]
        for comp in range(comp_count)
    ]

    forward = [(i, i + 1) for i in range(wall_count - 1)]
    backward = [(i + 1, i) for i in range(wall_count - 1)]
    low = lax.ppermute(field[:, :, :, row_count - PAD :], "wall", forward)
    high = lax.ppermute(field[:, :, :, :PAD], "wall", backward)
    rate = kx_index.astype(jnp.float32) * (0.25 * TAU)
    coef = jnp.broadcast_to(d2_coef[:, :, None], (STEN, row_count, LANES))
    flow = jnp.broadcast_to(mean_flow[:, :, None], (2, row_count, LANES))
    lower = jnp.where(wall_index == 0, wall_coef[0], 0.0)
    upper = jnp.where(wall_index == wall_count - 1, wall_coef[1, ::-1], 0.0)
    ends = jnp.stack([me % row_split == 0, me % row_split == row_split - 1])
    walls = jnp.stack([lower, upper])
    weight = jnp.broadcast_to(walls[:, :, None], (2, PAD, LANES))
    line_weight = jnp.where(ends[:, None, None], weight, 0.0)
    base, shear = local_terms(field, low, high, rate, coef, flow, weight)

    patches = lax.all_gather(patch_of, "span", tiled=True)
    names = jnp.arange(PATCH, dtype=jnp.int32)
    onehot = (patch_of[:, None] == names[None, :]).astype(jnp.float32)
    onehot_all = (patches.reshape(span, width)[:, :, None] == names).astype(jnp.float32)
    grad = jnp.einsum("mwz,zq->mwq", shear, onehot, precision=lax.Precision.HIGHEST)

    result = base
    for comp in range(comp_count):
        spots = jnp.stack([me, me // row_split, me % row_split * line_rows, comp]).astype(jnp.int32)
        sent = spanwise_operator(field, lines[comp], spots, line_weight, tables, comp == 0)
        if comp == 0:
            line_grad = jnp.einsum("szq,swz->wq", onehot_all, sent[span], precision=lax.Precision.HIGHEST)
            mine = jnp.arange(mode_count) == me // row_split
            grad = grad + jnp.where(mine[:, None, None], line_grad, 0.0)
            grad = grad.reshape(mode_count, 2, part_count, PATCH).transpose(1, 0, 2, 3)
            wall_grad = lax.psum(grad, ("wall", "span"))
        terms = [sent[0]] + [lax.ppermute(sent[x], "span", pairs[x]) for x in range(1, span)]
        result = add_term(result, terms, spots, row_split)
    return (result, wall_grad)


def solution(mesh):
    return jax.shard_map(
        on_device,
        mesh=mesh,
        in_specs=(
            P(None, None, None, "wall", "span"),
            P(None, "wall"),
            P(None, "wall"),
            P(),
            P(),
            P("span"),
        ),
        out_specs=(P(None, None, None, "wall", "span"), P()),
        check_vma=False,
    )
```

```python
import functools
import math

import jax
import jax.numpy as jnp
import numpy as np
from jax import lax
from jax.experimental import pallas as pl
from jax.experimental.pallas import tpu as pltpu
from jax.sharding import PartitionSpec as P

HALO = 7
STEN = 15
PATCH = 64
TAU = 0.25
VIS = 0.5

LANES = 128
OUTER = 48
PAD = 8
TILES = OUTER // 2

QUARTER = (0, 4, 2, 1, 5, 9)
KEPT = tuple(4 * q for q in QUARTER) + tuple(2 + 8 * t for t in range(6)) + tuple(4 * q + 1 for q in range(12))


@functools.cache
def spectral_tables(length):
    signed = np.arange(length)
    signed = np.where(signed > length // 2, signed - length, signed)
    cutoff = length // 3
    ratio = signed.astype(np.float64) / cutoff
    multiplier = np.where(np.abs(signed) < cutoff, -VIS * ratio * ratio, 0.0)
    shift = np.arange(LANES)[None, :] - np.arange(LANES)[:, None]
    inner = np.arange(LANES)

    def complex_table(k1):
        wave = k1 + OUTER * inner
        spots = np.arange(-LANES + 1, LANES)
        phase = np.exp(2j * np.pi * ((wave[:, None] * spots[None, :]) % length) / length)
        return ((multiplier[wave][:, None] * phase).sum(axis=0) / LANES)[shift + LANES - 1]

    tables = np.zeros((TILES, 2 * LANES, 2 * LANES))
    tables[0, :LANES, :LANES] = complex_table(0).real / OUTER
    tables[0, LANES:, LANES:] = complex_table(OUTER // 2).real / OUTER
    for tile, k1 in enumerate(KEPT[1:], 1):
        table = complex_table(k1) * 2.0 / OUTER
        tables[tile, :LANES, :LANES] = table.real
        tables[tile, :LANES, LANES:] = table.imag
        tables[tile, LANES:, :LANES] = -table.imag
        tables[tile, LANES:, LANES:] = table.real
    high = tables.astype(jnp.bfloat16)
    low = (tables - high.astype(np.float64)).astype(jnp.bfloat16)
    return np.stack([high, low], axis=1)


def turn(value, numerator, denominator):
    re, im = value
    numerator %= denominator
    if numerator == 0:
        return value
    if 2 * numerator == denominator:
        return (-re, -im)
    if 4 * numerator == denominator:
        return (-im, re)
    if 4 * numerator == 3 * denominator:
        return (im, -re)
    cos = math.cos(2 * math.pi * numerator / denominator)
    sin = math.sin(2 * math.pi * numerator / denominator)
    return (re * cos - im * sin, re * sin + im * cos)


def add(a, b):
    return (a[0] + b[0], a[1] + b[1])


def sub(a, b):
    return (a[0] - b[0], a[1] - b[1])


ROOT = math.sqrt(3.0) / 2.0


def dft3(x, sign):
    total = add(x[1], x[2])
    other = sub(x[1], x[2])
    middle = (x[0][0] - 0.5 * total[0], x[0][1] - 0.5 * total[1])
    side = (-sign * ROOT * other[1], sign * ROOT * other[0])
    return [add(x[0], total), add(middle, side), sub(middle, side)]


def dft6(x, sign):
    even = dft3([add(x[b], x[b + 3]) for b in range(3)], sign)
    odd = dft3([turn(sub(x[b], x[b + 3]), sign * b, 6) for b in range(3)], sign)
    return [even[0], odd[0], even[1], odd[1], even[2], odd[2]]


def dft12(x, sign):
    out = [None] * 12
    parts = [[], [], [], []]
    for b in range(3):
        a0, a1, a2, a3 = x[b], x[b + 3], x[b + 6], x[b + 9]
        s0, s1, d0, d1 = add(a0, a2), add(a1, a3), sub(a0, a2), turn(sub(a1, a3), sign, 4)
        for r, value in enumerate((add(s0, s1), add(d0, d1), sub(s0, s1), sub(d0, d1))):
            parts[r].append(turn(value, sign * b * r, 12))
    for r in range(4):
        for q, value in enumerate(dft3(parts[r], sign)):
            out[4 * q + r] = value
    return out


def real_forward(x):
    whole, halved, turned = [], [], []
    for b in range(12):
        s0, s1 = x[b] + x[b + 24], x[b + 12] + x[b + 36]
        whole.append(s0 + s1)
        halved.append(s0 - s1)
        turned.append(turn((x[b] - x[b + 24], x[b + 36] - x[b + 12]), -b, 48))
    w, h, t = [], [], []
    for b in range(3):
        s0, s1 = whole[b] + whole[b + 6], whole[b + 3] + whole[b + 9]
        w.append(s0 + s1)
        h.append(s0 - s1)
        t.append(turn((whole[b] - whole[b + 6], whole[b + 9] - whole[b + 3]), -b, 12))
    total, other = w[1] + w[2], w[1] - w[2]
    four = (w[0] - 0.5 * total, -ROOT * other)
    two = (h[0] + 0.5 * (h[1] - h[2]), -ROOT * (h[1] + h[2]))
    tiles = [(w[0] + total, h[0] - h[1] + h[2]), four, two] + dft3(t, -1)
    tiles += dft6([turn((halved[b], -halved[b + 6]), -b, 24) for b in range(6)], -1)
    return tiles + dft12(turned, -1)


def real_backward(tiles):
    (zero, half), four, two = tiles[:3]
    w0 = zero + four[0]
    rest, side = zero - 0.5 * four[0], ROOT * four[1]
    w = [w0, rest - side, rest + side]
    h_side = 0.5 * two[0] - ROOT * two[1]
    h = [two[0] + half, h_side - half, -0.5 * two[0] - ROOT * two[1] + half]
    t = [turn(value, b, 12) for b, value in enumerate(dft3(tiles[3:6], 1))]
    whole = [None] * 12
    for b in range(3):
        s, d = w[b] + h[b], w[b] - h[b]
        whole[b], whole[b + 6] = s + t[b][0], s - t[b][0]
        whole[b + 3], whole[b + 9] = d - t[b][1], d + t[b][1]
    halved = [None] * 12
    for b, value in enumerate(dft6(tiles[6:12], 1)):
        halved[b], halved[b + 6] = turn(value, b, 24)
        halved[b + 6] = -halved[b + 6]
    x = [None] * 48
    for b, value in enumerate(dft12(tiles[12:], 1)):
        re, im = turn(value, b, 48)
        s, d = whole[b] + halved[b], whole[b] - halved[b]
        x[b], x[b + 24] = s + re, s - re
        x[b + 12], x[b + 36] = d - im, d + im
    return x


def filter_lines(line_ref, wave_ref, table_ref):
    _, line_count, row_count, width = line_ref.shape
    pieces = width // LANES
    groups = row_count // PAD

    def spots(step):
        return step // groups, pl.ds(pl.multiple_of(step % groups * PAD, PAD), PAD), pl.ds(pl.multiple_of(step * PAD, PAD), PAD)

    def forward(step, _):
        line, rows, spot = spots(step)
        values = [line_ref[n1 // pieces, line, rows, pl.ds(n1 % pieces * LANES, LANES)] for n1 in range(OUTER)]
        for tile, (re, im) in enumerate(real_forward(values)):
            wave_ref[tile, spot, :LANES] = re
            wave_ref[tile, spot, LANES:] = im
        return 0

    lax.fori_loop(0, line_count * groups, forward, 0)

    def middle(tile, _):
        value = wave_ref[tile]
        high = value.astype(jnp.bfloat16)
        low = (value - high.astype(jnp.float32)).astype(jnp.bfloat16)
        table_high, table_low = table_ref[tile, 0], table_ref[tile, 1]
        wave_ref[tile] = (
            jnp.dot(high, table_low, preferred_element_type=jnp.float32)
            + jnp.dot(low, table_high, preferred_element_type=jnp.float32)
            + jnp.dot(high, table_high, preferred_element_type=jnp.float32)
        )
        return 0

    lax.fori_loop(0, TILES, middle, 0)

    def backward(step, _):
        line, rows, spot = spots(step)
        tiles = [(wave_ref[tile, spot, :LANES], wave_ref[tile, spot, LANES:]) for tile in range(TILES)]
        for n1, value in enumerate(real_backward(tiles)):
            line_ref[n1 // pieces, line, rows, pl.ds(n1 % pieces * LANES, LANES)] = value
        return 0

    lax.fori_loop(0, line_count * groups, backward, 0)


def paired_kernel(me_ref, table_ref, field_ref, *refs):
    line_ref, wave_ref, sems = refs[-3:]
    count, _, row_count, _ = line_ref.shape
    received, sent = refs[: count - 1], refs[count - 1 : 2 * count - 1]
    me, mode, top = me_ref[0], me_ref[1], me_ref[2]
    own = field_ref.at[mode, 0, :, pl.ds(pl.multiple_of(top, PAD), row_count)]
    sources = (own,) + received
    copies = [pltpu.make_async_copy(sources[x], line_ref.at[me ^ x], sems.at[x]) for x in range(count)]
    for copy in copies:
        copy.start()
    for copy in copies:
        copy.wait()
    filter_lines(line_ref, wave_ref, table_ref)
    copies = [pltpu.make_async_copy(line_ref.at[me ^ x], sent[x], sems.at[x]) for x in range(count)]
    for copy in copies:
        copy.start()
    for copy in copies:
        copy.wait()


def filter_cost(count, rows, width):
    flops = 3 * 2 * TILES * rows * (2 * LANES) ** 2
    return pl.CostEstimate(flops=flops, bytes_accessed=8 * count * rows * width, transcendentals=0)


def filter_paired(field, received, spots, tables):
    count = len(received) + 1
    part_count, row_count, width = received[0].shape
    rows = part_count * row_count
    anywhere = pl.BlockSpec(memory_space=pl.ANY)
    return pl.pallas_call(
        paired_kernel,
        out_shape=[jax.ShapeDtypeStruct(received[0].shape, jnp.float32)] * count,
        in_specs=[pl.BlockSpec(memory_space=pltpu.SMEM), pl.BlockSpec(memory_space=pltpu.VMEM)] + [anywhere] * count,
        out_specs=[anywhere] * count,
        scratch_shapes=[
            pltpu.VMEM((count, part_count, row_count, width), jnp.float32),
            pltpu.VMEM((TILES, rows, 2 * LANES), jnp.float32),
            pltpu.SemaphoreType.DMA((count,)),
        ],
        compiler_params=pltpu.CompilerParams(vmem_limit_bytes=24 << 20),
        cost_estimate=filter_cost(count, rows, width),
        name="filter_paired",
    )(spots, tables, field, *received)


def whole_kernel(table_ref, line_ref, out_ref, wave_ref):
    out_ref[...] = line_ref[...]
    filter_lines(out_ref, wave_ref, table_ref)


def filter_whole(lines, tables):
    count, line_count, row_count, width = lines.shape
    rows = line_count * row_count
    vector = pl.BlockSpec(memory_space=pltpu.VMEM)
    return pl.pallas_call(
        whole_kernel,
        out_shape=jax.ShapeDtypeStruct(lines.shape, jnp.float32),
        in_specs=[vector] * 2,
        out_specs=vector,
        scratch_shapes=[pltpu.VMEM((TILES, rows, 2 * LANES), jnp.float32)],
        compiler_params=pltpu.CompilerParams(vmem_limit_bytes=24 << 20),
        cost_estimate=filter_cost(count, rows, width),
        name="filter_whole",
    )(tables, lines)


def local_kernel(rate_ref, coef_ref, flow_ref, field_ref, low_ref, high_ref, out_ref, pad_ref):
    _, comp_count, part_count, row_count, width = field_ref.shape
    pad_ref[:, :, :PAD] = low_ref[0]
    pad_ref[:, :, PAD : PAD + row_count] = field_ref[0]
    pad_ref[:, :, PAD + row_count :] = high_ref[0]
    rate = rate_ref[pl.program_id(0)]

    def column(step, _):
        lanes = pl.ds(pl.multiple_of(step * LANES, LANES), LANES)
        for top in range(0, row_count, PAD):
            rows = pl.ds(top, PAD)
            advect = rate * flow_ref[0, rows, :]
            shear = TAU * flow_ref[1, rows, :]
            centre = [[field_ref[0, c, p, rows, lanes] for p in range(2)] for c in range(comp_count)]
            for c in range(comp_count):
                for p in range(2):
                    total = centre[c][p]
                    total = total - advect * centre[c][1] if p == 0 else total + advect * centre[c][0]
                    if c == 1:
                        total = total - shear * centre[0][p]
                    for offset in range(STEN):
                        near = pad_ref[c, p, pl.ds(top + offset + PAD - HALO, PAD), lanes]
                        total = total + coef_ref[offset, rows, :] * near
                    out_ref[0, c, p, rows, lanes] = total
        return 0

    lax.fori_loop(0, width // LANES, column, 0)


def local_terms(field, low, high, rate, coef, flow):
    mode_count, comp_count, part_count, row_count, width = field.shape
    block = (1, comp_count, part_count, row_count, width)
    edge = (1, comp_count, part_count, PAD, width)

    def by_mode(m):
        return (m, 0, 0, 0, 0)

    return pl.pallas_call(
        local_kernel,
        grid=(mode_count,),
        out_shape=jax.ShapeDtypeStruct(field.shape, jnp.float32),
        in_specs=[
            pl.BlockSpec(memory_space=pltpu.SMEM),
            pl.BlockSpec(coef.shape, lambda m: (0, 0, 0)),
            pl.BlockSpec(flow.shape, lambda m: (0, 0, 0)),
            pl.BlockSpec(block, by_mode),
            pl.BlockSpec(edge, by_mode),
            pl.BlockSpec(edge, by_mode),
        ],
        out_specs=pl.BlockSpec(block, by_mode),
        scratch_shapes=[pltpu.VMEM((comp_count, part_count, row_count + 2 * PAD, width), jnp.float32)],
        compiler_params=pltpu.CompilerParams(vmem_limit_bytes=24 << 20),
        cost_estimate=pl.CostEstimate(flops=40 * field.size, bytes_accessed=10 * field.size, transcendentals=0),
        name="local_terms",
    )(rate, coef, flow, field, low, high)


def add_paired_kernel(row_split, me_ref, weight_ref, base_ref, *refs):
    buffer_ref, sems = refs[-2:]
    count, part_count, row_count, _ = buffer_ref.shape
    terms, out_ref, shear_ref = refs[:count], refs[count], refs[count + 1]
    me = me_ref[0]

    def spot(ref, x):
        other = me ^ x
        top = pl.multiple_of(other % row_split * row_count, PAD)
        return ref.at[other // row_split, 0, :, pl.ds(top, row_count)]

    loads = [pltpu.make_async_copy(spot(base_ref, x), buffer_ref.at[x], sems.at[x]) for x in range(count)]
    stores = [pltpu.make_async_copy(buffer_ref.at[x], spot(out_ref, x), sems.at[x]) for x in range(count)]
    for load in loads:
        load.start()
    for x in range(count):
        loads[x].wait()
        buffer_ref[x] = buffer_ref[x] + terms[x][...]
        stores[x].start()
        for p in range(part_count):
            lower, upper = buffer_ref[x, p, :PAD], buffer_ref[x, p, row_count - PAD :]
            shear_ref[me ^ x, p] = jnp.sum(lower * weight_ref[x, 0][:, :1], axis=0)
            shear_ref[me ^ x, part_count + p] = jnp.sum(upper * weight_ref[x, 1][:, :1], axis=0)
    for store in stores:
        store.wait()


def add_paired(base, terms, weight, spots, row_split):
    count = len(terms)
    part_count, _, width = terms[0].shape
    size = count * terms[0].size
    anywhere, vector = pl.BlockSpec(memory_space=pl.ANY), pl.BlockSpec(memory_space=pltpu.VMEM)
    return pl.pallas_call(
        functools.partial(add_paired_kernel, row_split),
        out_shape=(
            jax.ShapeDtypeStruct(base.shape, jnp.float32),
            jax.ShapeDtypeStruct((count, 2 * part_count, width), jnp.float32),
        ),
        in_specs=[pl.BlockSpec(memory_space=pltpu.SMEM), vector, anywhere] + [vector] * count,
        out_specs=(anywhere, vector),
        scratch_shapes=[pltpu.VMEM((count,) + terms[0].shape, jnp.float32), pltpu.SemaphoreType.DMA((count,))],
        input_output_aliases={2: 0},
        compiler_params=pltpu.CompilerParams(vmem_limit_bytes=16 << 20),
        cost_estimate=pl.CostEstimate(flops=size, bytes_accessed=12 * size, transcendentals=0),
        name="add_paired",
    )(spots, weight, base, *terms)


def add_whole_kernel(row_split, base_ref, term_ref, out_ref, buffer_ref, sems):
    count, comps, _, row_count, _ = term_ref.shape

    def spot(ref, source):
        rows = pl.ds(source % row_split * row_count, row_count)
        return ref.at[source // row_split, pl.ds(1, comps), :, rows]

    loads = [pltpu.make_async_copy(spot(base_ref, x), buffer_ref.at[x], sems.at[x]) for x in range(count)]
    stores = [pltpu.make_async_copy(buffer_ref.at[x], spot(out_ref, x), sems.at[x]) for x in range(count)]
    for load in loads:
        load.start()
    for x in range(count):
        loads[x].wait()
        buffer_ref[x] = buffer_ref[x] + term_ref[x]
        stores[x].start()
    for store in stores:
        store.wait()


def add_whole(base, term, row_split):
    anywhere, vector = pl.BlockSpec(memory_space=pl.ANY), pl.BlockSpec(memory_space=pltpu.VMEM)
    return pl.pallas_call(
        functools.partial(add_whole_kernel, row_split),
        out_shape=jax.ShapeDtypeStruct(base.shape, jnp.float32),
        in_specs=[anywhere, vector],
        out_specs=anywhere,
        scratch_shapes=[pltpu.VMEM(term.shape, jnp.float32), pltpu.SemaphoreType.DMA((term.shape[0],))],
        input_output_aliases={0: 0},
        compiler_params=pltpu.CompilerParams(vmem_limit_bytes=16 << 20),
        cost_estimate=pl.CostEstimate(flops=term.size, bytes_accessed=12 * term.size, transcendentals=0),
        name="add_whole",
    )(base, term)


def after(value, *others):
    return lax.optimization_barrier((value,) + others)[0]


def on_device(field, mean_flow, d2_coef, wall_coef, kx_index, patch_of):
    mode_count, comp_count, part_count, row_count, width = field.shape
    span = lax.axis_size("span")
    me = lax.axis_index("span")
    wall_count = lax.axis_size("wall")
    wall_index = lax.axis_index("wall")
    mode_split = math.gcd(span, mode_count)
    row_split = span // mode_split
    line_rows = row_count // row_split
    tables = jnp.asarray(spectral_tables(width * span))
    pairs = [[(i, i ^ x) for i in range(span)] for x in range(span)]
    spots = jnp.stack([me, me // row_split, me % row_split * line_rows]).astype(jnp.int32)

    def block_of(x):
        other = me ^ x
        start = (other // row_split, 0, 0, other % row_split * line_rows, 0)
        return lax.dynamic_slice(field, start, (1, 1, part_count, line_rows, width))[0, 0]

    def exchange(lines):
        return lax.all_to_all(lines, "span", split_axis=0, concat_axis=0)

    forward = [(i, i + 1) for i in range(wall_count - 1)]
    backward = [(i + 1, i) for i in range(wall_count - 1)]
    first = [lax.ppermute(block_of(x), "span", pairs[x]) for x in range(span - 1, 0, -1)][::-1]
    rest = field[:, 1:].reshape(mode_split, -1, row_split, line_rows, width)
    rest = exchange(rest.transpose(0, 2, 1, 3, 4).reshape(span, -1, line_rows, width))
    low = lax.ppermute(field[:, :, :, row_count - PAD :], "wall", forward)
    high = lax.ppermute(field[:, :, :, :PAD], "wall", backward)

    rate = kx_index.astype(jnp.float32) * (0.25 * TAU)
    coef = jnp.broadcast_to(d2_coef[:, :, None], (STEN, row_count, LANES))
    flow = jnp.broadcast_to(mean_flow[:, :, None], (2, row_count, LANES))
    base = local_terms(field, low, high, rate, coef, flow)

    first = list(lax.optimization_barrier((tuple(first), base))[0])
    sent = filter_paired(field, first, spots, tables)
    terms = [sent[0]] + [lax.ppermute(sent[x], "span", pairs[x]) for x in range(span - 1, 0, -1)][::-1]
    filtered = filter_whole(after(rest, sent[0]), tables)
    back = exchange(filtered).reshape(span, comp_count - 1, part_count, line_rows, width)

    lower = jnp.where(wall_index == 0, wall_coef[0], 0.0)
    upper = jnp.where(wall_index == wall_count - 1, wall_coef[1, ::-1], 0.0)
    group = (me ^ jnp.arange(span)) % row_split
    weight = jnp.stack(
        [jnp.where((group == 0)[:, None], lower, 0.0), jnp.where((group == row_split - 1)[:, None], upper, 0.0)], axis=1
    )
    weight = jnp.broadcast_to(weight[..., None], (span, 2, PAD, LANES))
    onehot = (patch_of[:, None] == jnp.arange(PATCH, dtype=jnp.int32)[None, :]).astype(jnp.float32)
    terms[0] = after(terms[0], filtered)
    result, shear = add_paired(base, terms, weight, spots, row_split)
    grad = jnp.einsum("swz,zq->swq", shear, onehot, precision=lax.Precision.HIGHEST)
    grad = grad.reshape(mode_count, row_split, 2, part_count, PATCH).sum(axis=1)
    for axis, count in (("wall", wall_count), ("span", span)):
        distance = 1
        while distance < count:
            grad = grad + lax.ppermute(grad, axis, [(i, i ^ distance) for i in range(count)])
            distance *= 2
    return (add_whole(result, back, row_split), grad.transpose(1, 0, 2, 3))


def solution(mesh):
    return jax.shard_map(
        on_device,
        mesh=mesh,
        in_specs=(
            P(None, None, None, "wall", "span"),
            P(None, "wall"),
            P(None, "wall"),
            P(),
            P(),
            P("span"),
        ),
        out_specs=(P(None, None, None, "wall", "span"), P()),
        check_vma=False,
    )
```

```python
import functools
import math

import jax
import jax.numpy as jnp
import numpy as np
from jax import lax
from jax.experimental import pallas as pl
from jax.experimental.pallas import tpu as pltpu
from jax.sharding import PartitionSpec as P

HALO = 7
STEN = 15
PATCH = 64
TAU = 0.25
VIS = 0.5

LANES = 128
OUTER = 48
PAD = 8
TILES = OUTER // 2

QUARTER = (0, 4, 2, 1, 5, 9)
KEPT = tuple(4 * q for q in QUARTER) + tuple(2 + 8 * t for t in range(6)) + tuple(4 * q + 1 for q in range(12))


@functools.cache
def spectral_tables(length):
    signed = np.arange(length)
    signed = np.where(signed > length // 2, signed - length, signed)
    cutoff = length // 3
    ratio = signed.astype(np.float64) / cutoff
    multiplier = np.where(np.abs(signed) < cutoff, -VIS * ratio * ratio, 0.0)
    shift = np.arange(LANES)[None, :] - np.arange(LANES)[:, None]
    inner = np.arange(LANES)

    def complex_table(k1):
        wave = k1 + OUTER * inner
        spots = np.arange(-LANES + 1, LANES)
        phase = np.exp(2j * np.pi * ((wave[:, None] * spots[None, :]) % length) / length)
        return ((multiplier[wave][:, None] * phase).sum(axis=0) / LANES)[shift + LANES - 1]

    tables = np.zeros((TILES, 2 * LANES, 2 * LANES))
    tables[0, :LANES, :LANES] = complex_table(0).real / OUTER
    tables[0, LANES:, LANES:] = complex_table(OUTER // 2).real / OUTER
    for tile, k1 in enumerate(KEPT[1:], 1):
        table = complex_table(k1) * 2.0 / OUTER
        tables[tile, :LANES, :LANES] = table.real
        tables[tile, :LANES, LANES:] = table.imag
        tables[tile, LANES:, :LANES] = -table.imag
        tables[tile, LANES:, LANES:] = table.real
    high = tables.astype(jnp.bfloat16)
    low = (tables - high.astype(np.float64)).astype(jnp.bfloat16)
    return np.stack([high, low], axis=1)


def turn(value, numerator, denominator):
    re, im = value
    numerator %= denominator
    if numerator == 0:
        return value
    if 2 * numerator == denominator:
        return (-re, -im)
    if 4 * numerator == denominator:
        return (-im, re)
    if 4 * numerator == 3 * denominator:
        return (im, -re)
    cos = math.cos(2 * math.pi * numerator / denominator)
    sin = math.sin(2 * math.pi * numerator / denominator)
    return (re * cos - im * sin, re * sin + im * cos)


def add(a, b):
    return (a[0] + b[0], a[1] + b[1])


def sub(a, b):
    return (a[0] - b[0], a[1] - b[1])


ROOT = math.sqrt(3.0) / 2.0


def dft3(x, sign):
    total = add(x[1], x[2])
    other = sub(x[1], x[2])
    middle = (x[0][0] - 0.5 * total[0], x[0][1] - 0.5 * total[1])
    side = (-sign * ROOT * other[1], sign * ROOT * other[0])
    return [add(x[0], total), add(middle, side), sub(middle, side)]


def dft6(x, sign):
    even = dft3([add(x[b], x[b + 3]) for b in range(3)], sign)
    odd = dft3([turn(sub(x[b], x[b + 3]), sign * b, 6) for b in range(3)], sign)
    return [even[0], odd[0], even[1], odd[1], even[2], odd[2]]


def dft12(x, sign):
    out = [None] * 12
    parts = [[], [], [], []]
    for b in range(3):
        a0, a1, a2, a3 = x[b], x[b + 3], x[b + 6], x[b + 9]
        s0, s1, d0, d1 = add(a0, a2), add(a1, a3), sub(a0, a2), turn(sub(a1, a3), sign, 4)
        for r, value in enumerate((add(s0, s1), add(d0, d1), sub(s0, s1), sub(d0, d1))):
            parts[r].append(turn(value, sign * b * r, 12))
    for r in range(4):
        for q, value in enumerate(dft3(parts[r], sign)):
            out[4 * q + r] = value
    return out


def real_forward(x):
    whole, halved, turned = [], [], []
    for b in range(12):
        s0, s1 = x[b] + x[b + 24], x[b + 12] + x[b + 36]
        whole.append(s0 + s1)
        halved.append(s0 - s1)
        turned.append(turn((x[b] - x[b + 24], x[b + 36] - x[b + 12]), -b, 48))
    w, h, t = [], [], []
    for b in range(3):
        s0, s1 = whole[b] + whole[b + 6], whole[b + 3] + whole[b + 9]
        w.append(s0 + s1)
        h.append(s0 - s1)
        t.append(turn((whole[b] - whole[b + 6], whole[b + 9] - whole[b + 3]), -b, 12))
    total, other = w[1] + w[2], w[1] - w[2]
    four = (w[0] - 0.5 * total, -ROOT * other)
    two = (h[0] + 0.5 * (h[1] - h[2]), -ROOT * (h[1] + h[2]))
    tiles = [(w[0] + total, h[0] - h[1] + h[2]), four, two] + dft3(t, -1)
    tiles += dft6([turn((halved[b], -halved[b + 6]), -b, 24) for b in range(6)], -1)
    return tiles + dft12(turned, -1)


def real_backward(tiles):
    (zero, half), four, two = tiles[:3]
    w0 = zero + four[0]
    rest, side = zero - 0.5 * four[0], ROOT * four[1]
    w = [w0, rest - side, rest + side]
    h_side = 0.5 * two[0] - ROOT * two[1]
    h = [two[0] + half, h_side - half, -0.5 * two[0] - ROOT * two[1] + half]
    t = [turn(value, b, 12) for b, value in enumerate(dft3(tiles[3:6], 1))]
    whole = [None] * 12
    for b in range(3):
        s, d = w[b] + h[b], w[b] - h[b]
        whole[b], whole[b + 6] = s + t[b][0], s - t[b][0]
        whole[b + 3], whole[b + 9] = d - t[b][1], d + t[b][1]
    halved = [None] * 12
    for b, value in enumerate(dft6(tiles[6:12], 1)):
        halved[b], halved[b + 6] = turn(value, b, 24)
        halved[b + 6] = -halved[b + 6]
    x = [None] * 48
    for b, value in enumerate(dft12(tiles[12:], 1)):
        re, im = turn(value, b, 48)
        s, d = whole[b] + halved[b], whole[b] - halved[b]
        x[b], x[b + 24] = s + re, s - re
        x[b + 12], x[b + 36] = d - im, d + im
    return x


def filter_lines(line_ref, wave_ref, table_ref, table_copy):
    _, line_count, row_count, width = line_ref.shape
    pieces = width // LANES
    groups = row_count // PAD

    def spots(step):
        return step // groups, pl.ds(pl.multiple_of(step % groups * PAD, PAD), PAD), pl.ds(pl.multiple_of(step * PAD, PAD), PAD)

    def forward(step, _):
        line, rows, spot = spots(step)
        values = [line_ref[n1 // pieces, line, rows, pl.ds(n1 % pieces * LANES, LANES)] for n1 in range(OUTER)]
        for tile, (re, im) in enumerate(real_forward(values)):
            wave_ref[tile, spot, :LANES] = re
            wave_ref[tile, spot, LANES:] = im
        return 0

    lax.fori_loop(0, line_count * groups, forward, 0)

    def middle(tile, _):
        value = wave_ref[tile]
        high = value.astype(jnp.bfloat16)
        low = (value - high.astype(jnp.float32)).astype(jnp.bfloat16)
        rows = high.shape[0]
        both = jnp.dot(jnp.concatenate([high, low]), table_ref[tile, 0], preferred_element_type=jnp.float32)
        rest = jnp.dot(high, table_ref[tile, 1], preferred_element_type=jnp.float32)
        wave_ref[tile] = both[:rows] + both[rows:] + rest
        return 0

    table_copy.wait()
    lax.fori_loop(0, TILES, middle, 0, unroll=4)

    def backward(step, _):
        line, rows, spot = spots(step)
        tiles = [(wave_ref[tile, spot, :LANES], wave_ref[tile, spot, LANES:]) for tile in range(TILES)]
        for n1, value in enumerate(real_backward(tiles)):
            line_ref[n1 // pieces, line, rows, pl.ds(n1 % pieces * LANES, LANES)] = value
        return 0

    lax.fori_loop(0, line_count * groups, backward, 0)


def filter_kernel(me_ref, table_hbm, lines_hbm, *refs):
    line_ref, wave_ref, table_ref, table_sem, sems = refs[-5:]
    sent = refs[:-5]
    count = len(sent)
    me = me_ref[0]
    copies = [pltpu.make_async_copy(lines_hbm.at[x], line_ref.at[x], sems.at[x]) for x in range(count)]
    for copy in copies:
        copy.start()
    table_copy = pltpu.make_async_copy(table_hbm, table_ref, table_sem)
    table_copy.start()
    for copy in copies:
        copy.wait()
    filter_lines(line_ref, wave_ref, table_ref, table_copy)
    copies = [pltpu.make_async_copy(line_ref.at[me ^ x], sent[x], sems.at[x]) for x in range(count)]
    for copy in copies:
        copy.start()
    for copy in copies:
        copy.wait()


HBM = pl.BlockSpec(memory_space=pltpu.HBM)


def filter_component(lines, spots, tables):
    count, part_count, row_count, width = lines.shape
    rows = part_count * row_count
    flops = 3 * 2 * TILES * rows * (2 * LANES) ** 2
    return pl.pallas_call(
        filter_kernel,
        out_shape=[jax.ShapeDtypeStruct(lines.shape[1:], jnp.float32)] * count,
        in_specs=[pl.BlockSpec(memory_space=pltpu.SMEM), HBM, HBM],
        out_specs=[HBM] * count,
        scratch_shapes=[
            pltpu.VMEM(lines.shape, jnp.float32),
            pltpu.VMEM((TILES, rows, 2 * LANES), jnp.float32),
            pltpu.VMEM(tables.shape, tables.dtype),
            pltpu.SemaphoreType.DMA,
            pltpu.SemaphoreType.DMA((count,)),
        ],
        compiler_params=pltpu.CompilerParams(vmem_limit_bytes=24 << 20),
        cost_estimate=pl.CostEstimate(flops=flops, bytes_accessed=8 * lines.size, transcendentals=0),
        name="filter_component",
    )(spots, tables, lines)


def local_kernel(rate_ref, coef_ref, flow_ref, field_ref, low_ref, high_ref, out_ref, pad_ref):
    _, comp_count, part_count, row_count, width = field_ref.shape
    pad_ref[:, :, :PAD] = low_ref[0]
    pad_ref[:, :, PAD : PAD + row_count] = field_ref[0]
    pad_ref[:, :, PAD + row_count :] = high_ref[0]
    rate = rate_ref[pl.program_id(0)]

    def column(step, _):
        lanes = pl.ds(pl.multiple_of(step * LANES, LANES), LANES)
        for top in range(0, row_count, PAD):
            rows = pl.ds(top, PAD)
            advect = rate * flow_ref[0, rows, :]
            shear = TAU * flow_ref[1, rows, :]
            centre = [[field_ref[0, c, p, rows, lanes] for p in range(2)] for c in range(comp_count)]
            for c in range(comp_count):
                for p in range(2):
                    total = centre[c][p]
                    total = total - advect * centre[c][1] if p == 0 else total + advect * centre[c][0]
                    if c == 1:
                        total = total - shear * centre[0][p]
                    for offset in range(STEN):
                        near = pad_ref[c, p, pl.ds(top + offset + PAD - HALO, PAD), lanes]
                        total = total + coef_ref[offset, rows, :] * near
                    out_ref[0, c, p, rows, lanes] = total
        return 0

    lax.fori_loop(0, width // LANES, column, 0)


def local_terms(field, low, high, rate, coef, flow):
    mode_count, comp_count, part_count, row_count, width = field.shape
    block = (1, comp_count, part_count, row_count, width)
    edge = (1, comp_count, part_count, PAD, width)

    def by_mode(m):
        return (m, 0, 0, 0, 0)

    return pl.pallas_call(
        local_kernel,
        grid=(mode_count,),
        out_shape=jax.ShapeDtypeStruct(field.shape, jnp.float32),
        in_specs=[
            pl.BlockSpec(memory_space=pltpu.SMEM),
            pl.BlockSpec(coef.shape, lambda m: (0, 0, 0)),
            pl.BlockSpec(flow.shape, lambda m: (0, 0, 0)),
            pl.BlockSpec(block, by_mode),
            pl.BlockSpec(edge, by_mode),
            pl.BlockSpec(edge, by_mode),
        ],
        out_specs=pl.BlockSpec(block, by_mode),
        scratch_shapes=[pltpu.VMEM((comp_count, part_count, row_count + 2 * PAD, width), jnp.float32)],
        compiler_params=pltpu.CompilerParams(vmem_limit_bytes=24 << 20),
        cost_estimate=pl.CostEstimate(flops=40 * field.size, bytes_accessed=10 * field.size, transcendentals=0),
        name="local_terms",
    )(rate, coef, flow, field, low, high)


def add_kernel(row_split, comp, me_ref, *refs):
    weight_ref = refs[0] if comp == 0 else None
    base_hbm, *refs = refs[1:] if comp == 0 else refs
    base_ref, term_ref, base_sems, term_sems = refs[-4:]
    count, part_count, row_count, _ = base_ref.shape
    terms, out_hbm = refs[:count], refs[count]
    me = me_ref[0]

    def spot(ref, x):
        other = me ^ x
        top = pl.multiple_of(other % row_split * row_count, PAD)
        return ref.at[other // row_split, comp, :, pl.ds(top, row_count)]

    loads = [pltpu.make_async_copy(spot(base_hbm, x), base_ref.at[x], base_sems.at[x]) for x in range(count)]
    term_loads = [pltpu.make_async_copy(terms[x], term_ref.at[x], term_sems.at[x]) for x in range(count)]
    stores = [pltpu.make_async_copy(base_ref.at[x], spot(out_hbm, x), base_sems.at[x]) for x in range(count)]
    for x in range(count):
        loads[x].start()
        term_loads[x].start()
    for x in range(count):
        loads[x].wait()
        term_loads[x].wait()
        base_ref[x] = base_ref[x] + term_ref[x]
        stores[x].start()
        if comp == 0:
            shear_ref = refs[count + 1]
            for p in range(part_count):
                lower, upper = base_ref[x, p, :PAD], base_ref[x, p, row_count - PAD :]
                shear_ref[me ^ x, p] = jnp.sum(lower * weight_ref[x, 0][:, :1], axis=0)
                shear_ref[me ^ x, part_count + p] = jnp.sum(upper * weight_ref[x, 1][:, :1], axis=0)
    for store in stores:
        store.wait()


def add_component(base, terms, spots, row_split, comp, weight):
    count = len(terms)
    part_count, _, width = terms[0].shape
    size = count * terms[0].size
    vector = pl.BlockSpec(memory_space=pltpu.VMEM)
    first = comp == 0
    block = pltpu.VMEM((count,) + terms[0].shape, jnp.float32)
    sums = jax.ShapeDtypeStruct((count, 2 * part_count, width), jnp.float32)
    return pl.pallas_call(
        functools.partial(add_kernel, row_split, comp),
        out_shape=[jax.ShapeDtypeStruct(base.shape, jnp.float32)] + [sums] * first,
        in_specs=[pl.BlockSpec(memory_space=pltpu.SMEM)] + [vector] * first + [HBM] * (count + 1),
        out_specs=[HBM] + [vector] * first,
        scratch_shapes=[block, block, pltpu.SemaphoreType.DMA((count,)), pltpu.SemaphoreType.DMA((count,))],
        input_output_aliases={1 + first: 0},
        compiler_params=pltpu.CompilerParams(vmem_limit_bytes=16 << 20),
        cost_estimate=pl.CostEstimate(flops=size, bytes_accessed=12 * size, transcendentals=0),
        name="add_component",
    )(spots, *[weight] * first, base, *terms)


def after(value, *others):
    return lax.optimization_barrier((value,) + others)[0]


def on_device(field, mean_flow, d2_coef, wall_coef, kx_index, patch_of):
    mode_count, comp_count, part_count, row_count, width = field.shape
    span = lax.axis_size("span")
    me = lax.axis_index("span")
    wall_count = lax.axis_size("wall")
    wall_index = lax.axis_index("wall")
    mode_split = math.gcd(span, mode_count)
    row_split = span // mode_split
    line_rows = row_count // row_split
    tables = jnp.asarray(spectral_tables(width * span))
    pairs = [[(i, i ^ x) for i in range(span)] for x in range(span)]
    spots = jnp.stack([me, me // row_split, me % row_split * line_rows]).astype(jnp.int32)

    def to_lines(comp):
        lines = field[:, comp].reshape(mode_split, -1, row_split, line_rows, width)
        lines = lines.transpose(0, 2, 1, 3, 4).reshape(span, -1, line_rows, width)
        return lax.all_to_all(lines, "span", split_axis=0, concat_axis=0)

    def send_back(sent):
        return [sent[0]] + [lax.ppermute(sent[x], "span", pairs[x]) for x in range(span - 1, 0, -1)][::-1]

    forward = [(i, i + 1) for i in range(wall_count - 1)]
    backward = [(i + 1, i) for i in range(wall_count - 1)]
    lines = [to_lines(comp) for comp in range(comp_count)]
    low = lax.ppermute(field[:, :, :, row_count - PAD :], "wall", forward)
    high = lax.ppermute(field[:, :, :, :PAD], "wall", backward)

    sent = [filter_component(lines[0], spots, tables)]
    terms = [send_back(sent[0])]

    rate = kx_index.astype(jnp.float32) * (0.25 * TAU)
    coef = jnp.broadcast_to(d2_coef[:, :, None], (STEN, row_count, LANES))
    flow = jnp.broadcast_to(mean_flow[:, :, None], (2, row_count, LANES))
    base = local_terms(field, after(low, sent[0][0]), high, rate, coef, flow)

    sent.append(filter_component(after(lines[1], base), spots, tables))
    terms.append(send_back(sent[1]))

    lower = jnp.where(wall_index == 0, wall_coef[0], 0.0)
    upper = jnp.where(wall_index == wall_count - 1, wall_coef[1, ::-1], 0.0)
    group = (me ^ jnp.arange(span)) % row_split
    weight = jnp.stack(
        [jnp.where((group == 0)[:, None], lower, 0.0), jnp.where((group == row_split - 1)[:, None], upper, 0.0)], axis=1
    )
    weight = jnp.broadcast_to(weight[..., None], (span, 2, PAD, LANES))
    onehot = (patch_of[:, None] == jnp.arange(PATCH, dtype=jnp.int32)[None, :]).astype(jnp.float32)
    terms[0][0] = after(terms[0][0], sent[1][0])
    result, shear = add_component(base, terms[0], spots, row_split, 0, weight)
    grad = jnp.einsum("swz,zq->swq", shear, onehot, precision=lax.Precision.HIGHEST)
    grad = grad.reshape(mode_count, row_split, 2, part_count, PATCH).sum(axis=1)
    for axis, count in (("wall", wall_count), ("span", span)):
        distance = 1
        while distance < count:
            grad = grad + lax.ppermute(grad, axis, [(i, i ^ distance) for i in range(count)])
            distance *= 2

    for comp in range(2, comp_count):
        sent.append(filter_component(after(lines[comp], grad), spots, tables))
        terms.append(send_back(sent[comp]))
    for comp in range(1, comp_count):
        terms[comp][0] = after(terms[comp][0], sent[-1][0])
        (result,) = add_component(result, terms[comp], spots, row_split, comp, None)
    return (result, grad.transpose(1, 0, 2, 3))


def solution(mesh):
    return jax.shard_map(
        on_device,
        mesh=mesh,
        in_specs=(
            P(None, None, None, "wall", "span"),
            P(None, "wall"),
            P(None, "wall"),
            P(),
            P(),
            P("span"),
        ),
        out_specs=(P(None, None, None, "wall", "span"), P()),
        check_vma=False,
    )
```

```python
import functools
import math

import jax
import jax.numpy as jnp
import numpy as np
from jax import lax
from jax.experimental import pallas as pl
from jax.experimental.pallas import tpu as pltpu
from jax.sharding import PartitionSpec as P

HALO = 7
STEN = 15
PATCH = 64
TAU = 0.25
VIS = 0.5

LANES = 128
OUTER = 48
PAD = 8
TILES = OUTER // 2
FILTER_VMEM = 57_500_000

QUARTER = (0, 4, 2, 1, 5, 9)
KEPT = tuple(4 * q for q in QUARTER) + tuple(2 + 8 * t for t in range(6)) + tuple(4 * q + 1 for q in range(12))


@functools.cache
def spectral_tables(length):
    signed = np.arange(length)
    signed = np.where(signed > length // 2, signed - length, signed)
    cutoff = length // 3
    ratio = signed.astype(np.float64) / cutoff
    multiplier = np.where(np.abs(signed) < cutoff, -VIS * ratio * ratio, 0.0)
    shift = np.arange(LANES)[None, :] - np.arange(LANES)[:, None]
    inner = np.arange(LANES)

    def complex_table(k1):
        wave = k1 + OUTER * inner
        spots = np.arange(-LANES + 1, LANES)
        phase = np.exp(2j * np.pi * ((wave[:, None] * spots[None, :]) % length) / length)
        return ((multiplier[wave][:, None] * phase).sum(axis=0) / LANES)[shift + LANES - 1]

    tables = np.zeros((TILES, 2 * LANES, 2 * LANES))
    tables[0, :LANES, :LANES] = complex_table(0).real / OUTER
    tables[0, LANES:, LANES:] = complex_table(OUTER // 2).real / OUTER
    for tile, k1 in enumerate(KEPT[1:], 1):
        table = complex_table(k1) * 2.0 / OUTER
        tables[tile, :LANES, :LANES] = table.real
        tables[tile, :LANES, LANES:] = table.imag
        tables[tile, LANES:, :LANES] = -table.imag
        tables[tile, LANES:, LANES:] = table.real
    high = tables.astype(jnp.bfloat16)
    low = (tables - high.astype(np.float64)).astype(jnp.bfloat16)
    return np.stack([high, low], axis=1)


def turn(value, numerator, denominator):
    re, im = value
    numerator %= denominator
    if numerator == 0:
        return value
    if 2 * numerator == denominator:
        return (-re, -im)
    if 4 * numerator == denominator:
        return (-im, re)
    if 4 * numerator == 3 * denominator:
        return (im, -re)
    cos = math.cos(2 * math.pi * numerator / denominator)
    sin = math.sin(2 * math.pi * numerator / denominator)
    return (re * cos - im * sin, re * sin + im * cos)


def add(a, b):
    return (a[0] + b[0], a[1] + b[1])


def sub(a, b):
    return (a[0] - b[0], a[1] - b[1])


ROOT = math.sqrt(3.0) / 2.0


def dft3(x, sign):
    total = add(x[1], x[2])
    other = sub(x[1], x[2])
    middle = (x[0][0] - 0.5 * total[0], x[0][1] - 0.5 * total[1])
    side = (-sign * ROOT * other[1], sign * ROOT * other[0])
    return [add(x[0], total), add(middle, side), sub(middle, side)]


def dft6(x, sign):
    even = dft3([add(x[b], x[b + 3]) for b in range(3)], sign)
    odd = dft3([turn(sub(x[b], x[b + 3]), sign * b, 6) for b in range(3)], sign)
    return [even[0], odd[0], even[1], odd[1], even[2], odd[2]]


def dft12(x, sign):
    out = [None] * 12
    parts = [[], [], [], []]
    for b in range(3):
        a0, a1, a2, a3 = x[b], x[b + 3], x[b + 6], x[b + 9]
        s0, s1, d0, d1 = add(a0, a2), add(a1, a3), sub(a0, a2), turn(sub(a1, a3), sign, 4)
        for r, value in enumerate((add(s0, s1), add(d0, d1), sub(s0, s1), sub(d0, d1))):
            parts[r].append(turn(value, sign * b * r, 12))
    for r in range(4):
        for q, value in enumerate(dft3(parts[r], sign)):
            out[4 * q + r] = value
    return out


def real_forward(x):
    whole, halved, turned = [], [], []
    for b in range(12):
        s0, s1 = x[b] + x[b + 24], x[b + 12] + x[b + 36]
        whole.append(s0 + s1)
        halved.append(s0 - s1)
        turned.append(turn((x[b] - x[b + 24], x[b + 36] - x[b + 12]), -b, 48))
    w, h, t = [], [], []
    for b in range(3):
        s0, s1 = whole[b] + whole[b + 6], whole[b + 3] + whole[b + 9]
        w.append(s0 + s1)
        h.append(s0 - s1)
        t.append(turn((whole[b] - whole[b + 6], whole[b + 9] - whole[b + 3]), -b, 12))
    total, other = w[1] + w[2], w[1] - w[2]
    four = (w[0] - 0.5 * total, -ROOT * other)
    two = (h[0] + 0.5 * (h[1] - h[2]), -ROOT * (h[1] + h[2]))
    tiles = [(w[0] + total, h[0] - h[1] + h[2]), four, two] + dft3(t, -1)
    tiles += dft6([turn((halved[b], -halved[b + 6]), -b, 24) for b in range(6)], -1)
    return tiles + dft12(turned, -1)


def real_backward(tiles):
    (zero, half), four, two = tiles[:3]
    w0 = zero + four[0]
    rest, side = zero - 0.5 * four[0], ROOT * four[1]
    w = [w0, rest - side, rest + side]
    h_side = 0.5 * two[0] - ROOT * two[1]
    h = [two[0] + half, h_side - half, -0.5 * two[0] - ROOT * two[1] + half]
    t = [turn(value, b, 12) for b, value in enumerate(dft3(tiles[3:6], 1))]
    whole = [None] * 12
    for b in range(3):
        s, d = w[b] + h[b], w[b] - h[b]
        whole[b], whole[b + 6] = s + t[b][0], s - t[b][0]
        whole[b + 3], whole[b + 9] = d - t[b][1], d + t[b][1]
    halved = [None] * 12
    for b, value in enumerate(dft6(tiles[6:12], 1)):
        halved[b], halved[b + 6] = turn(value, b, 24)
        halved[b + 6] = -halved[b + 6]
    x = [None] * 48
    for b, value in enumerate(dft12(tiles[12:], 1)):
        re, im = turn(value, b, 48)
        s, d = whole[b] + halved[b], whole[b] - halved[b]
        x[b], x[b + 24] = s + re, s - re
        x[b + 12], x[b + 36] = d - im, d + im
    return x


def filter_lines(line_ref, wave_ref, table_ref, table_copy):
    _, line_count, row_count, width = line_ref.shape
    pieces = width // LANES
    groups = row_count // PAD

    def spots(step):
        return step // groups, pl.ds(pl.multiple_of(step % groups * PAD, PAD), PAD), pl.ds(pl.multiple_of(step * PAD, PAD), PAD)

    def forward(step, _):
        line, rows, spot = spots(step)
        values = [line_ref[n1 // pieces, line, rows, pl.ds(n1 % pieces * LANES, LANES)] for n1 in range(OUTER)]
        for tile, (re, im) in enumerate(real_forward(values)):
            wave_ref[tile, spot, :LANES] = re
            wave_ref[tile, spot, LANES:] = im
        return 0

    lax.fori_loop(0, line_count * groups, forward, 0)

    def middle(tile, _):
        value = wave_ref[tile]
        high = value.astype(jnp.bfloat16)
        low = (value - high.astype(jnp.float32)).astype(jnp.bfloat16)
        rows = high.shape[0]
        both = jnp.dot(jnp.concatenate([high, low]), table_ref[tile, 0], preferred_element_type=jnp.float32)
        rest = jnp.dot(high, table_ref[tile, 1], preferred_element_type=jnp.float32)
        wave_ref[tile] = both[:rows] + both[rows:] + rest
        return 0

    table_copy.wait()
    lax.fori_loop(0, TILES, middle, 0, unroll=4)

    def backward(step, _):
        line, rows, spot = spots(step)
        tiles = [(wave_ref[tile, spot, :LANES], wave_ref[tile, spot, LANES:]) for tile in range(TILES)]
        for n1, value in enumerate(real_backward(tiles)):
            line_ref[n1 // pieces, line, rows, pl.ds(n1 % pieces * LANES, LANES)] = value
        return 0

    lax.fori_loop(0, line_count * groups, backward, 0)


def filter_kernel(me_ref, table_hbm, lines_hbm, *refs):
    line_ref, wave_ref, table_ref, table_sem, sems = refs[-5:]
    sent = refs[:-5]
    count = len(sent)
    me = me_ref[0]
    copies = [pltpu.make_async_copy(lines_hbm.at[x], line_ref.at[x], sems.at[x]) for x in range(count)]
    for copy in copies:
        copy.start()
    table_copy = pltpu.make_async_copy(table_hbm, table_ref, table_sem)
    table_copy.start()
    for copy in copies:
        copy.wait()
    filter_lines(line_ref, wave_ref, table_ref, table_copy)
    copies = [pltpu.make_async_copy(line_ref.at[me ^ x], sent[x], sems.at[x]) for x in range(count)]
    for copy in copies:
        copy.start()
    for copy in copies:
        copy.wait()


HBM = pl.BlockSpec(memory_space=pltpu.HBM)


def filter_component(lines, spots, tables):
    count, part_count, row_count, width = lines.shape
    rows = part_count * row_count
    flops = 3 * 2 * TILES * rows * (2 * LANES) ** 2
    return pl.pallas_call(
        filter_kernel,
        out_shape=[jax.ShapeDtypeStruct(lines.shape[1:], jnp.float32)] * count,
        in_specs=[pl.BlockSpec(memory_space=pltpu.SMEM), HBM, HBM],
        out_specs=[HBM] * count,
        scratch_shapes=[
            pltpu.VMEM(lines.shape, jnp.float32),
            pltpu.VMEM((TILES, rows, 2 * LANES), jnp.float32),
            pltpu.VMEM(tables.shape, tables.dtype),
            pltpu.SemaphoreType.DMA,
            pltpu.SemaphoreType.DMA((count,)),
        ],
        compiler_params=pltpu.CompilerParams(vmem_limit_bytes=FILTER_VMEM),
        cost_estimate=pl.CostEstimate(flops=flops, bytes_accessed=8 * lines.size, transcendentals=0),
        name="filter_component",
    )(spots, tables, lines)


def local_kernel(rate_ref, coef_ref, flow_ref, field_ref, low_ref, high_ref, out_ref, pad_ref):
    _, comp_count, part_count, row_count, width = field_ref.shape
    pad_ref[:, :, :PAD] = low_ref[0]
    pad_ref[:, :, PAD : PAD + row_count] = field_ref[0]
    pad_ref[:, :, PAD + row_count :] = high_ref[0]
    rate = rate_ref[pl.program_id(0)]

    def column(step, _):
        lanes = pl.ds(pl.multiple_of(step * LANES, LANES), LANES)
        for top in range(0, row_count, PAD):
            rows = pl.ds(top, PAD)
            advect = rate * flow_ref[0, rows, :]
            shear = TAU * flow_ref[1, rows, :]
            centre = [[field_ref[0, c, p, rows, lanes] for p in range(2)] for c in range(comp_count)]
            for c in range(comp_count):
                for p in range(2):
                    total = centre[c][p]
                    total = total - advect * centre[c][1] if p == 0 else total + advect * centre[c][0]
                    if c == 1:
                        total = total - shear * centre[0][p]
                    for offset in range(STEN):
                        near = pad_ref[c, p, pl.ds(top + offset + PAD - HALO, PAD), lanes]
                        total = total + coef_ref[offset, rows, :] * near
                    out_ref[0, c, p, rows, lanes] = total
        return 0

    lax.fori_loop(0, width // LANES, column, 0)


def local_terms(field, low, high, rate, coef, flow):
    mode_count, comp_count, part_count, row_count, width = field.shape
    block = (1, comp_count, part_count, row_count, width)
    edge = (1, comp_count, part_count, PAD, width)

    def by_mode(m):
        return (m, 0, 0, 0, 0)

    return pl.pallas_call(
        local_kernel,
        grid=(mode_count,),
        out_shape=jax.ShapeDtypeStruct(field.shape, jnp.float32),
        in_specs=[
            pl.BlockSpec(memory_space=pltpu.SMEM),
            pl.BlockSpec(coef.shape, lambda m: (0, 0, 0)),
            pl.BlockSpec(flow.shape, lambda m: (0, 0, 0)),
            pl.BlockSpec(block, by_mode),
            pl.BlockSpec(edge, by_mode),
            pl.BlockSpec(edge, by_mode),
        ],
        out_specs=pl.BlockSpec(block, by_mode),
        scratch_shapes=[pltpu.VMEM((comp_count, part_count, row_count + 2 * PAD, width), jnp.float32)],
        compiler_params=pltpu.CompilerParams(vmem_limit_bytes=24 << 20),
        cost_estimate=pl.CostEstimate(flops=40 * field.size, bytes_accessed=10 * field.size, transcendentals=0),
        name="local_terms",
    )(rate, coef, flow, field, low, high)


def add_kernel(row_split, comp, me_ref, *refs):
    weight_ref = refs[0] if comp == 0 else None
    base_hbm, *refs = refs[1:] if comp == 0 else refs
    base_ref, term_ref, base_sems, term_sems = refs[-4:]
    count, part_count, row_count, _ = base_ref.shape
    terms, out_hbm = refs[:count], refs[count]
    me = me_ref[0]

    def spot(ref, x):
        other = me ^ x
        top = pl.multiple_of(other % row_split * row_count, PAD)
        return ref.at[other // row_split, comp, :, pl.ds(top, row_count)]

    loads = [pltpu.make_async_copy(spot(base_hbm, x), base_ref.at[x], base_sems.at[x]) for x in range(count)]
    term_loads = [pltpu.make_async_copy(terms[x], term_ref.at[x], term_sems.at[x]) for x in range(count)]
    stores = [pltpu.make_async_copy(base_ref.at[x], spot(out_hbm, x), base_sems.at[x]) for x in range(count)]
    for x in range(count):
        loads[x].start()
        term_loads[x].start()
    for x in range(count):
        loads[x].wait()
        term_loads[x].wait()
        base_ref[x] = base_ref[x] + term_ref[x]
        stores[x].start()
        if comp == 0:
            shear_ref = refs[count + 1]
            for p in range(part_count):
                lower, upper = base_ref[x, p, :PAD], base_ref[x, p, row_count - PAD :]
                shear_ref[me ^ x, p] = jnp.sum(lower * weight_ref[x, 0][:, :1], axis=0)
                shear_ref[me ^ x, part_count + p] = jnp.sum(upper * weight_ref[x, 1][:, :1], axis=0)
    for store in stores:
        store.wait()


def add_component(base, terms, spots, row_split, comp, weight):
    count = len(terms)
    part_count, _, width = terms[0].shape
    size = count * terms[0].size
    vector = pl.BlockSpec(memory_space=pltpu.VMEM)
    first = comp == 0
    block = pltpu.VMEM((count,) + terms[0].shape, jnp.float32)
    sums = jax.ShapeDtypeStruct((count, 2 * part_count, width), jnp.float32)
    return pl.pallas_call(
        functools.partial(add_kernel, row_split, comp),
        out_shape=[jax.ShapeDtypeStruct(base.shape, jnp.float32)] + [sums] * first,
        in_specs=[pl.BlockSpec(memory_space=pltpu.SMEM)] + [vector] * first + [HBM] * (count + 1),
        out_specs=[HBM] + [vector] * first,
        scratch_shapes=[block, block, pltpu.SemaphoreType.DMA((count,)), pltpu.SemaphoreType.DMA((count,))],
        input_output_aliases={1 + first: 0},
        compiler_params=pltpu.CompilerParams(vmem_limit_bytes=24 << 20),
        cost_estimate=pl.CostEstimate(flops=size, bytes_accessed=12 * size, transcendentals=0),
        name="add_component",
    )(spots, *[weight] * first, base, *terms)


def after(value, *others):
    return lax.optimization_barrier((value,) + others)[0]


def on_device(field, mean_flow, d2_coef, wall_coef, kx_index, patch_of):
    mode_count, comp_count, part_count, row_count, width = field.shape
    span = lax.axis_size("span")
    me = lax.axis_index("span")
    wall_count = lax.axis_size("wall")
    wall_index = lax.axis_index("wall")
    mode_split = math.gcd(span, mode_count)
    row_split = span // mode_split
    line_rows = row_count // row_split
    tables = jnp.asarray(spectral_tables(width * span))
    pairs = [[(i, i ^ x) for i in range(span)] for x in range(span)]
    spots = jnp.stack([me, me // row_split, me % row_split * line_rows]).astype(jnp.int32)

    def block_lines(source, comp):
        lines = source[:, comp].reshape(mode_split, -1, row_split, line_rows, width)
        return lines.transpose(0, 2, 1, 3, 4).reshape(span, -1, line_rows, width)

    def exchange(lines):
        return lax.all_to_all(lines, "span", split_axis=0, concat_axis=0)

    def send_back(sent, *earlier):
        if earlier:
            sent = lax.optimization_barrier((tuple(sent), earlier))[0]
        return [sent[0]] + [lax.ppermute(sent[x], "span", pairs[x]) for x in range(span - 1, 0, -1)][::-1]

    forward = [(i, i + 1) for i in range(wall_count - 1)]
    backward = [(i + 1, i) for i in range(wall_count - 1)]
    own = [block_lines(field, 0)]
    own.append(block_lines(after(field, own[0]), 1))
    lines = [exchange(own[0]), exchange(own[1])]
    low = lax.ppermute(field[:, :, :, row_count - PAD :], "wall", forward)
    high = lax.ppermute(field[:, :, :, :PAD], "wall", backward)

    sent = [filter_component(after(lines[0], low, high), spots, tables)]
    terms = [send_back(sent[0])]
    for comp in range(2, comp_count):
        own.append(block_lines(after(field, sent[0][0]), comp))
        lines.append(exchange(own[comp]))

    rate = kx_index.astype(jnp.float32) * (0.25 * TAU)
    coef = jnp.broadcast_to(d2_coef[:, :, None], (STEN, row_count, LANES))
    flow = jnp.broadcast_to(mean_flow[:, :, None], (2, row_count, LANES))
    base = local_terms(field, after(low, sent[0][0]), high, rate, coef, flow)

    sent.append(filter_component(after(lines[1], base), spots, tables))
    terms.append(send_back(sent[1], *terms[0]))

    for comp in range(2, comp_count):
        sent.append(filter_component(after(lines[comp], sent[comp - 1][0]), spots, tables))
        terms.append(send_back(sent[comp], *terms[comp - 1]))

    lower = jnp.where(wall_index == 0, wall_coef[0], 0.0)
    upper = jnp.where(wall_index == wall_count - 1, wall_coef[1, ::-1], 0.0)
    group = (me ^ jnp.arange(span)) % row_split
    weight = jnp.stack(
        [jnp.where((group == 0)[:, None], lower, 0.0), jnp.where((group == row_split - 1)[:, None], upper, 0.0)], axis=1
    )
    weight = jnp.broadcast_to(weight[..., None], (span, 2, PAD, LANES))
    onehot = (patch_of[:, None] == jnp.arange(PATCH, dtype=jnp.int32)[None, :]).astype(jnp.float32)
    terms[0][0] = after(terms[0][0], terms[1][1])
    result, shear = add_component(base, terms[0], spots, row_split, 0, weight)
    grad = jnp.einsum("swz,zq->swq", shear, onehot, precision=lax.Precision.HIGHEST)
    grad = grad.reshape(mode_count, row_split, 2, part_count, PATCH).sum(axis=1)
    for axis, count in (("wall", wall_count), ("span", span)):
        distance = 1
        while distance < count:
            grad = grad + lax.ppermute(grad, axis, [(i, i ^ distance) for i in range(count)])
            distance *= 2

    for comp in range(1, comp_count):
        terms[comp][0] = after(terms[comp][0], sent[-1][0])
        (result,) = add_component(result, terms[comp], spots, row_split, comp, None)
    return (result, grad.transpose(1, 0, 2, 3))


def solution(mesh):
    return jax.shard_map(
        on_device,
        mesh=mesh,
        in_specs=(
            P(None, None, None, "wall", "span"),
            P(None, "wall"),
            P(None, "wall"),
            P(),
            P(),
            P("span"),
        ),
        out_specs=(P(None, None, None, "wall", "span"), P()),
        check_vma=False,
    )
```

```python
import functools
import math

import jax
import jax.numpy as jnp
import numpy as np
from jax import lax
from jax.experimental import pallas as pl
from jax.experimental.pallas import tpu as pltpu
from jax.sharding import PartitionSpec as P

HALO = 7
STEN = 15
PATCH = 64
TAU = 0.25
VIS = 0.5

LANES = 128
OUTER = 48
PAD = 8
TILES = OUTER // 2
FILTER_VMEM = 57_500_000

QUARTER = (0, 4, 2, 1, 5, 9)
KEPT = tuple(4 * q for q in QUARTER) + tuple(2 + 8 * t for t in range(6)) + tuple(4 * q + 1 for q in range(12))


@functools.cache
def spectral_tables(length):
    signed = np.arange(length)
    signed = np.where(signed > length // 2, signed - length, signed)
    cutoff = length // 3
    ratio = signed.astype(np.float64) / cutoff
    multiplier = np.where(np.abs(signed) < cutoff, -VIS * ratio * ratio, 0.0)
    shift = np.arange(LANES)[None, :] - np.arange(LANES)[:, None]
    inner = np.arange(LANES)

    def complex_table(k1):
        wave = k1 + OUTER * inner
        spots = np.arange(-LANES + 1, LANES)
        phase = np.exp(2j * np.pi * ((wave[:, None] * spots[None, :]) % length) / length)
        return ((multiplier[wave][:, None] * phase).sum(axis=0) / LANES)[shift + LANES - 1]

    tables = np.zeros((TILES, 2 * LANES, 2 * LANES))
    tables[0, :LANES, :LANES] = complex_table(0).real / OUTER
    tables[0, LANES:, LANES:] = complex_table(OUTER // 2).real / OUTER
    for tile, k1 in enumerate(KEPT[1:], 1):
        table = complex_table(k1) * 2.0 / OUTER
        tables[tile, :LANES, :LANES] = table.real
        tables[tile, :LANES, LANES:] = table.imag
        tables[tile, LANES:, :LANES] = -table.imag
        tables[tile, LANES:, LANES:] = table.real
    high = tables.astype(jnp.bfloat16)
    low = (tables - high.astype(np.float64)).astype(jnp.bfloat16)
    return np.stack([high, low], axis=1)


def turn(value, numerator, denominator):
    re, im = value
    numerator %= denominator
    if numerator == 0:
        return value
    if 2 * numerator == denominator:
        return (-re, -im)
    if 4 * numerator == denominator:
        return (-im, re)
    if 4 * numerator == 3 * denominator:
        return (im, -re)
    cos = math.cos(2 * math.pi * numerator / denominator)
    sin = math.sin(2 * math.pi * numerator / denominator)
    return (re * cos - im * sin, re * sin + im * cos)


def add(a, b):
    return (a[0] + b[0], a[1] + b[1])


def sub(a, b):
    return (a[0] - b[0], a[1] - b[1])


ROOT = math.sqrt(3.0) / 2.0


def dft3(x, sign):
    total = add(x[1], x[2])
    other = sub(x[1], x[2])
    middle = (x[0][0] - 0.5 * total[0], x[0][1] - 0.5 * total[1])
    side = (-sign * ROOT * other[1], sign * ROOT * other[0])
    return [add(x[0], total), add(middle, side), sub(middle, side)]


def dft6(x, sign):
    even = dft3([add(x[b], x[b + 3]) for b in range(3)], sign)
    odd = dft3([turn(sub(x[b], x[b + 3]), sign * b, 6) for b in range(3)], sign)
    return [even[0], odd[0], even[1], odd[1], even[2], odd[2]]


def dft12(x, sign):
    out = [None] * 12
    parts = [[], [], [], []]
    for b in range(3):
        a0, a1, a2, a3 = x[b], x[b + 3], x[b + 6], x[b + 9]
        s0, s1, d0, d1 = add(a0, a2), add(a1, a3), sub(a0, a2), turn(sub(a1, a3), sign, 4)
        for r, value in enumerate((add(s0, s1), add(d0, d1), sub(s0, s1), sub(d0, d1))):
            parts[r].append(turn(value, sign * b * r, 12))
    for r in range(4):
        for q, value in enumerate(dft3(parts[r], sign)):
            out[4 * q + r] = value
    return out


def real_forward(x):
    whole, halved, turned = [], [], []
    for b in range(12):
        s0, s1 = x[b] + x[b + 24], x[b + 12] + x[b + 36]
        whole.append(s0 + s1)
        halved.append(s0 - s1)
        turned.append(turn((x[b] - x[b + 24], x[b + 36] - x[b + 12]), -b, 48))
    w, h, t = [], [], []
    for b in range(3):
        s0, s1 = whole[b] + whole[b + 6], whole[b + 3] + whole[b + 9]
        w.append(s0 + s1)
        h.append(s0 - s1)
        t.append(turn((whole[b] - whole[b + 6], whole[b + 9] - whole[b + 3]), -b, 12))
    total, other = w[1] + w[2], w[1] - w[2]
    four = (w[0] - 0.5 * total, -ROOT * other)
    two = (h[0] + 0.5 * (h[1] - h[2]), -ROOT * (h[1] + h[2]))
    tiles = [(w[0] + total, h[0] - h[1] + h[2]), four, two] + dft3(t, -1)
    tiles += dft6([turn((halved[b], -halved[b + 6]), -b, 24) for b in range(6)], -1)
    return tiles + dft12(turned, -1)


def real_backward(tiles):
    (zero, half), four, two = tiles[:3]
    w0 = zero + four[0]
    rest, side = zero - 0.5 * four[0], ROOT * four[1]
    w = [w0, rest - side, rest + side]
    h_side = 0.5 * two[0] - ROOT * two[1]
    h = [two[0] + half, h_side - half, -0.5 * two[0] - ROOT * two[1] + half]
    t = [turn(value, b, 12) for b, value in enumerate(dft3(tiles[3:6], 1))]
    whole = [None] * 12
    for b in range(3):
        s, d = w[b] + h[b], w[b] - h[b]
        whole[b], whole[b + 6] = s + t[b][0], s - t[b][0]
        whole[b + 3], whole[b + 9] = d - t[b][1], d + t[b][1]
    halved = [None] * 12
    for b, value in enumerate(dft6(tiles[6:12], 1)):
        halved[b], halved[b + 6] = turn(value, b, 24)
        halved[b + 6] = -halved[b + 6]
    x = [None] * 48
    for b, value in enumerate(dft12(tiles[12:], 1)):
        re, im = turn(value, b, 48)
        s, d = whole[b] + halved[b], whole[b] - halved[b]
        x[b], x[b + 24] = s + re, s - re
        x[b + 12], x[b + 36] = d - im, d + im
    return x


def filter_lines(line_ref, wave_ref, table_ref, table_copy):
    _, line_count, row_count, width = line_ref.shape
    pieces = width // LANES
    groups = row_count // PAD

    def spots(step):
        return step // groups, pl.ds(pl.multiple_of(step % groups * PAD, PAD), PAD), pl.ds(pl.multiple_of(step * PAD, PAD), PAD)

    def forward(step, _):
        line, rows, spot = spots(step)
        values = [line_ref[n1 // pieces, line, rows, pl.ds(n1 % pieces * LANES, LANES)] for n1 in range(OUTER)]
        for tile, (re, im) in enumerate(real_forward(values)):
            wave_ref[tile, spot, :LANES] = re
            wave_ref[tile, spot, LANES:] = im
        return 0

    lax.fori_loop(0, line_count * groups, forward, 0)

    def middle(tile, _):
        value = wave_ref[tile]
        high = value.astype(jnp.bfloat16)
        low = (value - high.astype(jnp.float32)).astype(jnp.bfloat16)
        rows = high.shape[0]
        both = jnp.dot(jnp.concatenate([high, low]), table_ref[tile, 0], preferred_element_type=jnp.float32)
        rest = jnp.dot(high, table_ref[tile, 1], preferred_element_type=jnp.float32)
        wave_ref[tile] = both[:rows] + both[rows:] + rest
        return 0

    table_copy.wait()
    lax.fori_loop(0, TILES, middle, 0, unroll=4)

    def backward(step, _):
        line, rows, spot = spots(step)
        tiles = [(wave_ref[tile, spot, :LANES], wave_ref[tile, spot, LANES:]) for tile in range(TILES)]
        for n1, value in enumerate(real_backward(tiles)):
            line_ref[n1 // pieces, line, rows, pl.ds(n1 % pieces * LANES, LANES)] = value
        return 0

    lax.fori_loop(0, line_count * groups, backward, 0)


def start_all(copies):
    for copy in copies:
        copy.start()
    return copies


def wait_all(copies):
    for copy in copies:
        copy.wait()


def wall_sums(block, weight):
    row_count = block.shape[1]
    lower = [jnp.sum(block[p, :PAD] * weight[0][:, :1], axis=0) for p in range(2)]
    upper = [jnp.sum(block[p, row_count - PAD :] * weight[1][:, :1], axis=0) for p in range(2)]
    return lower + upper


def filter_main_kernel(me_ref, table_hbm, weight_ref, lines_hbm, out_hbm, shear_ref, *scratch):
    line_ref, wave_ref, table_ref, table_sem, sems = scratch
    count = line_ref.shape[0]
    me = me_ref[0]
    copies = start_all([pltpu.make_async_copy(lines_hbm.at[x], line_ref.at[x], sems.at[x]) for x in range(count)])
    table_copy = pltpu.make_async_copy(table_hbm, table_ref, table_sem)
    table_copy.start()
    wait_all(copies)
    filter_lines(line_ref, wave_ref, table_ref, table_copy)
    copies = start_all([pltpu.make_async_copy(line_ref.at[x], out_hbm.at[x], sems.at[x]) for x in range(count)])
    for x in range(count):
        for spot, value in enumerate(wall_sums(line_ref.at[me ^ x], weight_ref)):
            shear_ref[x, spot] = value
    wait_all(copies)


def filter_last_kernel(me_ref, table_hbm, field_hbm, *refs):
    line_ref, wave_ref, table_ref, table_sem, sems = refs[-5:]
    count, _, row_count, _ = line_ref.shape
    received, sent = refs[: count - 1], refs[count - 1 : 2 * count - 1]
    me, mode, top = me_ref[0], me_ref[1], me_ref[2]
    comp = field_hbm.shape[1] - 1
    sources = (field_hbm.at[mode, comp, :, pl.ds(pl.multiple_of(top, PAD), row_count)],) + received
    copies = start_all([pltpu.make_async_copy(sources[x], line_ref.at[me ^ x], sems.at[x]) for x in range(count)])
    table_copy = pltpu.make_async_copy(table_hbm, table_ref, table_sem)
    table_copy.start()
    wait_all(copies)
    filter_lines(line_ref, wave_ref, table_ref, table_copy)
    wait_all(start_all([pltpu.make_async_copy(line_ref.at[me ^ x], sent[x], sems.at[x]) for x in range(count)]))


HBM = pl.BlockSpec(memory_space=pltpu.HBM)
SCALARS = pl.BlockSpec(memory_space=pltpu.SMEM)
WHOLE = pl.BlockSpec(memory_space=pltpu.VMEM)


def filter_call(kernel, name, block, tables, in_specs, out_specs, out_shape):
    count, line_count, row_count, width = block
    rows = line_count * row_count
    flops = 3 * 2 * TILES * rows * (2 * LANES) ** 2
    return pl.pallas_call(
        kernel,
        out_shape=out_shape,
        in_specs=in_specs,
        out_specs=out_specs,
        scratch_shapes=[
            pltpu.VMEM(block, jnp.float32),
            pltpu.VMEM((TILES, rows, 2 * LANES), jnp.float32),
            pltpu.VMEM(tables.shape, tables.dtype),
            pltpu.SemaphoreType.DMA,
            pltpu.SemaphoreType.DMA((count,)),
        ],
        compiler_params=pltpu.CompilerParams(vmem_limit_bytes=FILTER_VMEM),
        cost_estimate=pl.CostEstimate(flops=flops, bytes_accessed=8 * count * rows * width, transcendentals=0),
        name=name,
    )


def filter_main(lines, weight, spots, tables, part_count):
    shear = jax.ShapeDtypeStruct((lines.shape[0], 2 * part_count, lines.shape[3]), jnp.float32)
    out_shape = (jax.ShapeDtypeStruct(lines.shape, jnp.float32), shear)
    ins = [SCALARS, HBM, WHOLE, HBM]
    call = filter_call(
        filter_main_kernel, "filter_main", lines.shape, tables, ins, (HBM, WHOLE), out_shape
    )
    return call(spots, tables, weight, lines)


def filter_last(field, received, spots, tables):
    count = len(received) + 1
    shape = received[0].shape
    out_shape = [jax.ShapeDtypeStruct(shape, jnp.float32)] * count
    ins = [SCALARS] + [HBM] * (count + 1)
    call = filter_call(filter_last_kernel, "filter_last", (count,) + shape, tables, ins, [HBM] * count, out_shape)
    return call(spots, tables, field, *received)


def local_kernel(rate_ref, coef_ref, flow_ref, weight_ref, field_ref, low_ref, high_ref, out_ref, shear_ref, pad_ref):
    _, comp_count, part_count, row_count, width = field_ref.shape
    pad_ref[:, :, :PAD] = low_ref[0]
    pad_ref[:, :, PAD : PAD + row_count] = field_ref[0]
    pad_ref[:, :, PAD + row_count :] = high_ref[0]
    rate = rate_ref[pl.program_id(0)]

    def column(step, _):
        lanes = pl.ds(pl.multiple_of(step * LANES, LANES), LANES)
        for top in range(0, row_count, PAD):
            rows = pl.ds(top, PAD)
            advect = rate * flow_ref[0, rows, :]
            shear = TAU * flow_ref[1, rows, :]
            centre = [[field_ref[0, c, p, rows, lanes] for p in range(2)] for c in range(comp_count)]
            for c in range(comp_count):
                for p in range(2):
                    total = centre[c][p]
                    total = total - advect * centre[c][1] if p == 0 else total + advect * centre[c][0]
                    if c == 1:
                        total = total - shear * centre[0][p]
                    for offset in range(STEN):
                        near = pad_ref[c, p, pl.ds(top + offset + PAD - HALO, PAD), lanes]
                        total = total + coef_ref[offset, rows, :] * near
                    out_ref[0, c, p, rows, lanes] = total
        return 0

    lax.fori_loop(0, width // LANES, column, 0)
    for spot, value in enumerate(wall_sums(out_ref.at[0, 0], weight_ref)):
        shear_ref[0, spot] = value


def local_terms(field, low, high, rate, coef, flow, weight):
    mode_count, comp_count, part_count, row_count, width = field.shape
    block = (1, comp_count, part_count, row_count, width)
    edge = (1, comp_count, part_count, PAD, width)

    def by_mode(m):
        return (m, 0, 0, 0, 0)

    return pl.pallas_call(
        local_kernel,
        grid=(mode_count,),
        out_shape=(
            jax.ShapeDtypeStruct(field.shape, jnp.float32),
            jax.ShapeDtypeStruct((mode_count, 2 * part_count, width), jnp.float32),
        ),
        in_specs=[
            SCALARS,
            pl.BlockSpec(coef.shape, lambda m: (0, 0, 0)),
            pl.BlockSpec(flow.shape, lambda m: (0, 0, 0)),
            pl.BlockSpec(weight.shape, lambda m: (0, 0, 0)),
            pl.BlockSpec(block, by_mode),
            pl.BlockSpec(edge, by_mode),
            pl.BlockSpec(edge, by_mode),
        ],
        out_specs=(pl.BlockSpec(block, by_mode), pl.BlockSpec((1, 2 * part_count, width), lambda m: (m, 0, 0))),
        scratch_shapes=[pltpu.VMEM((comp_count, part_count, row_count + 2 * PAD, width), jnp.float32)],
        compiler_params=pltpu.CompilerParams(vmem_limit_bytes=24 << 20),
        cost_estimate=pl.CostEstimate(flops=40 * field.size, bytes_accessed=10 * field.size, transcendentals=0),
        name="local_terms",
    )(rate, coef, flow, weight, field, low, high)


def add_kernel(row_split, comps, me_ref, base_hbm, *refs):
    base_ref, term_ref, base_sems, term_sems = refs[-4:]
    count, _, _, row_count, _ = base_ref.shape
    *terms, out_hbm = refs[:-4]
    me = me_ref[0]

    def spot(ref, x):
        other = me ^ x
        top = pl.multiple_of(other % row_split * row_count, PAD)
        return ref.at[other // row_split, comps, :, pl.ds(top, row_count)]

    loads = [pltpu.make_async_copy(spot(base_hbm, x), base_ref.at[x], base_sems.at[x]) for x in range(count)]
    sources = [terms[0].at[me ^ x] if len(terms) == 1 else terms[x] for x in range(count)]
    term_loads = [pltpu.make_async_copy(sources[x], term_ref.at[x], term_sems.at[x]) for x in range(count)]
    stores = [pltpu.make_async_copy(base_ref.at[x], spot(out_hbm, x), base_sems.at[x]) for x in range(count)]
    for x in range(count):
        loads[x].start()
        term_loads[x].start()
    for x in range(count):
        loads[x].wait()
        term_loads[x].wait()
        base_ref[x] = base_ref[x] + term_ref[x]
        stores[x].start()
    wait_all(stores)


def add_components(base, terms, spots, span, row_split, comps):
    first, last = comps
    mode_count, _, part_count, row_count, width = base.shape
    block = (span, last - first, part_count, row_count // row_split, width)
    terms = [term.reshape(block[1:] if len(terms) > 1 else block) for term in terms]
    size = math.prod(block)
    buffer, sems = pltpu.VMEM(block, jnp.float32), pltpu.SemaphoreType.DMA((span,))
    return pl.pallas_call(
        functools.partial(add_kernel, row_split, pl.ds(first, last - first)),
        out_shape=jax.ShapeDtypeStruct(base.shape, jnp.float32),
        in_specs=[SCALARS] + [HBM] * (1 + len(terms)),
        out_specs=HBM,
        scratch_shapes=[buffer, buffer, sems, sems],
        input_output_aliases={1: 0},
        compiler_params=pltpu.CompilerParams(vmem_limit_bytes=24 << 20),
        cost_estimate=pl.CostEstimate(flops=size, bytes_accessed=12 * size, transcendentals=0),
        name="add_components",
    )(spots, base, *terms)


def after(value, *others):
    return lax.optimization_barrier((value,) + others)[0]


def on_device(field, mean_flow, d2_coef, wall_coef, kx_index, patch_of):
    mode_count, comp_count, part_count, row_count, width = field.shape
    span = lax.axis_size("span")
    me = lax.axis_index("span")
    wall_count = lax.axis_size("wall")
    wall_index = lax.axis_index("wall")
    mode_split = math.gcd(span, mode_count)
    row_split = span // mode_split
    line_rows = row_count // row_split
    tables = jnp.asarray(spectral_tables(width * span))
    pairs = [[(i, i ^ x) for i in range(span)] for x in range(span)]
    spots = jnp.stack([me, me // row_split, me % row_split * line_rows]).astype(jnp.int32)

    last = comp_count - 1

    def exchange(lines):
        return lax.all_to_all(lines, "span", split_axis=0, concat_axis=0)

    def swap(blocks):
        return [lax.ppermute(blocks[x], "span", pairs[x]) for x in range(span - 1, 0, -1)][::-1]

    main = field[:, :last].reshape(mode_split, -1, row_split, line_rows, width)
    main = exchange(main.transpose(0, 2, 1, 3, 4).reshape(span, -1, line_rows, width))

    forward = [(i, i + 1) for i in range(wall_count - 1)]
    backward = [(i + 1, i) for i in range(wall_count - 1)]
    low = lax.ppermute(field[:, :, :, row_count - PAD :], "wall", forward)
    high = lax.ppermute(field[:, :, :, :PAD], "wall", backward)
    patches = jnp.stack([patch_of] + swap([patch_of] * span))
    onehot = (patches[:, :, None] == jnp.arange(PATCH, dtype=jnp.int32)).astype(jnp.float32)

    lower = jnp.where(wall_index == 0, wall_coef[0], 0.0)
    upper = jnp.where(wall_index == wall_count - 1, wall_coef[1, ::-1], 0.0)
    weight = jnp.broadcast_to(jnp.stack([lower, upper])[:, :, None], (2, PAD, LANES))
    group = me % row_split
    ends = jnp.stack([group == 0, group == row_split - 1])
    line_weight = jnp.where(ends[:, None, None], weight, 0.0)

    rate = kx_index.astype(jnp.float32) * (0.25 * TAU)
    coef = jnp.broadcast_to(d2_coef[:, :, None], (STEN, row_count, LANES))
    flow = jnp.broadcast_to(mean_flow[:, :, None], (2, row_count, LANES))
    base, shear = local_terms(field, low, high, rate, coef, flow, weight)

    def last_block(x):
        other = me ^ x
        start = (other // row_split, last, 0, other % row_split * line_rows, 0)
        return lax.dynamic_slice(field, start, (1, 1, part_count, line_rows, width))[0, 0]

    blocks = [last_block(x) for x in range(1, span)]
    blocks = list(lax.optimization_barrier((tuple(blocks), base))[0])
    received = swap([None] + blocks)

    filtered, line_shear = filter_main(after(main, received[0]), line_weight, spots, tables, part_count)
    back = exchange(filtered)
    received[0] = after(received[0], filtered)
    sent = filter_last(field, received, spots, tables)
    returned = [sent[0]] + swap(sent)

    highest = lax.Precision.HIGHEST
    grad = jnp.einsum("mwz,zq->mwq", shear, onehot[0], precision=highest)
    line_grad = jnp.einsum("xwz,xzq->wq", line_shear, onehot, precision=highest)
    mine = jnp.arange(mode_count) == me // row_split
    grad = after(grad + jnp.where(mine[:, None, None], line_grad, 0.0), returned[1])
    for axis, count in (("wall", wall_count), ("span", span)):
        distance = 1
        while distance < count:
            grad = grad + lax.ppermute(grad, axis, [(i, i ^ distance) for i in range(count)])
            distance *= 2
    wall_grad = grad.reshape(mode_count, 2, part_count, PATCH).transpose(1, 0, 2, 3)

    result = add_components(base, [back], spots, span, row_split, (0, last))
    result = add_components(result, returned, spots, span, row_split, (last, comp_count))
    return (result, wall_grad)


def solution(mesh):
    return jax.shard_map(
        on_device,
        mesh=mesh,
        in_specs=(
            P(None, None, None, "wall", "span"),
            P(None, "wall"),
            P(None, "wall"),
            P(),
            P(),
            P("span"),
        ),
        out_specs=(P(None, None, None, "wall", "span"), P()),
        check_vma=False,
    )
```

```python
import functools
import math

import jax
import jax.numpy as jnp
import numpy as np
from jax import lax
from jax.experimental import pallas as pl
from jax.experimental.pallas import tpu as pltpu
from jax.sharding import PartitionSpec as P

HALO = 7
STEN = 15
PATCH = 64
TAU = 0.25
VIS = 0.5

LANES = 128
OUTER = 48
PAD = 8
TILES = OUTER // 2
FILTER_VMEM = 57_500_000

QUARTER = (0, 4, 2, 1, 5, 9)
KEPT = tuple(4 * q for q in QUARTER) + tuple(2 + 8 * t for t in range(6)) + tuple(4 * q + 1 for q in range(12))


@functools.cache
def spectral_tables(length):
    signed = np.arange(length)
    signed = np.where(signed > length // 2, signed - length, signed)
    cutoff = length // 3
    ratio = signed.astype(np.float64) / cutoff
    multiplier = np.where(np.abs(signed) < cutoff, -VIS * ratio * ratio, 0.0)
    shift = np.arange(LANES)[None, :] - np.arange(LANES)[:, None]
    inner = np.arange(LANES)

    def complex_table(k1):
        wave = k1 + OUTER * inner
        spots = np.arange(-LANES + 1, LANES)
        phase = np.exp(2j * np.pi * ((wave[:, None] * spots[None, :]) % length) / length)
        return ((multiplier[wave][:, None] * phase).sum(axis=0) / LANES)[shift + LANES - 1]

    tables = np.zeros((TILES, 2 * LANES, 2 * LANES))
    tables[0, :LANES, :LANES] = complex_table(0).real / OUTER
    tables[0, LANES:, LANES:] = complex_table(OUTER // 2).real / OUTER
    for tile, k1 in enumerate(KEPT[1:], 1):
        table = complex_table(k1) * 2.0 / OUTER
        tables[tile, :LANES, :LANES] = table.real
        tables[tile, :LANES, LANES:] = table.imag
        tables[tile, LANES:, :LANES] = -table.imag
        tables[tile, LANES:, LANES:] = table.real
    high = tables.astype(jnp.bfloat16)
    low = (tables - high.astype(np.float64)).astype(jnp.bfloat16)
    return np.stack([high, low], axis=1)


def turn(value, numerator, denominator):
    re, im = value
    numerator %= denominator
    if numerator == 0:
        return value
    if 2 * numerator == denominator:
        return (-re, -im)
    if 4 * numerator == denominator:
        return (-im, re)
    if 4 * numerator == 3 * denominator:
        return (im, -re)
    cos = math.cos(2 * math.pi * numerator / denominator)
    sin = math.sin(2 * math.pi * numerator / denominator)
    return (re * cos - im * sin, re * sin + im * cos)


def add(a, b):
    return (a[0] + b[0], a[1] + b[1])


def sub(a, b):
    return (a[0] - b[0], a[1] - b[1])


ROOT = math.sqrt(3.0) / 2.0


def dft3(x, sign):
    total = add(x[1], x[2])
    other = sub(x[1], x[2])
    middle = (x[0][0] - 0.5 * total[0], x[0][1] - 0.5 * total[1])
    side = (-sign * ROOT * other[1], sign * ROOT * other[0])
    return [add(x[0], total), add(middle, side), sub(middle, side)]


def dft6(x, sign):
    even = dft3([add(x[b], x[b + 3]) for b in range(3)], sign)
    odd = dft3([turn(sub(x[b], x[b + 3]), sign * b, 6) for b in range(3)], sign)
    return [even[0], odd[0], even[1], odd[1], even[2], odd[2]]


def dft12(x, sign):
    out = [None] * 12
    parts = [[], [], [], []]
    for b in range(3):
        a0, a1, a2, a3 = x[b], x[b + 3], x[b + 6], x[b + 9]
        s0, s1, d0, d1 = add(a0, a2), add(a1, a3), sub(a0, a2), turn(sub(a1, a3), sign, 4)
        for r, value in enumerate((add(s0, s1), add(d0, d1), sub(s0, s1), sub(d0, d1))):
            parts[r].append(turn(value, sign * b * r, 12))
    for r in range(4):
        for q, value in enumerate(dft3(parts[r], sign)):
            out[4 * q + r] = value
    return out


def real_forward(x):
    whole, halved, turned = [], [], []
    for b in range(12):
        s0, s1 = x[b] + x[b + 24], x[b + 12] + x[b + 36]
        whole.append(s0 + s1)
        halved.append(s0 - s1)
        turned.append(turn((x[b] - x[b + 24], x[b + 36] - x[b + 12]), -b, 48))
    w, h, t = [], [], []
    for b in range(3):
        s0, s1 = whole[b] + whole[b + 6], whole[b + 3] + whole[b + 9]
        w.append(s0 + s1)
        h.append(s0 - s1)
        t.append(turn((whole[b] - whole[b + 6], whole[b + 9] - whole[b + 3]), -b, 12))
    total, other = w[1] + w[2], w[1] - w[2]
    four = (w[0] - 0.5 * total, -ROOT * other)
    two = (h[0] + 0.5 * (h[1] - h[2]), -ROOT * (h[1] + h[2]))
    tiles = [(w[0] + total, h[0] - h[1] + h[2]), four, two] + dft3(t, -1)
    tiles += dft6([turn((halved[b], -halved[b + 6]), -b, 24) for b in range(6)], -1)
    return tiles + dft12(turned, -1)


def real_backward(tiles):
    (zero, half), four, two = tiles[:3]
    w0 = zero + four[0]
    rest, side = zero - 0.5 * four[0], ROOT * four[1]
    w = [w0, rest - side, rest + side]
    h_side = 0.5 * two[0] - ROOT * two[1]
    h = [two[0] + half, h_side - half, -0.5 * two[0] - ROOT * two[1] + half]
    t = [turn(value, b, 12) for b, value in enumerate(dft3(tiles[3:6], 1))]
    whole = [None] * 12
    for b in range(3):
        s, d = w[b] + h[b], w[b] - h[b]
        whole[b], whole[b + 6] = s + t[b][0], s - t[b][0]
        whole[b + 3], whole[b + 9] = d - t[b][1], d + t[b][1]
    halved = [None] * 12
    for b, value in enumerate(dft6(tiles[6:12], 1)):
        halved[b], halved[b + 6] = turn(value, b, 24)
        halved[b + 6] = -halved[b + 6]
    x = [None] * 48
    for b, value in enumerate(dft12(tiles[12:], 1)):
        re, im = turn(value, b, 48)
        s, d = whole[b] + halved[b], whole[b] - halved[b]
        x[b], x[b + 24] = s + re, s - re
        x[b + 12], x[b + 36] = d - im, d + im
    return x


def filter_lines(line_ref, wave_ref, table_ref, table_copy):
    _, line_count, row_count, width = line_ref.shape
    pieces = width // LANES
    groups = row_count // PAD

    def spots(step):
        return step // groups, pl.ds(pl.multiple_of(step % groups * PAD, PAD), PAD), pl.ds(pl.multiple_of(step * PAD, PAD), PAD)

    def forward(step, _):
        line, rows, spot = spots(step)
        values = [line_ref[n1 // pieces, line, rows, pl.ds(n1 % pieces * LANES, LANES)] for n1 in range(OUTER)]
        for tile, (re, im) in enumerate(real_forward(values)):
            wave_ref[tile, spot, :LANES] = re
            wave_ref[tile, spot, LANES:] = im
        return 0

    lax.fori_loop(0, line_count * groups, forward, 0)

    def middle(tile, _):
        value = wave_ref[tile]
        high = value.astype(jnp.bfloat16)
        low = (value - high.astype(jnp.float32)).astype(jnp.bfloat16)
        rows = high.shape[0]
        both = jnp.dot(jnp.concatenate([high, low]), table_ref[tile, 0], preferred_element_type=jnp.float32)
        rest = jnp.dot(high, table_ref[tile, 1], preferred_element_type=jnp.float32)
        wave_ref[tile] = both[:rows] + both[rows:] + rest
        return 0

    table_copy.wait()
    lax.fori_loop(0, TILES, middle, 0, unroll=4)

    def backward(step, _):
        line, rows, spot = spots(step)
        tiles = [(wave_ref[tile, spot, :LANES], wave_ref[tile, spot, LANES:]) for tile in range(TILES)]
        for n1, value in enumerate(real_backward(tiles)):
            line_ref[n1 // pieces, line, rows, pl.ds(n1 % pieces * LANES, LANES)] = value
        return 0

    lax.fori_loop(0, line_count * groups, backward, 0)


def start_all(copies):
    for copy in copies:
        copy.start()
    return copies


def wait_all(copies):
    for copy in copies:
        copy.wait()


def wall_sums(block, weight):
    row_count = block.shape[1]
    lower = [jnp.sum(block[p, :PAD] * weight[0][:, :1], axis=0) for p in range(2)]
    upper = [jnp.sum(block[p, row_count - PAD :] * weight[1][:, :1], axis=0) for p in range(2)]
    return lower + upper


def filter_main_kernel(me_ref, table_hbm, weight_ref, field_hbm, *refs):
    line_ref, wave_ref, table_ref, table_sem, sems = refs[-5:]
    count, line_count, row_count, _ = line_ref.shape
    received, (out_hbm, shear_ref) = refs[: count - 1], refs[count - 1 : count + 1]
    me, mode, rows = me_ref[0], me_ref[1], pl.ds(pl.multiple_of(me_ref[2], PAD), row_count)
    copies = [pltpu.make_async_copy(received[x - 1], line_ref.at[me ^ x], sems.at[x]) for x in range(1, count)]
    for comp in range(line_count // 2):
        target = line_ref.at[me, pl.ds(2 * comp, 2)]
        sem = sems.at[0 if comp == 0 else count - 1 + comp]
        copies.append(pltpu.make_async_copy(field_hbm.at[mode, comp, :, rows], target, sem))
    start_all(copies)
    table_copy = pltpu.make_async_copy(table_hbm, table_ref, table_sem)
    table_copy.start()
    wait_all(copies)
    filter_lines(line_ref, wave_ref, table_ref, table_copy)
    copies = start_all([pltpu.make_async_copy(line_ref.at[x], out_hbm.at[x], sems.at[x]) for x in range(count)])
    for x in range(count):
        for spot, value in enumerate(wall_sums(line_ref.at[me ^ x], weight_ref)):
            shear_ref[x, spot] = value
    wait_all(copies)


def filter_last_kernel(me_ref, table_hbm, lines_hbm, *refs):
    line_ref, wave_ref, table_ref, table_sem, sems = refs[-5:]
    count = line_ref.shape[0]
    sent, me = refs[:count], me_ref[0]
    copies = start_all([pltpu.make_async_copy(lines_hbm.at[x], line_ref.at[x], sems.at[x]) for x in range(count)])
    table_copy = pltpu.make_async_copy(table_hbm, table_ref, table_sem)
    table_copy.start()
    wait_all(copies)
    filter_lines(line_ref, wave_ref, table_ref, table_copy)
    wait_all(start_all([pltpu.make_async_copy(line_ref.at[me ^ x], sent[x], sems.at[x]) for x in range(count)]))


HBM = pl.BlockSpec(memory_space=pltpu.HBM)
SCALARS = pl.BlockSpec(memory_space=pltpu.SMEM)
WHOLE = pl.BlockSpec(memory_space=pltpu.VMEM)


def filter_call(kernel, name, block, tables, in_specs, out_specs, out_shape):
    count, line_count, row_count, width = block
    rows = line_count * row_count
    flops = 3 * 2 * TILES * rows * (2 * LANES) ** 2
    return pl.pallas_call(
        kernel,
        out_shape=out_shape,
        in_specs=in_specs,
        out_specs=out_specs,
        scratch_shapes=[
            pltpu.VMEM(block, jnp.float32),
            pltpu.VMEM((TILES, rows, 2 * LANES), jnp.float32),
            pltpu.VMEM(tables.shape, tables.dtype),
            pltpu.SemaphoreType.DMA,
            pltpu.SemaphoreType.DMA((count + line_count // 2,)),
        ],
        compiler_params=pltpu.CompilerParams(vmem_limit_bytes=FILTER_VMEM),
        cost_estimate=pl.CostEstimate(flops=flops, bytes_accessed=8 * count * rows * width, transcendentals=0),
        name=name,
    )


def filter_main(field, received, weight, spots, tables):
    count = len(received) + 1
    block = (count,) + received[0].shape
    shear = jax.ShapeDtypeStruct((count, 4, block[3]), jnp.float32)
    out_shape = (jax.ShapeDtypeStruct(block, jnp.float32), shear)
    ins = [SCALARS, HBM, WHOLE] + [HBM] * count
    call = filter_call(filter_main_kernel, "filter_main", block, tables, ins, (HBM, WHOLE), out_shape)
    return call(spots, tables, weight, field, *received)


def filter_last(lines, spots, tables):
    count = lines.shape[0]
    out_shape = [jax.ShapeDtypeStruct(lines.shape[1:], jnp.float32)] * count
    ins = [SCALARS, HBM, HBM]
    call = filter_call(filter_last_kernel, "filter_last", lines.shape, tables, ins, [HBM] * count, out_shape)
    return call(spots, tables, lines)


def local_kernel(rate_ref, coef_ref, flow_ref, weight_ref, field_ref, low_ref, high_ref, out_ref, shear_ref, pad_ref):
    _, comp_count, part_count, row_count, width = field_ref.shape
    pad_ref[:, :, :PAD] = low_ref[0]
    pad_ref[:, :, PAD : PAD + row_count] = field_ref[0]
    pad_ref[:, :, PAD + row_count :] = high_ref[0]
    rate = rate_ref[pl.program_id(0)]

    def column(step, _):
        lanes = pl.ds(pl.multiple_of(step * LANES, LANES), LANES)
        for top in range(0, row_count, PAD):
            rows = pl.ds(top, PAD)
            advect = rate * flow_ref[0, rows, :]
            shear = TAU * flow_ref[1, rows, :]
            centre = [[field_ref[0, c, p, rows, lanes] for p in range(2)] for c in range(comp_count)]
            for c in range(comp_count):
                for p in range(2):
                    total = centre[c][p]
                    total = total - advect * centre[c][1] if p == 0 else total + advect * centre[c][0]
                    if c == 1:
                        total = total - shear * centre[0][p]
                    for offset in range(STEN):
                        near = pad_ref[c, p, pl.ds(top + offset + PAD - HALO, PAD), lanes]
                        total = total + coef_ref[offset, rows, :] * near
                    out_ref[0, c, p, rows, lanes] = total
        return 0

    lax.fori_loop(0, width // LANES, column, 0)
    for spot, value in enumerate(wall_sums(out_ref.at[0, 0], weight_ref)):
        shear_ref[0, spot] = value


def local_terms(field, low, high, rate, coef, flow, weight):
    mode_count, comp_count, part_count, row_count, width = field.shape
    block = (1, comp_count, part_count, row_count, width)
    edge = (1, comp_count, part_count, PAD, width)

    def by_mode(m):
        return (m, 0, 0, 0, 0)

    return pl.pallas_call(
        local_kernel,
        grid=(mode_count,),
        out_shape=(
            jax.ShapeDtypeStruct(field.shape, jnp.float32),
            jax.ShapeDtypeStruct((mode_count, 2 * part_count, width), jnp.float32),
        ),
        in_specs=[
            SCALARS,
            pl.BlockSpec(coef.shape, lambda m: (0, 0, 0)),
            pl.BlockSpec(flow.shape, lambda m: (0, 0, 0)),
            pl.BlockSpec(weight.shape, lambda m: (0, 0, 0)),
            pl.BlockSpec(block, by_mode),
            pl.BlockSpec(edge, by_mode),
            pl.BlockSpec(edge, by_mode),
        ],
        out_specs=(pl.BlockSpec(block, by_mode), pl.BlockSpec((1, 2 * part_count, width), lambda m: (m, 0, 0))),
        scratch_shapes=[pltpu.VMEM((comp_count, part_count, row_count + 2 * PAD, width), jnp.float32)],
        compiler_params=pltpu.CompilerParams(vmem_limit_bytes=24 << 20),
        cost_estimate=pl.CostEstimate(flops=40 * field.size, bytes_accessed=10 * field.size, transcendentals=0),
        name="local_terms",
    )(rate, coef, flow, weight, field, low, high)


def add_kernel(row_split, comps, me_ref, base_hbm, *refs):
    base_ref, term_ref, base_sems, term_sems = refs[-4:]
    count, _, _, row_count, _ = base_ref.shape
    *terms, out_hbm = refs[:-4]
    me = me_ref[0]

    def spot(ref, x):
        other = me ^ x
        top = pl.multiple_of(other % row_split * row_count, PAD)
        return ref.at[other // row_split, comps, :, pl.ds(top, row_count)]

    loads = [pltpu.make_async_copy(spot(base_hbm, x), base_ref.at[x], base_sems.at[x]) for x in range(count)]
    sources = [terms[0].at[me ^ x] if len(terms) == 1 else terms[x] for x in range(count)]
    term_loads = [pltpu.make_async_copy(sources[x], term_ref.at[x], term_sems.at[x]) for x in range(count)]
    stores = [pltpu.make_async_copy(base_ref.at[x], spot(out_hbm, x), base_sems.at[x]) for x in range(count)]
    for x in range(count):
        loads[x].start()
        term_loads[x].start()
    for x in range(count):
        loads[x].wait()
        term_loads[x].wait()
        base_ref[x] = base_ref[x] + term_ref[x]
        stores[x].start()
    wait_all(stores)


def add_components(base, terms, spots, span, row_split, comps):
    first, last = comps
    mode_count, _, part_count, row_count, width = base.shape
    block = (span, last - first, part_count, row_count // row_split, width)
    terms = [term.reshape(block[1:] if len(terms) > 1 else block) for term in terms]
    size = math.prod(block)
    buffer, sems = pltpu.VMEM(block, jnp.float32), pltpu.SemaphoreType.DMA((span,))
    return pl.pallas_call(
        functools.partial(add_kernel, row_split, pl.ds(first, last - first)),
        out_shape=jax.ShapeDtypeStruct(base.shape, jnp.float32),
        in_specs=[SCALARS] + [HBM] * (1 + len(terms)),
        out_specs=HBM,
        scratch_shapes=[buffer, buffer, sems, sems],
        input_output_aliases={1: 0},
        compiler_params=pltpu.CompilerParams(vmem_limit_bytes=24 << 20),
        cost_estimate=pl.CostEstimate(flops=size, bytes_accessed=12 * size, transcendentals=0),
        name="add_components",
    )(spots, base, *terms)


def after(value, *others):
    return lax.optimization_barrier((value,) + others)[0]


def on_device(field, mean_flow, d2_coef, wall_coef, kx_index, patch_of):
    mode_count, comp_count, part_count, row_count, width = field.shape
    span = lax.axis_size("span")
    me = lax.axis_index("span")
    wall_count = lax.axis_size("wall")
    wall_index = lax.axis_index("wall")
    mode_split = math.gcd(span, mode_count)
    row_split = span // mode_split
    line_rows = row_count // row_split
    tables = jnp.asarray(spectral_tables(width * span))
    pairs = [[(i, i ^ x) for i in range(span)] for x in range(span)]
    spots = jnp.stack([me, me // row_split, me % row_split * line_rows]).astype(jnp.int32)

    last = comp_count - 1

    def exchange(lines):
        return lax.all_to_all(lines, "span", split_axis=0, concat_axis=0)

    def swap(blocks):
        return [lax.ppermute(blocks[x], "span", pairs[x]) for x in range(span - 1, 0, -1)][::-1]

    def main_block(x):
        other = me ^ x
        start = (other // row_split, 0, 0, other % row_split * line_rows, 0)
        block = lax.dynamic_slice(field, start, (1, last, part_count, line_rows, width))
        return block.reshape(-1, line_rows, width)

    received = swap([None] + [main_block(x) for x in range(1, span)])

    forward = [(i, i + 1) for i in range(wall_count - 1)]
    backward = [(i + 1, i) for i in range(wall_count - 1)]
    low = lax.ppermute(field[:, :, :, row_count - PAD :], "wall", forward)
    high = lax.ppermute(field[:, :, :, :PAD], "wall", backward)

    lower = jnp.where(wall_index == 0, wall_coef[0], 0.0)
    upper = jnp.where(wall_index == wall_count - 1, wall_coef[1, ::-1], 0.0)
    weight = jnp.broadcast_to(jnp.stack([lower, upper])[:, :, None], (2, PAD, LANES))
    group = me % row_split
    ends = jnp.stack([group == 0, group == row_split - 1])
    line_weight = jnp.where(ends[:, None, None], weight, 0.0)

    rate = kx_index.astype(jnp.float32) * (0.25 * TAU)
    coef = jnp.broadcast_to(d2_coef[:, :, None], (STEN, row_count, LANES))
    flow = jnp.broadcast_to(mean_flow[:, :, None], (2, row_count, LANES))
    base, shear = local_terms(field, low, high, rate, coef, flow, weight)

    lines = field[:, last].reshape(mode_split, -1, row_split, line_rows, width)
    lines = lines.transpose(0, 2, 1, 3, 4).reshape(span, -1, line_rows, width)
    lines = exchange(after(lines, base))

    received[0] = after(received[0], base)
    filtered, line_shear = filter_main(field, received, line_weight, spots, tables)
    back = exchange(filtered)

    patches, distance = after(patch_of, base)[None], 1
    while distance < span:
        patches = jnp.concatenate([patches, lax.ppermute(patches, "span", pairs[distance])])
        distance *= 2
    onehot = (patches[:, :, None] == jnp.arange(PATCH, dtype=jnp.int32)).astype(jnp.float32)

    highest = lax.Precision.HIGHEST
    grad = jnp.einsum("mwz,zq->mwq", shear, onehot[0], precision=highest)
    line_grad = jnp.einsum("xwz,xzq->wq", line_shear, onehot, precision=highest)
    mine = jnp.arange(mode_count) == me // row_split
    grad = after(grad + jnp.where(mine[:, None, None], line_grad, 0.0), lines)
    for axis, count in (("wall", wall_count), ("span", span)):
        distance = 1
        while distance < count:
            grad = grad + lax.ppermute(grad, axis, [(i, i ^ distance) for i in range(count)])
            distance *= 2
    sent = filter_last(after(lines, grad), spots, tables)
    returned = [sent[0]] + swap(sent)
    wall_grad = grad.reshape(mode_count, 2, part_count, PATCH).transpose(1, 0, 2, 3)

    result = add_components(base, [back], spots, span, row_split, (0, last))
    result = add_components(result, returned, spots, span, row_split, (last, comp_count))
    return (result, wall_grad)


def solution(mesh):
    return jax.shard_map(
        on_device,
        mesh=mesh,
        in_specs=(
            P(None, None, None, "wall", "span"),
            P(None, "wall"),
            P(None, "wall"),
            P(),
            P(),
            P("span"),
        ),
        out_specs=(P(None, None, None, "wall", "span"), P()),
        check_vma=False,
    )
```

```python
import functools
import math

import jax
import jax.numpy as jnp
import numpy as np
from jax import lax
from jax.experimental import pallas as pl
from jax.experimental.pallas import tpu as pltpu
from jax.sharding import PartitionSpec as P

HALO = 7
STEN = 15
PATCH = 64
TAU = 0.25
VIS = 0.5

LANES = 128
OUTER = 48
PAD = 8
TILES = OUTER // 2
FILTER_VMEM = 57_500_000
TABLE_COPIES = 4

QUARTER = (0, 4, 2, 1, 5, 9)
KEPT = tuple(4 * q for q in QUARTER) + tuple(2 + 8 * t for t in range(6)) + tuple(4 * q + 1 for q in range(12))


@functools.cache
def spectral_tables(length):
    signed = np.arange(length)
    signed = np.where(signed > length // 2, signed - length, signed)
    cutoff = length // 3
    ratio = signed.astype(np.float64) / cutoff
    multiplier = np.where(np.abs(signed) < cutoff, -VIS * ratio * ratio, 0.0)
    shift = np.arange(LANES)[None, :] - np.arange(LANES)[:, None]
    inner = np.arange(LANES)

    def complex_table(k1):
        wave = k1 + OUTER * inner
        spots = np.arange(-LANES + 1, LANES)
        phase = np.exp(2j * np.pi * ((wave[:, None] * spots[None, :]) % length) / length)
        return ((multiplier[wave][:, None] * phase).sum(axis=0) / LANES)[shift + LANES - 1]

    tables = np.zeros((TILES, 2 * LANES, 2 * LANES))
    tables[0, :LANES, :LANES] = complex_table(0).real / OUTER
    tables[0, LANES:, LANES:] = complex_table(OUTER // 2).real / OUTER
    for tile, k1 in enumerate(KEPT[1:], 1):
        table = complex_table(k1) * 2.0 / OUTER
        tables[tile, :LANES, :LANES] = table.real
        tables[tile, :LANES, LANES:] = table.imag
        tables[tile, LANES:, :LANES] = -table.imag
        tables[tile, LANES:, LANES:] = table.real
    high = tables.astype(jnp.bfloat16)
    low = (tables - high.astype(np.float64)).astype(jnp.bfloat16)
    return np.stack([high, low], axis=1)


def turn(value, numerator, denominator):
    re, im = value
    numerator %= denominator
    if numerator == 0:
        return value
    if 2 * numerator == denominator:
        return (-re, -im)
    if 4 * numerator == denominator:
        return (-im, re)
    if 4 * numerator == 3 * denominator:
        return (im, -re)
    cos = math.cos(2 * math.pi * numerator / denominator)
    sin = math.sin(2 * math.pi * numerator / denominator)
    return (re * cos - im * sin, re * sin + im * cos)


def add(a, b):
    return (a[0] + b[0], a[1] + b[1])


def sub(a, b):
    return (a[0] - b[0], a[1] - b[1])


ROOT = math.sqrt(3.0) / 2.0


def dft3(x, sign):
    total = add(x[1], x[2])
    other = sub(x[1], x[2])
    middle = (x[0][0] - 0.5 * total[0], x[0][1] - 0.5 * total[1])
    side = (-sign * ROOT * other[1], sign * ROOT * other[0])
    return [add(x[0], total), add(middle, side), sub(middle, side)]


def dft6(x, sign):
    even = dft3([add(x[b], x[b + 3]) for b in range(3)], sign)
    odd = dft3([turn(sub(x[b], x[b + 3]), sign * b, 6) for b in range(3)], sign)
    return [even[0], odd[0], even[1], odd[1], even[2], odd[2]]


def dft12(x, sign):
    out = [None] * 12
    parts = [[], [], [], []]
    for b in range(3):
        a0, a1, a2, a3 = x[b], x[b + 3], x[b + 6], x[b + 9]
        s0, s1, d0, d1 = add(a0, a2), add(a1, a3), sub(a0, a2), turn(sub(a1, a3), sign, 4)
        for r, value in enumerate((add(s0, s1), add(d0, d1), sub(s0, s1), sub(d0, d1))):
            parts[r].append(turn(value, sign * b * r, 12))
    for r in range(4):
        for q, value in enumerate(dft3(parts[r], sign)):
            out[4 * q + r] = value
    return out


def real_forward(x):
    whole, halved, turned = [], [], []
    for b in range(12):
        s0, s1 = x[b] + x[b + 24], x[b + 12] + x[b + 36]
        whole.append(s0 + s1)
        halved.append(s0 - s1)
        turned.append(turn((x[b] - x[b + 24], x[b + 36] - x[b + 12]), -b, 48))
    w, h, t = [], [], []
    for b in range(3):
        s0, s1 = whole[b] + whole[b + 6], whole[b + 3] + whole[b + 9]
        w.append(s0 + s1)
        h.append(s0 - s1)
        t.append(turn((whole[b] - whole[b + 6], whole[b + 9] - whole[b + 3]), -b, 12))
    total, other = w[1] + w[2], w[1] - w[2]
    four = (w[0] - 0.5 * total, -ROOT * other)
    two = (h[0] + 0.5 * (h[1] - h[2]), -ROOT * (h[1] + h[2]))
    tiles = [(w[0] + total, h[0] - h[1] + h[2]), four, two] + dft3(t, -1)
    tiles += dft6([turn((halved[b], -halved[b + 6]), -b, 24) for b in range(6)], -1)
    return tiles + dft12(turned, -1)


def real_backward(tiles):
    (zero, half), four, two = tiles[:3]
    w0 = zero + four[0]
    rest, side = zero - 0.5 * four[0], ROOT * four[1]
    w = [w0, rest - side, rest + side]
    h_side = 0.5 * two[0] - ROOT * two[1]
    h = [two[0] + half, h_side - half, -0.5 * two[0] - ROOT * two[1] + half]
    t = [turn(value, b, 12) for b, value in enumerate(dft3(tiles[3:6], 1))]
    whole = [None] * 12
    for b in range(3):
        s, d = w[b] + h[b], w[b] - h[b]
        whole[b], whole[b + 6] = s + t[b][0], s - t[b][0]
        whole[b + 3], whole[b + 9] = d - t[b][1], d + t[b][1]
    halved = [None] * 12
    for b, value in enumerate(dft6(tiles[6:12], 1)):
        halved[b], halved[b + 6] = turn(value, b, 24)
        halved[b + 6] = -halved[b + 6]
    x = [None] * 48
    for b, value in enumerate(dft12(tiles[12:], 1)):
        re, im = turn(value, b, 48)
        s, d = whole[b] + halved[b], whole[b] - halved[b]
        x[b], x[b + 24] = s + re, s - re
        x[b + 12], x[b + 36] = d - im, d + im
    return x


def filter_lines(line_ref, wave_ref, table_ref, table_copies):
    _, line_count, row_count, width = line_ref.shape
    pieces = width // LANES
    groups = row_count // PAD

    def spots(step):
        return step // groups, pl.ds(pl.multiple_of(step % groups * PAD, PAD), PAD), pl.ds(pl.multiple_of(step * PAD, PAD), PAD)

    def forward(step, _):
        line, rows, spot = spots(step)
        values = [line_ref[n1 // pieces, line, rows, pl.ds(n1 % pieces * LANES, LANES)] for n1 in range(OUTER)]
        for tile, (re, im) in enumerate(real_forward(values)):
            wave_ref[tile, spot, :LANES] = re
            wave_ref[tile, spot, LANES:] = im
        return 0

    lax.fori_loop(0, line_count * groups, forward, 0)

    def middle(tile, _):
        value = wave_ref[tile]
        high = value.astype(jnp.bfloat16)
        low = (value - high.astype(jnp.float32)).astype(jnp.bfloat16)
        rows = high.shape[0]
        both = jnp.dot(jnp.concatenate([high, low]), table_ref[tile, 0], preferred_element_type=jnp.float32)
        rest = jnp.dot(high, table_ref[tile, 1], preferred_element_type=jnp.float32)
        wave_ref[tile] = both[:rows] + both[rows:] + rest
        return 0

    step = TILES // len(table_copies)
    for i, copy in enumerate(table_copies):
        copy.wait()
        lax.fori_loop(i * step, (i + 1) * step, middle, 0, unroll=3)

    def backward(step, _):
        line, rows, spot = spots(step)
        tiles = [(wave_ref[tile, spot, :LANES], wave_ref[tile, spot, LANES:]) for tile in range(TILES)]
        for n1, value in enumerate(real_backward(tiles)):
            line_ref[n1 // pieces, line, rows, pl.ds(n1 % pieces * LANES, LANES)] = value
        return 0

    lax.fori_loop(0, line_count * groups, backward, 0)


def start_all(copies):
    for copy in copies:
        copy.start()
    return copies


def wait_all(copies):
    for copy in copies:
        copy.wait()


def wall_sums(block, weight):
    row_count = block.shape[1]
    lower = [jnp.sum(block[p, :PAD] * weight[0][:, :1], axis=0) for p in range(2)]
    upper = [jnp.sum(block[p, row_count - PAD :] * weight[1][:, :1], axis=0) for p in range(2)]
    return lower + upper


def run_filter(table_hbm, lines_hbm, first, scratch):
    line_ref, wave_ref, table_ref, table_sems, sems = scratch
    count, line_count, _, _ = line_ref.shape
    lines = pl.ds(first, line_count)
    copies = [pltpu.make_async_copy(lines_hbm.at[x, lines], line_ref.at[x], sems.at[x]) for x in range(count)]
    start_all(copies)
    step = TILES // TABLE_COPIES
    spans = [pl.ds(i * step, step) for i in range(TABLE_COPIES)]
    table_copies = [
        pltpu.make_async_copy(table_hbm.at[span], table_ref.at[span], table_sems.at[i]) for i, span in enumerate(spans)
    ]
    start_all(table_copies)
    wait_all(copies)
    filter_lines(line_ref, wave_ref, table_ref, table_copies)


def filter_first_kernel(me_ref, table_hbm, weight_ref, lines_hbm, out_hbm, shear_ref, *scratch):
    run_filter(table_hbm, lines_hbm, 0, scratch)
    line_ref, sems, me = scratch[0], scratch[-1], me_ref[0]
    count = line_ref.shape[0]
    copies = start_all([pltpu.make_async_copy(line_ref.at[x], out_hbm.at[x], sems.at[x]) for x in range(count)])
    for x in range(count):
        for spot, value in enumerate(wall_sums(line_ref.at[me ^ x], weight_ref)):
            shear_ref[x, spot] = value
    wait_all(copies)


def filter_rest_kernel(me_ref, table_hbm, lines_hbm, *refs):
    sent, scratch = refs[:-5], refs[-5:]
    line_ref, sems, me = scratch[0], scratch[-1], me_ref[0]
    run_filter(table_hbm, lines_hbm, lines_hbm.shape[1] - line_ref.shape[1], scratch)
    copies = [pltpu.make_async_copy(line_ref.at[me ^ x], sent[x], sems.at[x]) for x in range(len(sent))]
    wait_all(start_all(copies))


HBM = pl.BlockSpec(memory_space=pltpu.HBM)
SCALARS = pl.BlockSpec(memory_space=pltpu.SMEM)
WHOLE = pl.BlockSpec(memory_space=pltpu.VMEM)


def filter_call(kernel, name, block, tables, in_specs, out_specs, out_shape):
    count, line_count, row_count, width = block
    rows = line_count * row_count
    flops = 3 * 2 * TILES * rows * (2 * LANES) ** 2
    return pl.pallas_call(
        kernel,
        out_shape=out_shape,
        in_specs=in_specs,
        out_specs=out_specs,
        scratch_shapes=[
            pltpu.VMEM(block, jnp.float32),
            pltpu.VMEM((TILES, rows, 2 * LANES), jnp.float32),
            pltpu.VMEM(tables.shape, tables.dtype),
            pltpu.SemaphoreType.DMA((TABLE_COPIES,)),
            pltpu.SemaphoreType.DMA((count,)),
        ],
        compiler_params=pltpu.CompilerParams(vmem_limit_bytes=FILTER_VMEM),
        cost_estimate=pl.CostEstimate(flops=flops, bytes_accessed=8 * count * rows * width, transcendentals=0),
        name=name,
    )


def filter_first(lines, weight, spots, tables):
    block = (lines.shape[0], 2) + lines.shape[2:]
    shear = jax.ShapeDtypeStruct((block[0], 4, block[3]), jnp.float32)
    out_shape = (jax.ShapeDtypeStruct(block, jnp.float32), shear)
    ins = [SCALARS, HBM, WHOLE, HBM]
    call = filter_call(filter_first_kernel, "filter_first", block, tables, ins, (HBM, WHOLE), out_shape)
    return call(spots, tables, weight, lines)


def filter_rest(lines, spots, tables):
    count, line_count, row_count, width = lines.shape
    block = (count, line_count - 2, row_count, width)
    out_shape = [jax.ShapeDtypeStruct(block[1:], jnp.float32)] * count
    ins = [SCALARS, HBM, HBM]
    call = filter_call(filter_rest_kernel, "filter_rest", block, tables, ins, [HBM] * count, out_shape)
    return call(spots, tables, lines)


def local_kernel(rate_ref, coef_ref, flow_ref, weight_ref, field_ref, low_ref, high_ref, out_ref, shear_ref, pad_ref):
    _, comp_count, part_count, row_count, width = field_ref.shape
    pad_ref[:, :, :PAD] = low_ref[0]
    pad_ref[:, :, PAD : PAD + row_count] = field_ref[0]
    pad_ref[:, :, PAD + row_count :] = high_ref[0]
    rate = rate_ref[pl.program_id(0)]

    def column(step, _):
        lanes = pl.ds(pl.multiple_of(step * LANES, LANES), LANES)
        for top in range(0, row_count, PAD):
            rows = pl.ds(top, PAD)
            advect = rate * flow_ref[0, rows, :]
            shear = TAU * flow_ref[1, rows, :]
            centre = [[field_ref[0, c, p, rows, lanes] for p in range(2)] for c in range(comp_count)]
            for c in range(comp_count):
                for p in range(2):
                    total = centre[c][p]
                    total = total - advect * centre[c][1] if p == 0 else total + advect * centre[c][0]
                    if c == 1:
                        total = total - shear * centre[0][p]
                    for offset in range(STEN):
                        near = pad_ref[c, p, pl.ds(top + offset + PAD - HALO, PAD), lanes]
                        total = total + coef_ref[offset, rows, :] * near
                    out_ref[0, c, p, rows, lanes] = total
        return 0

    lax.fori_loop(0, width // LANES, column, 0)
    for spot, value in enumerate(wall_sums(out_ref.at[0, 0], weight_ref)):
        shear_ref[0, spot] = value


def local_terms(field, low, high, rate, coef, flow, weight):
    mode_count, comp_count, part_count, row_count, width = field.shape
    block = (1, comp_count, part_count, row_count, width)
    edge = (1, comp_count, part_count, PAD, width)

    def by_mode(m):
        return (m, 0, 0, 0, 0)

    return pl.pallas_call(
        local_kernel,
        grid=(mode_count,),
        out_shape=(
            jax.ShapeDtypeStruct(field.shape, jnp.float32),
            jax.ShapeDtypeStruct((mode_count, 2 * part_count, width), jnp.float32),
        ),
        in_specs=[
            SCALARS,
            pl.BlockSpec(coef.shape, lambda m: (0, 0, 0)),
            pl.BlockSpec(flow.shape, lambda m: (0, 0, 0)),
            pl.BlockSpec(weight.shape, lambda m: (0, 0, 0)),
            pl.BlockSpec(block, by_mode),
            pl.BlockSpec(edge, by_mode),
            pl.BlockSpec(edge, by_mode),
        ],
        out_specs=(pl.BlockSpec(block, by_mode), pl.BlockSpec((1, 2 * part_count, width), lambda m: (m, 0, 0))),
        scratch_shapes=[pltpu.VMEM((comp_count, part_count, row_count + 2 * PAD, width), jnp.float32)],
        compiler_params=pltpu.CompilerParams(vmem_limit_bytes=24 << 20),
        cost_estimate=pl.CostEstimate(flops=40 * field.size, bytes_accessed=10 * field.size, transcendentals=0),
        name="local_terms",
    )(rate, coef, flow, weight, field, low, high)


def add_kernel(row_split, comps, me_ref, base_hbm, *refs):
    base_ref, term_ref, base_sems, term_sems = refs[-4:]
    count, _, _, row_count, _ = base_ref.shape
    *terms, out_hbm = refs[:-4]
    me = me_ref[0]

    def spot(ref, x):
        other = me ^ x
        top = pl.multiple_of(other % row_split * row_count, PAD)
        return ref.at[other // row_split, comps, :, pl.ds(top, row_count)]

    loads = [pltpu.make_async_copy(spot(base_hbm, x), base_ref.at[x], base_sems.at[x]) for x in range(count)]
    sources = [terms[0].at[me ^ x] if len(terms) == 1 else terms[x] for x in range(count)]
    term_loads = [pltpu.make_async_copy(sources[x], term_ref.at[x], term_sems.at[x]) for x in range(count)]
    stores = [pltpu.make_async_copy(base_ref.at[x], spot(out_hbm, x), base_sems.at[x]) for x in range(count)]
    for x in range(count):
        loads[x].start()
        term_loads[x].start()
    for x in range(count):
        loads[x].wait()
        term_loads[x].wait()
        base_ref[x] = base_ref[x] + term_ref[x]
        stores[x].start()
    wait_all(stores)


def add_components(base, terms, spots, span, row_split, comps):
    first, last = comps
    mode_count, _, part_count, row_count, width = base.shape
    block = (span, last - first, part_count, row_count // row_split, width)
    terms = [term.reshape(block[1:] if len(terms) > 1 else block) for term in terms]
    size = math.prod(block)
    buffer, sems = pltpu.VMEM(block, jnp.float32), pltpu.SemaphoreType.DMA((span,))
    return pl.pallas_call(
        functools.partial(add_kernel, row_split, pl.ds(first, last - first)),
        out_shape=jax.ShapeDtypeStruct(base.shape, jnp.float32),
        in_specs=[SCALARS] + [HBM] * (1 + len(terms)),
        out_specs=HBM,
        scratch_shapes=[buffer, buffer, sems, sems],
        input_output_aliases={1: 0},
        compiler_params=pltpu.CompilerParams(vmem_limit_bytes=24 << 20),
        cost_estimate=pl.CostEstimate(flops=size, bytes_accessed=12 * size, transcendentals=0),
        name="add_components",
    )(spots, base, *terms)


def after(value, *others):
    return lax.optimization_barrier((value,) + others)[0]


def on_device(field, mean_flow, d2_coef, wall_coef, kx_index, patch_of):
    mode_count, comp_count, part_count, row_count, width = field.shape
    span = lax.axis_size("span")
    me = lax.axis_index("span")
    wall_count = lax.axis_size("wall")
    wall_index = lax.axis_index("wall")
    mode_split = math.gcd(span, mode_count)
    row_split = span // mode_split
    line_rows = row_count // row_split
    tables = jnp.asarray(spectral_tables(width * span))
    pairs = [[(i, i ^ x) for i in range(span)] for x in range(span)]
    spots = jnp.stack([me, me // row_split, me % row_split * line_rows]).astype(jnp.int32)

    def exchange(lines):
        return lax.all_to_all(lines, "span", split_axis=0, concat_axis=0)

    def swap(blocks):
        return [lax.ppermute(blocks[x], "span", pairs[x]) for x in range(span - 1, 0, -1)][::-1]

    lines = field.reshape(mode_split, -1, row_split, line_rows, width)
    lines = exchange(lines.transpose(0, 2, 1, 3, 4).reshape(span, -1, line_rows, width))

    forward = [(i, i + 1) for i in range(wall_count - 1)]
    backward = [(i + 1, i) for i in range(wall_count - 1)]
    low = lax.ppermute(field[:, :, :, row_count - PAD :], "wall", forward)
    high = lax.ppermute(field[:, :, :, :PAD], "wall", backward)

    patches, distance = patch_of[None], 1
    while distance < span:
        patches = jnp.concatenate([patches, lax.ppermute(patches, "span", pairs[distance])])
        distance *= 2
    onehot = (patches[:, :, None] == jnp.arange(PATCH, dtype=jnp.int32)).astype(jnp.float32)

    lower = jnp.where(wall_index == 0, wall_coef[0], 0.0)
    upper = jnp.where(wall_index == wall_count - 1, wall_coef[1, ::-1], 0.0)
    weight = jnp.broadcast_to(jnp.stack([lower, upper])[:, :, None], (2, PAD, LANES))
    group = me % row_split
    ends = jnp.stack([group == 0, group == row_split - 1])
    line_weight = jnp.where(ends[:, None, None], weight, 0.0)

    rate = kx_index.astype(jnp.float32) * (0.25 * TAU)
    coef = jnp.broadcast_to(d2_coef[:, :, None], (STEN, row_count, LANES))
    flow = jnp.broadcast_to(mean_flow[:, :, None], (2, row_count, LANES))
    base, shear = local_terms(field, low, high, rate, coef, flow, weight)

    lines = after(lines, base, patches)
    filtered, line_shear = filter_first(lines, line_weight, spots, tables)
    back = exchange(filtered)
    sent = filter_rest(after(lines, line_shear), spots, tables)
    returned = [sent[0]] + swap(sent)

    highest = lax.Precision.HIGHEST
    grad = jnp.einsum("mwz,zq->mwq", shear, onehot[0], precision=highest)
    line_grad = jnp.einsum("xwz,xzq->wq", line_shear, onehot, precision=highest)
    mine = jnp.arange(mode_count) == me // row_split
    grad = after(grad + jnp.where(mine[:, None, None], line_grad, 0.0), sent[0])
    grad = lax.psum(grad, ("wall", "span"))
    wall_grad = grad.reshape(mode_count, 2, part_count, PATCH).transpose(1, 0, 2, 3)

    result = add_components(base, [back], spots, span, row_split, (0, 1))
    result = add_components(result, returned, spots, span, row_split, (1, comp_count))
    return (result, wall_grad)


def solution(mesh):
    return jax.shard_map(
        on_device,
        mesh=mesh,
        in_specs=(
            P(None, None, None, "wall", "span"),
            P(None, "wall"),
            P(None, "wall"),
            P(),
            P(),
            P("span"),
        ),
        out_specs=(P(None, None, None, "wall", "span"), P()),
        check_vma=False,
    )
```

```python
import functools
import math

import jax
import jax.numpy as jnp
import numpy as np
from jax import lax
from jax.experimental import pallas as pl
from jax.experimental.pallas import tpu as pltpu
from jax.sharding import PartitionSpec as P

HALO = 7
STEN = 15
PATCH = 64
TAU = 0.25
VIS = 0.5

LANES = 128
OUTER = 48
PAD = 8
TILES = OUTER // 2
FILTER_VMEM = 57_500_000
TABLE_COPIES = 4

QUARTER = (0, 4, 2, 1, 5, 9)
KEPT = tuple(4 * q for q in QUARTER) + tuple(2 + 8 * t for t in range(6)) + tuple(4 * q + 1 for q in range(12))


@functools.cache
def spectral_tables(length):
    signed = np.arange(length)
    signed = np.where(signed > length // 2, signed - length, signed)
    cutoff = length // 3
    ratio = signed.astype(np.float64) / cutoff
    multiplier = np.where(np.abs(signed) < cutoff, -VIS * ratio * ratio, 0.0)
    shift = np.arange(LANES)[None, :] - np.arange(LANES)[:, None]
    inner = np.arange(LANES)

    def complex_table(k1):
        wave = k1 + OUTER * inner
        spots = np.arange(-LANES + 1, LANES)
        phase = np.exp(2j * np.pi * ((wave[:, None] * spots[None, :]) % length) / length)
        return ((multiplier[wave][:, None] * phase).sum(axis=0) / LANES)[shift + LANES - 1]

    tables = np.zeros((TILES, 2 * LANES, 2 * LANES))
    tables[0, :LANES, :LANES] = complex_table(0).real / OUTER
    tables[0, LANES:, LANES:] = complex_table(OUTER // 2).real / OUTER
    for tile, k1 in enumerate(KEPT[1:], 1):
        table = complex_table(k1) * 2.0 / OUTER
        tables[tile, :LANES, :LANES] = table.real
        tables[tile, :LANES, LANES:] = table.imag
        tables[tile, LANES:, :LANES] = -table.imag
        tables[tile, LANES:, LANES:] = table.real
    high = tables.astype(jnp.bfloat16)
    low = (tables - high.astype(np.float64)).astype(jnp.bfloat16)
    return np.stack([high, low], axis=1)


def turn(value, numerator, denominator):
    re, im = value
    numerator %= denominator
    if numerator == 0:
        return value
    if 2 * numerator == denominator:
        return (-re, -im)
    if 4 * numerator == denominator:
        return (-im, re)
    if 4 * numerator == 3 * denominator:
        return (im, -re)
    cos = math.cos(2 * math.pi * numerator / denominator)
    sin = math.sin(2 * math.pi * numerator / denominator)
    return (re * cos - im * sin, re * sin + im * cos)


def add(a, b):
    return (a[0] + b[0], a[1] + b[1])


def sub(a, b):
    return (a[0] - b[0], a[1] - b[1])


ROOT = math.sqrt(3.0) / 2.0


def dft3(x, sign):
    total = add(x[1], x[2])
    other = sub(x[1], x[2])
    middle = (x[0][0] - 0.5 * total[0], x[0][1] - 0.5 * total[1])
    side = (-sign * ROOT * other[1], sign * ROOT * other[0])
    return [add(x[0], total), add(middle, side), sub(middle, side)]


def dft6(x, sign):
    even = dft3([add(x[b], x[b + 3]) for b in range(3)], sign)
    odd = dft3([turn(sub(x[b], x[b + 3]), sign * b, 6) for b in range(3)], sign)
    return [even[0], odd[0], even[1], odd[1], even[2], odd[2]]


def dft12(x, sign):
    out = [None] * 12
    parts = [[], [], [], []]
    for b in range(3):
        a0, a1, a2, a3 = x[b], x[b + 3], x[b + 6], x[b + 9]
        s0, s1, d0, d1 = add(a0, a2), add(a1, a3), sub(a0, a2), turn(sub(a1, a3), sign, 4)
        for r, value in enumerate((add(s0, s1), add(d0, d1), sub(s0, s1), sub(d0, d1))):
            parts[r].append(turn(value, sign * b * r, 12))
    for r in range(4):
        for q, value in enumerate(dft3(parts[r], sign)):
            out[4 * q + r] = value
    return out


def real_forward(x):
    whole, halved, turned = [], [], []
    for b in range(12):
        s0, s1 = x[b] + x[b + 24], x[b + 12] + x[b + 36]
        whole.append(s0 + s1)
        halved.append(s0 - s1)
        turned.append(turn((x[b] - x[b + 24], x[b + 36] - x[b + 12]), -b, 48))
    w, h, t = [], [], []
    for b in range(3):
        s0, s1 = whole[b] + whole[b + 6], whole[b + 3] + whole[b + 9]
        w.append(s0 + s1)
        h.append(s0 - s1)
        t.append(turn((whole[b] - whole[b + 6], whole[b + 9] - whole[b + 3]), -b, 12))
    total, other = w[1] + w[2], w[1] - w[2]
    four = (w[0] - 0.5 * total, -ROOT * other)
    two = (h[0] + 0.5 * (h[1] - h[2]), -ROOT * (h[1] + h[2]))
    tiles = [(w[0] + total, h[0] - h[1] + h[2]), four, two] + dft3(t, -1)
    tiles += dft6([turn((halved[b], -halved[b + 6]), -b, 24) for b in range(6)], -1)
    return tiles + dft12(turned, -1)


def real_backward(tiles):
    (zero, half), four, two = tiles[:3]
    w0 = zero + four[0]
    rest, side = zero - 0.5 * four[0], ROOT * four[1]
    w = [w0, rest - side, rest + side]
    h_side = 0.5 * two[0] - ROOT * two[1]
    h = [two[0] + half, h_side - half, -0.5 * two[0] - ROOT * two[1] + half]
    t = [turn(value, b, 12) for b, value in enumerate(dft3(tiles[3:6], 1))]
    whole = [None] * 12
    for b in range(3):
        s, d = w[b] + h[b], w[b] - h[b]
        whole[b], whole[b + 6] = s + t[b][0], s - t[b][0]
        whole[b + 3], whole[b + 9] = d - t[b][1], d + t[b][1]
    halved = [None] * 12
    for b, value in enumerate(dft6(tiles[6:12], 1)):
        halved[b], halved[b + 6] = turn(value, b, 24)
        halved[b + 6] = -halved[b + 6]
    x = [None] * 48
    for b, value in enumerate(dft12(tiles[12:], 1)):
        re, im = turn(value, b, 48)
        s, d = whole[b] + halved[b], whole[b] - halved[b]
        x[b], x[b + 24] = s + re, s - re
        x[b + 12], x[b + 36] = d - im, d + im
    return x


def filter_lines(line_ref, wave_ref, table_ref, table_copies):
    _, line_count, row_count, width = line_ref.shape
    pieces = width // LANES
    groups = row_count // PAD

    def spots(step):
        return step // groups, pl.ds(pl.multiple_of(step % groups * PAD, PAD), PAD), pl.ds(pl.multiple_of(step * PAD, PAD), PAD)

    def forward(step, _):
        line, rows, spot = spots(step)
        values = [line_ref[n1 // pieces, line, rows, pl.ds(n1 % pieces * LANES, LANES)] for n1 in range(OUTER)]
        for tile, (re, im) in enumerate(real_forward(values)):
            wave_ref[tile, spot, :LANES] = re
            wave_ref[tile, spot, LANES:] = im
        return 0

    lax.fori_loop(0, line_count * groups, forward, 0)

    def middle(tile, _):
        value = wave_ref[tile]
        high = value.astype(jnp.bfloat16)
        low = (value - high.astype(jnp.float32)).astype(jnp.bfloat16)
        rows = high.shape[0]
        both = jnp.dot(jnp.concatenate([high, low]), table_ref[tile, 0], preferred_element_type=jnp.float32)
        rest = jnp.dot(high, table_ref[tile, 1], preferred_element_type=jnp.float32)
        wave_ref[tile] = both[:rows] + both[rows:] + rest
        return 0

    step = TILES // len(table_copies)
    for i, copy in enumerate(table_copies):
        copy.wait()
        lax.fori_loop(i * step, (i + 1) * step, middle, 0, unroll=3)

    def backward(step, _):
        line, rows, spot = spots(step)
        tiles = [(wave_ref[tile, spot, :LANES], wave_ref[tile, spot, LANES:]) for tile in range(TILES)]
        for n1, value in enumerate(real_backward(tiles)):
            line_ref[n1 // pieces, line, rows, pl.ds(n1 % pieces * LANES, LANES)] = value
        return 0

    lax.fori_loop(0, line_count * groups, backward, 0)


def start_all(copies):
    for copy in copies:
        copy.start()
    return copies


def wait_all(copies):
    for copy in copies:
        copy.wait()


def wall_sums(block, weight):
    row_count = block.shape[1]
    lower = [jnp.sum(block[p, :PAD] * weight[0][:, :1], axis=0) for p in range(2)]
    upper = [jnp.sum(block[p, row_count - PAD :] * weight[1][:, :1], axis=0) for p in range(2)]
    return lower + upper


def run_filter(table_hbm, lines_hbm, first, scratch):
    line_ref, wave_ref, table_ref, table_sems, sems = scratch
    count, line_count, _, _ = line_ref.shape
    lines = pl.ds(first, line_count)
    copies = [pltpu.make_async_copy(lines_hbm.at[x, lines], line_ref.at[x], sems.at[x]) for x in range(count)]
    start_all(copies)
    step = TILES // TABLE_COPIES
    spans = [pl.ds(i * step, step) for i in range(TABLE_COPIES)]
    table_copies = [
        pltpu.make_async_copy(table_hbm.at[span], table_ref.at[span], table_sems.at[i]) for i, span in enumerate(spans)
    ]
    start_all(table_copies)
    wait_all(copies)
    filter_lines(line_ref, wave_ref, table_ref, table_copies)


def filter_first_kernel(table_hbm, lines_hbm, out_hbm, *scratch):
    run_filter(table_hbm, lines_hbm, 0, scratch)
    line_ref, sems = scratch[0], scratch[-1]
    wait_all(start_all([pltpu.make_async_copy(line_ref.at[x], out_hbm.at[x], sems.at[x]) for x in range(sems.shape[0])]))


def filter_rest_kernel(me_ref, table_hbm, lines_hbm, *refs):
    sent, scratch = refs[:-5], refs[-5:]
    line_ref, sems, me = scratch[0], scratch[-1], me_ref[0]
    run_filter(table_hbm, lines_hbm, lines_hbm.shape[1] - line_ref.shape[1], scratch)
    copies = [pltpu.make_async_copy(line_ref.at[me ^ x], sent[x], sems.at[x]) for x in range(len(sent))]
    wait_all(start_all(copies))


HBM = pl.BlockSpec(memory_space=pltpu.HBM)
SCALARS = pl.BlockSpec(memory_space=pltpu.SMEM)
WHOLE = pl.BlockSpec(memory_space=pltpu.VMEM)


def filter_call(kernel, name, block, tables, in_specs, out_specs, out_shape):
    count, line_count, row_count, width = block
    rows = line_count * row_count
    flops = 3 * 2 * TILES * rows * (2 * LANES) ** 2
    return pl.pallas_call(
        kernel,
        out_shape=out_shape,
        in_specs=in_specs,
        out_specs=out_specs,
        scratch_shapes=[
            pltpu.VMEM(block, jnp.float32),
            pltpu.VMEM((TILES, rows, 2 * LANES), jnp.float32),
            pltpu.VMEM(tables.shape, tables.dtype),
            pltpu.SemaphoreType.DMA((TABLE_COPIES,)),
            pltpu.SemaphoreType.DMA((count,)),
        ],
        compiler_params=pltpu.CompilerParams(vmem_limit_bytes=FILTER_VMEM),
        cost_estimate=pl.CostEstimate(flops=flops, bytes_accessed=8 * count * rows * width, transcendentals=0),
        name=name,
    )


def filter_first(lines, tables):
    block = (lines.shape[0], 2) + lines.shape[2:]
    out_shape = jax.ShapeDtypeStruct(block, jnp.float32)
    call = filter_call(filter_first_kernel, "filter_first", block, tables, [HBM, HBM], HBM, out_shape)
    return call(tables, lines)


def filter_rest(lines, spots, tables):
    count, line_count, row_count, width = lines.shape
    block = (count, line_count - 2, row_count, width)
    out_shape = [jax.ShapeDtypeStruct(block[1:], jnp.float32)] * count
    ins = [SCALARS, HBM, HBM]
    call = filter_call(filter_rest_kernel, "filter_rest", block, tables, ins, [HBM] * count, out_shape)
    return call(spots, tables, lines)


def local_kernel(rate_ref, coef_ref, flow_ref, field_ref, low_ref, high_ref, out_ref, pad_ref):
    _, comp_count, part_count, row_count, width = field_ref.shape
    pad_ref[:, :, :PAD] = low_ref[0]
    pad_ref[:, :, PAD : PAD + row_count] = field_ref[0]
    pad_ref[:, :, PAD + row_count :] = high_ref[0]
    rate = rate_ref[pl.program_id(0)]

    def column(step, _):
        lanes = pl.ds(pl.multiple_of(step * LANES, LANES), LANES)
        for top in range(0, row_count, PAD):
            rows = pl.ds(top, PAD)
            advect = rate * flow_ref[0, rows, :]
            shear = TAU * flow_ref[1, rows, :]
            centre = [[field_ref[0, c, p, rows, lanes] for p in range(2)] for c in range(comp_count)]
            for c in range(comp_count):
                for p in range(2):
                    total = centre[c][p]
                    total = total - advect * centre[c][1] if p == 0 else total + advect * centre[c][0]
                    if c == 1:
                        total = total - shear * centre[0][p]
                    for offset in range(STEN):
                        near = pad_ref[c, p, pl.ds(top + offset + PAD - HALO, PAD), lanes]
                        total = total + coef_ref[offset, rows, :] * near
                    out_ref[0, c, p, rows, lanes] = total
        return 0

    lax.fori_loop(0, width // LANES, column, 0)


def local_terms(field, low, high, rate, coef, flow):
    mode_count, comp_count, part_count, row_count, width = field.shape
    block = (1, comp_count, part_count, row_count, width)
    edge = (1, comp_count, part_count, PAD, width)

    def by_mode(m):
        return (m, 0, 0, 0, 0)

    return pl.pallas_call(
        local_kernel,
        grid=(mode_count,),
        out_shape=jax.ShapeDtypeStruct(field.shape, jnp.float32),
        in_specs=[
            SCALARS,
            pl.BlockSpec(coef.shape, lambda m: (0, 0, 0)),
            pl.BlockSpec(flow.shape, lambda m: (0, 0, 0)),
            pl.BlockSpec(block, by_mode),
            pl.BlockSpec(edge, by_mode),
            pl.BlockSpec(edge, by_mode),
        ],
        out_specs=pl.BlockSpec(block, by_mode),
        scratch_shapes=[pltpu.VMEM((comp_count, part_count, row_count + 2 * PAD, width), jnp.float32)],
        compiler_params=pltpu.CompilerParams(vmem_limit_bytes=24 << 20),
        cost_estimate=pl.CostEstimate(flops=40 * field.size, bytes_accessed=10 * field.size, transcendentals=0),
        name="local_terms",
    )(rate, coef, flow, field, low, high)


def add_kernel(row_split, comps, me_ref, base_hbm, *refs):
    base_ref, term_ref, base_sems, term_sems = refs[-4:]
    count, _, _, row_count, _ = base_ref.shape
    sums = comps.start == 0
    if sums:
        weight_ref, *terms, out_hbm, shear_ref = refs[:-4]
    else:
        *terms, out_hbm = refs[:-4]
    me = me_ref[0]

    def spot(ref, x):
        other = me ^ x
        top = pl.multiple_of(other % row_split * row_count, PAD)
        return ref.at[other // row_split, comps, :, pl.ds(top, row_count)]

    loads = [pltpu.make_async_copy(spot(base_hbm, x), base_ref.at[x], base_sems.at[x]) for x in range(count)]
    sources = [terms[0].at[me ^ x] if len(terms) == 1 else terms[x] for x in range(count)]
    term_loads = [pltpu.make_async_copy(sources[x], term_ref.at[x], term_sems.at[x]) for x in range(count)]
    stores = [pltpu.make_async_copy(base_ref.at[x], spot(out_hbm, x), base_sems.at[x]) for x in range(count)]
    for x in range(count):
        loads[x].start()
        term_loads[x].start()
    for x in range(count):
        loads[x].wait()
        term_loads[x].wait()
        base_ref[x] = base_ref[x] + term_ref[x]
        stores[x].start()
        if sums:
            for place, value in enumerate(wall_sums(base_ref.at[x, 0], weight_ref[x])):
                shear_ref[me ^ x, place] = value
    wait_all(stores)


def add_components(base, terms, spots, row_split, comps, weight=None):
    first, last = comps
    _, _, part_count, row_count, width = base.shape
    span = weight.shape[0] if weight is not None else len(terms)
    block = (span, last - first, part_count, row_count // row_split, width)
    terms = [term.reshape(block[1:] if len(terms) > 1 else block) for term in terms]
    size = math.prod(block)
    buffer, sems = pltpu.VMEM(block, jnp.float32), pltpu.SemaphoreType.DMA((span,))
    out_shape, out_specs, weights = jax.ShapeDtypeStruct(base.shape, jnp.float32), HBM, []
    if weight is not None:
        out_shape, out_specs = (out_shape, jax.ShapeDtypeStruct((span, 4, width), jnp.float32)), (HBM, WHOLE)
        weights = [weight]
    return pl.pallas_call(
        functools.partial(add_kernel, row_split, pl.ds(first, last - first)),
        out_shape=out_shape,
        in_specs=[SCALARS, HBM] + [WHOLE] * len(weights) + [HBM] * len(terms),
        out_specs=out_specs,
        scratch_shapes=[buffer, buffer, sems, sems],
        input_output_aliases={1: 0},
        compiler_params=pltpu.CompilerParams(vmem_limit_bytes=24 << 20),
        cost_estimate=pl.CostEstimate(flops=size, bytes_accessed=12 * size, transcendentals=0),
        name="add_components",
    )(spots, base, *weights, *terms)


def after(value, *others):
    return lax.optimization_barrier((value,) + others)[0]


def on_device(field, mean_flow, d2_coef, wall_coef, kx_index, patch_of):
    mode_count, comp_count, part_count, row_count, width = field.shape
    span = lax.axis_size("span")
    me = lax.axis_index("span")
    wall_count = lax.axis_size("wall")
    wall_index = lax.axis_index("wall")
    mode_split = math.gcd(span, mode_count)
    row_split = span // mode_split
    line_rows = row_count // row_split
    tables = jnp.asarray(spectral_tables(width * span))
    pairs = [[(i, i ^ x) for i in range(span)] for x in range(span)]
    spots = jnp.stack([me, me // row_split, me % row_split * line_rows]).astype(jnp.int32)

    def exchange(lines):
        return lax.all_to_all(lines, "span", split_axis=0, concat_axis=0)

    def swap(blocks):
        return [lax.ppermute(blocks[x], "span", pairs[x]) for x in range(span - 1, 0, -1)][::-1]

    lines = field.reshape(mode_split, -1, row_split, line_rows, width)
    lines = exchange(lines.transpose(0, 2, 1, 3, 4).reshape(span, -1, line_rows, width))

    forward = [(i, i + 1) for i in range(wall_count - 1)]
    backward = [(i + 1, i) for i in range(wall_count - 1)]
    low = lax.ppermute(field[:, :, :, row_count - PAD :], "wall", forward)
    high = lax.ppermute(field[:, :, :, :PAD], "wall", backward)

    rate = kx_index.astype(jnp.float32) * (0.25 * TAU)
    coef = jnp.broadcast_to(d2_coef[:, :, None], (STEN, row_count, LANES))
    flow = jnp.broadcast_to(mean_flow[:, :, None], (2, row_count, LANES))
    base = local_terms(field, low, high, rate, coef, flow)

    lines = after(lines, base)
    filtered = filter_first(lines, tables)
    back = exchange(filtered)
    sent = filter_rest(after(lines, filtered), spots, tables)
    returned = [sent[0]] + swap(sent)

    lower = jnp.where(wall_index == 0, wall_coef[0], 0.0)
    upper = jnp.where(wall_index == wall_count - 1, wall_coef[1, ::-1], 0.0)
    group = ((me ^ jnp.arange(span)) % row_split)[:, None]
    ends = [jnp.where(group == 0, lower, 0.0), jnp.where(group == row_split - 1, upper, 0.0)]
    weight = jnp.broadcast_to(jnp.stack(ends, axis=1)[..., None], (span, 2, PAD, LANES))
    result, shear = add_components(base, [back], spots, row_split, (0, 1), weight)
    onehot = (patch_of[:, None] == jnp.arange(PATCH, dtype=jnp.int32)[None, :]).astype(jnp.float32)
    grad = jnp.einsum("swz,zq->swq", shear, onehot, precision=lax.Precision.HIGHEST)
    grad = grad.reshape(mode_count, row_split, 2, part_count, PATCH).sum(axis=1)
    distance = 1
    while distance < wall_count:
        grad = grad + lax.ppermute(grad, "wall", [(i, i ^ distance) for i in range(wall_count)])
        distance *= 2
    parts = jnp.stack([grad] + swap([grad] * span))
    parts = [lax.dynamic_index_in_dim(parts, me ^ x, 0, keepdims=False) for x in range(span)]
    wall_grad = functools.reduce(jnp.add, parts).transpose(1, 0, 2, 3)

    result = add_components(result, returned, spots, row_split, (1, comp_count))
    return (result, wall_grad)


def solution(mesh):
    return jax.shard_map(
        on_device,
        mesh=mesh,
        in_specs=(
            P(None, None, None, "wall", "span"),
            P(None, "wall"),
            P(None, "wall"),
            P(),
            P(),
            P("span"),
        ),
        out_specs=(P(None, None, None, "wall", "span"), P()),
        check_vma=False,
    )
```

```python
import functools
import math

import jax
import jax.numpy as jnp
import numpy as np
from jax import lax
from jax.experimental import pallas as pl
from jax.experimental.pallas import tpu as pltpu
from jax.sharding import PartitionSpec as P

HALO = 7
STEN = 15
PATCH = 64
TAU = 0.25
VIS = 0.5

LANES = 128
OUTER = 48
PAD = 8
TILES = OUTER // 2
FILTER_VMEM = 57_500_000
TABLE_COPIES = 4

QUARTER = (0, 4, 2, 1, 5, 9)
KEPT = tuple(4 * q for q in QUARTER) + tuple(2 + 8 * t for t in range(6)) + tuple(4 * q + 1 for q in range(12))


@functools.cache
def spectral_tables(length):
    signed = np.arange(length)
    signed = np.where(signed > length // 2, signed - length, signed)
    cutoff = length // 3
    ratio = signed.astype(np.float64) / cutoff
    multiplier = np.where(np.abs(signed) < cutoff, -VIS * ratio * ratio, 0.0)
    shift = np.arange(LANES)[None, :] - np.arange(LANES)[:, None]
    inner = np.arange(LANES)

    def complex_table(k1):
        wave = k1 + OUTER * inner
        spots = np.arange(-LANES + 1, LANES)
        phase = np.exp(2j * np.pi * ((wave[:, None] * spots[None, :]) % length) / length)
        return ((multiplier[wave][:, None] * phase).sum(axis=0) / LANES)[shift + LANES - 1]

    tables = np.zeros((TILES, 2 * LANES, 2 * LANES))
    tables[0, :LANES, :LANES] = complex_table(0).real / OUTER
    tables[0, LANES:, LANES:] = complex_table(OUTER // 2).real / OUTER
    for tile, k1 in enumerate(KEPT[1:], 1):
        table = complex_table(k1) * 2.0 / OUTER
        tables[tile, :LANES, :LANES] = table.real
        tables[tile, :LANES, LANES:] = table.imag
        tables[tile, LANES:, :LANES] = -table.imag
        tables[tile, LANES:, LANES:] = table.real
    high = tables.astype(jnp.bfloat16)
    low = (tables - high.astype(np.float64)).astype(jnp.bfloat16)
    return np.stack([high, low], axis=1)


def turn(value, numerator, denominator):
    re, im = value
    numerator %= denominator
    if numerator == 0:
        return value
    if 2 * numerator == denominator:
        return (-re, -im)
    if 4 * numerator == denominator:
        return (-im, re)
    if 4 * numerator == 3 * denominator:
        return (im, -re)
    cos = math.cos(2 * math.pi * numerator / denominator)
    sin = math.sin(2 * math.pi * numerator / denominator)
    return (re * cos - im * sin, re * sin + im * cos)


def add(a, b):
    return (a[0] + b[0], a[1] + b[1])


def sub(a, b):
    return (a[0] - b[0], a[1] - b[1])


ROOT = math.sqrt(3.0) / 2.0


def dft3(x, sign):
    total = add(x[1], x[2])
    other = sub(x[1], x[2])
    middle = (x[0][0] - 0.5 * total[0], x[0][1] - 0.5 * total[1])
    side = (-sign * ROOT * other[1], sign * ROOT * other[0])
    return [add(x[0], total), add(middle, side), sub(middle, side)]


def dft6(x, sign):
    even = dft3([add(x[b], x[b + 3]) for b in range(3)], sign)
    odd = dft3([turn(sub(x[b], x[b + 3]), sign * b, 6) for b in range(3)], sign)
    return [even[0], odd[0], even[1], odd[1], even[2], odd[2]]


def dft12(x, sign):
    out = [None] * 12
    parts = [[], [], [], []]
    for b in range(3):
        a0, a1, a2, a3 = x[b], x[b + 3], x[b + 6], x[b + 9]
        s0, s1, d0, d1 = add(a0, a2), add(a1, a3), sub(a0, a2), turn(sub(a1, a3), sign, 4)
        for r, value in enumerate((add(s0, s1), add(d0, d1), sub(s0, s1), sub(d0, d1))):
            parts[r].append(turn(value, sign * b * r, 12))
    for r in range(4):
        for q, value in enumerate(dft3(parts[r], sign)):
            out[4 * q + r] = value
    return out


def real_forward(x):
    whole, halved, turned = [], [], []
    for b in range(12):
        s0, s1 = x[b] + x[b + 24], x[b + 12] + x[b + 36]
        whole.append(s0 + s1)
        halved.append(s0 - s1)
        turned.append(turn((x[b] - x[b + 24], x[b + 36] - x[b + 12]), -b, 48))
    w, h, t = [], [], []
    for b in range(3):
        s0, s1 = whole[b] + whole[b + 6], whole[b + 3] + whole[b + 9]
        w.append(s0 + s1)
        h.append(s0 - s1)
        t.append(turn((whole[b] - whole[b + 6], whole[b + 9] - whole[b + 3]), -b, 12))
    total, other = w[1] + w[2], w[1] - w[2]
    four = (w[0] - 0.5 * total, -ROOT * other)
    two = (h[0] + 0.5 * (h[1] - h[2]), -ROOT * (h[1] + h[2]))
    tiles = [(w[0] + total, h[0] - h[1] + h[2]), four, two] + dft3(t, -1)
    tiles += dft6([turn((halved[b], -halved[b + 6]), -b, 24) for b in range(6)], -1)
    return tiles + dft12(turned, -1)


def real_backward(tiles):
    (zero, half), four, two = tiles[:3]
    w0 = zero + four[0]
    rest, side = zero - 0.5 * four[0], ROOT * four[1]
    w = [w0, rest - side, rest + side]
    h_side = 0.5 * two[0] - ROOT * two[1]
    h = [two[0] + half, h_side - half, -0.5 * two[0] - ROOT * two[1] + half]
    t = [turn(value, b, 12) for b, value in enumerate(dft3(tiles[3:6], 1))]
    whole = [None] * 12
    for b in range(3):
        s, d = w[b] + h[b], w[b] - h[b]
        whole[b], whole[b + 6] = s + t[b][0], s - t[b][0]
        whole[b + 3], whole[b + 9] = d - t[b][1], d + t[b][1]
    halved = [None] * 12
    for b, value in enumerate(dft6(tiles[6:12], 1)):
        halved[b], halved[b + 6] = turn(value, b, 24)
        halved[b + 6] = -halved[b + 6]
    x = [None] * 48
    for b, value in enumerate(dft12(tiles[12:], 1)):
        re, im = turn(value, b, 48)
        s, d = whole[b] + halved[b], whole[b] - halved[b]
        x[b], x[b + 24] = s + re, s - re
        x[b + 12], x[b + 36] = d - im, d + im
    return x


def group_count(piece):
    return piece[1] * piece[3]


def piece_at(ref, piece):
    return ref.at[:, pl.ds(piece[0], piece[1]), pl.ds(piece[2], piece[3])]


def start_all(copies):
    for copy in copies:
        copy.start()
    return copies


def wait_all(copies):
    for copy in copies:
        copy.wait()


def run_filter(pieces, table_hbm, lines_hbm, send, scratch):
    *line_refs, wave_ref, table_ref, table_sems, sems = scratch
    copies = [
        pltpu.make_async_copy(piece_at(lines_hbm, piece), line_ref, sems.at[i])
        for i, (piece, line_ref) in enumerate(zip(pieces, line_refs))
    ]
    start_all(copies)
    step = TILES // TABLE_COPIES
    spans = [pl.ds(i * step, step) for i in range(TABLE_COPIES)]
    table_copies = [
        pltpu.make_async_copy(table_hbm.at[span], table_ref.at[span], table_sems.at[i]) for i, span in enumerate(spans)
    ]
    start_all(table_copies)
    offsets = [sum(map(group_count, pieces[:i])) for i in range(len(pieces))]
    per_source = lines_hbm.shape[4] // LANES

    def spot(number):
        return pl.ds(pl.multiple_of(number * PAD, PAD), PAD)

    for piece, line_ref, offset, copy in zip(pieces, line_refs, offsets, copies):
        copy.wait()

        def forward(number, _, groups=piece[3], line_ref=line_ref, offset=offset):
            pair, group = number // groups, number % groups
            values = []
            for n1 in range(OUTER):
                lanes = pl.ds(n1 % per_source * LANES, LANES)
                values.append(line_ref[n1 // per_source, pair, group, :, lanes])
            for tile, (re, im) in enumerate(real_forward(values)):
                wave_ref[tile, spot(offset + number), :LANES] = re
                wave_ref[tile, spot(offset + number), LANES:] = im
            return 0

        lax.fori_loop(0, group_count(piece), forward, 0)

    def middle(tile, _):
        value = wave_ref[tile]
        high = value.astype(jnp.bfloat16)
        low = (value - high.astype(jnp.float32)).astype(jnp.bfloat16)
        rows = high.shape[0]
        both = jnp.dot(jnp.concatenate([high, low]), table_ref[tile, 0], preferred_element_type=jnp.float32)
        rest = jnp.dot(high, table_ref[tile, 1], preferred_element_type=jnp.float32)
        wave_ref[tile] = both[:rows] + both[rows:] + rest
        return 0

    for i, copy in enumerate(table_copies):
        copy.wait()
        lax.fori_loop(i * step, (i + 1) * step, middle, 0, unroll=3)

    away = []
    for i, (piece, line_ref, offset) in enumerate(zip(pieces, line_refs, offsets)):

        def backward(number, _, groups=piece[3], line_ref=line_ref, offset=offset):
            pair, group = number // groups, number % groups
            row = spot(offset + number)
            tiles = [(wave_ref[tile, row, :LANES], wave_ref[tile, row, LANES:]) for tile in range(TILES)]
            for n1, value in enumerate(real_backward(tiles)):
                line_ref[n1 // per_source, pair, group, :, pl.ds(n1 % per_source * LANES, LANES)] = value
            return 0

        lax.fori_loop(0, group_count(piece), backward, 0)
        away += start_all(send(i, line_ref))
    wait_all(away)


def filter_first_kernel(pieces, table_hbm, lines_hbm, out_hbm, *scratch):
    *scratch, out_sems = scratch

    def send(i, line_ref):
        return [pltpu.make_async_copy(line_ref.at[:, :, 0], out_hbm.at[:, i], out_sems.at[i])]

    run_filter(pieces, table_hbm, lines_hbm, send, scratch)


def filter_rest_kernel(pieces, me_ref, table_hbm, lines_hbm, *refs):
    count, me = lines_hbm.shape[0], me_ref[0]
    sent, scratch, out_sems = refs[:count], refs[count:-1], refs[-1]
    places = rest_places(pieces)

    def send(i, line_ref):
        copies = []
        for pair in range(pieces[i][1]):
            number, first = places[i][pair]
            target = pl.ds(first, pieces[i][3])
            for x in range(count):
                sem = out_sems.at[number * count + x]
                copies.append(pltpu.make_async_copy(line_ref.at[me ^ x, pair], sent[x].at[target], sem))
        return copies

    run_filter(pieces, table_hbm, lines_hbm, send, scratch)


def rest_places(pieces):
    places, number, first = [], 0, 0
    for piece in pieces:
        places.append([])
        for _ in range(piece[1]):
            places[-1].append((number, first))
            number, first = number + 1, first + piece[3]
    return places


HBM = pl.BlockSpec(memory_space=pltpu.HBM)
SCALARS = pl.BlockSpec(memory_space=pltpu.SMEM)
WHOLE = pl.BlockSpec(memory_space=pltpu.VMEM)


def filter_call(kernel, name, pieces, lines, tables, in_specs, out_specs, out_shape, out_sems):
    count, _, _, _, width = lines.shape
    rows = sum(map(group_count, pieces)) * PAD
    flops = 3 * 2 * TILES * rows * (2 * LANES) ** 2
    return pl.pallas_call(
        functools.partial(kernel, pieces),
        out_shape=out_shape,
        in_specs=in_specs,
        out_specs=out_specs,
        scratch_shapes=[pltpu.VMEM((count, piece[1], piece[3], PAD, width), jnp.float32) for piece in pieces]
        + [
            pltpu.VMEM((TILES, rows, 2 * LANES), jnp.float32),
            pltpu.VMEM(tables.shape, tables.dtype),
            pltpu.SemaphoreType.DMA((TABLE_COPIES,)),
            pltpu.SemaphoreType.DMA((len(pieces),)),
            pltpu.SemaphoreType.DMA((out_sems,)),
        ],
        compiler_params=pltpu.CompilerParams(vmem_limit_bytes=FILTER_VMEM),
        cost_estimate=pl.CostEstimate(flops=flops, bytes_accessed=8 * count * rows * width, transcendentals=0),
        name=name,
    )


def filter_first(lines, tables, pieces):
    count, _, _, _, width = lines.shape
    out_shape = jax.ShapeDtypeStruct((count, len(pieces), 2, PAD, width), jnp.float32)
    call = filter_call(
        filter_first_kernel, "filter_first", pieces, lines, tables, [HBM, HBM], HBM, out_shape, len(pieces)
    )
    return call(tables, lines)


def filter_rest(lines, spots, tables, pieces):
    count, _, _, _, width = lines.shape
    shape = (sum(map(group_count, pieces)), PAD, width)
    out_shape = [jax.ShapeDtypeStruct(shape, jnp.float32)] * count
    sems = count * sum(piece[1] for piece in pieces)
    ins = [SCALARS, HBM, HBM]
    call = filter_call(filter_rest_kernel, "filter_rest", pieces, lines, tables, ins, [HBM] * count, out_shape, sems)
    return call(spots, tables, lines)


def local_kernel(rate_ref, coef_ref, flow_ref, field_ref, low_ref, high_ref, out_ref, pad_ref):
    _, comp_count, part_count, row_count, width = field_ref.shape
    pad_ref[:, :, :PAD] = low_ref[0]
    pad_ref[:, :, PAD : PAD + row_count] = field_ref[0]
    pad_ref[:, :, PAD + row_count :] = high_ref[0]
    rate = rate_ref[pl.program_id(0)]

    def column(step, _):
        lanes = pl.ds(pl.multiple_of(step * LANES, LANES), LANES)
        for top in range(0, row_count, PAD):
            rows = pl.ds(top, PAD)
            advect = rate * flow_ref[0, rows, :]
            shear = TAU * flow_ref[1, rows, :]
            centre = [[field_ref[0, c, p, rows, lanes] for p in range(2)] for c in range(comp_count)]
            for c in range(comp_count):
                for p in range(2):
                    total = centre[c][p]
                    total = total - advect * centre[c][1] if p == 0 else total + advect * centre[c][0]
                    if c == 1:
                        total = total - shear * centre[0][p]
                    for offset in range(STEN):
                        near = pad_ref[c, p, pl.ds(top + offset + PAD - HALO, PAD), lanes]
                        total = total + coef_ref[offset, rows, :] * near
                    out_ref[0, c, p, rows, lanes] = total
        return 0

    lax.fori_loop(0, width // LANES, column, 0)


def local_terms(field, low, high, rate, coef, flow):
    mode_count, comp_count, part_count, row_count, width = field.shape
    block = (1, comp_count, part_count, row_count, width)
    edge = (1, comp_count, part_count, PAD, width)

    def by_mode(m):
        return (m, 0, 0, 0, 0)

    return pl.pallas_call(
        local_kernel,
        grid=(mode_count,),
        out_shape=jax.ShapeDtypeStruct(field.shape, jnp.float32),
        in_specs=[
            SCALARS,
            pl.BlockSpec(coef.shape, lambda m: (0, 0, 0)),
            pl.BlockSpec(flow.shape, lambda m: (0, 0, 0)),
            pl.BlockSpec(block, by_mode),
            pl.BlockSpec(edge, by_mode),
            pl.BlockSpec(edge, by_mode),
        ],
        out_specs=pl.BlockSpec(block, by_mode),
        scratch_shapes=[pltpu.VMEM((comp_count, part_count, row_count + 2 * PAD, width), jnp.float32)],
        compiler_params=pltpu.CompilerParams(vmem_limit_bytes=24 << 20),
        cost_estimate=pl.CostEstimate(flops=40 * field.size, bytes_accessed=10 * field.size, transcendentals=0),
        name="local_terms",
    )(rate, coef, flow, field, low, high)


def add_first_kernel(pieces, me_ref, base_hbm, weight_ref, term_hbm, out_hbm, shear_ref, *scratch):
    base_ref, term_ref, base_sems, term_sems = scratch
    count, split, me = term_hbm.shape[0], base_hbm.shape[2], me_ref[0]

    def spot(ref, x, i):
        other = me ^ x
        return ref.at[other // split, pl.ds(0, 2), other % split, pieces[i][2]]

    spots = [(x, i) for x in range(count) for i in range(len(pieces))]
    sem = [base_sems.at[x * len(pieces) + i] for x, i in spots]
    loads = [pltpu.make_async_copy(spot(base_hbm, *at), base_ref.at[at], sem[n]) for n, at in enumerate(spots)]
    stores = [pltpu.make_async_copy(base_ref.at[at], spot(out_hbm, *at), sem[n]) for n, at in enumerate(spots)]
    terms = [pltpu.make_async_copy(term_hbm.at[me ^ x], term_ref.at[x], term_sems.at[x]) for x in range(count)]
    start_all(loads)
    start_all(terms)
    wait_all(terms)
    wait_all(loads)
    for x in range(count):
        base_ref[x] = base_ref[x] + term_ref[x]
        start_all(stores[x * len(pieces) : (x + 1) * len(pieces)])
        for p in range(2):
            shear_ref[me ^ x, p] = jnp.sum(base_ref[x, 0, p] * weight_ref[x, 0][:, :1], axis=0)
            shear_ref[me ^ x, 2 + p] = jnp.sum(base_ref[x, len(pieces) - 1, p] * weight_ref[x, 1][:, :1], axis=0)
    wait_all(stores)


def add_first(base, term, weight, spots, pieces):
    count, width = term.shape[0], term.shape[4]
    buffer = pltpu.VMEM(term.shape, jnp.float32)
    return pl.pallas_call(
        functools.partial(add_first_kernel, pieces),
        out_shape=(
            jax.ShapeDtypeStruct(base.shape, jnp.float32),
            jax.ShapeDtypeStruct((count, 4, width), jnp.float32),
        ),
        in_specs=[SCALARS, HBM, WHOLE, HBM],
        out_specs=(HBM, WHOLE),
        scratch_shapes=[
            buffer,
            buffer,
            pltpu.SemaphoreType.DMA((count * len(pieces),)),
            pltpu.SemaphoreType.DMA((count,)),
        ],
        input_output_aliases={1: 0},
        compiler_params=pltpu.CompilerParams(vmem_limit_bytes=24 << 20),
        cost_estimate=pl.CostEstimate(flops=term.size, bytes_accessed=12 * term.size, transcendentals=0),
        name="add_first",
    )(spots, base, weight, term)


def add_rest_kernel(pieces, partners, me_ref, base_hbm, *refs):
    count = len(partners)
    terms, out_hbm = refs[:count], refs[count]
    base_ref, term_ref, base_sems, term_sems = refs[count + 1 :]
    split, me = base_hbm.shape[2], me_ref[0]
    places = rest_places(pieces)
    spots = []
    for n, x in enumerate(partners):
        for piece, pairs in zip(pieces, places):
            for pair, (number, first) in enumerate(pairs):
                spots.append((n, x, piece[0] + pair, pl.ds(piece[2], piece[3]), pl.ds(first, piece[3])))

    def far(ref, spot):
        other = me ^ spot[1]
        return ref.at[other // split, spot[2], other % split, spot[3]]

    def near(spot):
        return base_ref.at[spot[0], spot[4]]

    loads = [pltpu.make_async_copy(far(base_hbm, at), near(at), base_sems.at[n]) for n, at in enumerate(spots)]
    stores = [pltpu.make_async_copy(near(at), far(out_hbm, at), base_sems.at[n]) for n, at in enumerate(spots)]
    copies = [pltpu.make_async_copy(terms[n], term_ref.at[n], term_sems.at[n]) for n in range(count)]
    start_all(copies)
    start_all(loads)
    wait_all(copies)
    for load, store, at in zip(loads, stores, spots):
        load.wait()
        base_ref[at[0], at[4]] = base_ref[at[0], at[4]] + term_ref[at[0], at[4]]
        store.start()
    wait_all(stores)


def add_rest(base, terms, partners, spots, pieces):
    buffer = pltpu.VMEM((len(terms),) + terms[0].shape, jnp.float32)
    size = len(terms) * terms[0].size
    copies = len(terms) * sum(piece[1] for piece in pieces)
    return pl.pallas_call(
        functools.partial(add_rest_kernel, pieces, partners),
        out_shape=jax.ShapeDtypeStruct(base.shape, jnp.float32),
        in_specs=[SCALARS, HBM] + [HBM] * len(terms),
        out_specs=HBM,
        scratch_shapes=[
            buffer,
            buffer,
            pltpu.SemaphoreType.DMA((copies,)),
            pltpu.SemaphoreType.DMA((len(terms),)),
        ],
        input_output_aliases={1: 0},
        compiler_params=pltpu.CompilerParams(vmem_limit_bytes=24 << 20),
        cost_estimate=pl.CostEstimate(flops=size, bytes_accessed=12 * size, transcendentals=0),
        name="add_rest",
    )(spots, base, *terms)


def after(value, *others):
    return lax.optimization_barrier((value,) + others)[0]


def on_device(field, mean_flow, d2_coef, wall_coef, kx_index, patch_of):
    mode_count, comp_count, part_count, row_count, width = field.shape
    span = lax.axis_size("span")
    me = lax.axis_index("span")
    wall_count = lax.axis_size("wall")
    wall_index = lax.axis_index("wall")
    mode_split = math.gcd(span, mode_count)
    row_split = span // mode_split
    line_rows = row_count // row_split
    tables = jnp.asarray(spectral_tables(width * span))
    pairs = [[(i, i ^ x) for i in range(span)] for x in range(span)]
    spots = jnp.stack([me]).astype(jnp.int32)

    def exchange(lines):
        return lax.all_to_all(lines, "span", split_axis=0, concat_axis=0)

    def swap(blocks):
        return [lax.ppermute(blocks[x], "span", pairs[x]) for x in range(span - 1, 0, -1)][::-1]

    pairs_count, groups = comp_count * part_count, line_rows // PAD
    shares = (mode_split, pairs_count, row_split, groups, PAD, width)
    lines = field.reshape(shares).transpose(0, 2, 1, 3, 4, 5)
    lines = exchange(lines.reshape(span, pairs_count, groups, PAD, width))
    wall_groups = sorted({0, groups - 1})
    first_pieces = tuple((0, 2, group, 1) for group in wall_groups)
    rest_pieces = tuple((2 * comp, 2, 0, groups) for comp in range(1, comp_count))
    if groups > 2:
        rest_pieces = ((0, 2, 1, groups - 2),) + rest_pieces

    forward = [(i, i + 1) for i in range(wall_count - 1)]
    backward = [(i + 1, i) for i in range(wall_count - 1)]
    low = lax.ppermute(field[:, :, :, row_count - PAD :], "wall", forward)
    high = lax.ppermute(field[:, :, :, :PAD], "wall", backward)

    rate = kx_index.astype(jnp.float32) * (0.25 * TAU)
    coef = jnp.broadcast_to(d2_coef[:, :, None], (STEN, row_count, LANES))
    flow = jnp.broadcast_to(mean_flow[:, :, None], (2, row_count, LANES))
    base = local_terms(field, low, high, rate, coef, flow)

    lines = after(lines, base)
    filtered = filter_first(lines, tables, first_pieces)
    back = exchange(filtered)
    sent = filter_rest(after(lines, filtered), spots, tables, rest_pieces)
    returned = [sent[0]] + swap(sent)

    lower = jnp.where(wall_index == 0, wall_coef[0], 0.0)
    upper = jnp.where(wall_index == wall_count - 1, wall_coef[1, ::-1], 0.0)
    group = ((me ^ jnp.arange(span)) % row_split)[:, None]
    ends = [jnp.where(group == 0, lower, 0.0), jnp.where(group == row_split - 1, upper, 0.0)]
    weight = jnp.broadcast_to(jnp.stack(ends, axis=1)[..., None], (span, 2, PAD, LANES))
    result, shear = add_first(base.reshape(shares), back, weight, spots, first_pieces)
    onehot = (patch_of[:, None] == jnp.arange(PATCH, dtype=jnp.int32)[None, :]).astype(jnp.float32)
    grad = jnp.einsum("swz,zq->swq", shear, onehot, precision=lax.Precision.HIGHEST)
    grad = grad.reshape(mode_count, row_split, 2, part_count, PATCH).sum(axis=1)
    distance = 1
    while distance < wall_count:
        grad = grad + lax.ppermute(grad, "wall", [(i, i ^ distance) for i in range(wall_count)])
        distance *= 2
    parts = jnp.stack([grad] + swap([grad] * span))
    parts = [lax.dynamic_index_in_dim(parts, me ^ x, 0, keepdims=False) for x in range(span)]
    wall_grad = functools.reduce(jnp.add, parts).transpose(1, 0, 2, 3)

    cuts = [0, span // 2, 3 * span // 4, span]
    for low_cut, high_cut in zip(cuts, cuts[1:]):
        partners = range(low_cut, high_cut)
        result = add_rest(result, returned[low_cut:high_cut], partners, spots, rest_pieces)
    return (result.reshape(field.shape), wall_grad)


def solution(mesh):
    return jax.shard_map(
        on_device,
        mesh=mesh,
        in_specs=(
            P(None, None, None, "wall", "span"),
            P(None, "wall"),
            P(None, "wall"),
            P(),
            P(),
            P("span"),
        ),
        out_specs=(P(None, None, None, "wall", "span"), P()),
        check_vma=False,
    )
```

```python
import functools
import math

import jax
import jax.numpy as jnp
import numpy as np
from jax import lax
from jax.experimental import pallas as pl
from jax.experimental.pallas import tpu as pltpu
from jax.sharding import PartitionSpec as P

HALO = 7
STEN = 15
PATCH = 64
TAU = 0.25
VIS = 0.5

LANES = 128
OUTER = 48
PAD = 8
TILES = OUTER // 2
FILTER_VMEM = 57_500_000
TABLE_COPIES = 4

QUARTER = (0, 4, 2, 1, 5, 9)
KEPT = tuple(4 * q for q in QUARTER) + tuple(2 + 8 * t for t in range(6)) + tuple(4 * q + 1 for q in range(12))


@functools.cache
def spectral_tables(length):
    signed = np.arange(length)
    signed = np.where(signed > length // 2, signed - length, signed)
    cutoff = length // 3
    ratio = signed.astype(np.float64) / cutoff
    multiplier = np.where(np.abs(signed) < cutoff, -VIS * ratio * ratio, 0.0)
    shift = np.arange(LANES)[None, :] - np.arange(LANES)[:, None]
    inner = np.arange(LANES)

    def complex_table(k1):
        wave = k1 + OUTER * inner
        spots = np.arange(-LANES + 1, LANES)
        phase = np.exp(2j * np.pi * ((wave[:, None] * spots[None, :]) % length) / length)
        return ((multiplier[wave][:, None] * phase).sum(axis=0) / LANES)[shift + LANES - 1]

    tables = np.zeros((TILES, 2 * LANES, 2 * LANES))
    tables[0, :LANES, :LANES] = complex_table(0).real / OUTER
    tables[0, LANES:, LANES:] = complex_table(OUTER // 2).real / OUTER
    for tile, k1 in enumerate(KEPT[1:], 1):
        table = complex_table(k1) * 2.0 / OUTER
        tables[tile, :LANES, :LANES] = table.real
        tables[tile, :LANES, LANES:] = table.imag
        tables[tile, LANES:, :LANES] = -table.imag
        tables[tile, LANES:, LANES:] = table.real
    high = tables.astype(jnp.bfloat16)
    low = (tables - high.astype(np.float64)).astype(jnp.bfloat16)
    return np.stack([high, low], axis=1)


def turn(value, numerator, denominator):
    re, im = value
    numerator %= denominator
    if numerator == 0:
        return value
    if 2 * numerator == denominator:
        return (-re, -im)
    if 4 * numerator == denominator:
        return (-im, re)
    if 4 * numerator == 3 * denominator:
        return (im, -re)
    cos = math.cos(2 * math.pi * numerator / denominator)
    sin = math.sin(2 * math.pi * numerator / denominator)
    return (re * cos - im * sin, re * sin + im * cos)


def add(a, b):
    return (a[0] + b[0], a[1] + b[1])


def sub(a, b):
    return (a[0] - b[0], a[1] - b[1])


ROOT = math.sqrt(3.0) / 2.0


def dft3(x, sign):
    total = add(x[1], x[2])
    other = sub(x[1], x[2])
    middle = (x[0][0] - 0.5 * total[0], x[0][1] - 0.5 * total[1])
    side = (-sign * ROOT * other[1], sign * ROOT * other[0])
    return [add(x[0], total), add(middle, side), sub(middle, side)]


def dft6(x, sign):
    even = dft3([add(x[b], x[b + 3]) for b in range(3)], sign)
    odd = dft3([turn(sub(x[b], x[b + 3]), sign * b, 6) for b in range(3)], sign)
    return [even[0], odd[0], even[1], odd[1], even[2], odd[2]]


def dft12(x, sign):
    out = [None] * 12
    parts = [[], [], [], []]
    for b in range(3):
        a0, a1, a2, a3 = x[b], x[b + 3], x[b + 6], x[b + 9]
        s0, s1, d0, d1 = add(a0, a2), add(a1, a3), sub(a0, a2), turn(sub(a1, a3), sign, 4)
        for r, value in enumerate((add(s0, s1), add(d0, d1), sub(s0, s1), sub(d0, d1))):
            parts[r].append(turn(value, sign * b * r, 12))
    for r in range(4):
        for q, value in enumerate(dft3(parts[r], sign)):
            out[4 * q + r] = value
    return out


def real_forward(x):
    whole, halved, turned = [], [], []
    for b in range(12):
        s0, s1 = x[b] + x[b + 24], x[b + 12] + x[b + 36]
        whole.append(s0 + s1)
        halved.append(s0 - s1)
        turned.append(turn((x[b] - x[b + 24], x[b + 36] - x[b + 12]), -b, 48))
    w, h, t = [], [], []
    for b in range(3):
        s0, s1 = whole[b] + whole[b + 6], whole[b + 3] + whole[b + 9]
        w.append(s0 + s1)
        h.append(s0 - s1)
        t.append(turn((whole[b] - whole[b + 6], whole[b + 9] - whole[b + 3]), -b, 12))
    total, other = w[1] + w[2], w[1] - w[2]
    four = (w[0] - 0.5 * total, -ROOT * other)
    two = (h[0] + 0.5 * (h[1] - h[2]), -ROOT * (h[1] + h[2]))
    tiles = [(w[0] + total, h[0] - h[1] + h[2]), four, two] + dft3(t, -1)
    tiles += dft6([turn((halved[b], -halved[b + 6]), -b, 24) for b in range(6)], -1)
    return tiles + dft12(turned, -1)


def real_backward(tiles):
    (zero, half), four, two = tiles[:3]
    w0 = zero + four[0]
    rest, side = zero - 0.5 * four[0], ROOT * four[1]
    w = [w0, rest - side, rest + side]
    h_side = 0.5 * two[0] - ROOT * two[1]
    h = [two[0] + half, h_side - half, -0.5 * two[0] - ROOT * two[1] + half]
    t = [turn(value, b, 12) for b, value in enumerate(dft3(tiles[3:6], 1))]
    whole = [None] * 12
    for b in range(3):
        s, d = w[b] + h[b], w[b] - h[b]
        whole[b], whole[b + 6] = s + t[b][0], s - t[b][0]
        whole[b + 3], whole[b + 9] = d - t[b][1], d + t[b][1]
    halved = [None] * 12
    for b, value in enumerate(dft6(tiles[6:12], 1)):
        halved[b], halved[b + 6] = turn(value, b, 24)
        halved[b + 6] = -halved[b + 6]
    x = [None] * 48
    for b, value in enumerate(dft12(tiles[12:], 1)):
        re, im = turn(value, b, 48)
        s, d = whole[b] + halved[b], whole[b] - halved[b]
        x[b], x[b + 24] = s + re, s - re
        x[b + 12], x[b + 36] = d - im, d + im
    return x


def group_count(piece):
    return piece[1] * piece[3]


def line_copies(pieces, me_ref, field_hbm, received, line_refs, sems):
    count, split, me = len(received) + 1, field_hbm.shape[2], me_ref[0]
    copies = []
    for i, (piece, line_ref) in enumerate(zip(pieces, line_refs)):
        pairs, groups = pl.ds(piece[0], piece[1]), pl.ds(piece[2], piece[3])
        sources = [field_hbm.at[me // split, pairs, me % split, groups]]
        sources += [block.at[pairs, groups] for block in received]
        copies.append(
            [pltpu.make_async_copy(sources[x], line_ref.at[me ^ x], sems.at[i * count + x]) for x in range(count)]
        )
    return copies


def start_all(copies):
    for copy in copies:
        copy.start()
    return copies


def wait_all(copies):
    for copy in copies:
        copy.wait()


def run_filter(pieces, me_ref, table_hbm, field_hbm, received, send, scratch):
    *line_refs, wave_ref, table_ref, table_sems, sems = scratch
    copies = line_copies(pieces, me_ref, field_hbm, received, line_refs, sems)
    for piece_copies in copies:
        start_all(piece_copies)
    step = TILES // TABLE_COPIES
    spans = [pl.ds(i * step, step) for i in range(TABLE_COPIES)]
    table_copies = [
        pltpu.make_async_copy(table_hbm.at[span], table_ref.at[span], table_sems.at[i]) for i, span in enumerate(spans)
    ]
    start_all(table_copies)
    offsets = [sum(map(group_count, pieces[:i])) for i in range(len(pieces))]
    per_source = field_hbm.shape[5] // LANES

    def spot(number):
        return pl.ds(pl.multiple_of(number * PAD, PAD), PAD)

    for piece, line_ref, offset, copy in zip(pieces, line_refs, offsets, copies):
        wait_all(copy)

        def forward(number, _, groups=piece[3], line_ref=line_ref, offset=offset):
            pair, group = number // groups, number % groups
            values = []
            for n1 in range(OUTER):
                lanes = pl.ds(n1 % per_source * LANES, LANES)
                values.append(line_ref[n1 // per_source, pair, group, :, lanes])
            for tile, (re, im) in enumerate(real_forward(values)):
                wave_ref[tile, spot(offset + number), :LANES] = re
                wave_ref[tile, spot(offset + number), LANES:] = im
            return 0

        lax.fori_loop(0, group_count(piece), forward, 0)

    def middle(tile, _):
        value = wave_ref[tile]
        high = value.astype(jnp.bfloat16)
        low = (value - high.astype(jnp.float32)).astype(jnp.bfloat16)
        rows = high.shape[0]
        both = jnp.dot(jnp.concatenate([high, low]), table_ref[tile, 0], preferred_element_type=jnp.float32)
        rest = jnp.dot(high, table_ref[tile, 1], preferred_element_type=jnp.float32)
        wave_ref[tile] = both[:rows] + both[rows:] + rest
        return 0

    for i, copy in enumerate(table_copies):
        copy.wait()
        lax.fori_loop(i * step, (i + 1) * step, middle, 0, unroll=3)

    away = []
    for i, (piece, line_ref, offset) in enumerate(zip(pieces, line_refs, offsets)):

        def backward(number, _, groups=piece[3], line_ref=line_ref, offset=offset):
            pair, group = number // groups, number % groups
            row = spot(offset + number)
            tiles = [(wave_ref[tile, row, :LANES], wave_ref[tile, row, LANES:]) for tile in range(TILES)]
            for n1, value in enumerate(real_backward(tiles)):
                line_ref[n1 // per_source, pair, group, :, pl.ds(n1 % per_source * LANES, LANES)] = value
            return 0

        lax.fori_loop(0, group_count(piece), backward, 0)
        away += start_all(send(i, line_ref))
    wait_all(away)


def filter_first_kernel(pieces, count, me_ref, table_hbm, field_hbm, *refs):
    received, out_hbm, scratch, out_sems = refs[: count - 1], refs[count - 1], refs[count:-1], refs[-1]

    def send(i, line_ref):
        return [pltpu.make_async_copy(line_ref.at[:, :, 0], out_hbm.at[:, i], out_sems.at[i])]

    run_filter(pieces, me_ref, table_hbm, field_hbm, received, send, scratch)


def filter_rest_kernel(pieces, count, me_ref, table_hbm, field_hbm, *refs):
    me = me_ref[0]
    received, sent = refs[: count - 1], refs[count - 1 : 2 * count - 1]
    scratch, out_sems = refs[2 * count - 1 : -1], refs[-1]
    places = rest_places(pieces)

    def send(i, line_ref):
        copies = []
        for pair in range(pieces[i][1]):
            number, first = places[i][pair]
            target = pl.ds(first, pieces[i][3])
            for x in range(count):
                sem = out_sems.at[number * count + x]
                copies.append(pltpu.make_async_copy(line_ref.at[me ^ x, pair], sent[x].at[target], sem))
        return copies

    run_filter(pieces, me_ref, table_hbm, field_hbm, received, send, scratch)


def rest_places(pieces):
    places, number, first = [], 0, 0
    for piece in pieces:
        places.append([])
        for _ in range(piece[1]):
            places[-1].append((number, first))
            number, first = number + 1, first + piece[3]
    return places


HBM = pl.BlockSpec(memory_space=pltpu.HBM)
SCALARS = pl.BlockSpec(memory_space=pltpu.SMEM)
WHOLE = pl.BlockSpec(memory_space=pltpu.VMEM)


def filter_call(kernel, name, pieces, field, received, spots, tables, out_shape, out_sems):
    count, width = len(received) + 1, field.shape[5]
    rows = sum(map(group_count, pieces)) * PAD
    flops = 3 * 2 * TILES * rows * (2 * LANES) ** 2
    return pl.pallas_call(
        functools.partial(kernel, pieces, count),
        out_shape=out_shape,
        in_specs=[SCALARS] + [HBM] * (count + 1),
        out_specs=[HBM] * len(out_shape),
        scratch_shapes=[pltpu.VMEM((count, piece[1], piece[3], PAD, width), jnp.float32) for piece in pieces]
        + [
            pltpu.VMEM((TILES, rows, 2 * LANES), jnp.float32),
            pltpu.VMEM(tables.shape, tables.dtype),
            pltpu.SemaphoreType.DMA((TABLE_COPIES,)),
            pltpu.SemaphoreType.DMA((len(pieces) * count,)),
            pltpu.SemaphoreType.DMA((out_sems,)),
        ],
        compiler_params=pltpu.CompilerParams(vmem_limit_bytes=FILTER_VMEM),
        cost_estimate=pl.CostEstimate(flops=flops, bytes_accessed=8 * count * rows * width, transcendentals=0),
        name=name,
    )(spots, tables, field, *received)


def filter_first(field, received, spots, tables, pieces):
    count, width = len(received) + 1, field.shape[5]
    out_shape = [jax.ShapeDtypeStruct((count, len(pieces), 2, PAD, width), jnp.float32)]
    return filter_call(
        filter_first_kernel, "filter_first", pieces, field, received, spots, tables, out_shape, len(pieces)
    )[0]


def filter_rest(field, received, spots, tables, pieces):
    count, width = len(received) + 1, field.shape[5]
    shape = (sum(map(group_count, pieces)), PAD, width)
    out_shape = [jax.ShapeDtypeStruct(shape, jnp.float32)] * count
    sems = count * sum(piece[1] for piece in pieces)
    return filter_call(filter_rest_kernel, "filter_rest", pieces, field, received, spots, tables, out_shape, sems)


def local_kernel(rate_ref, coef_ref, flow_ref, field_ref, low_ref, high_ref, out_ref, pad_ref):
    _, comp_count, part_count, row_count, width = field_ref.shape
    pad_ref[:, :, :PAD] = low_ref[0]
    pad_ref[:, :, PAD : PAD + row_count] = field_ref[0]
    pad_ref[:, :, PAD + row_count :] = high_ref[0]
    rate = rate_ref[pl.program_id(0)]

    def column(step, _):
        lanes = pl.ds(pl.multiple_of(step * LANES, LANES), LANES)
        for top in range(0, row_count, PAD):
            rows = pl.ds(top, PAD)
            advect = rate * flow_ref[0, rows, :]
            shear = TAU * flow_ref[1, rows, :]
            centre = [[field_ref[0, c, p, rows, lanes] for p in range(2)] for c in range(comp_count)]
            for c in range(comp_count):
                for p in range(2):
                    total = centre[c][p]
                    total = total - advect * centre[c][1] if p == 0 else total + advect * centre[c][0]
                    if c == 1:
                        total = total - shear * centre[0][p]
                    for offset in range(STEN):
                        near = pad_ref[c, p, pl.ds(top + offset + PAD - HALO, PAD), lanes]
                        total = total + coef_ref[offset, rows, :] * near
                    out_ref[0, c, p, rows, lanes] = total
        return 0

    lax.fori_loop(0, width // LANES, column, 0)


def local_terms(field, low, high, rate, coef, flow):
    mode_count, comp_count, part_count, row_count, width = field.shape
    block = (1, comp_count, part_count, row_count, width)
    edge = (1, comp_count, part_count, PAD, width)

    def by_mode(m):
        return (m, 0, 0, 0, 0)

    return pl.pallas_call(
        local_kernel,
        grid=(mode_count,),
        out_shape=jax.ShapeDtypeStruct(field.shape, jnp.float32),
        in_specs=[
            SCALARS,
            pl.BlockSpec(coef.shape, lambda m: (0, 0, 0)),
            pl.BlockSpec(flow.shape, lambda m: (0, 0, 0)),
            pl.BlockSpec(block, by_mode),
            pl.BlockSpec(edge, by_mode),
            pl.BlockSpec(edge, by_mode),
        ],
        out_specs=pl.BlockSpec(block, by_mode),
        scratch_shapes=[pltpu.VMEM((comp_count, part_count, row_count + 2 * PAD, width), jnp.float32)],
        compiler_params=pltpu.CompilerParams(vmem_limit_bytes=24 << 20),
        cost_estimate=pl.CostEstimate(flops=40 * field.size, bytes_accessed=10 * field.size, transcendentals=0),
        name="local_terms",
    )(rate, coef, flow, field, low, high)


def add_first_kernel(pieces, me_ref, base_hbm, weight_ref, term_hbm, out_hbm, shear_ref, *scratch):
    base_ref, term_ref, base_sems, term_sems = scratch
    count, split, me = term_hbm.shape[0], base_hbm.shape[2], me_ref[0]

    def spot(ref, x, i):
        other = me ^ x
        return ref.at[other // split, pl.ds(0, 2), other % split, pieces[i][2]]

    spots = [(x, i) for x in range(count) for i in range(len(pieces))]
    sem = [base_sems.at[x * len(pieces) + i] for x, i in spots]
    loads = [pltpu.make_async_copy(spot(base_hbm, *at), base_ref.at[at], sem[n]) for n, at in enumerate(spots)]
    stores = [pltpu.make_async_copy(base_ref.at[at], spot(out_hbm, *at), sem[n]) for n, at in enumerate(spots)]
    terms = [pltpu.make_async_copy(term_hbm.at[me ^ x], term_ref.at[x], term_sems.at[x]) for x in range(count)]
    start_all(loads)
    start_all(terms)
    wait_all(terms)
    wait_all(loads)
    for x in range(count):
        base_ref[x] = base_ref[x] + term_ref[x]
        start_all(stores[x * len(pieces) : (x + 1) * len(pieces)])
        for p in range(2):
            shear_ref[me ^ x, p] = jnp.sum(base_ref[x, 0, p] * weight_ref[x, 0][:, :1], axis=0)
            shear_ref[me ^ x, 2 + p] = jnp.sum(base_ref[x, len(pieces) - 1, p] * weight_ref[x, 1][:, :1], axis=0)
    wait_all(stores)


def add_first(base, term, weight, spots, pieces):
    count, width = term.shape[0], term.shape[4]
    buffer = pltpu.VMEM(term.shape, jnp.float32)
    return pl.pallas_call(
        functools.partial(add_first_kernel, pieces),
        out_shape=(
            jax.ShapeDtypeStruct(base.shape, jnp.float32),
            jax.ShapeDtypeStruct((count, 4, width), jnp.float32),
        ),
        in_specs=[SCALARS, HBM, WHOLE, HBM],
        out_specs=(HBM, WHOLE),
        scratch_shapes=[
            buffer,
            buffer,
            pltpu.SemaphoreType.DMA((count * len(pieces),)),
            pltpu.SemaphoreType.DMA((count,)),
        ],
        input_output_aliases={1: 0},
        compiler_params=pltpu.CompilerParams(vmem_limit_bytes=24 << 20),
        cost_estimate=pl.CostEstimate(flops=term.size, bytes_accessed=12 * term.size, transcendentals=0),
        name="add_first",
    )(spots, base, weight, term)


def add_rest_kernel(pieces, partners, me_ref, base_hbm, *refs):
    count = len(partners)
    terms, out_hbm = refs[:count], refs[count]
    base_ref, term_ref, base_sems, term_sems = refs[count + 1 :]
    split, me = base_hbm.shape[2], me_ref[0]
    places = rest_places(pieces)
    spots = []
    for n, x in enumerate(partners):
        for piece, pairs in zip(pieces, places):
            for pair, (number, first) in enumerate(pairs):
                spots.append((n, x, piece[0] + pair, pl.ds(piece[2], piece[3]), pl.ds(first, piece[3])))

    def far(ref, spot):
        other = me ^ spot[1]
        return ref.at[other // split, spot[2], other % split, spot[3]]

    def near(spot):
        return base_ref.at[spot[0], spot[4]]

    loads = [pltpu.make_async_copy(far(base_hbm, at), near(at), base_sems.at[n]) for n, at in enumerate(spots)]
    stores = [pltpu.make_async_copy(near(at), far(out_hbm, at), base_sems.at[n]) for n, at in enumerate(spots)]
    copies = [pltpu.make_async_copy(terms[n], term_ref.at[n], term_sems.at[n]) for n in range(count)]
    start_all(copies)
    start_all(loads)
    wait_all(copies)
    for load, store, at in zip(loads, stores, spots):
        load.wait()
        base_ref[at[0], at[4]] = base_ref[at[0], at[4]] + term_ref[at[0], at[4]]
        store.start()
    wait_all(stores)


def add_rest(base, terms, partners, spots, pieces):
    buffer = pltpu.VMEM((len(terms),) + terms[0].shape, jnp.float32)
    size = len(terms) * terms[0].size
    copies = len(terms) * sum(piece[1] for piece in pieces)
    return pl.pallas_call(
        functools.partial(add_rest_kernel, pieces, partners),
        out_shape=jax.ShapeDtypeStruct(base.shape, jnp.float32),
        in_specs=[SCALARS, HBM] + [HBM] * len(terms),
        out_specs=HBM,
        scratch_shapes=[
            buffer,
            buffer,
            pltpu.SemaphoreType.DMA((copies,)),
            pltpu.SemaphoreType.DMA((len(terms),)),
        ],
        input_output_aliases={1: 0},
        compiler_params=pltpu.CompilerParams(vmem_limit_bytes=24 << 20),
        cost_estimate=pl.CostEstimate(flops=size, bytes_accessed=12 * size, transcendentals=0),
        name="add_rest",
    )(spots, base, *terms)


def after(value, *others):
    return lax.optimization_barrier((value,) + others)[0]


def on_device(field, mean_flow, d2_coef, wall_coef, kx_index, patch_of):
    mode_count, comp_count, part_count, row_count, width = field.shape
    span = lax.axis_size("span")
    me = lax.axis_index("span")
    wall_count = lax.axis_size("wall")
    wall_index = lax.axis_index("wall")
    mode_split = math.gcd(span, mode_count)
    row_split = span // mode_split
    line_rows = row_count // row_split
    tables = jnp.asarray(spectral_tables(width * span))
    pairs = [[(i, i ^ x) for i in range(span)] for x in range(span)]
    spots = jnp.stack([me]).astype(jnp.int32)

    def exchange(lines):
        return lax.all_to_all(lines, "span", split_axis=0, concat_axis=0)

    def swap(blocks):
        return [lax.ppermute(blocks[x], "span", pairs[x]) for x in range(span - 1, 0, -1)][::-1]

    pairs_count, groups = comp_count * part_count, line_rows // PAD
    shares = (mode_split, pairs_count, row_split, groups, PAD, width)
    shared = field.reshape(shares)
    blocks = [None] * span
    source = shared
    for x in range(span - 1, 0, -1):
        other = me ^ x
        start = (other // row_split, 0, other % row_split, 0, 0, 0)
        block = lax.dynamic_slice(source, start, (1, pairs_count, 1, groups, PAD, width))
        blocks[x] = block.reshape(pairs_count, groups, PAD, width)
        source = after(shared, blocks[x])
    received = swap(blocks)
    wall_groups = sorted({0, groups - 1})
    first_pieces = tuple((0, 2, group, 1) for group in wall_groups)
    rest_pieces = tuple((2 * comp, 2, 0, groups) for comp in range(1, comp_count))
    if groups > 2:
        rest_pieces = ((0, 2, 1, groups - 2),) + rest_pieces

    filtered = filter_first(shared, received, spots, tables, first_pieces)
    back = exchange(filtered)
    received[0] = after(received[0], filtered)
    sent = filter_rest(shared, received, spots, tables, rest_pieces)
    returned = [sent[0]] + swap(sent)

    forward = [(i, i + 1) for i in range(wall_count - 1)]
    backward = [(i + 1, i) for i in range(wall_count - 1)]
    late = after(field, back)
    low = lax.ppermute(late[:, :, :, row_count - PAD :], "wall", forward)
    high = lax.ppermute(late[:, :, :, :PAD], "wall", backward)

    rate = kx_index.astype(jnp.float32) * (0.25 * TAU)
    coef = jnp.broadcast_to(d2_coef[:, :, None], (STEN, row_count, LANES))
    flow = jnp.broadcast_to(mean_flow[:, :, None], (2, row_count, LANES))
    base = local_terms(field, low, high, rate, coef, flow)


    lower = jnp.where(wall_index == 0, wall_coef[0], 0.0)
    upper = jnp.where(wall_index == wall_count - 1, wall_coef[1, ::-1], 0.0)
    group = ((me ^ jnp.arange(span)) % row_split)[:, None]
    ends = [jnp.where(group == 0, lower, 0.0), jnp.where(group == row_split - 1, upper, 0.0)]
    weight = jnp.broadcast_to(jnp.stack(ends, axis=1)[..., None], (span, 2, PAD, LANES))
    result, shear = add_first(base.reshape(shares), back, weight, spots, first_pieces)
    onehot = (patch_of[:, None] == jnp.arange(PATCH, dtype=jnp.int32)[None, :]).astype(jnp.float32)
    grad = jnp.einsum("swz,zq->swq", shear, onehot, precision=lax.Precision.HIGHEST)
    grad = grad.reshape(mode_count, row_split, 2, part_count, PATCH).sum(axis=1)
    distance = 1
    while distance < wall_count:
        grad = grad + lax.ppermute(grad, "wall", [(i, i ^ distance) for i in range(wall_count)])
        distance *= 2
    parts = jnp.stack([grad] + swap([grad] * span))
    parts = [lax.dynamic_index_in_dim(parts, me ^ x, 0, keepdims=False) for x in range(span)]
    wall_grad = functools.reduce(jnp.add, parts).transpose(1, 0, 2, 3)

    cuts = [0, span // 2, 3 * span // 4, span]
    for low_cut, high_cut in zip(cuts, cuts[1:]):
        partners = range(low_cut, high_cut)
        result = add_rest(result, returned[low_cut:high_cut], partners, spots, rest_pieces)
    return (result.reshape(field.shape), wall_grad)


def solution(mesh):
    return jax.shard_map(
        on_device,
        mesh=mesh,
        in_specs=(
            P(None, None, None, "wall", "span"),
            P(None, "wall"),
            P(None, "wall"),
            P(),
            P(),
            P("span"),
        ),
        out_specs=(P(None, None, None, "wall", "span"), P()),
        check_vma=False,
    )
```

```python
import functools
import math

import jax
import jax.numpy as jnp
import numpy as np
from jax import lax
from jax.experimental import pallas as pl
from jax.experimental.pallas import tpu as pltpu
from jax.sharding import PartitionSpec as P

HALO = 7
STEN = 15
PATCH = 64
TAU = 0.25
VIS = 0.5

LANES = 128
OUTER = 48
PAD = 8
TILES = OUTER // 2
FILTER_VMEM = 57_500_000
TABLE_COPIES = 4

QUARTER = (0, 4, 2, 1, 5, 9)
KEPT = tuple(4 * q for q in QUARTER) + tuple(2 + 8 * t for t in range(6)) + tuple(4 * q + 1 for q in range(12))


@functools.cache
def spectral_tables(length):
    signed = np.arange(length)
    signed = np.where(signed > length // 2, signed - length, signed)
    cutoff = length // 3
    ratio = signed.astype(np.float64) / cutoff
    multiplier = np.where(np.abs(signed) < cutoff, -VIS * ratio * ratio, 0.0)
    shift = np.arange(LANES)[None, :] - np.arange(LANES)[:, None]
    inner = np.arange(LANES)

    def complex_table(k1):
        wave = k1 + OUTER * inner
        spots = np.arange(-LANES + 1, LANES)
        phase = np.exp(2j * np.pi * ((wave[:, None] * spots[None, :]) % length) / length)
        return ((multiplier[wave][:, None] * phase).sum(axis=0) / LANES)[shift + LANES - 1]

    tables = np.zeros((TILES, 2 * LANES, 2 * LANES))
    tables[0, :LANES, :LANES] = complex_table(0).real / OUTER
    tables[0, LANES:, LANES:] = complex_table(OUTER // 2).real / OUTER
    for tile, k1 in enumerate(KEPT[1:], 1):
        table = complex_table(k1) * 2.0 / OUTER
        tables[tile, :LANES, :LANES] = table.real
        tables[tile, :LANES, LANES:] = table.imag
        tables[tile, LANES:, :LANES] = -table.imag
        tables[tile, LANES:, LANES:] = table.real
    high = tables.astype(jnp.bfloat16)
    low = (tables - high.astype(np.float64)).astype(jnp.bfloat16)
    return np.stack([high, low], axis=1)


def turn(value, numerator, denominator):
    re, im = value
    numerator %= denominator
    if numerator == 0:
        return value
    if 2 * numerator == denominator:
        return (-re, -im)
    if 4 * numerator == denominator:
        return (-im, re)
    if 4 * numerator == 3 * denominator:
        return (im, -re)
    cos = math.cos(2 * math.pi * numerator / denominator)
    sin = math.sin(2 * math.pi * numerator / denominator)
    return (re * cos - im * sin, re * sin + im * cos)


def add(a, b):
    return (a[0] + b[0], a[1] + b[1])


def sub(a, b):
    return (a[0] - b[0], a[1] - b[1])


ROOT = math.sqrt(3.0) / 2.0


def dft3(x, sign):
    total = add(x[1], x[2])
    other = sub(x[1], x[2])
    middle = (x[0][0] - 0.5 * total[0], x[0][1] - 0.5 * total[1])
    side = (-sign * ROOT * other[1], sign * ROOT * other[0])
    return [add(x[0], total), add(middle, side), sub(middle, side)]


def dft6(x, sign):
    even = dft3([add(x[b], x[b + 3]) for b in range(3)], sign)
    odd = dft3([turn(sub(x[b], x[b + 3]), sign * b, 6) for b in range(3)], sign)
    return [even[0], odd[0], even[1], odd[1], even[2], odd[2]]


def dft12(x, sign):
    out = [None] * 12
    parts = [[], [], [], []]
    for b in range(3):
        a0, a1, a2, a3 = x[b], x[b + 3], x[b + 6], x[b + 9]
        s0, s1, d0, d1 = add(a0, a2), add(a1, a3), sub(a0, a2), turn(sub(a1, a3), sign, 4)
        for r, value in enumerate((add(s0, s1), add(d0, d1), sub(s0, s1), sub(d0, d1))):
            parts[r].append(turn(value, sign * b * r, 12))
    for r in range(4):
        for q, value in enumerate(dft3(parts[r], sign)):
            out[4 * q + r] = value
    return out


def real_forward(x):
    whole, halved, turned = [], [], []
    for b in range(12):
        s0, s1 = x[b] + x[b + 24], x[b + 12] + x[b + 36]
        whole.append(s0 + s1)
        halved.append(s0 - s1)
        turned.append(turn((x[b] - x[b + 24], x[b + 36] - x[b + 12]), -b, 48))
    w, h, t = [], [], []
    for b in range(3):
        s0, s1 = whole[b] + whole[b + 6], whole[b + 3] + whole[b + 9]
        w.append(s0 + s1)
        h.append(s0 - s1)
        t.append(turn((whole[b] - whole[b + 6], whole[b + 9] - whole[b + 3]), -b, 12))
    total, other = w[1] + w[2], w[1] - w[2]
    four = (w[0] - 0.5 * total, -ROOT * other)
    two = (h[0] + 0.5 * (h[1] - h[2]), -ROOT * (h[1] + h[2]))
    tiles = [(w[0] + total, h[0] - h[1] + h[2]), four, two] + dft3(t, -1)
    tiles += dft6([turn((halved[b], -halved[b + 6]), -b, 24) for b in range(6)], -1)
    return tiles + dft12(turned, -1)


def real_backward(tiles):
    (zero, half), four, two = tiles[:3]
    w0 = zero + four[0]
    rest, side = zero - 0.5 * four[0], ROOT * four[1]
    w = [w0, rest - side, rest + side]
    h_side = 0.5 * two[0] - ROOT * two[1]
    h = [two[0] + half, h_side - half, -0.5 * two[0] - ROOT * two[1] + half]
    t = [turn(value, b, 12) for b, value in enumerate(dft3(tiles[3:6], 1))]
    whole = [None] * 12
    for b in range(3):
        s, d = w[b] + h[b], w[b] - h[b]
        whole[b], whole[b + 6] = s + t[b][0], s - t[b][0]
        whole[b + 3], whole[b + 9] = d - t[b][1], d + t[b][1]
    halved = [None] * 12
    for b, value in enumerate(dft6(tiles[6:12], 1)):
        halved[b], halved[b + 6] = turn(value, b, 24)
        halved[b + 6] = -halved[b + 6]
    x = [None] * 48
    for b, value in enumerate(dft12(tiles[12:], 1)):
        re, im = turn(value, b, 48)
        s, d = whole[b] + halved[b], whole[b] - halved[b]
        x[b], x[b + 24] = s + re, s - re
        x[b + 12], x[b + 36] = d - im, d + im
    return x


def group_count(piece):
    return piece[1] * piece[3]


def piece_at(ref, piece):
    return ref.at[:, pl.ds(piece[0], piece[1]), pl.ds(piece[2], piece[3])]


def start_all(copies):
    for copy in copies:
        copy.start()
    return copies


def wait_all(copies):
    for copy in copies:
        copy.wait()


def run_filter(pieces, table_hbm, bring, send, scratch):
    *line_refs, wave_ref, table_ref, table_sems, sems = scratch
    copies = [start_all(bring(i, line_ref, sems)) for i, line_ref in enumerate(line_refs)]
    step = TILES // TABLE_COPIES
    spans = [pl.ds(i * step, step) for i in range(TABLE_COPIES)]
    table_copies = [
        pltpu.make_async_copy(table_hbm.at[span], table_ref.at[span], table_sems.at[i]) for i, span in enumerate(spans)
    ]
    start_all(table_copies)
    offsets = [sum(map(group_count, pieces[:i])) for i in range(len(pieces))]
    per_source = line_refs[0].shape[4] // LANES

    def spot(number):
        return pl.ds(pl.multiple_of(number * PAD, PAD), PAD)

    for piece, line_ref, offset, copy in zip(pieces, line_refs, offsets, copies):
        wait_all(copy)

        def forward(number, _, groups=piece[3], line_ref=line_ref, offset=offset):
            pair, group = number // groups, number % groups
            values = []
            for n1 in range(OUTER):
                lanes = pl.ds(n1 % per_source * LANES, LANES)
                values.append(line_ref[n1 // per_source, pair, group, :, lanes])
            for tile, (re, im) in enumerate(real_forward(values)):
                wave_ref[tile, spot(offset + number), :LANES] = re
                wave_ref[tile, spot(offset + number), LANES:] = im
            return 0

        lax.fori_loop(0, group_count(piece), forward, 0)

    def middle(tile, _):
        value = wave_ref[tile]
        high = value.astype(jnp.bfloat16)
        low = (value - high.astype(jnp.float32)).astype(jnp.bfloat16)
        rows = high.shape[0]
        both = jnp.dot(jnp.concatenate([high, low]), table_ref[tile, 0], preferred_element_type=jnp.float32)
        rest = jnp.dot(high, table_ref[tile, 1], preferred_element_type=jnp.float32)
        wave_ref[tile] = both[:rows] + both[rows:] + rest
        return 0

    for i, copy in enumerate(table_copies):
        copy.wait()
        lax.fori_loop(i * step, (i + 1) * step, middle, 0, unroll=3)

    away = []
    for i, (piece, line_ref, offset) in enumerate(zip(pieces, line_refs, offsets)):

        def backward(number, _, groups=piece[3], line_ref=line_ref, offset=offset):
            pair, group = number // groups, number % groups
            row = spot(offset + number)
            tiles = [(wave_ref[tile, row, :LANES], wave_ref[tile, row, LANES:]) for tile in range(TILES)]
            for n1, value in enumerate(real_backward(tiles)):
                line_ref[n1 // per_source, pair, group, :, pl.ds(n1 % per_source * LANES, LANES)] = value
            return 0

        lax.fori_loop(0, group_count(piece), backward, 0)
        away += start_all(send(i, line_ref))
    wait_all(away)


def filter_first_kernel(pieces, table_hbm, lines_hbm, out_hbm, *scratch):
    *scratch, out_sems = scratch

    def bring(i, line_ref, sems):
        return [pltpu.make_async_copy(piece_at(lines_hbm, pieces[i]), line_ref, sems.at[i])]

    def send(i, line_ref):
        return [pltpu.make_async_copy(line_ref.at[:, :, 0], out_hbm.at[:, i], out_sems.at[i])]

    run_filter(pieces, table_hbm, bring, send, scratch)


def filter_rest_kernel(pieces, me_ref, table_hbm, lines_hbm, field_hbm, *refs):
    count, split, me = lines_hbm.shape[0], field_hbm.shape[2], me_ref[0]
    received, sent, scratch, out_sems = refs[: count - 1], refs[count - 1 : 2 * count - 1], refs[2 * count - 1 : -1], refs[-1]
    places = rest_places(pieces)
    final = len(pieces) - 1

    def bring(i, line_ref, sems):
        if i < final:
            return [pltpu.make_async_copy(piece_at(lines_hbm, pieces[i]), line_ref, sems.at[i])]
        own = field_hbm.at[me // split, pl.ds(pieces[i][0], pieces[i][1]), me % split]
        sources = (own,) + received
        return [pltpu.make_async_copy(sources[x], line_ref.at[me ^ x], sems.at[i + x]) for x in range(count)]

    def send(i, line_ref):
        copies = []
        for pair in range(pieces[i][1]):
            number, first = places[i][pair]
            target = pl.ds(first, pieces[i][3])
            for x in range(count):
                sem = out_sems.at[number * count + x]
                copies.append(pltpu.make_async_copy(line_ref.at[me ^ x, pair], sent[x].at[target], sem))
        return copies

    run_filter(pieces, table_hbm, bring, send, scratch)


def rest_places(pieces):
    places, number, first = [], 0, 0
    for piece in pieces:
        places.append([])
        for _ in range(piece[1]):
            places[-1].append((number, first))
            number, first = number + 1, first + piece[3]
    return places


HBM = pl.BlockSpec(memory_space=pltpu.HBM)
SCALARS = pl.BlockSpec(memory_space=pltpu.SMEM)
WHOLE = pl.BlockSpec(memory_space=pltpu.VMEM)


def filter_call(kernel, name, pieces, lines, tables, in_specs, out_specs, out_shape, sems, flops):
    count, _, _, _, width = lines.shape
    rows = sum(map(group_count, pieces)) * PAD
    return pl.pallas_call(
        functools.partial(kernel, pieces),
        out_shape=out_shape,
        in_specs=in_specs,
        out_specs=out_specs,
        scratch_shapes=[pltpu.VMEM((count, piece[1], piece[3], PAD, width), jnp.float32) for piece in pieces]
        + [
            pltpu.VMEM((TILES, rows, 2 * LANES), jnp.float32),
            pltpu.VMEM(tables.shape, tables.dtype),
            pltpu.SemaphoreType.DMA((TABLE_COPIES,)),
            pltpu.SemaphoreType.DMA((sems[0],)),
            pltpu.SemaphoreType.DMA((sems[1],)),
        ],
        compiler_params=pltpu.CompilerParams(vmem_limit_bytes=FILTER_VMEM),
        cost_estimate=pl.CostEstimate(flops=flops, bytes_accessed=0, transcendentals=0),
        name=name,
    )


def filter_first(lines, tables, pieces):
    count, _, _, _, width = lines.shape
    out_shape = jax.ShapeDtypeStruct((count, len(pieces), 2, PAD, width), jnp.float32)
    sems = (len(pieces), len(pieces))
    call = filter_call(
        filter_first_kernel, "filter_first", pieces, lines, tables, [HBM, HBM], HBM, out_shape, sems, 10**6
    )
    return call(tables, lines)


def filter_rest(lines, field, received, spots, tables, pieces):
    count, _, _, _, width = lines.shape
    shape = (sum(map(group_count, pieces)), PAD, width)
    out_shape = [jax.ShapeDtypeStruct(shape, jnp.float32)] * count
    sems = (len(pieces) - 1 + count, count * sum(piece[1] for piece in pieces))
    ins = [SCALARS] + [HBM] * (count + 2)
    call = filter_call(
        filter_rest_kernel, "filter_rest", pieces, lines, tables, ins, [HBM] * count, out_shape, sems, 10**11
    )
    return call(spots, tables, lines, field, *received)


def local_kernel(rate_ref, coef_ref, flow_ref, field_ref, low_ref, high_ref, out_ref, pad_ref):
    _, comp_count, part_count, row_count, width = field_ref.shape
    pad_ref[:, :, :PAD] = low_ref[0]
    pad_ref[:, :, PAD : PAD + row_count] = field_ref[0]
    pad_ref[:, :, PAD + row_count :] = high_ref[0]
    rate = rate_ref[pl.program_id(0)]

    def column(step, _):
        lanes = pl.ds(pl.multiple_of(step * LANES, LANES), LANES)
        for top in range(0, row_count, PAD):
            rows = pl.ds(top, PAD)
            advect = rate * flow_ref[0, rows, :]
            shear = TAU * flow_ref[1, rows, :]
            centre = [[field_ref[0, c, p, rows, lanes] for p in range(2)] for c in range(comp_count)]
            for c in range(comp_count):
                for p in range(2):
                    total = centre[c][p]
                    total = total - advect * centre[c][1] if p == 0 else total + advect * centre[c][0]
                    if c == 1:
                        total = total - shear * centre[0][p]
                    for offset in range(STEN):
                        near = pad_ref[c, p, pl.ds(top + offset + PAD - HALO, PAD), lanes]
                        total = total + coef_ref[offset, rows, :] * near
                    out_ref[0, c, p, rows, lanes] = total
        return 0

    lax.fori_loop(0, width // LANES, column, 0)


def local_terms(field, low, high, rate, coef, flow):
    mode_count, comp_count, part_count, row_count, width = field.shape
    block = (1, comp_count, part_count, row_count, width)
    edge = (1, comp_count, part_count, PAD, width)

    def by_mode(m):
        return (m, 0, 0, 0, 0)

    return pl.pallas_call(
        local_kernel,
        grid=(mode_count,),
        out_shape=jax.ShapeDtypeStruct(field.shape, jnp.float32),
        in_specs=[
            SCALARS,
            pl.BlockSpec(coef.shape, lambda m: (0, 0, 0)),
            pl.BlockSpec(flow.shape, lambda m: (0, 0, 0)),
            pl.BlockSpec(block, by_mode),
            pl.BlockSpec(edge, by_mode),
            pl.BlockSpec(edge, by_mode),
        ],
        out_specs=pl.BlockSpec(block, by_mode),
        scratch_shapes=[pltpu.VMEM((comp_count, part_count, row_count + 2 * PAD, width), jnp.float32)],
        compiler_params=pltpu.CompilerParams(vmem_limit_bytes=24 << 20),
        cost_estimate=pl.CostEstimate(flops=40 * field.size, bytes_accessed=10 * field.size, transcendentals=0),
        name="local_terms",
    )(rate, coef, flow, field, low, high)


def add_first_kernel(pieces, me_ref, base_hbm, weight_ref, term_hbm, out_hbm, shear_ref, *scratch):
    base_ref, term_ref, base_sems, term_sems = scratch
    count, split, me = term_hbm.shape[0], base_hbm.shape[2], me_ref[0]

    def spot(ref, x, i):
        other = me ^ x
        return ref.at[other // split, pl.ds(0, 2), other % split, pieces[i][2]]

    spots = [(x, i) for x in range(count) for i in range(len(pieces))]
    sem = [base_sems.at[x * len(pieces) + i] for x, i in spots]
    loads = [pltpu.make_async_copy(spot(base_hbm, *at), base_ref.at[at], sem[n]) for n, at in enumerate(spots)]
    stores = [pltpu.make_async_copy(base_ref.at[at], spot(out_hbm, *at), sem[n]) for n, at in enumerate(spots)]
    terms = [pltpu.make_async_copy(term_hbm.at[me ^ x], term_ref.at[x], term_sems.at[x]) for x in range(count)]
    start_all(loads)
    start_all(terms)
    wait_all(terms)
    wait_all(loads)
    for x in range(count):
        base_ref[x] = base_ref[x] + term_ref[x]
        start_all(stores[x * len(pieces) : (x + 1) * len(pieces)])
        for p in range(2):
            shear_ref[me ^ x, p] = jnp.sum(base_ref[x, 0, p] * weight_ref[x, 0][:, :1], axis=0)
            shear_ref[me ^ x, 2 + p] = jnp.sum(base_ref[x, len(pieces) - 1, p] * weight_ref[x, 1][:, :1], axis=0)
    wait_all(stores)


def add_first(base, term, weight, spots, pieces):
    count, width = term.shape[0], term.shape[4]
    buffer = pltpu.VMEM(term.shape, jnp.float32)
    return pl.pallas_call(
        functools.partial(add_first_kernel, pieces),
        out_shape=(
            jax.ShapeDtypeStruct(base.shape, jnp.float32),
            jax.ShapeDtypeStruct((count, 4, width), jnp.float32),
        ),
        in_specs=[SCALARS, HBM, WHOLE, HBM],
        out_specs=(HBM, WHOLE),
        scratch_shapes=[
            buffer,
            buffer,
            pltpu.SemaphoreType.DMA((count * len(pieces),)),
            pltpu.SemaphoreType.DMA((count,)),
        ],
        input_output_aliases={1: 0},
        compiler_params=pltpu.CompilerParams(vmem_limit_bytes=24 << 20),
        cost_estimate=pl.CostEstimate(flops=term.size, bytes_accessed=12 * term.size, transcendentals=0),
        name="add_first",
    )(spots, base, weight, term)


def add_rest_kernel(pieces, partners, me_ref, base_hbm, *refs):
    count = len(partners)
    terms, out_hbm = refs[:count], refs[count]
    base_ref, term_ref, base_sems, term_sems = refs[count + 1 :]
    split, me = base_hbm.shape[2], me_ref[0]
    places = rest_places(pieces)
    spots = []
    for n, x in enumerate(partners):
        for piece, pairs in zip(pieces, places):
            for pair, (number, first) in enumerate(pairs):
                spots.append((n, x, piece[0] + pair, pl.ds(piece[2], piece[3]), pl.ds(first, piece[3])))

    def far(ref, spot):
        other = me ^ spot[1]
        return ref.at[other // split, spot[2], other % split, spot[3]]

    def near(spot):
        return base_ref.at[spot[0], spot[4]]

    loads = [pltpu.make_async_copy(far(base_hbm, at), near(at), base_sems.at[n]) for n, at in enumerate(spots)]
    stores = [pltpu.make_async_copy(near(at), far(out_hbm, at), base_sems.at[n]) for n, at in enumerate(spots)]
    copies = [pltpu.make_async_copy(terms[n], term_ref.at[n], term_sems.at[n]) for n in range(count)]
    start_all(copies)
    start_all(loads)
    wait_all(copies)
    for load, store, at in zip(loads, stores, spots):
        load.wait()
        base_ref[at[0], at[4]] = base_ref[at[0], at[4]] + term_ref[at[0], at[4]]
        store.start()
    wait_all(stores)


def add_rest(base, terms, partners, spots, pieces):
    buffer = pltpu.VMEM((len(terms),) + terms[0].shape, jnp.float32)
    size = len(terms) * terms[0].size
    copies = len(terms) * sum(piece[1] for piece in pieces)
    return pl.pallas_call(
        functools.partial(add_rest_kernel, pieces, partners),
        out_shape=jax.ShapeDtypeStruct(base.shape, jnp.float32),
        in_specs=[SCALARS, HBM] + [HBM] * len(terms),
        out_specs=HBM,
        scratch_shapes=[
            buffer,
            buffer,
            pltpu.SemaphoreType.DMA((copies,)),
            pltpu.SemaphoreType.DMA((len(terms),)),
        ],
        input_output_aliases={1: 0},
        compiler_params=pltpu.CompilerParams(vmem_limit_bytes=24 << 20),
        cost_estimate=pl.CostEstimate(flops=size, bytes_accessed=12 * size, transcendentals=0),
        name="add_rest",
    )(spots, base, *terms)


def after(value, *others):
    return lax.optimization_barrier((value,) + others)[0]


def on_device(field, mean_flow, d2_coef, wall_coef, kx_index, patch_of):
    mode_count, comp_count, part_count, row_count, width = field.shape
    span = lax.axis_size("span")
    me = lax.axis_index("span")
    wall_count = lax.axis_size("wall")
    wall_index = lax.axis_index("wall")
    mode_split = math.gcd(span, mode_count)
    row_split = span // mode_split
    line_rows = row_count // row_split
    tables = jnp.asarray(spectral_tables(width * span))
    pairs = [[(i, i ^ x) for i in range(span)] for x in range(span)]
    spots = jnp.stack([me]).astype(jnp.int32)

    def exchange(lines):
        return lax.all_to_all(lines, "span", split_axis=0, concat_axis=0)

    def swap(blocks):
        return [lax.ppermute(blocks[x], "span", pairs[x]) for x in range(span - 1, 0, -1)][::-1]

    pairs_count, groups = comp_count * part_count, line_rows // PAD
    shares = (mode_split, pairs_count, row_split, groups, PAD, width)
    shared = field.reshape(shares)
    last = pairs_count - part_count
    lines = exchange(shared[:, :last].transpose(0, 2, 1, 3, 4, 5).reshape(span, last, groups, PAD, width))

    wall_groups = sorted({0, groups - 1})
    first_pieces = tuple((0, 2, group, 1) for group in wall_groups)
    rest_pieces = tuple((2 * comp, 2, 0, groups) for comp in range(1, comp_count))
    if groups > 2:
        rest_pieces = ((0, 2, 1, groups - 2),) + rest_pieces

    forward = [(i, i + 1) for i in range(wall_count - 1)]
    backward = [(i + 1, i) for i in range(wall_count - 1)]
    low = lax.ppermute(field[:, :, :, row_count - PAD :], "wall", forward)
    high = lax.ppermute(field[:, :, :, :PAD], "wall", backward)

    rate = kx_index.astype(jnp.float32) * (0.25 * TAU)
    coef = jnp.broadcast_to(d2_coef[:, :, None], (STEN, row_count, LANES))
    flow = jnp.broadcast_to(mean_flow[:, :, None], (2, row_count, LANES))
    base = local_terms(field, low, high, rate, coef, flow)

    def last_block(x):
        other = me ^ x
        start = (other // row_split, last, other % row_split, 0, 0, 0)
        block = lax.dynamic_slice(shared, start, (1, part_count, 1, groups, PAD, width))
        return block.reshape(part_count, groups, PAD, width)

    blocks = tuple(last_block(x) for x in range(1, span))
    received = swap((None,) + lax.optimization_barrier((blocks, base))[0])
    lines = after(lines, base)
    filtered = filter_first(lines, tables, first_pieces)
    back = exchange(filtered)
    received[0] = after(received[0], filtered)
    sent = filter_rest(lines, shared, received, spots, tables, rest_pieces)
    returned = [sent[0]] + swap(sent)

    lower = jnp.where(wall_index == 0, wall_coef[0], 0.0)
    upper = jnp.where(wall_index == wall_count - 1, wall_coef[1, ::-1], 0.0)
    group = ((me ^ jnp.arange(span)) % row_split)[:, None]
    ends = [jnp.where(group == 0, lower, 0.0), jnp.where(group == row_split - 1, upper, 0.0)]
    weight = jnp.broadcast_to(jnp.stack(ends, axis=1)[..., None], (span, 2, PAD, LANES))
    result, shear = add_first(base.reshape(shares), back, weight, spots, first_pieces)
    onehot = (patch_of[:, None] == jnp.arange(PATCH, dtype=jnp.int32)[None, :]).astype(jnp.float32)
    grad = jnp.einsum("swz,zq->swq", shear, onehot, precision=lax.Precision.HIGHEST)
    grad = grad.reshape(mode_count, row_split, 2, part_count, PATCH).sum(axis=1)
    distance = 1
    while distance < wall_count:
        grad = grad + lax.ppermute(grad, "wall", [(i, i ^ distance) for i in range(wall_count)])
        distance *= 2
    parts = jnp.stack([grad] + swap([grad] * span))
    parts = [lax.dynamic_index_in_dim(parts, me ^ x, 0, keepdims=False) for x in range(span)]
    wall_grad = functools.reduce(jnp.add, parts).transpose(1, 0, 2, 3)

    cuts = [0, span // 2, 3 * span // 4, span]
    for low_cut, high_cut in zip(cuts, cuts[1:]):
        partners = range(low_cut, high_cut)
        result = add_rest(result, returned[low_cut:high_cut], partners, spots, rest_pieces)
    return (result.reshape(field.shape), wall_grad)


def solution(mesh):
    return jax.shard_map(
        on_device,
        mesh=mesh,
        in_specs=(
            P(None, None, None, "wall", "span"),
            P(None, "wall"),
            P(None, "wall"),
            P(),
            P(),
            P("span"),
        ),
        out_specs=(P(None, None, None, "wall", "span"), P()),
        check_vma=False,
    )
```

```python
import functools
import math

import jax
import jax.numpy as jnp
import numpy as np
from jax import lax
from jax.experimental import pallas as pl
from jax.experimental.pallas import tpu as pltpu
from jax.sharding import PartitionSpec as P

HALO = 7
STEN = 15
PATCH = 64
TAU = 0.25
VIS = 0.5

LANES = 128
OUTER = 48
PAD = 8
TILES = OUTER // 2
FILTER_VMEM = 57_500_000
TABLE_COPIES = 4

QUARTER = (0, 4, 2, 1, 5, 9)
KEPT = tuple(4 * q for q in QUARTER) + tuple(2 + 8 * t for t in range(6)) + tuple(4 * q + 1 for q in range(12))


@functools.cache
def spectral_tables(length):
    signed = np.arange(length)
    signed = np.where(signed > length // 2, signed - length, signed)
    cutoff = length // 3
    ratio = signed.astype(np.float64) / cutoff
    multiplier = np.where(np.abs(signed) < cutoff, -VIS * ratio * ratio, 0.0)
    shift = np.arange(LANES)[None, :] - np.arange(LANES)[:, None]
    inner = np.arange(LANES)

    def complex_table(k1):
        wave = k1 + OUTER * inner
        spots = np.arange(-LANES + 1, LANES)
        phase = np.exp(2j * np.pi * ((wave[:, None] * spots[None, :]) % length) / length)
        return ((multiplier[wave][:, None] * phase).sum(axis=0) / LANES)[shift + LANES - 1]

    tables = np.zeros((TILES, 2 * LANES, 2 * LANES))
    tables[0, :LANES, :LANES] = complex_table(0).real / OUTER
    tables[0, LANES:, LANES:] = complex_table(OUTER // 2).real / OUTER
    for tile, k1 in enumerate(KEPT[1:], 1):
        table = complex_table(k1) * 2.0 / OUTER
        tables[tile, :LANES, :LANES] = table.real
        tables[tile, :LANES, LANES:] = table.imag
        tables[tile, LANES:, :LANES] = -table.imag
        tables[tile, LANES:, LANES:] = table.real
    high = tables.astype(jnp.bfloat16)
    low = (tables - high.astype(np.float64)).astype(jnp.bfloat16)
    return np.stack([high, low], axis=1)


def turn(value, numerator, denominator):
    re, im = value
    numerator %= denominator
    if numerator == 0:
        return value
    if 2 * numerator == denominator:
        return (-re, -im)
    if 4 * numerator == denominator:
        return (-im, re)
    if 4 * numerator == 3 * denominator:
        return (im, -re)
    cos = math.cos(2 * math.pi * numerator / denominator)
    sin = math.sin(2 * math.pi * numerator / denominator)
    return (re * cos - im * sin, re * sin + im * cos)


def add(a, b):
    return (a[0] + b[0], a[1] + b[1])


def sub(a, b):
    return (a[0] - b[0], a[1] - b[1])


ROOT = math.sqrt(3.0) / 2.0


def dft3(x, sign):
    total = add(x[1], x[2])
    other = sub(x[1], x[2])
    middle = (x[0][0] - 0.5 * total[0], x[0][1] - 0.5 * total[1])
    side = (-sign * ROOT * other[1], sign * ROOT * other[0])
    return [add(x[0], total), add(middle, side), sub(middle, side)]


def dft6(x, sign):
    even = dft3([add(x[b], x[b + 3]) for b in range(3)], sign)
    odd = dft3([turn(sub(x[b], x[b + 3]), sign * b, 6) for b in range(3)], sign)
    return [even[0], odd[0], even[1], odd[1], even[2], odd[2]]


def dft12(x, sign):
    out = [None] * 12
    parts = [[], [], [], []]
    for b in range(3):
        a0, a1, a2, a3 = x[b], x[b + 3], x[b + 6], x[b + 9]
        s0, s1, d0, d1 = add(a0, a2), add(a1, a3), sub(a0, a2), turn(sub(a1, a3), sign, 4)
        for r, value in enumerate((add(s0, s1), add(d0, d1), sub(s0, s1), sub(d0, d1))):
            parts[r].append(turn(value, sign * b * r, 12))
    for r in range(4):
        for q, value in enumerate(dft3(parts[r], sign)):
            out[4 * q + r] = value
    return out


def real_forward(x):
    whole, halved, turned = [], [], []
    for b in range(12):
        s0, s1 = x[b] + x[b + 24], x[b + 12] + x[b + 36]
        whole.append(s0 + s1)
        halved.append(s0 - s1)
        turned.append(turn((x[b] - x[b + 24], x[b + 36] - x[b + 12]), -b, 48))
    w, h, t = [], [], []
    for b in range(3):
        s0, s1 = whole[b] + whole[b + 6], whole[b + 3] + whole[b + 9]
        w.append(s0 + s1)
        h.append(s0 - s1)
        t.append(turn((whole[b] - whole[b + 6], whole[b + 9] - whole[b + 3]), -b, 12))
    total, other = w[1] + w[2], w[1] - w[2]
    four = (w[0] - 0.5 * total, -ROOT * other)
    two = (h[0] + 0.5 * (h[1] - h[2]), -ROOT * (h[1] + h[2]))
    tiles = [(w[0] + total, h[0] - h[1] + h[2]), four, two] + dft3(t, -1)
    tiles += dft6([turn((halved[b], -halved[b + 6]), -b, 24) for b in range(6)], -1)
    return tiles + dft12(turned, -1)


def real_backward(tiles):
    (zero, half), four, two = tiles[:3]
    w0 = zero + four[0]
    rest, side = zero - 0.5 * four[0], ROOT * four[1]
    w = [w0, rest - side, rest + side]
    h_side = 0.5 * two[0] - ROOT * two[1]
    h = [two[0] + half, h_side - half, -0.5 * two[0] - ROOT * two[1] + half]
    t = [turn(value, b, 12) for b, value in enumerate(dft3(tiles[3:6], 1))]
    whole = [None] * 12
    for b in range(3):
        s, d = w[b] + h[b], w[b] - h[b]
        whole[b], whole[b + 6] = s + t[b][0], s - t[b][0]
        whole[b + 3], whole[b + 9] = d - t[b][1], d + t[b][1]
    halved = [None] * 12
    for b, value in enumerate(dft6(tiles[6:12], 1)):
        halved[b], halved[b + 6] = turn(value, b, 24)
        halved[b + 6] = -halved[b + 6]
    x = [None] * 48
    for b, value in enumerate(dft12(tiles[12:], 1)):
        re, im = turn(value, b, 48)
        s, d = whole[b] + halved[b], whole[b] - halved[b]
        x[b], x[b + 24] = s + re, s - re
        x[b + 12], x[b + 36] = d - im, d + im
    return x


def group_count(piece):
    return piece[1] * piece[3]


def piece_at(ref, piece):
    return ref.at[:, pl.ds(piece[0], piece[1]), pl.ds(piece[2], piece[3])]


def start_all(copies):
    for copy in copies:
        copy.start()
    return copies


def wait_all(copies):
    for copy in copies:
        copy.wait()


def run_filter(pieces, table_hbm, bring, send, scratch):
    *line_refs, wave_ref, table_ref, table_sems, sems = scratch
    copies = [start_all(bring(i, line_ref, sems)) for i, line_ref in enumerate(line_refs)]
    step = TILES // TABLE_COPIES
    spans = [pl.ds(i * step, step) for i in range(TABLE_COPIES)]
    table_copies = [
        pltpu.make_async_copy(table_hbm.at[span], table_ref.at[span], table_sems.at[i]) for i, span in enumerate(spans)
    ]
    start_all(table_copies)
    offsets = [sum(map(group_count, pieces[:i])) for i in range(len(pieces))]
    per_source = line_refs[0].shape[4] // LANES

    def spot(number):
        return pl.ds(pl.multiple_of(number * PAD, PAD), PAD)

    for piece, line_ref, offset, copy in zip(pieces, line_refs, offsets, copies):
        wait_all(copy)

        def forward(number, _, groups=piece[3], line_ref=line_ref, offset=offset):
            pair, group = number // groups, number % groups
            values = []
            for n1 in range(OUTER):
                lanes = pl.ds(n1 % per_source * LANES, LANES)
                values.append(line_ref[n1 // per_source, pair, group, :, lanes])
            for tile, (re, im) in enumerate(real_forward(values)):
                wave_ref[tile, spot(offset + number), :LANES] = re
                wave_ref[tile, spot(offset + number), LANES:] = im
            return 0

        lax.fori_loop(0, group_count(piece), forward, 0)

    def middle(tile, _):
        value = wave_ref[tile]
        high = value.astype(jnp.bfloat16)
        low = (value - high.astype(jnp.float32)).astype(jnp.bfloat16)
        rows = high.shape[0]
        both = jnp.dot(jnp.concatenate([high, low]), table_ref[tile, 0], preferred_element_type=jnp.float32)
        rest = jnp.dot(high, table_ref[tile, 1], preferred_element_type=jnp.float32)
        wave_ref[tile] = both[:rows] + both[rows:] + rest
        return 0

    for i, copy in enumerate(table_copies):
        copy.wait()
        lax.fori_loop(i * step, (i + 1) * step, middle, 0, unroll=3)

    away = []
    for i, (piece, line_ref, offset) in enumerate(zip(pieces, line_refs, offsets)):

        def backward(number, _, groups=piece[3], line_ref=line_ref, offset=offset):
            pair, group = number // groups, number % groups
            row = spot(offset + number)
            tiles = [(wave_ref[tile, row, :LANES], wave_ref[tile, row, LANES:]) for tile in range(TILES)]
            for n1, value in enumerate(real_backward(tiles)):
                line_ref[n1 // per_source, pair, group, :, pl.ds(n1 % per_source * LANES, LANES)] = value
            return 0

        lax.fori_loop(0, group_count(piece), backward, 0)
        away += start_all(send(i, line_ref))
    wait_all(away)


def filter_first_kernel(pieces, table_hbm, lines_hbm, out_hbm, *scratch):
    *scratch, out_sems = scratch

    def bring(i, line_ref, sems):
        return [pltpu.make_async_copy(piece_at(lines_hbm, pieces[i]), line_ref, sems.at[i])]

    def send(i, line_ref):
        return [pltpu.make_async_copy(line_ref.at[:, :, 0], out_hbm.at[:, i], out_sems.at[i])]

    run_filter(pieces, table_hbm, bring, send, scratch)


def filter_rest_kernel(pieces, me_ref, table_hbm, lines_hbm, field_hbm, *refs):
    count, split, me = lines_hbm.shape[0], field_hbm.shape[2], me_ref[0]
    received, sent, scratch, out_sems = refs[: count - 1], refs[count - 1 : 2 * count - 1], refs[2 * count - 1 : -1], refs[-1]
    places = rest_places(pieces)
    final = len(pieces) - 1

    def bring(i, line_ref, sems):
        if i < final:
            return [pltpu.make_async_copy(piece_at(lines_hbm, pieces[i]), line_ref, sems.at[i])]
        own = field_hbm.at[me // split, pl.ds(pieces[i][0], pieces[i][1]), me % split]
        sources = (own,) + received
        return [pltpu.make_async_copy(sources[x], line_ref.at[me ^ x], sems.at[i + x]) for x in range(count)]

    def send(i, line_ref):
        copies = []
        for pair in range(pieces[i][1]):
            number, first = places[i][pair]
            target = pl.ds(first, pieces[i][3])
            for x in range(count):
                sem = out_sems.at[number * count + x]
                copies.append(pltpu.make_async_copy(line_ref.at[me ^ x, pair], sent[x].at[target], sem))
        return copies

    run_filter(pieces, table_hbm, bring, send, scratch)


def rest_places(pieces):
    places, number, first = [], 0, 0
    for piece in pieces:
        places.append([])
        for _ in range(piece[1]):
            places[-1].append((number, first))
            number, first = number + 1, first + piece[3]
    return places


HBM = pl.BlockSpec(memory_space=pltpu.HBM)
SCALARS = pl.BlockSpec(memory_space=pltpu.SMEM)
WHOLE = pl.BlockSpec(memory_space=pltpu.VMEM)


def filter_call(kernel, name, pieces, lines, tables, in_specs, out_specs, out_shape, sems, flops):
    count, _, _, _, width = lines.shape
    rows = sum(map(group_count, pieces)) * PAD
    return pl.pallas_call(
        functools.partial(kernel, pieces),
        out_shape=out_shape,
        in_specs=in_specs,
        out_specs=out_specs,
        scratch_shapes=[pltpu.VMEM((count, piece[1], piece[3], PAD, width), jnp.float32) for piece in pieces]
        + [
            pltpu.VMEM((TILES, rows, 2 * LANES), jnp.float32),
            pltpu.VMEM(tables.shape, tables.dtype),
            pltpu.SemaphoreType.DMA((TABLE_COPIES,)),
            pltpu.SemaphoreType.DMA((sems[0],)),
            pltpu.SemaphoreType.DMA((sems[1],)),
        ],
        compiler_params=pltpu.CompilerParams(vmem_limit_bytes=FILTER_VMEM),
        cost_estimate=pl.CostEstimate(flops=flops, bytes_accessed=0, transcendentals=0),
        name=name,
    )


def filter_first(lines, tables, pieces):
    count, _, _, _, width = lines.shape
    out_shape = jax.ShapeDtypeStruct((count, len(pieces), 2, PAD, width), jnp.float32)
    sems = (len(pieces), len(pieces))
    call = filter_call(
        filter_first_kernel, "filter_first", pieces, lines, tables, [HBM, HBM], HBM, out_shape, sems, 10**6
    )
    return call(tables, lines)


def filter_rest(lines, field, received, spots, tables, pieces):
    count, _, _, _, width = lines.shape
    shape = (sum(map(group_count, pieces)), PAD, width)
    out_shape = [jax.ShapeDtypeStruct(shape, jnp.float32)] * count
    sems = (len(pieces) - 1 + count, count * sum(piece[1] for piece in pieces))
    ins = [SCALARS] + [HBM] * (count + 2)
    call = filter_call(
        filter_rest_kernel, "filter_rest", pieces, lines, tables, ins, [HBM] * count, out_shape, sems, 10**11
    )
    return call(spots, tables, lines, field, *received)


def local_kernel(rate_ref, coef_ref, flow_ref, field_ref, low_ref, high_ref, out_ref, pad_ref):
    _, comp_count, part_count, row_count, width = field_ref.shape
    pad_ref[:, :, :PAD] = low_ref[0]
    pad_ref[:, :, PAD : PAD + row_count] = field_ref[0]
    pad_ref[:, :, PAD + row_count :] = high_ref[0]
    rate = rate_ref[pl.program_id(0)]

    def column(step, _):
        lanes = pl.ds(pl.multiple_of(step * LANES, LANES), LANES)
        for top in range(0, row_count, PAD):
            rows = pl.ds(top, PAD)
            advect = rate * flow_ref[0, rows, :]
            shear = TAU * flow_ref[1, rows, :]
            centre = [[field_ref[0, c, p, rows, lanes] for p in range(2)] for c in range(comp_count)]
            for c in range(comp_count):
                for p in range(2):
                    total = centre[c][p]
                    total = total - advect * centre[c][1] if p == 0 else total + advect * centre[c][0]
                    if c == 1:
                        total = total - shear * centre[0][p]
                    for offset in range(STEN):
                        near = pad_ref[c, p, pl.ds(top + offset + PAD - HALO, PAD), lanes]
                        total = total + coef_ref[offset, rows, :] * near
                    out_ref[0, c, p, rows, lanes] = total
        return 0

    lax.fori_loop(0, width // LANES, column, 0)


def local_terms(field, low, high, rate, coef, flow):
    mode_count, comp_count, part_count, row_count, width = field.shape
    block = (1, comp_count, part_count, row_count, width)
    edge = (1, comp_count, part_count, PAD, width)

    def by_mode(m):
        return (m, 0, 0, 0, 0)

    return pl.pallas_call(
        local_kernel,
        grid=(mode_count,),
        out_shape=jax.ShapeDtypeStruct(field.shape, jnp.float32),
        in_specs=[
            SCALARS,
            pl.BlockSpec(coef.shape, lambda m: (0, 0, 0)),
            pl.BlockSpec(flow.shape, lambda m: (0, 0, 0)),
            pl.BlockSpec(block, by_mode),
            pl.BlockSpec(edge, by_mode),
            pl.BlockSpec(edge, by_mode),
        ],
        out_specs=pl.BlockSpec(block, by_mode),
        scratch_shapes=[pltpu.VMEM((comp_count, part_count, row_count + 2 * PAD, width), jnp.float32)],
        compiler_params=pltpu.CompilerParams(vmem_limit_bytes=24 << 20),
        cost_estimate=pl.CostEstimate(flops=40 * field.size, bytes_accessed=10 * field.size, transcendentals=0),
        name="local_terms",
    )(rate, coef, flow, field, low, high)


def add_first_kernel(pieces, me_ref, base_hbm, weight_ref, term_hbm, out_hbm, shear_ref, *scratch):
    base_ref, term_ref, base_sems, term_sems = scratch
    count, split, me = term_hbm.shape[0], base_hbm.shape[2], me_ref[0]

    def spot(ref, x, i):
        other = me ^ x
        return ref.at[other // split, pl.ds(0, 2), other % split, pieces[i][2]]

    spots = [(x, i) for x in range(count) for i in range(len(pieces))]
    sem = [base_sems.at[x * len(pieces) + i] for x, i in spots]
    loads = [pltpu.make_async_copy(spot(base_hbm, *at), base_ref.at[at], sem[n]) for n, at in enumerate(spots)]
    stores = [pltpu.make_async_copy(base_ref.at[at], spot(out_hbm, *at), sem[n]) for n, at in enumerate(spots)]
    terms = [pltpu.make_async_copy(term_hbm.at[me ^ x], term_ref.at[x], term_sems.at[x]) for x in range(count)]
    start_all(loads)
    start_all(terms)
    wait_all(terms)
    wait_all(loads)
    for x in range(count):
        base_ref[x] = base_ref[x] + term_ref[x]
        start_all(stores[x * len(pieces) : (x + 1) * len(pieces)])
        for p in range(2):
            shear_ref[me ^ x, p] = jnp.sum(base_ref[x, 0, p] * weight_ref[x, 0][:, :1], axis=0)
            shear_ref[me ^ x, 2 + p] = jnp.sum(base_ref[x, len(pieces) - 1, p] * weight_ref[x, 1][:, :1], axis=0)
    wait_all(stores)


def add_first(base, term, weight, spots, pieces):
    count, width = term.shape[0], term.shape[4]
    buffer = pltpu.VMEM(term.shape, jnp.float32)
    return pl.pallas_call(
        functools.partial(add_first_kernel, pieces),
        out_shape=(
            jax.ShapeDtypeStruct(base.shape, jnp.float32),
            jax.ShapeDtypeStruct((count, 4, width), jnp.float32),
        ),
        in_specs=[SCALARS, HBM, WHOLE, HBM],
        out_specs=(HBM, WHOLE),
        scratch_shapes=[
            buffer,
            buffer,
            pltpu.SemaphoreType.DMA((count * len(pieces),)),
            pltpu.SemaphoreType.DMA((count,)),
        ],
        input_output_aliases={1: 0},
        compiler_params=pltpu.CompilerParams(vmem_limit_bytes=24 << 20),
        cost_estimate=pl.CostEstimate(flops=term.size, bytes_accessed=12 * term.size, transcendentals=0),
        name="add_first",
    )(spots, base, weight, term)


def add_rest_kernel(pieces, partners, me_ref, base_hbm, *refs):
    count = len(partners)
    terms, out_hbm = refs[:count], refs[count]
    base_ref, term_ref, base_sems, term_sems = refs[count + 1 :]
    split, me = base_hbm.shape[2], me_ref[0]
    places = rest_places(pieces)
    spots = []
    for n, x in enumerate(partners):
        for piece, pairs in zip(pieces, places):
            for pair, (number, first) in enumerate(pairs):
                spots.append((n, x, piece[0] + pair, pl.ds(piece[2], piece[3]), pl.ds(first, piece[3])))

    def far(ref, spot):
        other = me ^ spot[1]
        return ref.at[other // split, spot[2], other % split, spot[3]]

    def near(spot):
        return base_ref.at[spot[0], spot[4]]

    loads = [pltpu.make_async_copy(far(base_hbm, at), near(at), base_sems.at[n]) for n, at in enumerate(spots)]
    stores = [pltpu.make_async_copy(near(at), far(out_hbm, at), base_sems.at[n]) for n, at in enumerate(spots)]
    copies = [pltpu.make_async_copy(terms[n], term_ref.at[n], term_sems.at[n]) for n in range(count)]
    start_all(copies)
    start_all(loads)
    wait_all(copies)
    for load, store, at in zip(loads, stores, spots):
        load.wait()
        base_ref[at[0], at[4]] = base_ref[at[0], at[4]] + term_ref[at[0], at[4]]
        store.start()
    wait_all(stores)


def add_rest(base, terms, partners, spots, pieces):
    buffer = pltpu.VMEM((len(terms),) + terms[0].shape, jnp.float32)
    size = len(terms) * terms[0].size
    copies = len(terms) * sum(piece[1] for piece in pieces)
    return pl.pallas_call(
        functools.partial(add_rest_kernel, pieces, partners),
        out_shape=jax.ShapeDtypeStruct(base.shape, jnp.float32),
        in_specs=[SCALARS, HBM] + [HBM] * len(terms),
        out_specs=HBM,
        scratch_shapes=[
            buffer,
            buffer,
            pltpu.SemaphoreType.DMA((copies,)),
            pltpu.SemaphoreType.DMA((len(terms),)),
        ],
        input_output_aliases={1: 0},
        compiler_params=pltpu.CompilerParams(vmem_limit_bytes=24 << 20),
        cost_estimate=pl.CostEstimate(flops=size, bytes_accessed=12 * size, transcendentals=0),
        name="add_rest",
    )(spots, base, *terms)


def after(value, *others):
    return lax.optimization_barrier((value,) + others)[0]


def on_device(field, mean_flow, d2_coef, wall_coef, kx_index, patch_of):
    mode_count, comp_count, part_count, row_count, width = field.shape
    span = lax.axis_size("span")
    me = lax.axis_index("span")
    wall_count = lax.axis_size("wall")
    wall_index = lax.axis_index("wall")
    mode_split = math.gcd(span, mode_count)
    row_split = span // mode_split
    line_rows = row_count // row_split
    tables = jnp.asarray(spectral_tables(width * span))
    pairs = [[(i, i ^ x) for i in range(span)] for x in range(span)]
    spots = jnp.stack([me]).astype(jnp.int32)

    def exchange(lines):
        return lax.all_to_all(lines, "span", split_axis=0, concat_axis=0)

    def swap(blocks):
        return [lax.ppermute(blocks[x], "span", pairs[x]) for x in range(span - 1, 0, -1)][::-1]

    pairs_count, groups = comp_count * part_count, line_rows // PAD
    shares = (mode_split, pairs_count, row_split, groups, PAD, width)
    shared = field.reshape(shares)
    last = pairs_count - part_count
    lines = exchange(shared[:, :last].transpose(0, 2, 1, 3, 4, 5).reshape(span, last, groups, PAD, width))

    first_pieces = tuple((0, 2, group, 1) for group in range(groups))
    rest_pieces = tuple((2 * comp, 2, 0, groups) for comp in range(1, comp_count))

    forward = [(i, i + 1) for i in range(wall_count - 1)]
    backward = [(i + 1, i) for i in range(wall_count - 1)]
    low = lax.ppermute(field[:, :, :, row_count - PAD :], "wall", forward)
    high = lax.ppermute(field[:, :, :, :PAD], "wall", backward)

    rate = kx_index.astype(jnp.float32) * (0.25 * TAU)
    coef = jnp.broadcast_to(d2_coef[:, :, None], (STEN, row_count, LANES))
    flow = jnp.broadcast_to(mean_flow[:, :, None], (2, row_count, LANES))
    base = local_terms(field, low, high, rate, coef, flow)

    def last_block(x):
        other = me ^ x
        start = (other // row_split, last, other % row_split, 0, 0, 0)
        block = lax.dynamic_slice(shared, start, (1, part_count, 1, groups, PAD, width))
        return block.reshape(part_count, groups, PAD, width)

    blocks = tuple(last_block(x) for x in range(1, span))
    received = swap((None,) + lax.optimization_barrier((blocks, base))[0])
    lines = after(lines, base)
    filtered = filter_first(lines, tables, first_pieces)
    back = exchange(filtered)
    received[0] = after(received[0], filtered)
    sent = filter_rest(lines, shared, received, spots, tables, rest_pieces)
    returned = [sent[0]] + swap(sent)

    lower = jnp.where(wall_index == 0, wall_coef[0], 0.0)
    upper = jnp.where(wall_index == wall_count - 1, wall_coef[1, ::-1], 0.0)
    group = ((me ^ jnp.arange(span)) % row_split)[:, None]
    ends = [jnp.where(group == 0, lower, 0.0), jnp.where(group == row_split - 1, upper, 0.0)]
    weight = jnp.broadcast_to(jnp.stack(ends, axis=1)[..., None], (span, 2, PAD, LANES))
    result, shear = add_first(base.reshape(shares), back, weight, spots, first_pieces)
    onehot = (patch_of[:, None] == jnp.arange(PATCH, dtype=jnp.int32)[None, :]).astype(jnp.float32)
    grad = jnp.einsum("swz,zq->swq", shear, onehot, precision=lax.Precision.HIGHEST)
    grad = grad.reshape(mode_count, row_split, 2, part_count, PATCH).sum(axis=1)
    distance = 1
    while distance < wall_count:
        grad = grad + lax.ppermute(grad, "wall", [(i, i ^ distance) for i in range(wall_count)])
        distance *= 2
    parts = jnp.stack([grad] + swap([grad] * span))
    parts = [lax.dynamic_index_in_dim(parts, me ^ x, 0, keepdims=False) for x in range(span)]
    wall_grad = functools.reduce(jnp.add, parts).transpose(1, 0, 2, 3)

    cuts = [0, span // 2, 3 * span // 4, span]
    for low_cut, high_cut in zip(cuts, cuts[1:]):
        partners = range(low_cut, high_cut)
        result = add_rest(result, returned[low_cut:high_cut], partners, spots, rest_pieces)
    return (result.reshape(field.shape), wall_grad)


def solution(mesh):
    return jax.shard_map(
        on_device,
        mesh=mesh,
        in_specs=(
            P(None, None, None, "wall", "span"),
            P(None, "wall"),
            P(None, "wall"),
            P(),
            P(),
            P("span"),
        ),
        out_specs=(P(None, None, None, "wall", "span"), P()),
        check_vma=False,
    )
```

```python
import functools
import math

import jax
import jax.numpy as jnp
import numpy as np
from jax import lax
from jax.experimental import pallas as pl
from jax.experimental.pallas import tpu as pltpu
from jax.sharding import PartitionSpec as P

HALO = 7
STEN = 15
PATCH = 64
TAU = 0.25
VIS = 0.5

LANES = 128
OUTER = 48
PAD = 8
TILES = OUTER // 2
FILTER_VMEM = 57_500_000
TABLE_COPIES = 4

QUARTER = (0, 4, 2, 1, 5, 9)
KEPT = tuple(4 * q for q in QUARTER) + tuple(2 + 8 * t for t in range(6)) + tuple(4 * q + 1 for q in range(12))


@functools.cache
def spectral_tables(length):
    signed = np.arange(length)
    signed = np.where(signed > length // 2, signed - length, signed)
    cutoff = length // 3
    ratio = signed.astype(np.float64) / cutoff
    multiplier = np.where(np.abs(signed) < cutoff, -VIS * ratio * ratio, 0.0)
    shift = np.arange(LANES)[None, :] - np.arange(LANES)[:, None]
    inner = np.arange(LANES)

    def complex_table(k1):
        wave = k1 + OUTER * inner
        spots = np.arange(-LANES + 1, LANES)
        phase = np.exp(2j * np.pi * ((wave[:, None] * spots[None, :]) % length) / length)
        return ((multiplier[wave][:, None] * phase).sum(axis=0) / LANES)[shift + LANES - 1]

    tables = np.zeros((TILES, 2 * LANES, 2 * LANES))
    tables[0, :LANES, :LANES] = complex_table(0).real / OUTER
    tables[0, LANES:, LANES:] = complex_table(OUTER // 2).real / OUTER
    for tile, k1 in enumerate(KEPT[1:], 1):
        table = complex_table(k1) * 2.0 / OUTER
        tables[tile, :LANES, :LANES] = table.real
        tables[tile, :LANES, LANES:] = table.imag
        tables[tile, LANES:, :LANES] = -table.imag
        tables[tile, LANES:, LANES:] = table.real
    high = tables.astype(jnp.bfloat16)
    low = (tables - high.astype(np.float64)).astype(jnp.bfloat16)
    return np.stack([high, low], axis=1)


def turn(value, numerator, denominator):
    re, im = value
    numerator %= denominator
    if numerator == 0:
        return value
    if 2 * numerator == denominator:
        return (-re, -im)
    if 4 * numerator == denominator:
        return (-im, re)
    if 4 * numerator == 3 * denominator:
        return (im, -re)
    cos = math.cos(2 * math.pi * numerator / denominator)
    sin = math.sin(2 * math.pi * numerator / denominator)
    return (re * cos - im * sin, re * sin + im * cos)


def add(a, b):
    return (a[0] + b[0], a[1] + b[1])


def sub(a, b):
    return (a[0] - b[0], a[1] - b[1])


ROOT = math.sqrt(3.0) / 2.0


def dft3(x, sign):
    total = add(x[1], x[2])
    other = sub(x[1], x[2])
    middle = (x[0][0] - 0.5 * total[0], x[0][1] - 0.5 * total[1])
    side = (-sign * ROOT * other[1], sign * ROOT * other[0])
    return [add(x[0], total), add(middle, side), sub(middle, side)]


def dft6(x, sign):
    even = dft3([add(x[b], x[b + 3]) for b in range(3)], sign)
    odd = dft3([turn(sub(x[b], x[b + 3]), sign * b, 6) for b in range(3)], sign)
    return [even[0], odd[0], even[1], odd[1], even[2], odd[2]]


def dft12(x, sign):
    out = [None] * 12
    parts = [[], [], [], []]
    for b in range(3):
        a0, a1, a2, a3 = x[b], x[b + 3], x[b + 6], x[b + 9]
        s0, s1, d0, d1 = add(a0, a2), add(a1, a3), sub(a0, a2), turn(sub(a1, a3), sign, 4)
        for r, value in enumerate((add(s0, s1), add(d0, d1), sub(s0, s1), sub(d0, d1))):
            parts[r].append(turn(value, sign * b * r, 12))
    for r in range(4):
        for q, value in enumerate(dft3(parts[r], sign)):
            out[4 * q + r] = value
    return out


def real_forward(x):
    whole, halved, turned = [], [], []
    for b in range(12):
        s0, s1 = x[b] + x[b + 24], x[b + 12] + x[b + 36]
        whole.append(s0 + s1)
        halved.append(s0 - s1)
        turned.append(turn((x[b] - x[b + 24], x[b + 36] - x[b + 12]), -b, 48))
    w, h, t = [], [], []
    for b in range(3):
        s0, s1 = whole[b] + whole[b + 6], whole[b + 3] + whole[b + 9]
        w.append(s0 + s1)
        h.append(s0 - s1)
        t.append(turn((whole[b] - whole[b + 6], whole[b + 9] - whole[b + 3]), -b, 12))
    total, other = w[1] + w[2], w[1] - w[2]
    four = (w[0] - 0.5 * total, -ROOT * other)
    two = (h[0] + 0.5 * (h[1] - h[2]), -ROOT * (h[1] + h[2]))
    tiles = [(w[0] + total, h[0] - h[1] + h[2]), four, two] + dft3(t, -1)
    tiles += dft6([turn((halved[b], -halved[b + 6]), -b, 24) for b in range(6)], -1)
    return tiles + dft12(turned, -1)


def real_backward(tiles):
    (zero, half), four, two = tiles[:3]
    w0 = zero + four[0]
    rest, side = zero - 0.5 * four[0], ROOT * four[1]
    w = [w0, rest - side, rest + side]
    h_side = 0.5 * two[0] - ROOT * two[1]
    h = [two[0] + half, h_side - half, -0.5 * two[0] - ROOT * two[1] + half]
    t = [turn(value, b, 12) for b, value in enumerate(dft3(tiles[3:6], 1))]
    whole = [None] * 12
    for b in range(3):
        s, d = w[b] + h[b], w[b] - h[b]
        whole[b], whole[b + 6] = s + t[b][0], s - t[b][0]
        whole[b + 3], whole[b + 9] = d - t[b][1], d + t[b][1]
    halved = [None] * 12
    for b, value in enumerate(dft6(tiles[6:12], 1)):
        halved[b], halved[b + 6] = turn(value, b, 24)
        halved[b + 6] = -halved[b + 6]
    x = [None] * 48
    for b, value in enumerate(dft12(tiles[12:], 1)):
        re, im = turn(value, b, 48)
        s, d = whole[b] + halved[b], whole[b] - halved[b]
        x[b], x[b + 24] = s + re, s - re
        x[b + 12], x[b + 36] = d - im, d + im
    return x


def group_count(piece):
    return piece[1] * piece[3]


def piece_at(ref, piece):
    return ref.at[:, pl.ds(piece[0], piece[1]), pl.ds(piece[2], piece[3])]


def start_all(copies):
    for copy in copies:
        copy.start()
    return copies


def wait_all(copies):
    for copy in copies:
        copy.wait()


def run_filter(pieces, table_hbm, bring, send, scratch):
    *line_refs, wave_ref, table_ref, table_sems, sems = scratch
    copies = [start_all(bring(i, line_ref, sems)) for i, line_ref in enumerate(line_refs)]
    step = TILES // TABLE_COPIES
    spans = [pl.ds(i * step, step) for i in range(TABLE_COPIES)]
    table_copies = [
        pltpu.make_async_copy(table_hbm.at[span], table_ref.at[span], table_sems.at[i]) for i, span in enumerate(spans)
    ]
    start_all(table_copies)
    offsets = [sum(map(group_count, pieces[:i])) for i in range(len(pieces))]
    per_source = line_refs[0].shape[4] // LANES

    def spot(number):
        return pl.ds(pl.multiple_of(number * PAD, PAD), PAD)

    for piece, line_ref, offset, copy in zip(pieces, line_refs, offsets, copies):
        wait_all(copy)

        def forward(number, _, groups=piece[3], line_ref=line_ref, offset=offset):
            pair, group = number // groups, number % groups
            values = []
            for n1 in range(OUTER):
                lanes = pl.ds(n1 % per_source * LANES, LANES)
                values.append(line_ref[n1 // per_source, pair, group, :, lanes])
            for tile, (re, im) in enumerate(real_forward(values)):
                wave_ref[tile, spot(offset + number), :LANES] = re
                wave_ref[tile, spot(offset + number), LANES:] = im
            return 0

        lax.fori_loop(0, group_count(piece), forward, 0)

    def middle(tile, _):
        value = wave_ref[tile]
        high = value.astype(jnp.bfloat16)
        low = (value - high.astype(jnp.float32)).astype(jnp.bfloat16)
        rows = high.shape[0]
        both = jnp.dot(jnp.concatenate([high, low]), table_ref[tile, 0], preferred_element_type=jnp.float32)
        rest = jnp.dot(high, table_ref[tile, 1], preferred_element_type=jnp.float32)
        wave_ref[tile] = both[:rows] + both[rows:] + rest
        return 0

    for i, copy in enumerate(table_copies):
        copy.wait()
        lax.fori_loop(i * step, (i + 1) * step, middle, 0, unroll=3)

    away = []
    for i, (piece, line_ref, offset) in enumerate(zip(pieces, line_refs, offsets)):

        def backward(number, _, groups=piece[3], line_ref=line_ref, offset=offset):
            pair, group = number // groups, number % groups
            row = spot(offset + number)
            tiles = [(wave_ref[tile, row, :LANES], wave_ref[tile, row, LANES:]) for tile in range(TILES)]
            for n1, value in enumerate(real_backward(tiles)):
                line_ref[n1 // per_source, pair, group, :, pl.ds(n1 % per_source * LANES, LANES)] = value
            return 0

        lax.fori_loop(0, group_count(piece), backward, 0)
        away += start_all(send(i, line_ref))
    wait_all(away)


def gather_kernel(field_hbm, out_hbm, sems):
    count, pairs = out_hbm.shape[:2]
    split = field_hbm.shape[2]
    copies = []
    for x in range(count):
        for pair in range(pairs):
            source = field_hbm.at[x // split, pair, x % split]
            copies.append(pltpu.make_async_copy(source, out_hbm.at[x, pair], sems.at[x * pairs + pair]))
    wait_all(start_all(copies))


def gather_lines(field, count, pairs):
    anywhere = pl.BlockSpec(memory_space=pl.ANY)
    shape = (count, pairs) + field.shape[3:]
    return pl.pallas_call(
        gather_kernel,
        out_shape=jax.ShapeDtypeStruct(shape, jnp.float32),
        in_specs=[anywhere],
        out_specs=anywhere,
        scratch_shapes=[pltpu.SemaphoreType.DMA((count * pairs,))],
        cost_estimate=pl.CostEstimate(flops=0, bytes_accessed=8 * math.prod(shape), transcendentals=0),
        name="gather_lines",
    )(field)


def filter_first_kernel(pieces, table_hbm, lines_hbm, out_hbm, *scratch):
    *scratch, out_sems = scratch

    def bring(i, line_ref, sems):
        return [pltpu.make_async_copy(piece_at(lines_hbm, pieces[i]), line_ref, sems.at[i])]

    def send(i, line_ref):
        return [pltpu.make_async_copy(line_ref.at[:, :, 0], out_hbm.at[:, i], out_sems.at[i])]

    run_filter(pieces, table_hbm, bring, send, scratch)


def filter_rest_kernel(pieces, me_ref, table_hbm, lines_hbm, field_hbm, *refs):
    count, split, me = lines_hbm.shape[0], field_hbm.shape[2], me_ref[0]
    received, sent, scratch, out_sems = refs[: count - 1], refs[count - 1 : 2 * count - 1], refs[2 * count - 1 : -1], refs[-1]
    places = rest_places(pieces)
    final = len(pieces) - 1

    def bring(i, line_ref, sems):
        if i < final:
            return [pltpu.make_async_copy(piece_at(lines_hbm, pieces[i]), line_ref, sems.at[i])]
        own = field_hbm.at[me // split, pl.ds(pieces[i][0], pieces[i][1]), me % split]
        sources = (own,) + received
        return [pltpu.make_async_copy(sources[x], line_ref.at[me ^ x], sems.at[i + x]) for x in range(count)]

    def send(i, line_ref):
        copies = []
        for pair in range(pieces[i][1]):
            number, first = places[i][pair]
            target = pl.ds(first, pieces[i][3])
            for x in range(count):
                sem = out_sems.at[number * count + x]
                copies.append(pltpu.make_async_copy(line_ref.at[me ^ x, pair], sent[x].at[target], sem))
        return copies

    run_filter(pieces, table_hbm, bring, send, scratch)


def rest_places(pieces):
    places, number, first = [], 0, 0
    for piece in pieces:
        places.append([])
        for _ in range(piece[1]):
            places[-1].append((number, first))
            number, first = number + 1, first + piece[3]
    return places


HBM = pl.BlockSpec(memory_space=pltpu.HBM)
SCALARS = pl.BlockSpec(memory_space=pltpu.SMEM)
WHOLE = pl.BlockSpec(memory_space=pltpu.VMEM)


def filter_call(kernel, name, pieces, lines, tables, in_specs, out_specs, out_shape, sems, flops):
    count, _, _, _, width = lines.shape
    rows = sum(map(group_count, pieces)) * PAD
    return pl.pallas_call(
        functools.partial(kernel, pieces),
        out_shape=out_shape,
        in_specs=in_specs,
        out_specs=out_specs,
        scratch_shapes=[pltpu.VMEM((count, piece[1], piece[3], PAD, width), jnp.float32) for piece in pieces]
        + [
            pltpu.VMEM((TILES, rows, 2 * LANES), jnp.float32),
            pltpu.VMEM(tables.shape, tables.dtype),
            pltpu.SemaphoreType.DMA((TABLE_COPIES,)),
            pltpu.SemaphoreType.DMA((sems[0],)),
            pltpu.SemaphoreType.DMA((sems[1],)),
        ],
        compiler_params=pltpu.CompilerParams(vmem_limit_bytes=FILTER_VMEM),
        cost_estimate=pl.CostEstimate(flops=flops, bytes_accessed=0, transcendentals=0),
        name=name,
    )


def filter_first(lines, tables, pieces):
    count, _, _, _, width = lines.shape
    out_shape = jax.ShapeDtypeStruct((count, len(pieces), 2, PAD, width), jnp.float32)
    sems = (len(pieces), len(pieces))
    call = filter_call(
        filter_first_kernel, "filter_first", pieces, lines, tables, [HBM, HBM], HBM, out_shape, sems, 10**6
    )
    return call(tables, lines)


def filter_rest(lines, field, received, spots, tables, pieces):
    count, _, _, _, width = lines.shape
    shape = (sum(map(group_count, pieces)), PAD, width)
    out_shape = [jax.ShapeDtypeStruct(shape, jnp.float32)] * count
    sems = (len(pieces) - 1 + count, count * sum(piece[1] for piece in pieces))
    ins = [SCALARS] + [HBM] * (count + 2)
    call = filter_call(
        filter_rest_kernel, "filter_rest", pieces, lines, tables, ins, [HBM] * count, out_shape, sems, 10**11
    )
    return call(spots, tables, lines, field, *received)


def local_kernel(rate_ref, coef_ref, flow_ref, field_ref, low_ref, high_ref, out_ref, pad_ref):
    _, comp_count, part_count, row_count, width = field_ref.shape
    pad_ref[:, :, :PAD] = low_ref[0]
    pad_ref[:, :, PAD : PAD + row_count] = field_ref[0]
    pad_ref[:, :, PAD + row_count :] = high_ref[0]
    rate = rate_ref[pl.program_id(0)]

    def column(step, _):
        lanes = pl.ds(pl.multiple_of(step * LANES, LANES), LANES)
        for top in range(0, row_count, PAD):
            rows = pl.ds(top, PAD)
            advect = rate * flow_ref[0, rows, :]
            shear = TAU * flow_ref[1, rows, :]
            centre = [[field_ref[0, c, p, rows, lanes] for p in range(2)] for c in range(comp_count)]
            for c in range(comp_count):
                for p in range(2):
                    total = centre[c][p]
                    total = total - advect * centre[c][1] if p == 0 else total + advect * centre[c][0]
                    if c == 1:
                        total = total - shear * centre[0][p]
                    for offset in range(STEN):
                        near = pad_ref[c, p, pl.ds(top + offset + PAD - HALO, PAD), lanes]
                        total = total + coef_ref[offset, rows, :] * near
                    out_ref[0, c, p, rows, lanes] = total
        return 0

    lax.fori_loop(0, width // LANES, column, 0)


def local_terms(field, low, high, rate, coef, flow):
    mode_count, comp_count, part_count, row_count, width = field.shape
    block = (1, comp_count, part_count, row_count, width)
    edge = (1, comp_count, part_count, PAD, width)

    def by_mode(m):
        return (m, 0, 0, 0, 0)

    return pl.pallas_call(
        local_kernel,
        grid=(mode_count,),
        out_shape=jax.ShapeDtypeStruct(field.shape, jnp.float32),
        in_specs=[
            SCALARS,
            pl.BlockSpec(coef.shape, lambda m: (0, 0, 0)),
            pl.BlockSpec(flow.shape, lambda m: (0, 0, 0)),
            pl.BlockSpec(block, by_mode),
            pl.BlockSpec(edge, by_mode),
            pl.BlockSpec(edge, by_mode),
        ],
        out_specs=pl.BlockSpec(block, by_mode),
        scratch_shapes=[pltpu.VMEM((comp_count, part_count, row_count + 2 * PAD, width), jnp.float32)],
        compiler_params=pltpu.CompilerParams(vmem_limit_bytes=24 << 20),
        cost_estimate=pl.CostEstimate(flops=40 * field.size, bytes_accessed=10 * field.size, transcendentals=0),
        name="local_terms",
    )(rate, coef, flow, field, low, high)


def add_first_kernel(pieces, me_ref, base_hbm, weight_ref, term_hbm, out_hbm, shear_ref, *scratch):
    base_ref, term_ref, base_sems, term_sems = scratch
    count, split, me = term_hbm.shape[0], base_hbm.shape[2], me_ref[0]

    def spot(ref, x, i):
        other = me ^ x
        return ref.at[other // split, pl.ds(0, 2), other % split, pieces[i][2]]

    spots = [(x, i) for x in range(count) for i in range(len(pieces))]
    sem = [base_sems.at[x * len(pieces) + i] for x, i in spots]
    loads = [pltpu.make_async_copy(spot(base_hbm, *at), base_ref.at[at], sem[n]) for n, at in enumerate(spots)]
    stores = [pltpu.make_async_copy(base_ref.at[at], spot(out_hbm, *at), sem[n]) for n, at in enumerate(spots)]
    terms = [pltpu.make_async_copy(term_hbm.at[me ^ x], term_ref.at[x], term_sems.at[x]) for x in range(count)]
    start_all(loads)
    start_all(terms)
    wait_all(terms)
    wait_all(loads)
    for x in range(count):
        base_ref[x] = base_ref[x] + term_ref[x]
        start_all(stores[x * len(pieces) : (x + 1) * len(pieces)])
        for p in range(2):
            shear_ref[me ^ x, p] = jnp.sum(base_ref[x, 0, p] * weight_ref[x, 0][:, :1], axis=0)
            shear_ref[me ^ x, 2 + p] = jnp.sum(base_ref[x, len(pieces) - 1, p] * weight_ref[x, 1][:, :1], axis=0)
    wait_all(stores)


def add_first(base, term, weight, spots, pieces):
    count, width = term.shape[0], term.shape[4]
    buffer = pltpu.VMEM(term.shape, jnp.float32)
    return pl.pallas_call(
        functools.partial(add_first_kernel, pieces),
        out_shape=(
            jax.ShapeDtypeStruct(base.shape, jnp.float32),
            jax.ShapeDtypeStruct((count, 4, width), jnp.float32),
        ),
        in_specs=[SCALARS, HBM, WHOLE, HBM],
        out_specs=(HBM, WHOLE),
        scratch_shapes=[
            buffer,
            buffer,
            pltpu.SemaphoreType.DMA((count * len(pieces),)),
            pltpu.SemaphoreType.DMA((count,)),
        ],
        input_output_aliases={1: 0},
        compiler_params=pltpu.CompilerParams(vmem_limit_bytes=24 << 20),
        cost_estimate=pl.CostEstimate(flops=term.size, bytes_accessed=12 * term.size, transcendentals=0),
        name="add_first",
    )(spots, base, weight, term)


def add_rest_kernel(pieces, partners, me_ref, base_hbm, *refs):
    count = len(partners)
    terms, out_hbm = refs[:count], refs[count]
    base_ref, term_ref, base_sems, term_sems = refs[count + 1 :]
    split, me = base_hbm.shape[2], me_ref[0]
    places = rest_places(pieces)
    spots = []
    for n, x in enumerate(partners):
        for piece, pairs in zip(pieces, places):
            for pair, (number, first) in enumerate(pairs):
                spots.append((n, x, piece[0] + pair, pl.ds(piece[2], piece[3]), pl.ds(first, piece[3])))

    def far(ref, spot):
        other = me ^ spot[1]
        return ref.at[other // split, spot[2], other % split, spot[3]]

    def near(spot):
        return base_ref.at[spot[0], spot[4]]

    loads = [pltpu.make_async_copy(far(base_hbm, at), near(at), base_sems.at[n]) for n, at in enumerate(spots)]
    stores = [pltpu.make_async_copy(near(at), far(out_hbm, at), base_sems.at[n]) for n, at in enumerate(spots)]
    copies = [pltpu.make_async_copy(terms[n], term_ref.at[n], term_sems.at[n]) for n in range(count)]
    start_all(copies)
    start_all(loads)
    wait_all(copies)
    for load, store, at in zip(loads, stores, spots):
        load.wait()
        base_ref[at[0], at[4]] = base_ref[at[0], at[4]] + term_ref[at[0], at[4]]
        store.start()
    wait_all(stores)


def add_rest(base, terms, partners, spots, pieces):
    buffer = pltpu.VMEM((len(terms),) + terms[0].shape, jnp.float32)
    size = len(terms) * terms[0].size
    copies = len(terms) * sum(piece[1] for piece in pieces)
    return pl.pallas_call(
        functools.partial(add_rest_kernel, pieces, partners),
        out_shape=jax.ShapeDtypeStruct(base.shape, jnp.float32),
        in_specs=[SCALARS, HBM] + [HBM] * len(terms),
        out_specs=HBM,
        scratch_shapes=[
            buffer,
            buffer,
            pltpu.SemaphoreType.DMA((copies,)),
            pltpu.SemaphoreType.DMA((len(terms),)),
        ],
        input_output_aliases={1: 0},
        compiler_params=pltpu.CompilerParams(vmem_limit_bytes=24 << 20),
        cost_estimate=pl.CostEstimate(flops=size, bytes_accessed=12 * size, transcendentals=0),
        name="add_rest",
    )(spots, base, *terms)


def after(value, *others):
    return lax.optimization_barrier((value,) + others)[0]


def on_device(field, mean_flow, d2_coef, wall_coef, kx_index, patch_of):
    mode_count, comp_count, part_count, row_count, width = field.shape
    span = lax.axis_size("span")
    me = lax.axis_index("span")
    wall_count = lax.axis_size("wall")
    wall_index = lax.axis_index("wall")
    mode_split = math.gcd(span, mode_count)
    row_split = span // mode_split
    line_rows = row_count // row_split
    tables = jnp.asarray(spectral_tables(width * span))
    pairs = [[(i, i ^ x) for i in range(span)] for x in range(span)]
    spots = jnp.stack([me]).astype(jnp.int32)

    def exchange(lines):
        return lax.all_to_all(lines, "span", split_axis=0, concat_axis=0)

    def swap(blocks):
        return [lax.ppermute(blocks[x], "span", pairs[x]) for x in range(span - 1, 0, -1)][::-1]

    pairs_count, groups = comp_count * part_count, line_rows // PAD
    shares = (mode_split, pairs_count, row_split, groups, PAD, width)
    shared = field.reshape(shares)
    last = pairs_count - part_count
    lines = exchange(gather_lines(shared, span, last))

    first_pieces = tuple((0, 2, group, 1) for group in range(groups))
    rest_pieces = tuple((2 * comp, 2, 0, groups) for comp in range(1, comp_count))

    forward = [(i, i + 1) for i in range(wall_count - 1)]
    backward = [(i + 1, i) for i in range(wall_count - 1)]
    low = lax.ppermute(field[:, :, :, row_count - PAD :], "wall", forward)
    high = lax.ppermute(field[:, :, :, :PAD], "wall", backward)

    rate = kx_index.astype(jnp.float32) * (0.25 * TAU)
    coef = jnp.broadcast_to(d2_coef[:, :, None], (STEN, row_count, LANES))
    flow = jnp.broadcast_to(mean_flow[:, :, None], (2, row_count, LANES))
    base = local_terms(field, low, high, rate, coef, flow)

    def last_block(x):
        other = me ^ x
        start = (other // row_split, last, other % row_split, 0, 0, 0)
        block = lax.dynamic_slice(shared, start, (1, part_count, 1, groups, PAD, width))
        return block.reshape(part_count, groups, PAD, width)

    blocks = tuple(last_block(x) for x in range(1, span))
    received = swap((None,) + lax.optimization_barrier((blocks, base))[0])
    lines = after(lines, base)
    filtered = filter_first(lines, tables, first_pieces)
    back = exchange(filtered)
    received[0] = after(received[0], filtered)
    sent = filter_rest(lines, shared, received, spots, tables, rest_pieces)
    returned = [sent[0]] + swap(sent)

    lower = jnp.where(wall_index == 0, wall_coef[0], 0.0)
    upper = jnp.where(wall_index == wall_count - 1, wall_coef[1, ::-1], 0.0)
    group = ((me ^ jnp.arange(span)) % row_split)[:, None]
    ends = [jnp.where(group == 0, lower, 0.0), jnp.where(group == row_split - 1, upper, 0.0)]
    weight = jnp.broadcast_to(jnp.stack(ends, axis=1)[..., None], (span, 2, PAD, LANES))
    result, shear = add_first(base.reshape(shares), back, weight, spots, first_pieces)
    onehot = (patch_of[:, None] == jnp.arange(PATCH, dtype=jnp.int32)[None, :]).astype(jnp.float32)
    grad = jnp.einsum("swz,zq->swq", shear, onehot, precision=lax.Precision.HIGHEST)
    grad = grad.reshape(mode_count, row_split, 2, part_count, PATCH).sum(axis=1)
    distance = 1
    while distance < wall_count:
        grad = grad + lax.ppermute(grad, "wall", [(i, i ^ distance) for i in range(wall_count)])
        distance *= 2
    parts = jnp.stack([grad] + swap([grad] * span))
    parts = [lax.dynamic_index_in_dim(parts, me ^ x, 0, keepdims=False) for x in range(span)]
    wall_grad = functools.reduce(jnp.add, parts).transpose(1, 0, 2, 3)

    cuts = [0, span // 2, 3 * span // 4, span]
    for low_cut, high_cut in zip(cuts, cuts[1:]):
        partners = range(low_cut, high_cut)
        result = add_rest(result, returned[low_cut:high_cut], partners, spots, rest_pieces)
    return (result.reshape(field.shape), wall_grad)


def solution(mesh):
    return jax.shard_map(
        on_device,
        mesh=mesh,
        in_specs=(
            P(None, None, None, "wall", "span"),
            P(None, "wall"),
            P(None, "wall"),
            P(),
            P(),
            P("span"),
        ),
        out_specs=(P(None, None, None, "wall", "span"), P()),
        check_vma=False,
    )
```

```python
import functools
import math

import jax
import jax.numpy as jnp
import numpy as np
from jax import lax
from jax.experimental import pallas as pl
from jax.experimental.pallas import tpu as pltpu
from jax.sharding import PartitionSpec as P

HALO = 7
STEN = 15
PATCH = 64
TAU = 0.25
VIS = 0.5

LANES = 128
OUTER = 48
PAD = 8
TILES = OUTER // 2
FILTER_VMEM = 57_500_000
TABLE_COPIES = 4

QUARTER = (0, 4, 2, 1, 5, 9)
KEPT = tuple(4 * q for q in QUARTER) + tuple(2 + 8 * t for t in range(6)) + tuple(4 * q + 1 for q in range(12))


@functools.cache
def spectral_tables(length):
    signed = np.arange(length)
    signed = np.where(signed > length // 2, signed - length, signed)
    cutoff = length // 3
    ratio = signed.astype(np.float64) / cutoff
    multiplier = np.where(np.abs(signed) < cutoff, -VIS * ratio * ratio, 0.0)
    shift = np.arange(LANES)[None, :] - np.arange(LANES)[:, None]
    inner = np.arange(LANES)

    def complex_table(k1):
        wave = k1 + OUTER * inner
        spots = np.arange(-LANES + 1, LANES)
        phase = np.exp(2j * np.pi * ((wave[:, None] * spots[None, :]) % length) / length)
        return ((multiplier[wave][:, None] * phase).sum(axis=0) / LANES)[shift + LANES - 1]

    tables = np.zeros((TILES, 2 * LANES, 2 * LANES))
    tables[0, :LANES, :LANES] = complex_table(0).real / OUTER
    tables[0, LANES:, LANES:] = complex_table(OUTER // 2).real / OUTER
    for tile, k1 in enumerate(KEPT[1:], 1):
        table = complex_table(k1) * 2.0 / OUTER
        tables[tile, :LANES, :LANES] = table.real
        tables[tile, :LANES, LANES:] = table.imag
        tables[tile, LANES:, :LANES] = -table.imag
        tables[tile, LANES:, LANES:] = table.real
    high = tables.astype(jnp.bfloat16)
    low = (tables - high.astype(np.float64)).astype(jnp.bfloat16)
    return np.stack([high, low], axis=1)


def turn(value, numerator, denominator):
    re, im = value
    numerator %= denominator
    if numerator == 0:
        return value
    if 2 * numerator == denominator:
        return (-re, -im)
    if 4 * numerator == denominator:
        return (-im, re)
    if 4 * numerator == 3 * denominator:
        return (im, -re)
    cos = math.cos(2 * math.pi * numerator / denominator)
    sin = math.sin(2 * math.pi * numerator / denominator)
    return (re * cos - im * sin, re * sin + im * cos)


def add(a, b):
    return (a[0] + b[0], a[1] + b[1])


def sub(a, b):
    return (a[0] - b[0], a[1] - b[1])


ROOT = math.sqrt(3.0) / 2.0


def dft3(x, sign):
    total = add(x[1], x[2])
    other = sub(x[1], x[2])
    middle = (x[0][0] - 0.5 * total[0], x[0][1] - 0.5 * total[1])
    side = (-sign * ROOT * other[1], sign * ROOT * other[0])
    return [add(x[0], total), add(middle, side), sub(middle, side)]


def dft6(x, sign):
    even = dft3([add(x[b], x[b + 3]) for b in range(3)], sign)
    odd = dft3([turn(sub(x[b], x[b + 3]), sign * b, 6) for b in range(3)], sign)
    return [even[0], odd[0], even[1], odd[1], even[2], odd[2]]


def dft12(x, sign):
    out = [None] * 12
    parts = [[], [], [], []]
    for b in range(3):
        a0, a1, a2, a3 = x[b], x[b + 3], x[b + 6], x[b + 9]
        s0, s1, d0, d1 = add(a0, a2), add(a1, a3), sub(a0, a2), turn(sub(a1, a3), sign, 4)
        for r, value in enumerate((add(s0, s1), add(d0, d1), sub(s0, s1), sub(d0, d1))):
            parts[r].append(turn(value, sign * b * r, 12))
    for r in range(4):
        for q, value in enumerate(dft3(parts[r], sign)):
            out[4 * q + r] = value
    return out


def real_forward(x):
    whole, halved, turned = [], [], []
    for b in range(12):
        s0, s1 = x[b] + x[b + 24], x[b + 12] + x[b + 36]
        whole.append(s0 + s1)
        halved.append(s0 - s1)
        turned.append(turn((x[b] - x[b + 24], x[b + 36] - x[b + 12]), -b, 48))
    w, h, t = [], [], []
    for b in range(3):
        s0, s1 = whole[b] + whole[b + 6], whole[b + 3] + whole[b + 9]
        w.append(s0 + s1)
        h.append(s0 - s1)
        t.append(turn((whole[b] - whole[b + 6], whole[b + 9] - whole[b + 3]), -b, 12))
    total, other = w[1] + w[2], w[1] - w[2]
    four = (w[0] - 0.5 * total, -ROOT * other)
    two = (h[0] + 0.5 * (h[1] - h[2]), -ROOT * (h[1] + h[2]))
    tiles = [(w[0] + total, h[0] - h[1] + h[2]), four, two] + dft3(t, -1)
    tiles += dft6([turn((halved[b], -halved[b + 6]), -b, 24) for b in range(6)], -1)
    return tiles + dft12(turned, -1)


def real_backward(tiles):
    (zero, half), four, two = tiles[:3]
    w0 = zero + four[0]
    rest, side = zero - 0.5 * four[0], ROOT * four[1]
    w = [w0, rest - side, rest + side]
    h_side = 0.5 * two[0] - ROOT * two[1]
    h = [two[0] + half, h_side - half, -0.5 * two[0] - ROOT * two[1] + half]
    t = [turn(value, b, 12) for b, value in enumerate(dft3(tiles[3:6], 1))]
    whole = [None] * 12
    for b in range(3):
        s, d = w[b] + h[b], w[b] - h[b]
        whole[b], whole[b + 6] = s + t[b][0], s - t[b][0]
        whole[b + 3], whole[b + 9] = d - t[b][1], d + t[b][1]
    halved = [None] * 12
    for b, value in enumerate(dft6(tiles[6:12], 1)):
        halved[b], halved[b + 6] = turn(value, b, 24)
        halved[b + 6] = -halved[b + 6]
    x = [None] * 48
    for b, value in enumerate(dft12(tiles[12:], 1)):
        re, im = turn(value, b, 48)
        s, d = whole[b] + halved[b], whole[b] - halved[b]
        x[b], x[b + 24] = s + re, s - re
        x[b + 12], x[b + 36] = d - im, d + im
    return x


def group_count(piece):
    return piece[1] * piece[3]


def piece_at(ref, piece):
    return ref.at[:, pl.ds(piece[0], piece[1]), pl.ds(piece[2], piece[3])]


def start_all(copies):
    for copy in copies:
        copy.start()
    return copies


def wait_all(copies):
    for copy in copies:
        copy.wait()


def run_filter(pieces, table_hbm, bring, send, scratch):
    *line_refs, wave_ref, table_ref, table_sems, sems = scratch
    copies = [start_all(bring(i, line_ref, sems)) for i, line_ref in enumerate(line_refs)]
    step = TILES // TABLE_COPIES
    spans = [pl.ds(i * step, step) for i in range(TABLE_COPIES)]
    table_copies = [
        pltpu.make_async_copy(table_hbm.at[span], table_ref.at[span], table_sems.at[i]) for i, span in enumerate(spans)
    ]
    start_all(table_copies)
    offsets = [sum(map(group_count, pieces[:i])) for i in range(len(pieces))]
    per_source = line_refs[0].shape[4] // LANES

    def spot(number):
        return pl.ds(pl.multiple_of(number * PAD, PAD), PAD)

    for piece, line_ref, offset, copy in zip(pieces, line_refs, offsets, copies):
        wait_all(copy)

        def forward(number, _, groups=piece[3], line_ref=line_ref, offset=offset):
            pair, group = number // groups, number % groups
            values = []
            for n1 in range(OUTER):
                lanes = pl.ds(n1 % per_source * LANES, LANES)
                values.append(line_ref[n1 // per_source, pair, group, :, lanes])
            for tile, (re, im) in enumerate(real_forward(values)):
                wave_ref[tile, spot(offset + number), :LANES] = re
                wave_ref[tile, spot(offset + number), LANES:] = im
            return 0

        lax.fori_loop(0, group_count(piece), forward, 0)

    def middle(tile, _):
        value = wave_ref[tile]
        high = value.astype(jnp.bfloat16)
        low = (value - high.astype(jnp.float32)).astype(jnp.bfloat16)
        rows = high.shape[0]
        both = jnp.dot(jnp.concatenate([high, low]), table_ref[tile, 0], preferred_element_type=jnp.float32)
        rest = jnp.dot(high, table_ref[tile, 1], preferred_element_type=jnp.float32)
        wave_ref[tile] = both[:rows] + both[rows:] + rest
        return 0

    for i, copy in enumerate(table_copies):
        copy.wait()
        lax.fori_loop(i * step, (i + 1) * step, middle, 0, unroll=3)

    away = []
    for i, (piece, line_ref, offset) in enumerate(zip(pieces, line_refs, offsets)):

        def backward(number, _, groups=piece[3], line_ref=line_ref, offset=offset):
            pair, group = number // groups, number % groups
            row = spot(offset + number)
            tiles = [(wave_ref[tile, row, :LANES], wave_ref[tile, row, LANES:]) for tile in range(TILES)]
            for n1, value in enumerate(real_backward(tiles)):
                line_ref[n1 // per_source, pair, group, :, pl.ds(n1 % per_source * LANES, LANES)] = value
            return 0

        lax.fori_loop(0, group_count(piece), backward, 0)
        away += start_all(send(i, line_ref))
    wait_all(away)


def gather_kernel(field_hbm, out_hbm, buffer_ref, in_sems, out_sems):
    count, pairs = out_hbm.shape[:2]
    split = field_hbm.shape[2]
    loads, stores = [], []
    for x in range(count):
        for pair in range(pairs):
            source, number = field_hbm.at[x // split, pair, x % split], x * pairs + pair
            loads.append(pltpu.make_async_copy(source, buffer_ref.at[x, pair], in_sems.at[number]))
            stores.append(pltpu.make_async_copy(buffer_ref.at[x, pair], out_hbm.at[x, pair], out_sems.at[number]))
    start_all(loads)
    for load, store in zip(loads, stores):
        load.wait()
        store.start()
    wait_all(stores)


def gather_lines(field, count, pairs):
    anywhere = pl.BlockSpec(memory_space=pl.ANY)
    shape = (count, pairs) + field.shape[3:]
    return pl.pallas_call(
        gather_kernel,
        out_shape=jax.ShapeDtypeStruct(shape, jnp.float32),
        in_specs=[anywhere],
        out_specs=anywhere,
        scratch_shapes=[
            pltpu.VMEM(shape, jnp.float32),
            pltpu.SemaphoreType.DMA((count * pairs,)),
            pltpu.SemaphoreType.DMA((count * pairs,)),
        ],
        compiler_params=pltpu.CompilerParams(vmem_limit_bytes=FILTER_VMEM),
        cost_estimate=pl.CostEstimate(flops=0, bytes_accessed=8 * math.prod(shape), transcendentals=0),
        name="gather_lines",
    )(field)


def filter_first_kernel(pieces, table_hbm, lines_hbm, out_hbm, *scratch):
    *scratch, out_sems = scratch

    def bring(i, line_ref, sems):
        return [pltpu.make_async_copy(piece_at(lines_hbm, pieces[i]), line_ref, sems.at[i])]

    def send(i, line_ref):
        return [pltpu.make_async_copy(line_ref.at[:, :, 0], out_hbm.at[:, i], out_sems.at[i])]

    run_filter(pieces, table_hbm, bring, send, scratch)


def filter_rest_kernel(pieces, me_ref, table_hbm, lines_hbm, field_hbm, *refs):
    count, split, me = lines_hbm.shape[0], field_hbm.shape[2], me_ref[0]
    received, sent, scratch, out_sems = refs[: count - 1], refs[count - 1 : 2 * count - 1], refs[2 * count - 1 : -1], refs[-1]
    places = rest_places(pieces)
    final = len(pieces) - 1

    def bring(i, line_ref, sems):
        if i < final:
            return [pltpu.make_async_copy(piece_at(lines_hbm, pieces[i]), line_ref, sems.at[i])]
        own = field_hbm.at[me // split, pl.ds(pieces[i][0], pieces[i][1]), me % split]
        sources = (own,) + received
        return [pltpu.make_async_copy(sources[x], line_ref.at[me ^ x], sems.at[i + x]) for x in range(count)]

    def send(i, line_ref):
        copies = []
        for pair in range(pieces[i][1]):
            number, first = places[i][pair]
            target = pl.ds(first, pieces[i][3])
            for x in range(count):
                sem = out_sems.at[number * count + x]
                copies.append(pltpu.make_async_copy(line_ref.at[me ^ x, pair], sent[x].at[target], sem))
        return copies

    run_filter(pieces, table_hbm, bring, send, scratch)


def rest_places(pieces):
    places, number, first = [], 0, 0
    for piece in pieces:
        places.append([])
        for _ in range(piece[1]):
            places[-1].append((number, first))
            number, first = number + 1, first + piece[3]
    return places


HBM = pl.BlockSpec(memory_space=pltpu.HBM)
SCALARS = pl.BlockSpec(memory_space=pltpu.SMEM)
WHOLE = pl.BlockSpec(memory_space=pltpu.VMEM)


def filter_call(kernel, name, pieces, lines, tables, in_specs, out_specs, out_shape, sems, flops):
    count, _, _, _, width = lines.shape
    rows = sum(map(group_count, pieces)) * PAD
    return pl.pallas_call(
        functools.partial(kernel, pieces),
        out_shape=out_shape,
        in_specs=in_specs,
        out_specs=out_specs,
        scratch_shapes=[pltpu.VMEM((count, piece[1], piece[3], PAD, width), jnp.float32) for piece in pieces]
        + [
            pltpu.VMEM((TILES, rows, 2 * LANES), jnp.float32),
            pltpu.VMEM(tables.shape, tables.dtype),
            pltpu.SemaphoreType.DMA((TABLE_COPIES,)),
            pltpu.SemaphoreType.DMA((sems[0],)),
            pltpu.SemaphoreType.DMA((sems[1],)),
        ],
        compiler_params=pltpu.CompilerParams(vmem_limit_bytes=FILTER_VMEM),
        cost_estimate=pl.CostEstimate(flops=flops, bytes_accessed=0, transcendentals=0),
        name=name,
    )


def filter_first(lines, tables, pieces):
    count, _, _, _, width = lines.shape
    out_shape = jax.ShapeDtypeStruct((count, len(pieces), 2, PAD, width), jnp.float32)
    sems = (len(pieces), len(pieces))
    call = filter_call(
        filter_first_kernel, "filter_first", pieces, lines, tables, [HBM, HBM], HBM, out_shape, sems, 10**6
    )
    return call(tables, lines)


def filter_rest(lines, field, received, spots, tables, pieces):
    count, _, _, _, width = lines.shape
    shape = (sum(map(group_count, pieces)), PAD, width)
    out_shape = [jax.ShapeDtypeStruct(shape, jnp.float32)] * count
    sems = (len(pieces) - 1 + count, count * sum(piece[1] for piece in pieces))
    ins = [SCALARS] + [HBM] * (count + 2)
    call = filter_call(
        filter_rest_kernel, "filter_rest", pieces, lines, tables, ins, [HBM] * count, out_shape, sems, 10**11
    )
    return call(spots, tables, lines, field, *received)


def local_kernel(rate_ref, coef_ref, flow_ref, field_ref, low_ref, high_ref, out_ref, pad_ref):
    _, comp_count, part_count, row_count, width = field_ref.shape
    pad_ref[:, :, :PAD] = low_ref[0]
    pad_ref[:, :, PAD : PAD + row_count] = field_ref[0]
    pad_ref[:, :, PAD + row_count :] = high_ref[0]
    rate = rate_ref[pl.program_id(0)]

    def column(step, _):
        lanes = pl.ds(pl.multiple_of(step * LANES, LANES), LANES)
        for top in range(0, row_count, PAD):
            rows = pl.ds(top, PAD)
            advect = rate * flow_ref[0, rows, :]
            shear = TAU * flow_ref[1, rows, :]
            centre = [[field_ref[0, c, p, rows, lanes] for p in range(2)] for c in range(comp_count)]
            for c in range(comp_count):
                for p in range(2):
                    total = centre[c][p]
                    total = total - advect * centre[c][1] if p == 0 else total + advect * centre[c][0]
                    if c == 1:
                        total = total - shear * centre[0][p]
                    for offset in range(STEN):
                        near = pad_ref[c, p, pl.ds(top + offset + PAD - HALO, PAD), lanes]
                        total = total + coef_ref[offset, rows, :] * near
                    out_ref[0, c, p, rows, lanes] = total
        return 0

    lax.fori_loop(0, width // LANES, column, 0)


def local_terms(field, low, high, rate, coef, flow):
    mode_count, comp_count, part_count, row_count, width = field.shape
    block = (1, comp_count, part_count, row_count, width)
    edge = (1, comp_count, part_count, PAD, width)

    def by_mode(m):
        return (m, 0, 0, 0, 0)

    return pl.pallas_call(
        local_kernel,
        grid=(mode_count,),
        out_shape=jax.ShapeDtypeStruct(field.shape, jnp.float32),
        in_specs=[
            SCALARS,
            pl.BlockSpec(coef.shape, lambda m: (0, 0, 0)),
            pl.BlockSpec(flow.shape, lambda m: (0, 0, 0)),
            pl.BlockSpec(block, by_mode),
            pl.BlockSpec(edge, by_mode),
            pl.BlockSpec(edge, by_mode),
        ],
        out_specs=pl.BlockSpec(block, by_mode),
        scratch_shapes=[pltpu.VMEM((comp_count, part_count, row_count + 2 * PAD, width), jnp.float32)],
        compiler_params=pltpu.CompilerParams(vmem_limit_bytes=24 << 20),
        cost_estimate=pl.CostEstimate(flops=40 * field.size, bytes_accessed=10 * field.size, transcendentals=0),
        name="local_terms",
    )(rate, coef, flow, field, low, high)


def add_first_kernel(pieces, me_ref, base_hbm, weight_ref, term_hbm, out_hbm, shear_ref, *scratch):
    base_ref, term_ref, base_sems, term_sems = scratch
    count, split, me = term_hbm.shape[0], base_hbm.shape[2], me_ref[0]

    def spot(ref, x, i):
        other = me ^ x
        return ref.at[other // split, pl.ds(0, 2), other % split, pieces[i][2]]

    spots = [(x, i) for x in range(count) for i in range(len(pieces))]
    sem = [base_sems.at[x * len(pieces) + i] for x, i in spots]
    loads = [pltpu.make_async_copy(spot(base_hbm, *at), base_ref.at[at], sem[n]) for n, at in enumerate(spots)]
    stores = [pltpu.make_async_copy(base_ref.at[at], spot(out_hbm, *at), sem[n]) for n, at in enumerate(spots)]
    terms = [pltpu.make_async_copy(term_hbm.at[me ^ x], term_ref.at[x], term_sems.at[x]) for x in range(count)]
    start_all(loads)
    start_all(terms)
    wait_all(terms)
    wait_all(loads)
    for x in range(count):
        base_ref[x] = base_ref[x] + term_ref[x]
        start_all(stores[x * len(pieces) : (x + 1) * len(pieces)])
        for p in range(2):
            shear_ref[me ^ x, p] = jnp.sum(base_ref[x, 0, p] * weight_ref[x, 0][:, :1], axis=0)
            shear_ref[me ^ x, 2 + p] = jnp.sum(base_ref[x, len(pieces) - 1, p] * weight_ref[x, 1][:, :1], axis=0)
    wait_all(stores)


def add_first(base, term, weight, spots, pieces):
    count, width = term.shape[0], term.shape[4]
    buffer = pltpu.VMEM(term.shape, jnp.float32)
    return pl.pallas_call(
        functools.partial(add_first_kernel, pieces),
        out_shape=(
            jax.ShapeDtypeStruct(base.shape, jnp.float32),
            jax.ShapeDtypeStruct((count, 4, width), jnp.float32),
        ),
        in_specs=[SCALARS, HBM, WHOLE, HBM],
        out_specs=(HBM, WHOLE),
        scratch_shapes=[
            buffer,
            buffer,
            pltpu.SemaphoreType.DMA((count * len(pieces),)),
            pltpu.SemaphoreType.DMA((count,)),
        ],
        input_output_aliases={1: 0},
        compiler_params=pltpu.CompilerParams(vmem_limit_bytes=24 << 20),
        cost_estimate=pl.CostEstimate(flops=term.size, bytes_accessed=12 * term.size, transcendentals=0),
        name="add_first",
    )(spots, base, weight, term)


def add_rest_kernel(pieces, partners, me_ref, base_hbm, *refs):
    count = len(partners)
    terms, out_hbm = refs[:count], refs[count]
    base_ref, term_ref, base_sems, term_sems = refs[count + 1 :]
    split, me = base_hbm.shape[2], me_ref[0]
    places = rest_places(pieces)
    spots = []
    for n, x in enumerate(partners):
        for piece, pairs in zip(pieces, places):
            for pair, (number, first) in enumerate(pairs):
                spots.append((n, x, piece[0] + pair, pl.ds(piece[2], piece[3]), pl.ds(first, piece[3])))

    def far(ref, spot):
        other = me ^ spot[1]
        return ref.at[other // split, spot[2], other % split, spot[3]]

    def near(spot):
        return base_ref.at[spot[0], spot[4]]

    loads = [pltpu.make_async_copy(far(base_hbm, at), near(at), base_sems.at[n]) for n, at in enumerate(spots)]
    stores = [pltpu.make_async_copy(near(at), far(out_hbm, at), base_sems.at[n]) for n, at in enumerate(spots)]
    copies = [pltpu.make_async_copy(terms[n], term_ref.at[n], term_sems.at[n]) for n in range(count)]
    start_all(copies)
    start_all(loads)
    wait_all(copies)
    for load, store, at in zip(loads, stores, spots):
        load.wait()
        base_ref[at[0], at[4]] = base_ref[at[0], at[4]] + term_ref[at[0], at[4]]
        store.start()
    wait_all(stores)


def add_rest(base, terms, partners, spots, pieces):
    buffer = pltpu.VMEM((len(terms),) + terms[0].shape, jnp.float32)
    size = len(terms) * terms[0].size
    copies = len(terms) * sum(piece[1] for piece in pieces)
    return pl.pallas_call(
        functools.partial(add_rest_kernel, pieces, partners),
        out_shape=jax.ShapeDtypeStruct(base.shape, jnp.float32),
        in_specs=[SCALARS, HBM] + [HBM] * len(terms),
        out_specs=HBM,
        scratch_shapes=[
            buffer,
            buffer,
            pltpu.SemaphoreType.DMA((copies,)),
            pltpu.SemaphoreType.DMA((len(terms),)),
        ],
        input_output_aliases={1: 0},
        compiler_params=pltpu.CompilerParams(vmem_limit_bytes=24 << 20),
        cost_estimate=pl.CostEstimate(flops=size, bytes_accessed=12 * size, transcendentals=0),
        name="add_rest",
    )(spots, base, *terms)


def after(value, *others):
    return lax.optimization_barrier((value,) + others)[0]


def on_device(field, mean_flow, d2_coef, wall_coef, kx_index, patch_of):
    mode_count, comp_count, part_count, row_count, width = field.shape
    span = lax.axis_size("span")
    me = lax.axis_index("span")
    wall_count = lax.axis_size("wall")
    wall_index = lax.axis_index("wall")
    mode_split = math.gcd(span, mode_count)
    row_split = span // mode_split
    line_rows = row_count // row_split
    tables = jnp.asarray(spectral_tables(width * span))
    pairs = [[(i, i ^ x) for i in range(span)] for x in range(span)]
    spots = jnp.stack([me]).astype(jnp.int32)

    def exchange(lines):
        return lax.all_to_all(lines, "span", split_axis=0, concat_axis=0)

    def swap(blocks):
        return [lax.ppermute(blocks[x], "span", pairs[x]) for x in range(span - 1, 0, -1)][::-1]

    pairs_count, groups = comp_count * part_count, line_rows // PAD
    shares = (mode_split, pairs_count, row_split, groups, PAD, width)
    shared = field.reshape(shares)
    last = pairs_count - part_count
    lines = exchange(gather_lines(shared, span, last))

    first_pieces = tuple((0, 2, group, 1) for group in range(groups))
    rest_pieces = tuple((2 * comp, 2, 0, groups) for comp in range(1, comp_count))

    forward = [(i, i + 1) for i in range(wall_count - 1)]
    backward = [(i + 1, i) for i in range(wall_count - 1)]
    low = lax.ppermute(field[:, :, :, row_count - PAD :], "wall", forward)
    high = lax.ppermute(field[:, :, :, :PAD], "wall", backward)

    rate = kx_index.astype(jnp.float32) * (0.25 * TAU)
    coef = jnp.broadcast_to(d2_coef[:, :, None], (STEN, row_count, LANES))
    flow = jnp.broadcast_to(mean_flow[:, :, None], (2, row_count, LANES))
    base = local_terms(field, low, high, rate, coef, flow)

    def last_block(x):
        other = me ^ x
        start = (other // row_split, last, other % row_split, 0, 0, 0)
        block = lax.dynamic_slice(shared, start, (1, part_count, 1, groups, PAD, width))
        return block.reshape(part_count, groups, PAD, width)

    blocks = tuple(last_block(x) for x in range(1, span))
    received = swap((None,) + lax.optimization_barrier((blocks, base))[0])
    lines = after(lines, base)
    filtered = filter_first(lines, tables, first_pieces)
    back = exchange(filtered)
    received[0] = after(received[0], filtered)
    sent = filter_rest(lines, shared, received, spots, tables, rest_pieces)
    returned = [sent[0]] + swap(sent)

    lower = jnp.where(wall_index == 0, wall_coef[0], 0.0)
    upper = jnp.where(wall_index == wall_count - 1, wall_coef[1, ::-1], 0.0)
    group = ((me ^ jnp.arange(span)) % row_split)[:, None]
    ends = [jnp.where(group == 0, lower, 0.0), jnp.where(group == row_split - 1, upper, 0.0)]
    weight = jnp.broadcast_to(jnp.stack(ends, axis=1)[..., None], (span, 2, PAD, LANES))
    result, shear = add_first(base.reshape(shares), back, weight, spots, first_pieces)
    onehot = (patch_of[:, None] == jnp.arange(PATCH, dtype=jnp.int32)[None, :]).astype(jnp.float32)
    grad = jnp.einsum("swz,zq->swq", shear, onehot, precision=lax.Precision.HIGHEST)
    grad = grad.reshape(mode_count, row_split, 2, part_count, PATCH).sum(axis=1)
    distance = 1
    while distance < wall_count:
        grad = grad + lax.ppermute(grad, "wall", [(i, i ^ distance) for i in range(wall_count)])
        distance *= 2
    parts = jnp.stack([grad] + swap([grad] * span))
    parts = [lax.dynamic_index_in_dim(parts, me ^ x, 0, keepdims=False) for x in range(span)]
    wall_grad = functools.reduce(jnp.add, parts).transpose(1, 0, 2, 3)

    cuts = [0, span // 2, 3 * span // 4, span]
    for low_cut, high_cut in zip(cuts, cuts[1:]):
        partners = range(low_cut, high_cut)
        result = add_rest(result, returned[low_cut:high_cut], partners, spots, rest_pieces)
    return (result.reshape(field.shape), wall_grad)


def solution(mesh):
    return jax.shard_map(
        on_device,
        mesh=mesh,
        in_specs=(
            P(None, None, None, "wall", "span"),
            P(None, "wall"),
            P(None, "wall"),
            P(),
            P(),
            P("span"),
        ),
        out_specs=(P(None, None, None, "wall", "span"), P()),
        check_vma=False,
    )
```

```python
import functools
import math

import jax
import jax.numpy as jnp
import numpy as np
from jax import lax
from jax.experimental import pallas as pl
from jax.experimental.pallas import tpu as pltpu
from jax.sharding import PartitionSpec as P

HALO = 7
STEN = 15
PATCH = 64
TAU = 0.25
VIS = 0.5

LANES = 128
OUTER = 48
PAD = 8
TILES = OUTER // 2
FILTER_VMEM = 57_500_000
TABLE_COPIES = 4

QUARTER = (0, 4, 2, 1, 5, 9)
KEPT = tuple(4 * q for q in QUARTER) + tuple(2 + 8 * t for t in range(6)) + tuple(4 * q + 1 for q in range(12))


@functools.cache
def spectral_tables(length):
    signed = np.arange(length)
    signed = np.where(signed > length // 2, signed - length, signed)
    cutoff = length // 3
    ratio = signed.astype(np.float64) / cutoff
    multiplier = np.where(np.abs(signed) < cutoff, -VIS * ratio * ratio, 0.0)
    shift = np.arange(LANES)[None, :] - np.arange(LANES)[:, None]
    inner = np.arange(LANES)

    def complex_table(k1):
        wave = k1 + OUTER * inner
        spots = np.arange(-LANES + 1, LANES)
        phase = np.exp(2j * np.pi * ((wave[:, None] * spots[None, :]) % length) / length)
        return ((multiplier[wave][:, None] * phase).sum(axis=0) / LANES)[shift + LANES - 1]

    tables = np.zeros((TILES, 2 * LANES, 2 * LANES))
    tables[0, :LANES, :LANES] = complex_table(0).real / OUTER
    tables[0, LANES:, LANES:] = complex_table(OUTER // 2).real / OUTER
    for tile, k1 in enumerate(KEPT[1:], 1):
        table = complex_table(k1) * 2.0 / OUTER
        tables[tile, :LANES, :LANES] = table.real
        tables[tile, :LANES, LANES:] = table.imag
        tables[tile, LANES:, :LANES] = -table.imag
        tables[tile, LANES:, LANES:] = table.real
    high = tables.astype(jnp.bfloat16)
    low = (tables - high.astype(np.float64)).astype(jnp.bfloat16)
    return np.stack([high, low], axis=1)


def turn(value, numerator, denominator):
    re, im = value
    numerator %= denominator
    if numerator == 0:
        return value
    if 2 * numerator == denominator:
        return (-re, -im)
    if 4 * numerator == denominator:
        return (-im, re)
    if 4 * numerator == 3 * denominator:
        return (im, -re)
    cos = math.cos(2 * math.pi * numerator / denominator)
    sin = math.sin(2 * math.pi * numerator / denominator)
    return (re * cos - im * sin, re * sin + im * cos)


def add(a, b):
    return (a[0] + b[0], a[1] + b[1])


def sub(a, b):
    return (a[0] - b[0], a[1] - b[1])


ROOT = math.sqrt(3.0) / 2.0


def dft3(x, sign):
    total = add(x[1], x[2])
    other = sub(x[1], x[2])
    middle = (x[0][0] - 0.5 * total[0], x[0][1] - 0.5 * total[1])
    side = (-sign * ROOT * other[1], sign * ROOT * other[0])
    return [add(x[0], total), add(middle, side), sub(middle, side)]


def dft6(x, sign):
    even = dft3([add(x[b], x[b + 3]) for b in range(3)], sign)
    odd = dft3([turn(sub(x[b], x[b + 3]), sign * b, 6) for b in range(3)], sign)
    return [even[0], odd[0], even[1], odd[1], even[2], odd[2]]


def dft12(x, sign):
    out = [None] * 12
    parts = [[], [], [], []]
    for b in range(3):
        a0, a1, a2, a3 = x[b], x[b + 3], x[b + 6], x[b + 9]
        s0, s1, d0, d1 = add(a0, a2), add(a1, a3), sub(a0, a2), turn(sub(a1, a3), sign, 4)
        for r, value in enumerate((add(s0, s1), add(d0, d1), sub(s0, s1), sub(d0, d1))):
            parts[r].append(turn(value, sign * b * r, 12))
    for r in range(4):
        for q, value in enumerate(dft3(parts[r], sign)):
            out[4 * q + r] = value
    return out


def real_forward(x):
    whole, halved, turned = [], [], []
    for b in range(12):
        s0, s1 = x[b] + x[b + 24], x[b + 12] + x[b + 36]
        whole.append(s0 + s1)
        halved.append(s0 - s1)
        turned.append(turn((x[b] - x[b + 24], x[b + 36] - x[b + 12]), -b, 48))
    w, h, t = [], [], []
    for b in range(3):
        s0, s1 = whole[b] + whole[b + 6], whole[b + 3] + whole[b + 9]
        w.append(s0 + s1)
        h.append(s0 - s1)
        t.append(turn((whole[b] - whole[b + 6], whole[b + 9] - whole[b + 3]), -b, 12))
    total, other = w[1] + w[2], w[1] - w[2]
    four = (w[0] - 0.5 * total, -ROOT * other)
    two = (h[0] + 0.5 * (h[1] - h[2]), -ROOT * (h[1] + h[2]))
    tiles = [(w[0] + total, h[0] - h[1] + h[2]), four, two] + dft3(t, -1)
    tiles += dft6([turn((halved[b], -halved[b + 6]), -b, 24) for b in range(6)], -1)
    return tiles + dft12(turned, -1)


def real_backward(tiles):
    (zero, half), four, two = tiles[:3]
    w0 = zero + four[0]
    rest, side = zero - 0.5 * four[0], ROOT * four[1]
    w = [w0, rest - side, rest + side]
    h_side = 0.5 * two[0] - ROOT * two[1]
    h = [two[0] + half, h_side - half, -0.5 * two[0] - ROOT * two[1] + half]
    t = [turn(value, b, 12) for b, value in enumerate(dft3(tiles[3:6], 1))]
    whole = [None] * 12
    for b in range(3):
        s, d = w[b] + h[b], w[b] - h[b]
        whole[b], whole[b + 6] = s + t[b][0], s - t[b][0]
        whole[b + 3], whole[b + 9] = d - t[b][1], d + t[b][1]
    halved = [None] * 12
    for b, value in enumerate(dft6(tiles[6:12], 1)):
        halved[b], halved[b + 6] = turn(value, b, 24)
        halved[b + 6] = -halved[b + 6]
    x = [None] * 48
    for b, value in enumerate(dft12(tiles[12:], 1)):
        re, im = turn(value, b, 48)
        s, d = whole[b] + halved[b], whole[b] - halved[b]
        x[b], x[b + 24] = s + re, s - re
        x[b + 12], x[b + 36] = d - im, d + im
    return x


def group_count(piece):
    return piece[1] * piece[3]


def bring_piece(piece, first_pair, me, field_hbm, received, line_ref, sems, start):
    count, split = len(received) + 1, field_hbm.shape[2]
    groups = pl.ds(piece[2], piece[3])
    sources = [field_hbm.at[me // split, pl.ds(piece[0], piece[1]), me % split, groups]]
    sources += [block.at[pl.ds(piece[0] - first_pair, piece[1]), groups] for block in received]
    return [pltpu.make_async_copy(sources[x], line_ref.at[me ^ x], sems.at[start + x]) for x in range(count)]


def start_all(copies):
    for copy in copies:
        copy.start()
    return copies


def wait_all(copies):
    for copy in copies:
        copy.wait()


def run_filter(pieces, table_hbm, bring, send, scratch):
    *line_refs, wave_ref, table_ref, table_sems, sems = scratch
    copies = [start_all(bring(i, line_ref, sems)) for i, line_ref in enumerate(line_refs)]
    step = TILES // TABLE_COPIES
    spans = [pl.ds(i * step, step) for i in range(TABLE_COPIES)]
    table_copies = [
        pltpu.make_async_copy(table_hbm.at[span], table_ref.at[span], table_sems.at[i]) for i, span in enumerate(spans)
    ]
    start_all(table_copies)
    offsets = [sum(map(group_count, pieces[:i])) for i in range(len(pieces))]
    per_source = line_refs[0].shape[4] // LANES

    def spot(number):
        return pl.ds(pl.multiple_of(number * PAD, PAD), PAD)

    for piece, line_ref, offset, copy in zip(pieces, line_refs, offsets, copies):
        wait_all(copy)

        def forward(number, _, groups=piece[3], line_ref=line_ref, offset=offset):
            pair, group = number // groups, number % groups
            values = []
            for n1 in range(OUTER):
                lanes = pl.ds(n1 % per_source * LANES, LANES)
                values.append(line_ref[n1 // per_source, pair, group, :, lanes])
            for tile, (re, im) in enumerate(real_forward(values)):
                wave_ref[tile, spot(offset + number), :LANES] = re
                wave_ref[tile, spot(offset + number), LANES:] = im
            return 0

        lax.fori_loop(0, group_count(piece), forward, 0)

    def middle(tile, _):
        value = wave_ref[tile]
        high = value.astype(jnp.bfloat16)
        low = (value - high.astype(jnp.float32)).astype(jnp.bfloat16)
        rows = high.shape[0]
        both = jnp.dot(jnp.concatenate([high, low]), table_ref[tile, 0], preferred_element_type=jnp.float32)
        rest = jnp.dot(high, table_ref[tile, 1], preferred_element_type=jnp.float32)
        wave_ref[tile] = both[:rows] + both[rows:] + rest
        return 0

    for i, copy in enumerate(table_copies):
        copy.wait()
        lax.fori_loop(i * step, (i + 1) * step, middle, 0, unroll=3)

    away = []
    for i, (piece, line_ref, offset) in enumerate(zip(pieces, line_refs, offsets)):

        def backward(number, _, groups=piece[3], line_ref=line_ref, offset=offset):
            pair, group = number // groups, number % groups
            row = spot(offset + number)
            tiles = [(wave_ref[tile, row, :LANES], wave_ref[tile, row, LANES:]) for tile in range(TILES)]
            for n1, value in enumerate(real_backward(tiles)):
                line_ref[n1 // per_source, pair, group, :, pl.ds(n1 % per_source * LANES, LANES)] = value
            return 0

        lax.fori_loop(0, group_count(piece), backward, 0)
        away += start_all(send(i, line_ref))
    wait_all(away)


def filter_first_kernel(pieces, count, me_ref, table_hbm, field_hbm, *refs):
    received, out_hbm, scratch, out_sems = refs[: count - 1], refs[count - 1], refs[count:-1], refs[-1]

    def bring(i, line_ref, sems):
        return bring_piece(pieces[i], 0, me_ref[0], field_hbm, received, line_ref, sems, i * count)

    def send(i, line_ref):
        return [pltpu.make_async_copy(line_ref.at[:, :, 0], out_hbm.at[:, i], out_sems.at[i])]

    run_filter(pieces, table_hbm, bring, send, scratch)


def filter_rest_kernel(pieces, count, me_ref, table_hbm, field_hbm, *refs):
    main, tail, sent = refs[: count - 1], refs[count - 1 : 2 * count - 2], refs[2 * count - 2 : 3 * count - 2]
    scratch, out_sems, me = refs[3 * count - 2 : -1], refs[-1], me_ref[0]
    places = rest_places(pieces)

    def bring(i, line_ref, sems):
        received, first_pair = (main, 0) if i < len(pieces) - 1 else (tail, pieces[i][0])
        return bring_piece(pieces[i], first_pair, me, field_hbm, received, line_ref, sems, i * count)

    def send(i, line_ref):
        copies = []
        for pair in range(pieces[i][1]):
            number, first = places[i][pair]
            target = pl.ds(first, pieces[i][3])
            for x in range(count):
                sem = out_sems.at[number * count + x]
                copies.append(pltpu.make_async_copy(line_ref.at[me ^ x, pair], sent[x].at[target], sem))
        return copies

    run_filter(pieces, table_hbm, bring, send, scratch)


def rest_places(pieces):
    places, number, first = [], 0, 0
    for piece in pieces:
        places.append([])
        for _ in range(piece[1]):
            places[-1].append((number, first))
            number, first = number + 1, first + piece[3]
    return places


HBM = pl.BlockSpec(memory_space=pltpu.HBM)
SCALARS = pl.BlockSpec(memory_space=pltpu.SMEM)
WHOLE = pl.BlockSpec(memory_space=pltpu.VMEM)


def filter_call(kernel, name, pieces, field, received, spots, tables, out_shape, out_sems, flops):
    count, width = field.shape[0] * field.shape[2], field.shape[5]
    rows = sum(map(group_count, pieces)) * PAD
    return pl.pallas_call(
        functools.partial(kernel, pieces, count),
        out_shape=out_shape,
        in_specs=[SCALARS] + [HBM] * (2 + len(received)),
        out_specs=[HBM] * len(out_shape),
        scratch_shapes=[pltpu.VMEM((count, piece[1], piece[3], PAD, width), jnp.float32) for piece in pieces]
        + [
            pltpu.VMEM((TILES, rows, 2 * LANES), jnp.float32),
            pltpu.VMEM(tables.shape, tables.dtype),
            pltpu.SemaphoreType.DMA((TABLE_COPIES,)),
            pltpu.SemaphoreType.DMA((len(pieces) * count,)),
            pltpu.SemaphoreType.DMA((out_sems,)),
        ],
        compiler_params=pltpu.CompilerParams(vmem_limit_bytes=FILTER_VMEM),
        cost_estimate=pl.CostEstimate(flops=flops, bytes_accessed=0, transcendentals=0),
        name=name,
    )(spots, tables, field, *received)


def filter_first(field, main, spots, tables, pieces):
    out_shape = [jax.ShapeDtypeStruct((len(main) + 1, len(pieces), 2, PAD, field.shape[5]), jnp.float32)]
    return filter_call(
        filter_first_kernel, "filter_first", pieces, field, main, spots, tables, out_shape, len(pieces), 10**6
    )[0]


def filter_rest(field, main, tail, spots, tables, pieces):
    count = len(main) + 1
    shape = (sum(map(group_count, pieces)), PAD, field.shape[5])
    out_shape = [jax.ShapeDtypeStruct(shape, jnp.float32)] * count
    sems = count * sum(piece[1] for piece in pieces)
    received = list(main) + list(tail)
    return filter_call(
        filter_rest_kernel, "filter_rest", pieces, field, received, spots, tables, out_shape, sems, 10**11
    )


def local_kernel(rate_ref, coef_ref, flow_ref, field_ref, low_ref, high_ref, out_ref, pad_ref):
    _, comp_count, part_count, row_count, width = field_ref.shape
    pad_ref[:, :, :PAD] = low_ref[0]
    pad_ref[:, :, PAD : PAD + row_count] = field_ref[0]
    pad_ref[:, :, PAD + row_count :] = high_ref[0]
    rate = rate_ref[pl.program_id(0)]

    def column(step, _):
        lanes = pl.ds(pl.multiple_of(step * LANES, LANES), LANES)
        for top in range(0, row_count, PAD):
            rows = pl.ds(top, PAD)
            advect = rate * flow_ref[0, rows, :]
            shear = TAU * flow_ref[1, rows, :]
            centre = [[field_ref[0, c, p, rows, lanes] for p in range(2)] for c in range(comp_count)]
            for c in range(comp_count):
                for p in range(2):
                    total = centre[c][p]
                    total = total - advect * centre[c][1] if p == 0 else total + advect * centre[c][0]
                    if c == 1:
                        total = total - shear * centre[0][p]
                    for offset in range(STEN):
                        near = pad_ref[c, p, pl.ds(top + offset + PAD - HALO, PAD), lanes]
                        total = total + coef_ref[offset, rows, :] * near
                    out_ref[0, c, p, rows, lanes] = total
        return 0

    lax.fori_loop(0, width // LANES, column, 0)


def local_terms(field, low, high, rate, coef, flow):
    mode_count, comp_count, part_count, row_count, width = field.shape
    block = (1, comp_count, part_count, row_count, width)
    edge = (1, comp_count, part_count, PAD, width)

    def by_mode(m):
        return (m, 0, 0, 0, 0)

    return pl.pallas_call(
        local_kernel,
        grid=(mode_count,),
        out_shape=jax.ShapeDtypeStruct(field.shape, jnp.float32),
        in_specs=[
            SCALARS,
            pl.BlockSpec(coef.shape, lambda m: (0, 0, 0)),
            pl.BlockSpec(flow.shape, lambda m: (0, 0, 0)),
            pl.BlockSpec(block, by_mode),
            pl.BlockSpec(edge, by_mode),
            pl.BlockSpec(edge, by_mode),
        ],
        out_specs=pl.BlockSpec(block, by_mode),
        scratch_shapes=[pltpu.VMEM((comp_count, part_count, row_count + 2 * PAD, width), jnp.float32)],
        compiler_params=pltpu.CompilerParams(vmem_limit_bytes=24 << 20),
        cost_estimate=pl.CostEstimate(flops=10**6, bytes_accessed=0, transcendentals=0),
        name="local_terms",
    )(rate, coef, flow, field, low, high)


def add_first_kernel(pieces, me_ref, base_hbm, weight_ref, term_hbm, out_hbm, shear_ref, *scratch):
    base_ref, term_ref, base_sems, term_sems = scratch
    count, split, me = term_hbm.shape[0], base_hbm.shape[2], me_ref[0]

    def spot(ref, x, i):
        other = me ^ x
        return ref.at[other // split, pl.ds(0, 2), other % split, pieces[i][2]]

    spots = [(x, i) for x in range(count) for i in range(len(pieces))]
    sem = [base_sems.at[x * len(pieces) + i] for x, i in spots]
    loads = [pltpu.make_async_copy(spot(base_hbm, *at), base_ref.at[at], sem[n]) for n, at in enumerate(spots)]
    stores = [pltpu.make_async_copy(base_ref.at[at], spot(out_hbm, *at), sem[n]) for n, at in enumerate(spots)]
    terms = [pltpu.make_async_copy(term_hbm.at[me ^ x], term_ref.at[x], term_sems.at[x]) for x in range(count)]
    start_all(loads)
    start_all(terms)
    wait_all(terms)
    wait_all(loads)
    for x in range(count):
        base_ref[x] = base_ref[x] + term_ref[x]
        start_all(stores[x * len(pieces) : (x + 1) * len(pieces)])
        for p in range(2):
            shear_ref[me ^ x, p] = jnp.sum(base_ref[x, 0, p] * weight_ref[x, 0][:, :1], axis=0)
            shear_ref[me ^ x, 2 + p] = jnp.sum(base_ref[x, len(pieces) - 1, p] * weight_ref[x, 1][:, :1], axis=0)
    wait_all(stores)


def add_first(base, term, weight, spots, pieces):
    count, width = term.shape[0], term.shape[4]
    buffer = pltpu.VMEM(term.shape, jnp.float32)
    return pl.pallas_call(
        functools.partial(add_first_kernel, pieces),
        out_shape=(
            jax.ShapeDtypeStruct(base.shape, jnp.float32),
            jax.ShapeDtypeStruct((count, 4, width), jnp.float32),
        ),
        in_specs=[SCALARS, HBM, WHOLE, HBM],
        out_specs=(HBM, WHOLE),
        scratch_shapes=[
            buffer,
            buffer,
            pltpu.SemaphoreType.DMA((count * len(pieces),)),
            pltpu.SemaphoreType.DMA((count,)),
        ],
        input_output_aliases={1: 0},
        compiler_params=pltpu.CompilerParams(vmem_limit_bytes=24 << 20),
        cost_estimate=pl.CostEstimate(flops=term.size, bytes_accessed=12 * term.size, transcendentals=0),
        name="add_first",
    )(spots, base, weight, term)


def add_rest_kernel(pieces, partners, me_ref, base_hbm, *refs):
    count = len(partners)
    terms, out_hbm = refs[:count], refs[count]
    base_ref, term_ref, base_sems, term_sems = refs[count + 1 :]
    split, me = base_hbm.shape[2], me_ref[0]
    places = rest_places(pieces)
    spots = []
    for n, x in enumerate(partners):
        for piece, pairs in zip(pieces, places):
            for pair, (number, first) in enumerate(pairs):
                spots.append((n, x, piece[0] + pair, pl.ds(piece[2], piece[3]), pl.ds(first, piece[3])))

    def far(ref, spot):
        other = me ^ spot[1]
        return ref.at[other // split, spot[2], other % split, spot[3]]

    def near(spot):
        return base_ref.at[spot[0], spot[4]]

    loads = [pltpu.make_async_copy(far(base_hbm, at), near(at), base_sems.at[n]) for n, at in enumerate(spots)]
    stores = [pltpu.make_async_copy(near(at), far(out_hbm, at), base_sems.at[n]) for n, at in enumerate(spots)]
    copies = [pltpu.make_async_copy(terms[n], term_ref.at[n], term_sems.at[n]) for n in range(count)]
    start_all(copies)
    start_all(loads)
    wait_all(copies)
    for load, store, at in zip(loads, stores, spots):
        load.wait()
        base_ref[at[0], at[4]] = base_ref[at[0], at[4]] + term_ref[at[0], at[4]]
        store.start()
    wait_all(stores)


def add_rest(base, terms, partners, spots, pieces):
    buffer = pltpu.VMEM((len(terms),) + terms[0].shape, jnp.float32)
    size = len(terms) * terms[0].size
    copies = len(terms) * sum(piece[1] for piece in pieces)
    return pl.pallas_call(
        functools.partial(add_rest_kernel, pieces, partners),
        out_shape=jax.ShapeDtypeStruct(base.shape, jnp.float32),
        in_specs=[SCALARS, HBM] + [HBM] * len(terms),
        out_specs=HBM,
        scratch_shapes=[
            buffer,
            buffer,
            pltpu.SemaphoreType.DMA((copies,)),
            pltpu.SemaphoreType.DMA((len(terms),)),
        ],
        input_output_aliases={1: 0},
        compiler_params=pltpu.CompilerParams(vmem_limit_bytes=24 << 20),
        cost_estimate=pl.CostEstimate(flops=size, bytes_accessed=12 * size, transcendentals=0),
        name="add_rest",
    )(spots, base, *terms)


def after(value, *others):
    return lax.optimization_barrier((value,) + others)[0]


def on_device(field, mean_flow, d2_coef, wall_coef, kx_index, patch_of):
    mode_count, comp_count, part_count, row_count, width = field.shape
    span = lax.axis_size("span")
    me = lax.axis_index("span")
    wall_count = lax.axis_size("wall")
    wall_index = lax.axis_index("wall")
    mode_split = math.gcd(span, mode_count)
    row_split = span // mode_split
    line_rows = row_count // row_split
    tables = jnp.asarray(spectral_tables(width * span))
    pairs = [[(i, i ^ x) for i in range(span)] for x in range(span)]
    spots = jnp.stack([me]).astype(jnp.int32)

    def exchange(lines):
        return lax.all_to_all(lines, "span", split_axis=0, concat_axis=0)

    def swap(blocks):
        return [lax.ppermute(blocks[x], "span", pairs[x]) for x in range(span - 1, 0, -1)][::-1]

    pairs_count, groups = comp_count * part_count, line_rows // PAD
    shares = (mode_split, pairs_count, row_split, groups, PAD, width)
    shared = field.reshape(shares)
    last = pairs_count - part_count

    def block_of(x, first_pair, pairs_here):
        other = me ^ x
        start = (other // row_split, first_pair, other % row_split, 0, 0, 0)
        block = lax.dynamic_slice(shared, start, (1, pairs_here, 1, groups, PAD, width))
        return block.reshape(pairs_here, groups, PAD, width)

    main = swap([None] + [block_of(x, 0, last) for x in range(1, span)])

    first_pieces = tuple((0, 2, group, 1) for group in range(groups))
    rest_pieces = tuple((2 * comp, 2, 0, groups) for comp in range(1, comp_count))

    forward = [(i, i + 1) for i in range(wall_count - 1)]
    backward = [(i + 1, i) for i in range(wall_count - 1)]
    low = lax.ppermute(field[:, :, :, row_count - PAD :], "wall", forward)
    high = lax.ppermute(field[:, :, :, :PAD], "wall", backward)

    rate = kx_index.astype(jnp.float32) * (0.25 * TAU)
    coef = jnp.broadcast_to(d2_coef[:, :, None], (STEN, row_count, LANES))
    flow = jnp.broadcast_to(mean_flow[:, :, None], (2, row_count, LANES))
    base = local_terms(field, low, high, rate, coef, flow)

    blocks = tuple(block_of(x, last, part_count) for x in range(1, span))
    tail = swap((None,) + lax.optimization_barrier((blocks, base))[0])
    main[0] = after(main[0], base)
    filtered = filter_first(shared, main, spots, tables, first_pieces)
    back = exchange(filtered)
    tail[0] = after(tail[0], filtered)
    sent = filter_rest(shared, main, tail, spots, tables, rest_pieces)
    returned = [sent[0]] + swap(sent)

    lower = jnp.where(wall_index == 0, wall_coef[0], 0.0)
    upper = jnp.where(wall_index == wall_count - 1, wall_coef[1, ::-1], 0.0)
    group = ((me ^ jnp.arange(span)) % row_split)[:, None]
    ends = [jnp.where(group == 0, lower, 0.0), jnp.where(group == row_split - 1, upper, 0.0)]
    weight = jnp.broadcast_to(jnp.stack(ends, axis=1)[..., None], (span, 2, PAD, LANES))
    result, shear = add_first(base.reshape(shares), back, weight, spots, first_pieces)
    onehot = (patch_of[:, None] == jnp.arange(PATCH, dtype=jnp.int32)[None, :]).astype(jnp.float32)
    grad = jnp.einsum("swz,zq->swq", shear, onehot, precision=lax.Precision.HIGHEST)
    grad = grad.reshape(mode_count, row_split, 2, part_count, PATCH).sum(axis=1)
    distance = 1
    while distance < wall_count:
        grad = grad + lax.ppermute(grad, "wall", [(i, i ^ distance) for i in range(wall_count)])
        distance *= 2
    parts = jnp.stack([grad] + swap([grad] * span))
    parts = [lax.dynamic_index_in_dim(parts, me ^ x, 0, keepdims=False) for x in range(span)]
    wall_grad = functools.reduce(jnp.add, parts).transpose(1, 0, 2, 3)

    cuts = [0, span // 2, 3 * span // 4, span]
    for low_cut, high_cut in zip(cuts, cuts[1:]):
        partners = range(low_cut, high_cut)
        result = add_rest(result, returned[low_cut:high_cut], partners, spots, rest_pieces)
    return (result.reshape(field.shape), wall_grad)


def solution(mesh):
    return jax.shard_map(
        on_device,
        mesh=mesh,
        in_specs=(
            P(None, None, None, "wall", "span"),
            P(None, "wall"),
            P(None, "wall"),
            P(),
            P(),
            P("span"),
        ),
        out_specs=(P(None, None, None, "wall", "span"), P()),
        check_vma=False,
    )
```

```python
import functools
import math

import jax
import jax.numpy as jnp
import numpy as np
from jax import lax
from jax.experimental import pallas as pl
from jax.experimental.pallas import tpu as pltpu
from jax.sharding import PartitionSpec as P

HALO = 7
STEN = 15
PATCH = 64
TAU = 0.25
VIS = 0.5

LANES = 128
OUTER = 48
PAD = 8
TILES = OUTER // 2
FILTER_VMEM = 57_500_000
TABLE_COPIES = 4

QUARTER = (0, 4, 2, 1, 5, 9)
KEPT = tuple(4 * q for q in QUARTER) + tuple(2 + 8 * t for t in range(6)) + tuple(4 * q + 1 for q in range(12))


@functools.cache
def spectral_tables(length):
    signed = np.arange(length)
    signed = np.where(signed > length // 2, signed - length, signed)
    cutoff = length // 3
    ratio = signed.astype(np.float64) / cutoff
    multiplier = np.where(np.abs(signed) < cutoff, -VIS * ratio * ratio, 0.0)
    shift = np.arange(LANES)[None, :] - np.arange(LANES)[:, None]
    inner = np.arange(LANES)

    def complex_table(k1):
        wave = k1 + OUTER * inner
        spots = np.arange(-LANES + 1, LANES)
        phase = np.exp(2j * np.pi * ((wave[:, None] * spots[None, :]) % length) / length)
        return ((multiplier[wave][:, None] * phase).sum(axis=0) / LANES)[shift + LANES - 1]

    tables = np.zeros((TILES, 2 * LANES, 2 * LANES))
    tables[0, :LANES, :LANES] = complex_table(0).real / OUTER
    tables[0, LANES:, LANES:] = complex_table(OUTER // 2).real / OUTER
    for tile, k1 in enumerate(KEPT[1:], 1):
        table = complex_table(k1) * 2.0 / OUTER
        tables[tile, :LANES, :LANES] = table.real
        tables[tile, :LANES, LANES:] = table.imag
        tables[tile, LANES:, :LANES] = -table.imag
        tables[tile, LANES:, LANES:] = table.real
    high = tables.astype(jnp.bfloat16)
    low = (tables - high.astype(np.float64)).astype(jnp.bfloat16)
    return np.stack([high, low], axis=1)


def turn(value, numerator, denominator):
    re, im = value
    numerator %= denominator
    if numerator == 0:
        return value
    if 2 * numerator == denominator:
        return (-re, -im)
    if 4 * numerator == denominator:
        return (-im, re)
    if 4 * numerator == 3 * denominator:
        return (im, -re)
    cos = math.cos(2 * math.pi * numerator / denominator)
    sin = math.sin(2 * math.pi * numerator / denominator)
    return (re * cos - im * sin, re * sin + im * cos)


def add(a, b):
    return (a[0] + b[0], a[1] + b[1])


def sub(a, b):
    return (a[0] - b[0], a[1] - b[1])


ROOT = math.sqrt(3.0) / 2.0


def dft3(x, sign):
    total = add(x[1], x[2])
    other = sub(x[1], x[2])
    middle = (x[0][0] - 0.5 * total[0], x[0][1] - 0.5 * total[1])
    side = (-sign * ROOT * other[1], sign * ROOT * other[0])
    return [add(x[0], total), add(middle, side), sub(middle, side)]


def dft6(x, sign):
    even = dft3([add(x[b], x[b + 3]) for b in range(3)], sign)
    odd = dft3([turn(sub(x[b], x[b + 3]), sign * b, 6) for b in range(3)], sign)
    return [even[0], odd[0], even[1], odd[1], even[2], odd[2]]


def dft12(x, sign):
    out = [None] * 12
    parts = [[], [], [], []]
    for b in range(3):
        a0, a1, a2, a3 = x[b], x[b + 3], x[b + 6], x[b + 9]
        s0, s1, d0, d1 = add(a0, a2), add(a1, a3), sub(a0, a2), turn(sub(a1, a3), sign, 4)
        for r, value in enumerate((add(s0, s1), add(d0, d1), sub(s0, s1), sub(d0, d1))):
            parts[r].append(turn(value, sign * b * r, 12))
    for r in range(4):
        for q, value in enumerate(dft3(parts[r], sign)):
            out[4 * q + r] = value
    return out


def real_forward(x):
    whole, halved, turned = [], [], []
    for b in range(12):
        s0, s1 = x[b] + x[b + 24], x[b + 12] + x[b + 36]
        whole.append(s0 + s1)
        halved.append(s0 - s1)
        turned.append(turn((x[b] - x[b + 24], x[b + 36] - x[b + 12]), -b, 48))
    w, h, t = [], [], []
    for b in range(3):
        s0, s1 = whole[b] + whole[b + 6], whole[b + 3] + whole[b + 9]
        w.append(s0 + s1)
        h.append(s0 - s1)
        t.append(turn((whole[b] - whole[b + 6], whole[b + 9] - whole[b + 3]), -b, 12))
    total, other = w[1] + w[2], w[1] - w[2]
    four = (w[0] - 0.5 * total, -ROOT * other)
    two = (h[0] + 0.5 * (h[1] - h[2]), -ROOT * (h[1] + h[2]))
    tiles = [(w[0] + total, h[0] - h[1] + h[2]), four, two] + dft3(t, -1)
    tiles += dft6([turn((halved[b], -halved[b + 6]), -b, 24) for b in range(6)], -1)
    return tiles + dft12(turned, -1)


def real_backward(tiles):
    (zero, half), four, two = tiles[:3]
    w0 = zero + four[0]
    rest, side = zero - 0.5 * four[0], ROOT * four[1]
    w = [w0, rest - side, rest + side]
    h_side = 0.5 * two[0] - ROOT * two[1]
    h = [two[0] + half, h_side - half, -0.5 * two[0] - ROOT * two[1] + half]
    t = [turn(value, b, 12) for b, value in enumerate(dft3(tiles[3:6], 1))]
    whole = [None] * 12
    for b in range(3):
        s, d = w[b] + h[b], w[b] - h[b]
        whole[b], whole[b + 6] = s + t[b][0], s - t[b][0]
        whole[b + 3], whole[b + 9] = d - t[b][1], d + t[b][1]
    halved = [None] * 12
    for b, value in enumerate(dft6(tiles[6:12], 1)):
        halved[b], halved[b + 6] = turn(value, b, 24)
        halved[b + 6] = -halved[b + 6]
    x = [None] * 48
    for b, value in enumerate(dft12(tiles[12:], 1)):
        re, im = turn(value, b, 48)
        s, d = whole[b] + halved[b], whole[b] - halved[b]
        x[b], x[b + 24] = s + re, s - re
        x[b + 12], x[b + 36] = d - im, d + im
    return x


def group_count(piece):
    return piece[1] * piece[3]


def piece_at(ref, piece):
    return ref.at[:, pl.ds(piece[0], piece[1]), pl.ds(piece[2], piece[3])]


def start_all(copies):
    for copy in copies:
        copy.start()
    return copies


def wait_all(copies):
    for copy in copies:
        copy.wait()


def run_filter(pieces, table_hbm, bring, send, scratch):
    *line_refs, wave_ref, table_ref, table_sems, sems = scratch
    copies = [start_all(bring(i, line_ref, sems)) for i, line_ref in enumerate(line_refs)]
    step = TILES // TABLE_COPIES
    spans = [pl.ds(i * step, step) for i in range(TABLE_COPIES)]
    table_copies = [
        pltpu.make_async_copy(table_hbm.at[span], table_ref.at[span], table_sems.at[i]) for i, span in enumerate(spans)
    ]
    start_all(table_copies)
    offsets = [sum(map(group_count, pieces[:i])) for i in range(len(pieces))]
    per_source = line_refs[0].shape[4] // LANES

    def spot(number):
        return pl.ds(pl.multiple_of(number * PAD, PAD), PAD)

    for piece, line_ref, offset, copy in zip(pieces, line_refs, offsets, copies):
        wait_all(copy)

        def forward(number, _, groups=piece[3], line_ref=line_ref, offset=offset):
            pair, group = number // groups, number % groups
            values = []
            for n1 in range(OUTER):
                lanes = pl.ds(n1 % per_source * LANES, LANES)
                values.append(line_ref[n1 // per_source, pair, group, :, lanes])
            for tile, (re, im) in enumerate(real_forward(values)):
                wave_ref[tile, spot(offset + number), :LANES] = re
                wave_ref[tile, spot(offset + number), LANES:] = im
            return 0

        lax.fori_loop(0, group_count(piece), forward, 0)

    def middle(tile, _):
        value = wave_ref[tile]
        high = value.astype(jnp.bfloat16)
        low = (value - high.astype(jnp.float32)).astype(jnp.bfloat16)
        rows = high.shape[0]
        both = jnp.dot(jnp.concatenate([high, low]), table_ref[tile, 0], preferred_element_type=jnp.float32)
        rest = jnp.dot(high, table_ref[tile, 1], preferred_element_type=jnp.float32)
        wave_ref[tile] = both[:rows] + both[rows:] + rest
        return 0

    for i, copy in enumerate(table_copies):
        copy.wait()
        lax.fori_loop(i * step, (i + 1) * step, middle, 0, unroll=3)

    away = []
    for i, (piece, line_ref, offset) in enumerate(zip(pieces, line_refs, offsets)):

        def backward(number, _, groups=piece[3], line_ref=line_ref, offset=offset):
            pair, group = number // groups, number % groups
            row = spot(offset + number)
            tiles = [(wave_ref[tile, row, :LANES], wave_ref[tile, row, LANES:]) for tile in range(TILES)]
            for n1, value in enumerate(real_backward(tiles)):
                line_ref[n1 // per_source, pair, group, :, pl.ds(n1 % per_source * LANES, LANES)] = value
            return 0

        lax.fori_loop(0, group_count(piece), backward, 0)
        away += start_all(send(i, line_ref))
    wait_all(away)


def gather_kernel(field_hbm, out_hbm, buffer_ref, in_sems, out_sems):
    count, pairs = out_hbm.shape[:2]
    split = field_hbm.shape[2]
    loads, stores = [], []
    for x in range(count):
        for pair in range(pairs):
            source, number = field_hbm.at[x // split, pair, x % split], x * pairs + pair
            loads.append(pltpu.make_async_copy(source, buffer_ref.at[x, pair], in_sems.at[number]))
            stores.append(pltpu.make_async_copy(buffer_ref.at[x, pair], out_hbm.at[x, pair], out_sems.at[number]))
    start_all(loads)
    for load, store in zip(loads, stores):
        load.wait()
        store.start()
    wait_all(stores)


def gather_lines(field, count, pairs):
    anywhere = pl.BlockSpec(memory_space=pl.ANY)
    shape = (count, pairs) + field.shape[3:]
    return pl.pallas_call(
        gather_kernel,
        out_shape=jax.ShapeDtypeStruct(shape, jnp.float32),
        in_specs=[anywhere],
        out_specs=anywhere,
        scratch_shapes=[
            pltpu.VMEM(shape, jnp.float32),
            pltpu.SemaphoreType.DMA((count * pairs,)),
            pltpu.SemaphoreType.DMA((count * pairs,)),
        ],
        compiler_params=pltpu.CompilerParams(vmem_limit_bytes=FILTER_VMEM),
        cost_estimate=pl.CostEstimate(flops=0, bytes_accessed=8 * math.prod(shape), transcendentals=0),
        name="gather_lines",
    )(field)


def filter_first_kernel(pieces, table_hbm, lines_hbm, out_hbm, *scratch):
    *scratch, out_sems = scratch

    def bring(i, line_ref, sems):
        return [pltpu.make_async_copy(piece_at(lines_hbm, pieces[i]), line_ref, sems.at[i])]

    def send(i, line_ref):
        return [pltpu.make_async_copy(line_ref.at[:, :, 0], out_hbm.at[:, i], out_sems.at[i])]

    run_filter(pieces, table_hbm, bring, send, scratch)


def filter_rest_kernel(pieces, me_ref, table_hbm, lines_hbm, field_hbm, *refs):
    count, split, me = lines_hbm.shape[0], field_hbm.shape[2], me_ref[0]
    received, sent, scratch, out_sems = refs[: count - 1], refs[count - 1 : 2 * count - 1], refs[2 * count - 1 : -1], refs[-1]
    places = rest_places(pieces)
    final = len(pieces) - 1

    def bring(i, line_ref, sems):
        if i < final:
            return [pltpu.make_async_copy(piece_at(lines_hbm, pieces[i]), line_ref, sems.at[i])]
        own = field_hbm.at[me // split, pl.ds(pieces[i][0], pieces[i][1]), me % split]
        sources = (own,) + received
        return [pltpu.make_async_copy(sources[x], line_ref.at[me ^ x], sems.at[i + x]) for x in range(count)]

    def send(i, line_ref):
        copies = []
        for pair in range(pieces[i][1]):
            number, first = places[i][pair]
            target = pl.ds(first, pieces[i][3])
            for x in range(count):
                sem = out_sems.at[number * count + x]
                copies.append(pltpu.make_async_copy(line_ref.at[me ^ x, pair], sent[x].at[target], sem))
        return copies

    run_filter(pieces, table_hbm, bring, send, scratch)


def rest_places(pieces):
    places, number, first = [], 0, 0
    for piece in pieces:
        places.append([])
        for _ in range(piece[1]):
            places[-1].append((number, first))
            number, first = number + 1, first + piece[3]
    return places


HBM = pl.BlockSpec(memory_space=pltpu.HBM)
SCALARS = pl.BlockSpec(memory_space=pltpu.SMEM)
WHOLE = pl.BlockSpec(memory_space=pltpu.VMEM)


def filter_call(kernel, name, pieces, lines, tables, in_specs, out_specs, out_shape, sems, flops):
    count, _, _, _, width = lines.shape
    rows = sum(map(group_count, pieces)) * PAD
    return pl.pallas_call(
        functools.partial(kernel, pieces),
        out_shape=out_shape,
        in_specs=in_specs,
        out_specs=out_specs,
        scratch_shapes=[pltpu.VMEM((count, piece[1], piece[3], PAD, width), jnp.float32) for piece in pieces]
        + [
            pltpu.VMEM((TILES, rows, 2 * LANES), jnp.float32),
            pltpu.VMEM(tables.shape, tables.dtype),
            pltpu.SemaphoreType.DMA((TABLE_COPIES,)),
            pltpu.SemaphoreType.DMA((sems[0],)),
            pltpu.SemaphoreType.DMA((sems[1],)),
        ],
        compiler_params=pltpu.CompilerParams(vmem_limit_bytes=FILTER_VMEM),
        cost_estimate=pl.CostEstimate(flops=flops, bytes_accessed=0, transcendentals=0),
        name=name,
    )


def filter_first(lines, tables, pieces):
    count, _, _, _, width = lines.shape
    out_shape = jax.ShapeDtypeStruct((count, len(pieces), 2, PAD, width), jnp.float32)
    sems = (len(pieces), len(pieces))
    call = filter_call(
        filter_first_kernel, "filter_first", pieces, lines, tables, [HBM, HBM], HBM, out_shape, sems, 10**6
    )
    return call(tables, lines)


def filter_rest(lines, field, received, spots, tables, pieces):
    count, _, _, _, width = lines.shape
    shape = (sum(map(group_count, pieces)), PAD, width)
    out_shape = [jax.ShapeDtypeStruct(shape, jnp.float32)] * count
    sems = (len(pieces) - 1 + count, count * sum(piece[1] for piece in pieces))
    ins = [SCALARS] + [HBM] * (count + 2)
    call = filter_call(
        filter_rest_kernel, "filter_rest", pieces, lines, tables, ins, [HBM] * count, out_shape, sems, 10**11
    )
    return call(spots, tables, lines, field, *received)


def local_kernel(rate_ref, coef_ref, flow_ref, field_ref, low_ref, high_ref, out_ref, pad_ref):
    _, comp_count, part_count, row_count, width = field_ref.shape
    pad_ref[:, :, :PAD] = low_ref[0]
    pad_ref[:, :, PAD : PAD + row_count] = field_ref[0]
    pad_ref[:, :, PAD + row_count :] = high_ref[0]
    rate = rate_ref[pl.program_id(0)]

    def column(step, _):
        lanes = pl.ds(pl.multiple_of(step * LANES, LANES), LANES)
        for top in range(0, row_count, PAD):
            rows = pl.ds(top, PAD)
            advect = rate * flow_ref[0, rows, :]
            shear = TAU * flow_ref[1, rows, :]
            centre = [[field_ref[0, c, p, rows, lanes] for p in range(2)] for c in range(comp_count)]
            for c in range(comp_count):
                for p in range(2):
                    total = centre[c][p]
                    total = total - advect * centre[c][1] if p == 0 else total + advect * centre[c][0]
                    if c == 1:
                        total = total - shear * centre[0][p]
                    for offset in range(STEN):
                        near = pad_ref[c, p, pl.ds(top + offset + PAD - HALO, PAD), lanes]
                        total = total + coef_ref[offset, rows, :] * near
                    out_ref[0, c, p, rows, lanes] = total
        return 0

    lax.fori_loop(0, width // LANES, column, 0)


def local_terms(field, low, high, rate, coef, flow):
    mode_count, comp_count, part_count, row_count, width = field.shape
    block = (1, comp_count, part_count, row_count, width)
    edge = (1, comp_count, part_count, PAD, width)

    def by_mode(m):
        return (m, 0, 0, 0, 0)

    return pl.pallas_call(
        local_kernel,
        grid=(mode_count,),
        out_shape=jax.ShapeDtypeStruct(field.shape, jnp.float32),
        in_specs=[
            SCALARS,
            pl.BlockSpec(coef.shape, lambda m: (0, 0, 0)),
            pl.BlockSpec(flow.shape, lambda m: (0, 0, 0)),
            pl.BlockSpec(block, by_mode),
            pl.BlockSpec(edge, by_mode),
            pl.BlockSpec(edge, by_mode),
        ],
        out_specs=pl.BlockSpec(block, by_mode),
        scratch_shapes=[pltpu.VMEM((comp_count, part_count, row_count + 2 * PAD, width), jnp.float32)],
        compiler_params=pltpu.CompilerParams(vmem_limit_bytes=24 << 20),
        cost_estimate=pl.CostEstimate(flops=40 * field.size, bytes_accessed=10 * field.size, transcendentals=0),
        name="local_terms",
    )(rate, coef, flow, field, low, high)


def add_first_kernel(pieces, me_ref, base_hbm, weight_ref, term_hbm, out_hbm, shear_ref, *scratch):
    base_ref, term_ref, base_sems, term_sems = scratch
    count, split, me = term_hbm.shape[0], base_hbm.shape[2], me_ref[0]

    def spot(ref, x, i):
        other = me ^ x
        return ref.at[other // split, pl.ds(0, 2), other % split, pieces[i][2]]

    spots = [(x, i) for x in range(count) for i in range(len(pieces))]
    sem = [base_sems.at[x * len(pieces) + i] for x, i in spots]
    loads = [pltpu.make_async_copy(spot(base_hbm, *at), base_ref.at[at], sem[n]) for n, at in enumerate(spots)]
    stores = [pltpu.make_async_copy(base_ref.at[at], spot(out_hbm, *at), sem[n]) for n, at in enumerate(spots)]
    terms = [pltpu.make_async_copy(term_hbm.at[me ^ x], term_ref.at[x], term_sems.at[x]) for x in range(count)]
    start_all(loads)
    start_all(terms)
    wait_all(terms)
    wait_all(loads)
    for x in range(count):
        base_ref[x] = base_ref[x] + term_ref[x]
        start_all(stores[x * len(pieces) : (x + 1) * len(pieces)])
        for p in range(2):
            shear_ref[me ^ x, p] = jnp.sum(base_ref[x, 0, p] * weight_ref[x, 0][:, :1], axis=0)
            shear_ref[me ^ x, 2 + p] = jnp.sum(base_ref[x, len(pieces) - 1, p] * weight_ref[x, 1][:, :1], axis=0)
    wait_all(stores)


def add_first(base, term, weight, spots, pieces):
    count, width = term.shape[0], term.shape[4]
    buffer = pltpu.VMEM(term.shape, jnp.float32)
    return pl.pallas_call(
        functools.partial(add_first_kernel, pieces),
        out_shape=(
            jax.ShapeDtypeStruct(base.shape, jnp.float32),
            jax.ShapeDtypeStruct((count, 4, width), jnp.float32),
        ),
        in_specs=[SCALARS, HBM, WHOLE, HBM],
        out_specs=(HBM, WHOLE),
        scratch_shapes=[
            buffer,
            buffer,
            pltpu.SemaphoreType.DMA((count * len(pieces),)),
            pltpu.SemaphoreType.DMA((count,)),
        ],
        input_output_aliases={1: 0},
        compiler_params=pltpu.CompilerParams(vmem_limit_bytes=24 << 20),
        cost_estimate=pl.CostEstimate(flops=term.size, bytes_accessed=12 * term.size, transcendentals=0),
        name="add_first",
    )(spots, base, weight, term)


def add_rest_kernel(pieces, partners, me_ref, base_hbm, *refs):
    count = len(partners)
    terms, out_hbm = refs[:count], refs[count]
    base_ref, term_ref, base_sems, term_sems = refs[count + 1 :]
    split, me = base_hbm.shape[2], me_ref[0]
    places = rest_places(pieces)
    spots = []
    for n, x in enumerate(partners):
        for piece, pairs in zip(pieces, places):
            for pair, (number, first) in enumerate(pairs):
                spots.append((n, x, piece[0] + pair, pl.ds(piece[2], piece[3]), pl.ds(first, piece[3])))

    def far(ref, spot):
        other = me ^ spot[1]
        return ref.at[other // split, spot[2], other % split, spot[3]]

    def near(spot):
        return base_ref.at[spot[0], spot[4]]

    loads = [pltpu.make_async_copy(far(base_hbm, at), near(at), base_sems.at[n]) for n, at in enumerate(spots)]
    stores = [pltpu.make_async_copy(near(at), far(out_hbm, at), base_sems.at[n]) for n, at in enumerate(spots)]
    copies = [
        pltpu.make_async_copy(terms[at[0]].at[at[4]], term_ref.at[at[0], at[4]], term_sems.at[n])
        for n, at in enumerate(spots)
    ]
    for load, copy in zip(loads, copies):
        load.start()
        copy.start()
    for load, copy, store, at in zip(loads, copies, stores, spots):
        load.wait()
        copy.wait()
        base_ref[at[0], at[4]] = base_ref[at[0], at[4]] + term_ref[at[0], at[4]]
        store.start()
    wait_all(stores)


def add_rest(base, terms, partners, spots, pieces):
    buffer = pltpu.VMEM((len(terms),) + terms[0].shape, jnp.float32)
    size = len(terms) * terms[0].size
    copies = len(terms) * sum(piece[1] for piece in pieces)
    return pl.pallas_call(
        functools.partial(add_rest_kernel, pieces, partners),
        out_shape=jax.ShapeDtypeStruct(base.shape, jnp.float32),
        in_specs=[SCALARS, HBM] + [HBM] * len(terms),
        out_specs=HBM,
        scratch_shapes=[
            buffer,
            buffer,
            pltpu.SemaphoreType.DMA((copies,)),
            pltpu.SemaphoreType.DMA((copies,)),
        ],
        input_output_aliases={1: 0},
        compiler_params=pltpu.CompilerParams(vmem_limit_bytes=24 << 20),
        cost_estimate=pl.CostEstimate(flops=size, bytes_accessed=12 * size, transcendentals=0),
        name="add_rest",
    )(spots, base, *terms)


def after(value, *others):
    return lax.optimization_barrier((value,) + others)[0]


def on_device(field, mean_flow, d2_coef, wall_coef, kx_index, patch_of):
    mode_count, comp_count, part_count, row_count, width = field.shape
    span = lax.axis_size("span")
    me = lax.axis_index("span")
    wall_count = lax.axis_size("wall")
    wall_index = lax.axis_index("wall")
    mode_split = math.gcd(span, mode_count)
    row_split = span // mode_split
    line_rows = row_count // row_split
    tables = jnp.asarray(spectral_tables(width * span))
    pairs = [[(i, i ^ x) for i in range(span)] for x in range(span)]
    spots = jnp.stack([me]).astype(jnp.int32)

    def exchange(lines):
        return lax.all_to_all(lines, "span", split_axis=0, concat_axis=0)

    def swap(blocks):
        return [lax.ppermute(blocks[x], "span", pairs[x]) for x in range(span - 1, 0, -1)][::-1]

    pairs_count, groups = comp_count * part_count, line_rows // PAD
    shares = (mode_split, pairs_count, row_split, groups, PAD, width)
    shared = field.reshape(shares)
    last = pairs_count - part_count
    lines = exchange(gather_lines(shared, span, last))

    first_pieces = tuple((0, 2, group, 1) for group in range(groups))
    rest_pieces = tuple((2 * comp, 2, 0, groups) for comp in range(1, comp_count))

    forward = [(i, i + 1) for i in range(wall_count - 1)]
    backward = [(i + 1, i) for i in range(wall_count - 1)]
    low = lax.ppermute(field[:, :, :, row_count - PAD :], "wall", forward)
    high = lax.ppermute(field[:, :, :, :PAD], "wall", backward)

    rate = kx_index.astype(jnp.float32) * (0.25 * TAU)
    coef = jnp.broadcast_to(d2_coef[:, :, None], (STEN, row_count, LANES))
    flow = jnp.broadcast_to(mean_flow[:, :, None], (2, row_count, LANES))
    base = local_terms(field, low, high, rate, coef, flow)

    def last_block(x):
        other = me ^ x
        start = (other // row_split, last, other % row_split, 0, 0, 0)
        block = lax.dynamic_slice(shared, start, (1, part_count, 1, groups, PAD, width))
        return block.reshape(part_count, groups, PAD, width)

    blocks = tuple(last_block(x) for x in range(1, span))
    received = swap((None,) + lax.optimization_barrier((blocks, base))[0])
    lines = after(lines, base)
    filtered = filter_first(lines, tables, first_pieces)
    back = exchange(filtered)
    received[0] = after(received[0], filtered)
    sent = filter_rest(lines, shared, received, spots, tables, rest_pieces)
    returned = [sent[0]] + swap(sent)

    lower = jnp.where(wall_index == 0, wall_coef[0], 0.0)
    upper = jnp.where(wall_index == wall_count - 1, wall_coef[1, ::-1], 0.0)
    group = ((me ^ jnp.arange(span)) % row_split)[:, None]
    ends = [jnp.where(group == 0, lower, 0.0), jnp.where(group == row_split - 1, upper, 0.0)]
    weight = jnp.broadcast_to(jnp.stack(ends, axis=1)[..., None], (span, 2, PAD, LANES))
    result, shear = add_first(base.reshape(shares), back, weight, spots, first_pieces)
    onehot = (patch_of[:, None] == jnp.arange(PATCH, dtype=jnp.int32)[None, :]).astype(jnp.float32)
    grad = jnp.einsum("swz,zq->swq", shear, onehot, precision=lax.Precision.HIGHEST)
    grad = grad.reshape(mode_count, row_split, 2, part_count, PATCH).sum(axis=1)
    distance = 1
    while distance < wall_count:
        grad = grad + lax.ppermute(grad, "wall", [(i, i ^ distance) for i in range(wall_count)])
        distance *= 2
    parts = jnp.stack([grad] + swap([grad] * span))
    parts = [lax.dynamic_index_in_dim(parts, me ^ x, 0, keepdims=False) for x in range(span)]
    wall_grad = functools.reduce(jnp.add, parts).transpose(1, 0, 2, 3)

    cuts = [0, span // 2, 3 * span // 4, span]
    for low_cut, high_cut in zip(cuts, cuts[1:]):
        partners = range(low_cut, high_cut)
        result = add_rest(result, returned[low_cut:high_cut], partners, spots, rest_pieces)
    return (result.reshape(field.shape), wall_grad)


def solution(mesh):
    return jax.shard_map(
        on_device,
        mesh=mesh,
        in_specs=(
            P(None, None, None, "wall", "span"),
            P(None, "wall"),
            P(None, "wall"),
            P(),
            P(),
            P("span"),
        ),
        out_specs=(P(None, None, None, "wall", "span"), P()),
        check_vma=False,
    )
```
